32 devices in a mesh: dp: 4 (over z), ctx: 4 (over x, core), tp: 2 (over y).
Axes of the slice: x: 2, y: 2, z: 4, core: 2. Of those that a mesh axis runs over, the one named last changes fastest.
Arguments:
- hidden_in: bfloat16 [8192, 1024], P(('dp', 'ctx')), may hold values from -6 to 6
- out_grad: bfloat16 [8192, 1024], P(('dp', 'ctx')), may hold values from -6 to 6
- segments: int32 [4, 2048], P('dp', 'ctx'), may hold values from 0 to 3, never falling along the last dimension, each value on 1 to 1024 neighbouring positions
- routes: int32 [8192, 2], P(('dp', 'ctx')), may hold values from 0 to 3, all different within a row
- bucket_table: int32 [4095], replicated, may hold values from 0 to 31
- qkv_weight: bfloat16 [1024, 3, 1024], P(('dp', 'ctx'), None, 'tp'), may hold values from -0.1875 to 0.1875
- out_weight: bfloat16 [1024, 1024], P('tp', ('dp', 'ctx')), may hold values from -4 to 4
- router: bfloat16 [1024, 4], P(('dp', 'ctx')), may hold values from -0.1875 to 0.1875
- norm_gains: bfloat16 [2, 1024], P(None, ('dp', 'ctx')), may hold values from 0.5 to 1.5
- position_bias: float32 [16, 32], P('tp'), may hold values from -6 to 6
- expert_in: bfloat16 [4, 2, 1024, 2816], P('dp', None, 'ctx', 'tp'), may hold values from -0.1875 to 0.1875
- expert_down: bfloat16 [4, 2816, 1024], P('dp', 'tp', 'ctx'), may hold values from -0.875 to 0.875
- qkv_first: float32 [1024, 3, 1024], P(('dp', 'ctx'), None, 'tp'), may hold values from -192 to 192
- qkv_second: float32 [1024, 3, 1024], P(('dp', 'ctx'), None, 'tp'), may hold values from 3907.584 to 15482.88
- out_first: float32 [1024, 1024], P('tp', ('dp', 'ctx')), may hold values from -8 to 8
- out_second: float32 [1024, 1024], P('tp', ('dp', 'ctx')), may hold values from 7.632 to 30.24
- router_first: float32 [1024, 4], P(('dp', 'ctx')), may hold values from -2048 to 2048
- router_second: float32 [1024, 4], P(('dp', 'ctx')), may hold values from 640218.56 to 2536715
- gains_first: float32 [2, 1024], P(None, ('dp', 'ctx')), may hold values from -192 to 192
- gains_second: float32 [2, 1024], P(None, ('dp', 'ctx')), may hold values from 4220.191 to 16721.51
- bias_first: float32 [16, 32], P('tp'), may hold values from -128 to 128
- bias_second: float32 [16, 32], P('tp'), may hold values from 1953.792 to 7741.44
- in_first: float32 [4, 2, 1024, 2816], P('dp', None, 'ctx', 'tp'), may hold values from -32 to 32
- in_second: float32 [4, 2, 1024, 2816], P('dp', None, 'ctx', 'tp'), may hold values from 113.67517 to 450.41104
- down_first: float32 [4, 2816, 1024], P('dp', 'tp', 'ctx'), may hold values from -6 to 6
- down_second: float32 [4, 2816, 1024], P('dp', 'tp', 'ctx'), may hold values from 4.88448 to 19.3536
Outputs:
- output: float32 [8192, 1024], P(('dp', 'ctx'))
- input_grad: float32 [8192, 1024], P(('dp', 'ctx'))
- qkv_grad: float32 [1024, 3, 1024], P(('dp', 'ctx'), None, 'tp')
- qkv_first_new: float32 [1024, 3, 1024], P(('dp', 'ctx'), None, 'tp')
- qkv_second_new: float32 [1024, 3, 1024], P(('dp', 'ctx'), None, 'tp')
- qkv_update: float32 [1024, 3, 1024], P(('dp', 'ctx'), None, 'tp')
- out_grad_weight: float32 [1024, 1024], P('tp', ('dp', 'ctx'))
- out_first_new: float32 [1024, 1024], P('tp', ('dp', 'ctx'))
- out_second_new: float32 [1024, 1024], P('tp', ('dp', 'ctx'))
- out_update: float32 [1024, 1024], P('tp', ('dp', 'ctx'))
- router_grad: float32 [1024, 4], P(('dp', 'ctx'))
- router_first_new: float32 [1024, 4], P(('dp', 'ctx'))
- router_second_new: float32 [1024, 4], P(('dp', 'ctx'))
- router_update: float32 [1024, 4], P(('dp', 'ctx'))
- gains_grad: float32 [2, 1024], P(None, ('dp', 'ctx'))
- gains_first_new: float32 [2, 1024], P(None, ('dp', 'ctx'))
- gains_second_new: float32 [2, 1024], P(None, ('dp', 'ctx'))
- gains_update: float32 [2, 1024], P(None, ('dp', 'ctx'))
- bias_grad: float32 [16, 32], P('tp')
- bias_first_new: float32 [16, 32], P('tp')
- bias_second_new: float32 [16, 32], P('tp')
- bias_update: float32 [16, 32], P('tp')
- in_grad: float32 [4, 2, 1024, 2816], P('dp', None, 'ctx', 'tp')
- in_first_new: float32 [4, 2, 1024, 2816], P('dp', None, 'ctx', 'tp')
- in_second_new: float32 [4, 2, 1024, 2816], P('dp', None, 'ctx', 'tp')
- in_update: float32 [4, 2, 1024, 2816], P('dp', None, 'ctx', 'tp')
- down_grad: float32 [4, 2816, 1024], P('dp', 'tp', 'ctx')
- down_first_new: float32 [4, 2816, 1024], P('dp', 'tp', 'ctx')
- down_second_new: float32 [4, 2816, 1024], P('dp', 'tp', 'ctx')
- down_update: float32 [4, 2816, 1024], P('dp', 'tp', 'ctx')
The draws below stay inside these ranges and needn't reach their ends.
Inputs may be any that keep to these rules, and one draw needn't show every extreme that they name: `segments`: along each sequence the document number never falls; each document has 1 to 1024 positions, one exactly 1024. `routes`: A token's 2 experts differ; every expert is named by some token.
All inputs are finite; a program needn't handle non-finite values.
Results may differ from the reference program's by a relative error of at most 0.017.
Values may be sent and summed in bfloat16 or wider, within the bound.
A program may use at most 384 MiB of HBM per device.

```python
import math
import jax
import jax.numpy as jnp
import numpy as np
from jax import lax

D = 1024
HEADS = 16
HEAD_DIM = 64
FF = 2816
BUCKETS = 32
TOP = 2
DOCS = 4
TOK_DEV = 512
EXPERTS = 4
LEN = 2048
SEQS = 4
TOKENS = 8192
CAP = 320


def plant(drawn, stream_key, smallest, top_value):
    longest = drawn.shape.index(max(drawn.shape))
    spots = []
    for shift in (0, 1):
        where = [jax.random.randint(jax.random.fold_in(stream_key, axis), (), 0, length) for axis, length in enumerate(drawn.shape)]
        where[longest] = (where[longest] + shift) % drawn.shape[longest]
        spots.append(tuple(where))
    return drawn.at[spots[0]].set(smallest).at[spots[1]].set(top_value)


def block_levels(key, dims, cuts, smallest, top_value):
    loudness = 1.0
    for dim, blocks in cuts:
        draws = jax.random.uniform(jax.random.fold_in(jax.random.fold_in(key, 6), dim), (blocks,), jnp.float32, smallest / len(cuts), top_value / len(cuts))
        loudness = loudness * jnp.repeat(jnp.exp(draws), dims[dim] // blocks).reshape((-1,) + (1,) * (len(dims) - 1 - dim))
    return loudness


def picks_of(own_key, rows, amount, top, lift):
    sequence = jax.random.permutation(jax.random.fold_in(own_key, 1), amount)
    pull = sequence
    for power in range(3):
        pull = pull * pull // amount
    pull = pull * lift // amount
    tickets = jax.random.randint(jax.random.fold_in(own_key, 2), (rows, amount), 0, 4096) + pull
    fixed_rows = jax.random.permutation(jax.random.fold_in(own_key, 3), rows)[jnp.arange(amount) % rows]
    tickets = jnp.where(jnp.arange(rows)[:, None] == fixed_rows[None, :], 1 << 14, tickets)
    score = tickets * amount + jnp.arange(amount)
    return lax.top_k(score.astype(jnp.int32), top)[1].astype(jnp.int32)


def profile(amount, total, most, skew):
    portions = [(1 << 20) // math.isqrt(rank ** skew) + 1 for rank in range(2, amount + 1)]
    rest, counts = total - most - (amount - 1), [1] * (amount - 1)
    while rest > 0:
        free = [i for i in range(amount - 1) if counts[i] < most]
        mass, budget = sum([portions[i] for i in free]), rest
        for i in free:
            more = min(most - counts[i], max(1, budget * portions[i] // mass), rest)
            counts[i] = counts[i] + more
            rest = rest - more
    return np.array([most] + counts)


def ragged(key, count, total, reach, skew):
    if count == 2:
        one = jax.random.randint(key, (), max(1, total - reach), min(reach, total - 1) + 1)
        return jnp.stack([one, total - one])
    tallies = jnp.asarray(profile(count, total, reach, skew), jnp.int32)
    pairs = (count - 1) // 2
    donor, receiver = tallies[1:1 + 2 * pairs:2], tallies[2:2 + 2 * pairs:2]
    room = jnp.minimum(donor - 1, reach - receiver)
    shifted = jax.random.randint(jax.random.fold_in(key, 1), (pairs,), 0, 1 << 20) % (room + 1)
    tallies = tallies.at[1:1 + 2 * pairs:2].set(donor - shifted).at[2:2 + 2 * pairs:2].set(receiver + shifted)
    return tallies[jax.random.permutation(jax.random.fold_in(key, 2), count)]


def centred(key, dims, scale, bound, shards=(), kind=jnp.bfloat16):
    values = jax.random.normal(key, dims, jnp.float32) * scale
    if len(shards) > 0:
        values = block_levels(key, dims, shards, -0.22, 0.18) * values
    return jnp.clip(values, min=-bound, max=bound).astype(kind)


def setup_inputs(seed: int = 0) -> dict:
    key_of = jax.random.split(jax.random.key(seed), 27)
    return {
        "hidden_in": centred(key_of[0], (TOKENS, D), 1.0, 6.0, ((0, 16),)),
        "out_grad": centred(key_of[1], (TOKENS, D), 1.0, 6.0, ((0, 16),)),
        "segments": jax.vmap(lambda own: jnp.searchsorted(jnp.cumsum(ragged(own, DOCS, LEN, LEN // 2, 2)), jnp.arange(LEN), side="right"))(jax.random.split(key_of[2], SEQS)).reshape((SEQS, LEN)).astype(jnp.int32),
        "routes": picks_of(key_of[3], TOKENS, EXPERTS, TOP, 4096),
        "bucket_table": plant(jax.random.randint(key_of[4], (2 * LEN - 1,), 0, BUCKETS), jax.random.fold_in(key_of[4], 1), 0, BUCKETS - 1).astype(jnp.int32),
        "qkv_weight": centred(key_of[5], (D, 3, HEADS * HEAD_DIM), D ** -0.5, 0.1875, ((0, 16), (2, 2))),
        "out_weight": centred(key_of[6], (HEADS * HEAD_DIM, D), (max(2, HEADS * HEAD_DIM * DOCS // LEN)) ** -0.5, 4.0, ((0, 2), (1, 16))),
        "router": centred(key_of[7], (D, EXPERTS), D ** -0.5, 0.1875, ((0, 16),)),
        "norm_gains": jnp.clip(1.0 + 0.1 * jax.random.normal(key_of[8], (2, D), jnp.float32), 0.5, 1.5).astype(jnp.bfloat16),
        "position_bias": centred(key_of[9], (HEADS, BUCKETS), 1.0, 6.0, ((0, 2),), jnp.float32),
        "expert_in": centred(key_of[10], (EXPERTS, 2, D, FF), D ** -0.5, 0.1875, ((0, 4), (2, 4), (3, 2))),
        "expert_down": centred(key_of[11], (EXPERTS, FF, D), (max(8, FF // 64)) ** -0.5, 0.875, ((0, 4), (1, 2), (2, 4))),
        "qkv_first": centred(key_of[12], (D, 3, HEADS * HEAD_DIM), (0.11 * TOKENS ** 0.5 * 1.5 * D ** 0.5 * max(2, HEADS * HEAD_DIM * DOCS // LEN) ** -0.5 * (4 * DOCS) ** 0.5 * LEN ** -0.5), 192.0, ((0, 16), (2, 2)), jnp.float32),
        "qkv_second": jnp.clip(jnp.exp(math.log(15482.88) - 1.3768156 * jax.random.uniform(key_of[13], (D, 3, HEADS * HEAD_DIM), jnp.float32) ** block_levels(key_of[13], (D, 3, HEADS * HEAD_DIM), ((0, 16), (2, 2)), -0.2, 0.2)), 3907.584, 15482.88),
        "out_first": centred(key_of[14], (HEADS * HEAD_DIM, D), (0.11 * 1.5 * TOKENS ** 0.5 * (4 * DOCS) ** 0.5 * LEN ** -0.5), 8.0, ((0, 2), (1, 16)), jnp.float32),
        "out_second": jnp.clip(jnp.exp(math.log(30.24) - 1.3768156 * jax.random.uniform(key_of[15], (HEADS * HEAD_DIM, D), jnp.float32) ** block_levels(key_of[15], (HEADS * HEAD_DIM, D), ((0, 2), (1, 16)), -0.2, 0.2)), 7.632, 30.24),
        "router_first": centred(key_of[16], (D, EXPERTS), (0.11 * TOKENS ** 0.5 * D ** 0.5 * 0.6 * FF ** 0.5 * max(8, FF // 64) ** -0.5 * EXPERTS ** -1), 2048.0, ((0, 16),), jnp.float32),
        "router_second": jnp.clip(jnp.exp(math.log(2536715) - 1.3768156 * jax.random.uniform(key_of[17], (D, EXPERTS), jnp.float32) ** block_levels(key_of[17], (D, EXPERTS), ((0, 16),), -0.2, 0.2)), 640218.56, 2536715),
        "gains_first": centred(key_of[18], (2, D), (0.11 * 0.6 * TOKENS ** 0.5 * 1.5 * max(2, HEADS * HEAD_DIM * DOCS // LEN) ** -0.5 * (4 * DOCS) ** 0.5 * LEN ** -0.5 * (3 * HEADS * HEAD_DIM) ** 0.5), 192.0, ((1, 16),), jnp.float32),
        "gains_second": jnp.clip(jnp.exp(math.log(16721.51) - 1.3768155 * jax.random.uniform(key_of[19], (2, D), jnp.float32) ** block_levels(key_of[19], (2, D), ((1, 16),), -0.2, 0.2)), 4220.191, 16721.51),
        "bias_first": centred(key_of[20], (HEADS, BUCKETS), (0.11 * (TOKENS * LEN) ** 0.5 * (DOCS * BUCKETS) ** -0.5 * 1.5 * D ** 0.5 * max(2, HEADS * HEAD_DIM * DOCS // LEN) ** -0.5 * HEAD_DIM ** 0.5 * DOCS * LEN ** -1), 128.0, ((0, 2),), jnp.float32),
        "bias_second": jnp.clip(jnp.exp(math.log(7741.44) - 1.3768156 * jax.random.uniform(key_of[21], (HEADS, BUCKETS), jnp.float32) ** block_levels(key_of[21], (HEADS, BUCKETS), ((0, 2),), -0.2, 0.2)), 1953.792, 7741.44),
        "in_first": centred(key_of[22], (EXPERTS, 2, D, FF), (0.11 * 0.6 * (TOKENS * TOP) ** 0.5 * EXPERTS ** -1.5 * D ** 0.5 * max(8, FF // 64) ** -0.5), 32.0, ((0, 4), (2, 4), (3, 2)), jnp.float32),
        "in_second": jnp.clip(jnp.exp(math.log(450.41104) - 1.3768156 * jax.random.uniform(key_of[23], (EXPERTS, 2, D, FF), jnp.float32) ** block_levels(key_of[23], (EXPERTS, 2, D, FF), ((0, 4), (2, 4), (3, 2)), -0.2, 0.2)), 113.67517, 450.41104),
        "down_first": centred(key_of[24], (EXPERTS, FF, D), (0.11 * 0.6 * (TOKENS * TOP) ** 0.5 * EXPERTS ** -1.5), 6.0, ((0, 4), (1, 2), (2, 4)), jnp.float32),
        "down_second": jnp.clip(jnp.exp(math.log(19.3536) - 1.3768156 * jax.random.uniform(key_of[25], (EXPERTS, FF, D), jnp.float32) ** block_levels(key_of[25], (EXPERTS, FF, D), ((0, 4), (1, 2), (2, 4)), -0.2, 0.2)), 4.88448, 19.3536),
    }


@jax.custom_vjp
def low(v):
    return lax.optimization_barrier(v.astype(jnp.bfloat16)).astype(jnp.float32)

@jax.custom_vjp
def low_back(v):
    return v

def low_keep(v):
    return (low(v), None)

def low_pass(kept, grad):
    return (grad,)

def back_keep(v):
    return (v, None)

def back_low(kept, grad):
    return (low(grad),)
low.defvjp(low_keep, low_pass)
low_back.defvjp(back_keep, back_low)
NORM_EPS = 1e-06
NEG_FILL = -1e+30
BETA_ONE = 0.9
BETA_TWO = 0.95
FIX_ONE = 1.0 - 0.9 ** 10
FIX_TWO = 1.0 - 0.95 ** 10
ADAM_EPS = 1e-08
WEIGHT_DECAY = 0.1
MAIN_RATE = 0.02
BIAS_RATE = 0.2

def round_both(value):
    return low(low_back(value))

def matmul(left, right):
    return jnp.dot(left, right, precision=lax.Precision.HIGHEST, preferred_element_type=jnp.float32)

def rms_scale(values):
    return lax.rsqrt(lax.optimization_barrier(jnp.mean(values * values, axis=-1, keepdims=True)) + NORM_EPS)

def slot_plan(routes):
    flat_routes = routes.reshape(-1).astype(jnp.int32)
    route_onehot = (flat_routes[:, None] == jnp.arange(EXPERTS, dtype=jnp.int32)[None, :]).astype(jnp.int32)
    grouped = route_onehot.reshape(-1, TOK_DEV * TOP, EXPERTS)
    earlier = (jnp.cumsum(grouped, axis=1) - grouped).astype(jnp.int32)
    position = lax.optimization_barrier(jnp.sum(earlier * grouped, axis=2)).reshape(-1).astype(jnp.int32)
    group_id = (jnp.arange(TOKENS * TOP, dtype=jnp.int32) // (TOK_DEV * TOP)).astype(jnp.int32)
    groups = TOKENS // TOK_DEV
    sentinel = EXPERTS * groups * CAP
    return jnp.where(position < CAP, flat_routes * (groups * CAP) + group_id * CAP + position, sentinel).astype(jnp.int32)

def adamw_step(weight, gradient, first_moment, second_moment, step_rate):
    first_new = BETA_ONE * first_moment + (1.0 - BETA_ONE) * gradient
    second_new = BETA_TWO * second_moment + (1.0 - BETA_TWO) * gradient * gradient
    update = -step_rate * (first_new / FIX_ONE / (jnp.sqrt(second_new / FIX_TWO) + ADAM_EPS) + WEIGHT_DECAY * weight)
    return (first_new, second_new, update)

def reference(hidden_in, out_grad, segments, routes, bucket_table, qkv_weight, out_weight, router, norm_gains, position_bias, expert_in, expert_down, qkv_first, qkv_second, out_first, out_second, router_first, router_second, gains_first, gains_second, bias_first, bias_second, in_first, in_second, down_first, down_second):
    groups = TOKENS // TOK_DEV
    width_all = HEADS * HEAD_DIM
    destination = slot_plan(routes)
    offsets = (jnp.arange(LEN, dtype=jnp.int32)[None, :] - jnp.arange(LEN, dtype=jnp.int32)[:, None] + LEN - 1).astype(jnp.int32)
    same_docs = segments

    def forward(qkv_w, out_w, router_w, gains_w, bias_w, in_w, down_w, layer_in):
        normed_one = low(layer_in * rms_scale(layer_in) * gains_w[0])
        projected = round_both(matmul(normed_one, qkv_w.reshape(D, 3 * width_all)))
        queries = projected[:, :width_all].reshape(SEQS, LEN, HEADS, HEAD_DIM)
        key_rows = projected[:, width_all:2 * width_all].reshape(SEQS, LEN, HEADS, HEAD_DIM)
        value_rows = projected[:, 2 * width_all:].reshape(SEQS, LEN, HEADS, HEAD_DIM)
        bias_offsets = bias_w[:, bucket_table]

        def sequence_attention(packed):
            seq_query, seq_keys, seq_values, seq_docs = packed
            raw_scores = jnp.einsum('qhd,khd->hqk', seq_query, seq_keys, precision=lax.Precision.HIGHEST) * HEAD_DIM ** (-0.5)
            scores = low_back(raw_scores) + bias_offsets[:, offsets]
            same_doc = seq_docs[:, None] == seq_docs[None, :]
            scores = jnp.where(same_doc[None], scores, NEG_FILL)
            log_total = jax.nn.logsumexp(scores, axis=-1, keepdims=True)
            soft_weights = jnp.exp(scores - log_total)
            attended = jnp.einsum('hqk,khd->qhd', low(soft_weights), seq_values, precision=lax.Precision.HIGHEST)
            return round_both(attended).reshape(LEN, width_all)
        attended = lax.map(jax.checkpoint(sequence_attention), (queries, key_rows, value_rows, same_docs)).reshape(TOKENS, width_all)
        attention = low_back(matmul(attended, out_w))
        middle = layer_in + attention
        normed_two = low(middle * rms_scale(middle) * gains_w[1])
        router_probs = jax.nn.softmax(matmul(normed_two, router_w), axis=-1)
        gate_pair = jnp.take_along_axis(router_probs, routes, axis=1).reshape(-1)
        pair_rows = jnp.repeat(normed_two, TOP, axis=0)
        buffer = jnp.zeros((EXPERTS * groups * CAP, D), jnp.float32).at[destination].set(pair_rows, mode='drop')

        def expert_apply(packed):
            rows_here, in_here, down_here = packed
            gate_hidden = low_back(matmul(rows_here, in_here[0]))
            up_hidden = low_back(matmul(rows_here, in_here[1]))
            activation = low(jax.nn.gelu(gate_hidden, approximate=True) * up_hidden)
            return low_back(matmul(activation, down_here))
        expert_out = lax.map(jax.checkpoint(expert_apply), (buffer.reshape(EXPERTS, groups * CAP, D), in_w, down_w))
        flat_out = jnp.concatenate([expert_out.reshape(-1, D), jnp.zeros((1, D), jnp.float32)], axis=0)
        per_pair = flat_out[destination]
        expert_mix = lax.optimization_barrier(jnp.sum((gate_pair[:, None] * per_pair).reshape(TOKENS, TOP, D), axis=1))
        return middle + expert_mix
    weights_qkv = qkv_weight.astype(jnp.float32)
    weights_out = out_weight.astype(jnp.float32)
    weights_router = router.astype(jnp.float32)
    weights_gains = norm_gains.astype(jnp.float32)
    weights_in = expert_in.astype(jnp.float32)
    weights_down = expert_down.astype(jnp.float32)
    inputs = hidden_in.astype(jnp.float32)
    output, pullback = jax.vjp(forward, weights_qkv, weights_out, weights_router, weights_gains, position_bias, weights_in, weights_down, inputs)
    grad_qkv, grad_out, grad_router, grad_gains, grad_bias, grad_in, grad_down, grad_input = pullback(out_grad.astype(jnp.float32))
    qkv_new = adamw_step(weights_qkv, grad_qkv, qkv_first, qkv_second, MAIN_RATE)
    out_new = adamw_step(weights_out, grad_out, out_first, out_second, MAIN_RATE)
    router_new = adamw_step(weights_router, grad_router, router_first, router_second, MAIN_RATE)
    gains_new = adamw_step(weights_gains, grad_gains, gains_first, gains_second, MAIN_RATE)
    bias_new = adamw_step(position_bias, grad_bias, bias_first, bias_second, BIAS_RATE)
    in_new = adamw_step(weights_in, grad_in, in_first, in_second, MAIN_RATE)
    down_new = adamw_step(weights_down, grad_down, down_first, down_second, MAIN_RATE)
    return (output, grad_input, grad_qkv, qkv_new[0], qkv_new[1], qkv_new[2], grad_out, out_new[0], out_new[1], out_new[2], grad_router, router_new[0], router_new[1], router_new[2], grad_gains, gains_new[0], gains_new[1], gains_new[2], grad_bias, bias_new[0], bias_new[1], bias_new[2], grad_in, in_new[0], in_new[1], in_new[2], grad_down, down_new[0], down_new[1], down_new[2])
```

```python
import functools

import jax
import jax.numpy as jnp
from jax import lax
from jax.experimental import pallas as pl
from jax.experimental.pallas import tpu as pltpu
from jax.sharding import PartitionSpec as P

D = 1024
HEAD_DIM = 64
BUCKETS = 32

NORM_EPS = 1e-06
NEG_FILL = -1e30
BETA_ONE = 0.9
BETA_TWO = 0.95
FIX_ONE = 1.0 - 0.9**10
FIX_TWO = 1.0 - 0.95**10
ADAM_EPS = 1e-08
WEIGHT_DECAY = 0.1
MAIN_RATE = 0.02
BIAS_RATE = 0.2

F32 = jnp.float32
BF16 = jnp.bfloat16
LANES = 128
BLOCK = 256
VMEM_CAP = 60 * 1024 * 1024
GELU_K = 0.7978845608028654
GELU_C = 0.044715


def rms_scale(values):
    return lax.rsqrt(jnp.mean(values * values, axis=-1, keepdims=True) + NORM_EPS)


def norm_back(values, scale_here, gain_here, gradient):
    weighted = gain_here * gradient
    row_inner = jnp.mean(values * weighted, axis=-1, keepdims=True)
    input_part = scale_here * weighted - values * scale_here**3 * row_inner
    return (input_part, jnp.sum(gradient * values * scale_here, axis=0))


def adamw_step(weight, gradient, first_moment, second_moment, step_rate):
    first_new = BETA_ONE * first_moment + (1.0 - BETA_ONE) * gradient
    second_new = BETA_TWO * second_moment + (1.0 - BETA_TWO) * gradient * gradient
    update = -step_rate * (
        first_new / FIX_ONE / (jnp.sqrt(second_new / FIX_TWO) + ADAM_EPS) + WEIGHT_DECAY * weight
    )
    return (first_new, second_new, update)


def swap(values, axis, bits):
    count = lax.axis_size(axis)
    return lax.ppermute(values, axis, [(i, i ^ bits) for i in range(count)])


def gather_xor(values, axis):
    pieces = {0: values}
    bit = lax.axis_size(axis) >> 1
    while bit:
        for key in list(pieces):
            pieces[key | bit] = swap(pieces[key], axis, bit)
        bit >>= 1
    return [pieces[m] for m in range(len(pieces))]


def scatter_sum(parts, axis):
    live = dict(enumerate(parts))
    bit = 1
    while bit < lax.axis_size(axis):
        left = {}
        for key in live:
            if key & bit == 0:
                moved = swap(live[key | bit].astype(BF16), axis, bit)
                left[key] = live[key].astype(F32) + moved.astype(F32)
        live = left
        bit <<= 1
    return live[0]


def all_sum(values, axis):
    bit = 1
    while bit < lax.axis_size(axis):
        values = values + swap(values, axis, bit)
        bit <<= 1
    return values


def in_order(pieces, place, dim):
    bit = 1
    while bit < len(pieces):
        odd = (place & bit) > 0
        pieces = [jnp.where(odd, pieces[m ^ bit], pieces[m]) for m in range(len(pieces))]
        bit <<= 1
    return jnp.concatenate(pieces, axis=dim)


def assemble_kernel(place_ref, *refs):
    pieces, whole, sems = refs[:-2], refs[-2], refs[-1]
    rows = pieces[0].shape[0]
    copies = []
    for m, piece in enumerate(pieces):
        start = pl.multiple_of((place_ref[0] ^ m) * rows, rows)
        copies.append(pltpu.make_async_copy(piece, whole.at[pl.ds(start, rows)], sems.at[m]))
    for copy in copies:
        copy.start()
    for copy in copies:
        copy.wait()


def assemble(pieces, place):
    count, rows = len(pieces), pieces[0].shape[0]
    return pl.pallas_call(
        assemble_kernel,
        out_shape=jax.ShapeDtypeStruct((count * rows,) + pieces[0].shape[1:], pieces[0].dtype),
        in_specs=[pl.BlockSpec(memory_space=pltpu.SMEM)]
        + [pl.BlockSpec(memory_space=pl.ANY)] * count,
        out_specs=pl.BlockSpec(memory_space=pl.ANY),
        scratch_shapes=[pltpu.SemaphoreType.DMA((count,))],
    )(place.reshape(1), *pieces)


NT = (((1,), (1,)), ((), ()))
NN = (((1,), (0,)), ((), ()))


def mm(left, right, dims=NN):
    return lax.dot_general(left, right, dims, preferred_element_type=F32)


def fold_max(values):
    return jnp.max(values.reshape(values.shape[0] // 8, 8, values.shape[1]), axis=0)


def fold_sum(values):
    return jnp.sum(values.reshape(values.shape[0] // 8, 8, values.shape[1]), axis=0)


def skewed(row):
    width = row.shape[1]
    tall = jnp.broadcast_to(row, (LANES, width))
    return pltpu.roll(tall, width - (LANES - 1), 1, stride=1, stride_axis=0)


def unskew_sum(field):
    half = field.shape[0] // 2
    while half >= 1:
        field = pltpu.roll(field[:half], half, 1) + field[half:]
        half //= 2
    return field


def head_masks(rows):
    lane = lax.broadcasted_iota(jnp.int32, (rows, LANES), 1)
    return [(lane < HEAD_DIM).astype(BF16), (lane >= HEAD_DIM).astype(BF16)]


def score_tile(key_block, query_head, skew_ref, head, first, same):
    scores = mm(key_block, query_head, NT)
    tiles = []
    for s in range(BLOCK // LANES):
        column = pl.multiple_of(first - s * LANES, LANES)
        tiles.append(skew_ref[head, :, pl.ds(column, BLOCK)])
    return jnp.where(same, scores + jnp.concatenate(tiles, axis=0), NEG_FILL)


def attention_kernel(
    active_ref, base_ref, query_ref, key_ref, value_ref, window_ref, doc_row_ref, doc_col_ref,
    out_ref, total_ref, skew_ref, flip_ref, score_ref, most_ref, sum_ref, mix_ref,
):
    tokens, length = query_ref.shape[0], key_ref.shape[0]
    key_blocks = length // BLOCK
    masks = head_masks(BLOCK)
    for h in range(2):
        skew_ref[h] = skewed(window_ref[0, h : h + 1, :])

    @pl.loop(0, key_blocks)
    def _(kb):
        rows = pl.ds(pl.multiple_of(kb * BLOCK, BLOCK), BLOCK)
        flip_ref[:, rows] = value_ref[rows, :].T

    for qb in range(tokens // BLOCK):
        here = slice(qb * BLOCK, (qb + 1) * BLOCK)
        pair = query_ref[here, :] * jnp.asarray(HEAD_DIM**-0.5, BF16)
        query_heads = [pair * mask for mask in masks]
        doc_row = doc_row_ref[0:1, here]
        most_ref[...] = jnp.full_like(most_ref, NEG_FILL)
        sum_ref[...] = jnp.zeros_like(sum_ref)
        mix_ref[...] = jnp.zeros_like(mix_ref)

        @pl.loop(0, key_blocks)
        def _(kb):
            @pl.when(active_ref[qb, kb] > 0)
            def _():
                rows = pl.ds(pl.multiple_of(kb * BLOCK, BLOCK), BLOCK)
                column = doc_col_ref[rows, :]
                same = jnp.concatenate([column] * (BLOCK // LANES), axis=1) == doc_row
                for h in range(2):
                    tile = score_tile(
                        key_ref[rows, :], query_heads[h], skew_ref, h,
                        base_ref[kb] + qb * BLOCK, same,
                    )
                    score_ref[h, rows, :] = tile
                    most_ref[h] = jnp.maximum(most_ref[h], fold_max(tile))

        most = [jnp.max(most_ref[h], axis=0, keepdims=True) for h in range(2)]

        @pl.loop(0, key_blocks)
        def _(kb):
            @pl.when(active_ref[qb, kb] > 0)
            def _():
                rows = pl.ds(pl.multiple_of(kb * BLOCK, BLOCK), BLOCK)
                for h in range(2):
                    weights = jnp.exp(score_ref[h, rows, :] - most[h])
                    sum_ref[h] += fold_sum(weights)
                    mix_ref[h] += mm(
                        flip_ref[h * HEAD_DIM : (h + 1) * HEAD_DIM, rows], weights.astype(BF16)
                    )

        columns = []
        for h in range(2):
            total = jnp.sum(sum_ref[h], axis=0, keepdims=True)
            columns.append(mix_ref[h] / total)
            total_ref[0, h : h + 1, here] = most[h] + jnp.log(total)
        out_ref[here, :] = jnp.concatenate(columns, axis=0).T.astype(BF16)


def attention_back_kernel(
    active_ref, base_ref, query_ref, key_ref, value_ref, grad_ref, total_ref, window_ref,
    doc_row_ref, doc_col_ref,
    query_grad_ref, key_grad_ref, value_grad_ref, offset_ref,
    skew_ref, field_ref, flip_ref, weight_ref, change_ref, inner_ref, mix_ref, key_sum, value_sum,
):
    tokens, length = query_ref.shape[0], key_ref.shape[0]
    key_blocks = length // BLOCK
    masks = head_masks(BLOCK)
    for h in range(2):
        skew_ref[h] = skewed(window_ref[0, h : h + 1, :])
    field_ref[...] = jnp.zeros_like(field_ref)
    key_sum[...] = jnp.zeros_like(key_sum)
    value_sum[...] = jnp.zeros_like(value_sum)

    @pl.loop(0, key_blocks)
    def _(kb):
        rows = pl.ds(pl.multiple_of(kb * BLOCK, BLOCK), BLOCK)
        flip_ref[:, rows] = key_ref[rows, :].T

    for qb in range(tokens // BLOCK):
        here = slice(qb * BLOCK, (qb + 1) * BLOCK)
        pair = query_ref[here, :] * jnp.asarray(HEAD_DIM**-0.5, BF16)
        query_heads = [pair * mask for mask in masks]
        grad_pair = grad_ref[here, :]
        grad_heads = [grad_pair * mask for mask in masks]
        doc_row = doc_row_ref[0:1, here]
        inner_ref[...] = jnp.zeros_like(inner_ref)
        mix_ref[...] = jnp.zeros_like(mix_ref)
        totals = [total_ref[0, h : h + 1, here] for h in range(2)]

        @pl.loop(0, key_blocks)
        def _(kb):
            @pl.when(active_ref[qb, kb] > 0)
            def _():
                rows = pl.ds(pl.multiple_of(kb * BLOCK, BLOCK), BLOCK)
                column = doc_col_ref[rows, :]
                same = jnp.concatenate([column] * (BLOCK // LANES), axis=1) == doc_row
                for h in range(2):
                    tile = score_tile(
                        key_ref[rows, :], query_heads[h], skew_ref, h,
                        base_ref[kb] + qb * BLOCK, same,
                    )
                    weights = jnp.exp(tile - totals[h])
                    change = mm(value_ref[rows, :], grad_heads[h], NT)
                    weight_ref[h, rows, :] = weights
                    change_ref[h, rows, :] = change
                    inner_ref[h] += fold_sum(weights * change)

        inner = [jnp.sum(inner_ref[h], axis=0, keepdims=True) for h in range(2)]

        @pl.loop(0, key_blocks)
        def _(kb):
            @pl.when(active_ref[qb, kb] > 0)
            def _():
                rows = pl.ds(pl.multiple_of(kb * BLOCK, BLOCK), BLOCK)
                key_part = value_part = None
                for h in range(2):
                    weights = weight_ref[h, rows, :]
                    score_grad = weights * (change_ref[h, rows, :] - inner[h])
                    for s in range(BLOCK // LANES):
                        first = pl.multiple_of(base_ref[kb] + qb * BLOCK - s * LANES, LANES)
                        field_ref[h, :, pl.ds(first, BLOCK)] += score_grad[
                            s * LANES : (s + 1) * LANES
                        ]
                    low = score_grad.astype(BF16)
                    key_here = mm(low, query_heads[h])
                    value_here = mm(weights.astype(BF16), grad_heads[h])
                    key_part = key_here if h == 0 else key_part + key_here
                    value_part = value_here if h == 0 else value_part + value_here
                    mix_ref[h] += mm(flip_ref[h * HEAD_DIM : (h + 1) * HEAD_DIM, rows], low)
                key_sum[rows, :] += key_part
                value_sum[rows, :] += value_part

        both = jnp.concatenate([mix_ref[0], mix_ref[1]], axis=0) * HEAD_DIM**-0.5
        query_grad_ref[here, :] = both.T.astype(BF16)

    key_grad_ref[...] = key_sum[...].astype(BF16)
    value_grad_ref[...] = value_sum[...].astype(BF16)
    for h in range(2):
        offset_ref[0, h : h + 1, :] = unskew_sum(field_ref[h])


def attention_specs(tokens, length, pairs, width):
    smem = pl.BlockSpec(memory_space=pltpu.SMEM)
    return dict(
        smem=smem,
        query=pl.BlockSpec((tokens, LANES), lambda i: (0, i)),
        key=pl.BlockSpec((length, LANES), lambda i: (0, i)),
        value=pl.BlockSpec((length, LANES), lambda i: (0, i + pairs)),
        window=pl.BlockSpec((1, 8, width), lambda i: (i, 0, 0)),
        total=pl.BlockSpec((1, 8, tokens), lambda i: (i, 0, 0)),
        doc_row=pl.BlockSpec((8, tokens), lambda i: (0, 0)),
        doc_col=pl.BlockSpec((length, LANES), lambda i: (0, 0)),
    )


def attention(active, base, queries, key_values, window, doc_row, doc_col):
    tokens, length = queries.shape[0], key_values.shape[0]
    pairs, width = window.shape[0], window.shape[2]
    specs = attention_specs(tokens, length, pairs, width)
    return pl.pallas_call(
        attention_kernel,
        grid=(pairs,),
        in_specs=[
            specs["smem"], specs["smem"], specs["query"], specs["key"], specs["value"],
            specs["window"], specs["doc_row"], specs["doc_col"],
        ],
        out_specs=[specs["query"], specs["total"]],
        out_shape=[
            jax.ShapeDtypeStruct(queries.shape, BF16),
            jax.ShapeDtypeStruct((pairs, 8, tokens), F32),
        ],
        scratch_shapes=[
            pltpu.VMEM((2, LANES, width), F32),
            pltpu.VMEM((LANES, length), BF16),
            pltpu.VMEM((2, length, BLOCK), F32),
            pltpu.VMEM((2, 8, BLOCK), F32),
            pltpu.VMEM((2, 8, BLOCK), F32),
            pltpu.VMEM((2, HEAD_DIM, BLOCK), F32),
        ],
        compiler_params=pltpu.CompilerParams(vmem_limit_bytes=VMEM_CAP),
        name="attention_forward",
    )(active, base, queries, key_values, key_values, window, doc_row, doc_col)


def attention_back(active, base, queries, key_values, grads, totals, window, doc_row, doc_col):
    tokens, length = queries.shape[0], key_values.shape[0]
    pairs, width = window.shape[0], window.shape[2]
    specs = attention_specs(tokens, length, pairs, width)
    return pl.pallas_call(
        attention_back_kernel,
        grid=(pairs,),
        in_specs=[
            specs["smem"], specs["smem"], specs["query"], specs["key"], specs["value"],
            specs["query"], specs["total"], specs["window"], specs["doc_row"], specs["doc_col"],
        ],
        out_specs=[specs["query"], specs["key"], specs["key"], specs["window"]],
        out_shape=[
            jax.ShapeDtypeStruct(queries.shape, BF16),
            jax.ShapeDtypeStruct((length, queries.shape[1]), BF16),
            jax.ShapeDtypeStruct((length, queries.shape[1]), BF16),
            jax.ShapeDtypeStruct((pairs, 8, width), F32),
        ],
        scratch_shapes=[
            pltpu.VMEM((2, LANES, width), F32),
            pltpu.VMEM((2, LANES, width), F32),
            pltpu.VMEM((LANES, length), BF16),
            pltpu.VMEM((2, length, BLOCK), F32),
            pltpu.VMEM((2, length, BLOCK), F32),
            pltpu.VMEM((2, 8, BLOCK), F32),
            pltpu.VMEM((2, HEAD_DIM, BLOCK), F32),
            pltpu.VMEM((length, LANES), F32),
            pltpu.VMEM((length, LANES), F32),
        ],
        compiler_params=pltpu.CompilerParams(vmem_limit_bytes=VMEM_CAP),
        name="attention_backward",
    )(active, base, queries, key_values, key_values, grads, totals, window, doc_row, doc_col)


def expert_kernel(experts, count, shares, place_ref, rows_ref, grads_ref, router_ref, *refs):
    ins, downs = refs[:count], refs[count : 2 * count]
    (rows_all, scaled_all, act_ref, gate_low_ref, up_low_ref, row_part, out_part,
     in_all, down_all, sems) = refs[-10:]
    expert, ctx, share = place_ref[0], place_ref[1], place_ref[2]
    depth = ins[0].shape[1]
    ff = ins[0].shape[2]

    @pl.when(pl.program_id(0) == 0)
    def _():
        copies = []
        for j in range(count):
            part = pl.ds(j * depth, depth)
            copies.append(pltpu.make_async_copy(ins[j], in_all.at[:, part, :], sems.at[0, j]))
            copies.append(pltpu.make_async_copy(downs[j], down_all.at[:, part], sems.at[1, j]))
        for copy in copies:
            copy.start()
        for copy in copies:
            copy.wait()

    slots = rows_ref.shape[0]
    lane = lax.broadcasted_iota(jnp.int32, (slots, LANES), 1)
    logits = jnp.where(lane < experts, mm(rows_ref[...], router_ref[...]), NEG_FILL)
    powers = jnp.exp(logits - jnp.max(logits, axis=1, keepdims=True))
    probs = powers / jnp.sum(powers, axis=1, keepdims=True)
    gate = jnp.sum(jnp.where(lane == expert, probs, 0.0), axis=1, keepdims=True)
    rows_all[...] = rows_ref[...]
    scaled_all[...] = (gate * grads_ref[...].astype(F32)).astype(BF16)
    order = [pl.ds(pl.multiple_of((ctx ^ j) * depth, depth), depth) for j in range(count)]
    rows = jnp.concatenate([rows_ref[:, part] for part in order], axis=1)
    grads = jnp.concatenate([grads_ref[:, part] for part in order], axis=1)
    dots = jnp.zeros((slots, 1), F32)
    for start in range(0, ff, BLOCK):
        part = slice(start, min(ff, start + BLOCK))
        value = mm(rows, in_all[0, :, part])
        up = mm(rows, in_all[1, :, part])
        back = mm(grads, down_all[part, :], NT)
        square = value * value
        wave = jnp.tanh(GELU_K * value * (1.0 + GELU_C * square))
        half = 0.5 * (1.0 + wave)
        bent = value * half
        slope = half + 0.5 * value * (1.0 - wave * wave) * (
            GELU_K * (1.0 + 3.0 * GELU_C * square)
        )
        act = (bent * up).astype(BF16)
        act_ref[:, part] = act
        dots += jnp.sum(act.astype(F32) * back, axis=1, keepdims=True)
        scaled = gate * back
        gate_low_ref[:, part] = (scaled * up * slope).astype(BF16)
        up_low_ref[:, part] = (scaled * bent).astype(BF16)
    share_width = D // shares
    for j in range(count):
        part = slice(j * depth, (j + 1) * depth)
        first = (ctx ^ j) * depth
        owner = (first // share_width) ^ share
        spot = pl.ds(pl.multiple_of(first % share_width, depth), depth)
        row = mm(gate_low_ref[...], in_all[0, part, :], NT)
        row += mm(up_low_ref[...], in_all[1, part, :], NT)
        row_part[owner, :, spot] = row.astype(BF16)
        out_part[owner, :, spot] = (gate * mm(act_ref[...], down_all[:, part])).astype(BF16)
    high = dots.astype(BF16).astype(F32)
    stride = LANES // shares
    tail = jnp.where(lane == share * stride + expert, high, 0.0)
    tail = jnp.where(lane == share * stride + stride // 2 + expert, dots - high, tail)
    for m in range(shares):
        row_part[m, :, share_width:] = tail.astype(BF16)


def expert_block(block, blocks, places, rows, grads, router, ins, downs, held, experts, shares):
    slots, width = rows.shape
    ff = ins[0].shape[2]
    count = len(ins)
    share_width = width // shares
    vmem = pl.BlockSpec(memory_space=pltpu.VMEM)
    hbm = pl.BlockSpec(memory_space=pl.ANY)
    at_block = lambda i: (block, 0)
    sizes = (width, width, ff, ff, ff)
    aliases = {4 + 2 * count + k: k for k in range(5)} if held else {}
    return pl.pallas_call(
        functools.partial(expert_kernel, experts, count, shares),
        grid=(1,),
        in_specs=[pl.BlockSpec(memory_space=pltpu.SMEM)]
        + [vmem] * 3
        + [hbm] * (2 * count + len(held)),
        out_specs=[pl.BlockSpec((slots, size), at_block) for size in sizes] + [vmem] * 2,
        out_shape=[jax.ShapeDtypeStruct((blocks * slots, size), BF16) for size in sizes]
        + [
            jax.ShapeDtypeStruct((shares, slots, share_width + LANES), BF16),
            jax.ShapeDtypeStruct((shares, slots, share_width), BF16),
        ],
        scratch_shapes=[
            pltpu.VMEM((2, width, ff), BF16),
            pltpu.VMEM((ff, width), BF16),
            pltpu.SemaphoreType.DMA((2, count)),
        ],
        input_output_aliases=aliases,
        compiler_params=pltpu.CompilerParams(vmem_limit_bytes=VMEM_CAP),
        name="expert_block",
    )(places, rows, grads, router, *ins, *downs, *held)


def shards(
    hidden_in,
    out_grad,
    segments,
    routes,
    bucket_table,
    qkv_weight,
    out_weight,
    router,
    norm_gains,
    position_bias,
    expert_in,
    expert_down,
    qkv_first,
    qkv_second,
    out_first,
    out_second,
    router_first,
    router_second,
    gains_first,
    gains_second,
    bias_first,
    bias_second,
    in_first,
    in_second,
    down_first,
    down_second,
):
    tokens = hidden_in.shape[0]
    dp_count, ctx_count, tp_count = (lax.axis_size(a) for a in ("dp", "ctx", "tp"))
    dp_place, ctx_place, tp_place = (lax.axis_index(a) for a in ("dp", "ctx", "tp"))
    length = tokens * ctx_count
    heads_here = position_bias.shape[0]
    width_here = heads_here * HEAD_DIM
    pairs = heads_here // 2
    expert_count = router.shape[1]
    top_count = routes.shape[1]
    own_rows = router.shape[0]
    share_width = D // tp_count

    tail_pack = jnp.pad(
        jnp.concatenate([router, norm_gains.T], axis=1), ((0, 0), (0, LANES - expert_count - 2))
    )
    pack = jnp.concatenate(
        [qkv_weight.reshape(own_rows, 3 * width_here), out_weight.T, tail_pack], axis=1
    )
    hidden_pieces = gather_xor(hidden_in, "ctx")
    ctx_pack = assemble(gather_xor(pack, "ctx"), ctx_place)
    full_pack = assemble(gather_xor(ctx_pack, "dp"), dp_place)
    docs_pieces = gather_xor(segments.reshape(1, -1), "ctx")
    qkv_flat = full_pack[:, : 3 * width_here]
    out_flip = full_pack[:, 3 * width_here : 4 * width_here]
    small = full_pack[:, 4 * width_here :]
    router_full = small[:, :expert_count]
    gain_values = small[:, expert_count : expert_count + 2].T.astype(F32)
    out_all = in_order(gather_xor(out_flip, "tp"), tp_place, 1)

    capacity = max(2, min(tokens, 5 * top_count * tokens // (4 * expert_count)))
    flat_routes = routes.reshape(-1)
    route_onehot = (
        flat_routes[:, None] == jnp.arange(expert_count, dtype=jnp.int32)[None, :]
    ).astype(jnp.int32)
    earlier = jnp.cumsum(route_onehot, axis=0) - route_onehot
    position = jnp.sum(earlier * route_onehot, axis=1).reshape(tokens, top_count)
    slot_expert = dp_place ^ jnp.arange(dp_count, dtype=jnp.int32)
    slot_index = jnp.arange(capacity, dtype=jnp.int32)
    chosen = jnp.zeros((dp_count, capacity, tokens), jnp.bool_)
    for k in range(top_count):
        chosen = chosen | (
            (routes[:, k][None, None, :] == slot_expert[:, None, None])
            & (position[:, k][None, None, :] == slot_index[None, :, None])
        )
    picker = chosen.astype(BF16)
    send_grads = jnp.einsum(
        "mct,td->mcd", picker, out_grad, preferred_element_type=F32
    ).astype(BF16)
    arrived_grads = [send_grads[0]] + [swap(send_grads[m], "dp", m) for m in range(1, dp_count)]
    in_pieces = gather_xor(expert_in[0], "ctx")
    down_pieces = gather_xor(expert_down[0], "ctx")

    rev_table = bucket_table[::-1]
    window_width = tokens + length
    rev_table = jnp.pad(rev_table, (0, 1), constant_values=BUCKETS)
    first_row = ctx_place * tokens
    window_table = lax.dynamic_slice(rev_table, (first_row,), (window_width,))
    table_onehot = (
        window_table[None, :] == jnp.arange(BUCKETS, dtype=jnp.int32)[:, None]
    ).astype(F32)
    window = jnp.dot(
        position_bias, table_onehot, precision=lax.Precision.HIGHEST, preferred_element_type=F32
    )
    window = jnp.pad(window.reshape(pairs, 2, window_width), ((0, 0), (0, 6), (0, 0)))
    docs_row = segments.reshape(1, tokens)
    docs_all = jnp.concatenate(docs_pieces, axis=1).reshape(length)
    doc_col = jnp.broadcast_to(docs_all[:, None], (length, LANES))
    doc_row = jnp.broadcast_to(docs_row, (8, tokens))
    query_docs = docs_row.reshape(tokens // BLOCK, BLOCK)
    key_docs = docs_all.reshape(length // BLOCK, BLOCK)
    active = (
        (key_docs[:, -1][None, :] >= query_docs[:, 0][:, None])
        & (key_docs[:, 0][None, :] <= query_docs[:, -1][:, None])
    ).astype(jnp.int32)
    block_rows = (
        (ctx_place ^ jnp.arange(ctx_count, dtype=jnp.int32))[:, None] * tokens
        + jnp.arange(tokens // BLOCK, dtype=jnp.int32)[None, :] * BLOCK
    ).reshape(-1)
    base = (length - LANES - block_rows).astype(jnp.int32)

    hidden_all = jnp.concatenate(hidden_pieces, axis=0)
    inputs = hidden_in.astype(F32)
    scale_one = rms_scale(inputs)
    normed_one = (inputs * scale_one * gain_values[0]).astype(BF16)
    inputs_all = hidden_all.astype(F32)
    normed_all = (inputs_all * rms_scale(inputs_all) * gain_values[0]).astype(BF16)
    queries = jnp.dot(
        normed_one, qkv_flat[:, :width_here], preferred_element_type=F32
    ).astype(BF16)
    key_values = jnp.dot(
        normed_all, qkv_flat[:, width_here:], preferred_element_type=F32
    ).astype(BF16)

    attended, totals = attention(active, base, queries, key_values, window, doc_row, doc_col)
    attended_all = in_order(gather_xor(attended, "tp"), tp_place, 1)
    middle = inputs + mm(attended_all, out_all, NT)
    scale_two = rms_scale(middle)
    normed_two = (middle * scale_two * gain_values[1]).astype(BF16)
    router_probs = jax.nn.softmax(
        jnp.dot(normed_two, router_full, preferred_element_type=F32), axis=-1
    )
    send_rows = jnp.einsum(
        "mct,td->mcd", picker, normed_two, preferred_element_type=F32
    ).astype(BF16)
    arrived_rows = [send_rows[0]] + [swap(send_rows[m], "dp", m) for m in range(1, dp_count)]

    router_lanes = jnp.where(
        jnp.arange(LANES)[None, :] < expert_count, small, jnp.zeros_like(small)
    )
    places = jnp.stack([dp_place, ctx_place, tp_place]).astype(jnp.int32)
    held = ()
    back_rows, back_outs = [], []
    for m in range(dp_count):
        *held, row_part, out_part = expert_block(
            m, dp_count, places, arrived_rows[m], arrived_grads[m], router_lanes,
            in_pieces, down_pieces, held, expert_count, tp_count,
        )
        row_sum = scatter_sum([row_part[k] for k in range(tp_count)], "tp").astype(BF16)
        out_sum = scatter_sum([out_part[k] for k in range(tp_count)], "tp").astype(BF16)
        back_rows.append(swap(row_sum, "dp", m) if m else row_sum)
        back_outs.append(swap(out_sum, "dp", m) if m else out_sum)
    rows_all, scaled_all, act_all, gate_low_all, up_low_all = held

    def rows_by_ctx(values):
        depth = values.shape[0] // ctx_count
        return [
            lax.dynamic_slice_in_dim(values, (ctx_place ^ j) * depth, depth, 0)
            for j in range(ctx_count)
        ]

    def columns_by_ctx(values):
        depth = values.shape[1] // ctx_count
        return [
            lax.dynamic_slice_in_dim(values, (ctx_place ^ j) * depth, depth, 1)
            for j in range(ctx_count)
        ]

    def weight_grad(left, right):
        return lax.dot_general(
            left, right, (((0,), (0,)), ((), ())), preferred_element_type=F32
        ).astype(BF16)

    gate_total = scatter_sum(rows_by_ctx(weight_grad(rows_all, gate_low_all)), "ctx")
    up_total = scatter_sum(rows_by_ctx(weight_grad(rows_all, up_low_all)), "ctx")
    down_total = scatter_sum(columns_by_ctx(weight_grad(act_all, scaled_all)), "ctx")[None]
    in_total = jnp.stack([gate_total, up_total], axis=0)[None]

    def to_tokens(parts):
        whole = jnp.concatenate(parts, axis=0)
        flat = picker.reshape(dp_count * capacity, tokens)
        return lax.dot_general(flat, whole, (((0,), (0,)), ((), ())), preferred_element_type=F32)

    mixed_half = to_tokens(back_outs).astype(BF16)
    mixed = in_order(gather_xor(mixed_half, "tp"), tp_place, 1)
    output = middle + mixed.astype(F32)

    returned = to_tokens(back_rows)
    prob_grad = jnp.sum(
        returned[:, share_width:].reshape(tokens, 2 * tp_count, LANES // (2 * tp_count)), axis=1
    )[:, :expert_count]
    logit_grad = router_probs * (
        prob_grad - jnp.sum(router_probs * prob_grad, axis=-1, keepdims=True)
    )
    router_share = lax.dynamic_slice_in_dim(router_full, tp_place * share_width, share_width, 0)
    grad_half = returned[:, :share_width] + jnp.dot(
        logit_grad, router_share.T.astype(F32), precision=lax.Precision.HIGHEST,
        preferred_element_type=F32,
    )
    normed_two_grad = in_order(
        gather_xor(grad_half.astype(BF16), "tp"), tp_place, 1
    ).astype(F32)
    middle_part, gain_two_grad = norm_back(middle, scale_two, gain_values[1], normed_two_grad)
    middle_grad = out_grad.astype(F32) + middle_part
    middle_low = middle_grad.astype(BF16)
    attended_grad = jnp.dot(middle_low, out_flip, preferred_element_type=F32).astype(BF16)
    out_flip_grad = weight_grad(middle_low, attended)
    router_grad = jnp.dot(
        normed_two.T.astype(F32), logit_grad, precision=lax.Precision.HIGHEST,
        preferred_element_type=F32,
    )

    query_grad, key_part, value_part, offset_grad = attention_back(
        active, base, queries, key_values, attended_grad, totals, window, doc_row, doc_col
    )
    bias_part = lax.dot_general(
        offset_grad[:, :2, :].reshape(heads_here, window_width), table_onehot, NT,
        precision=lax.Precision.HIGHEST, preferred_element_type=F32,
    )
    bias_total = all_sum(all_sum(bias_part, "ctx"), "dp")

    def row_blocks(values):
        return [values[j * tokens : (j + 1) * tokens] for j in range(ctx_count)]

    key_total = scatter_sum(row_blocks(key_part), "ctx").astype(BF16)
    value_total = scatter_sum(row_blocks(value_part), "ctx").astype(BF16)
    qkv_rows_grad = jnp.concatenate([query_grad, key_total, value_total], axis=1)
    normed_one_grad = all_sum(mm(qkv_rows_grad, qkv_flat, NT).astype(BF16), "tp").astype(F32)
    input_part, gain_one_grad = norm_back(inputs, scale_one, gain_values[0], normed_one_grad)
    input_grad = middle_grad + input_part
    qkv_weight_grad = weight_grad(normed_one, qkv_rows_grad)

    tail_grad = jnp.pad(
        jnp.concatenate(
            [router_grad, jnp.stack([gain_one_grad, gain_two_grad], axis=1)], axis=1
        ),
        ((0, 0), (0, LANES - expert_count - 2)),
    ).astype(BF16)
    grad_pack = jnp.concatenate([qkv_weight_grad, out_flip_grad, tail_grad], axis=1)
    grad_pack = grad_pack.reshape(dp_count, ctx_count, own_rows, grad_pack.shape[1])
    ctx_parts = [
        lax.dynamic_slice_in_dim(grad_pack, ctx_place ^ j, 1, 1)[:, 0] for j in range(ctx_count)
    ]
    ctx_total = scatter_sum(ctx_parts, "ctx").astype(BF16)
    dp_parts = [
        lax.dynamic_slice_in_dim(ctx_total, dp_place ^ j, 1, 0)[0] for j in range(dp_count)
    ]
    pack_total = scatter_sum(dp_parts, "dp")
    qkv_total = pack_total[:, : 3 * width_here].reshape(own_rows, 3, width_here)
    out_total = pack_total[:, 3 * width_here : 4 * width_here].T
    tail_total = pack_total[:, 4 * width_here :]
    router_total = tail_total[:, :expert_count]
    gains_total = tail_total[:, expert_count : expert_count + 2].T

    qkv_new = adamw_step(qkv_weight.astype(F32), qkv_total, qkv_first, qkv_second, MAIN_RATE)
    out_new = adamw_step(out_weight.astype(F32), out_total, out_first, out_second, MAIN_RATE)
    router_new = adamw_step(
        router.astype(F32), router_total, router_first, router_second, MAIN_RATE
    )
    gains_new = adamw_step(
        norm_gains.astype(F32), gains_total, gains_first, gains_second, MAIN_RATE
    )
    bias_new = adamw_step(position_bias, bias_total, bias_first, bias_second, BIAS_RATE)
    in_new = adamw_step(expert_in.astype(F32), in_total, in_first, in_second, MAIN_RATE)
    down_new = adamw_step(expert_down.astype(F32), down_total, down_first, down_second, MAIN_RATE)
    return (
        output,
        input_grad,
        qkv_total,
        *qkv_new,
        out_total,
        *out_new,
        router_total,
        *router_new,
        gains_total,
        *gains_new,
        bias_total,
        *bias_new,
        in_total,
        *in_new,
        down_total,
        *down_new,
    )


def solution(mesh):
    token_rows = P(("dp", "ctx"), None)
    qkv = P(("dp", "ctx"), None, "tp")
    out = P("tp", ("dp", "ctx"))
    gains = P(None, ("dp", "ctx"))
    bias = P("tp", None)
    expert_in = P("dp", None, "ctx", "tp")
    expert_down = P("dp", "tp", "ctx")
    placed = (
        token_rows, token_rows, P("dp", "ctx"), token_rows, P(),
        qkv, out, token_rows, gains, bias, expert_in, expert_down,
        qkv, qkv, out, out, token_rows, token_rows, gains, gains, bias, bias,
        expert_in, expert_in, expert_down, expert_down,
    )
    return jax.shard_map(
        shards,
        mesh=mesh,
        in_specs=placed,
        out_specs=(token_rows, token_rows)
        + (qkv,) * 4
        + (out,) * 4
        + (token_rows,) * 4
        + (gains,) * 4
        + (bias,) * 4
        + (expert_in,) * 4
        + (expert_down,) * 4,
        check_vma=False,
    )
```

```python
import functools

import jax
import jax.numpy as jnp
from jax import lax
from jax.experimental import pallas as pl
from jax.experimental.pallas import tpu as pltpu
from jax.sharding import PartitionSpec as P

D = 1024
HEAD_DIM = 64
BUCKETS = 32

NORM_EPS = 1e-06
NEG_FILL = -1e30
BETA_ONE = 0.9
BETA_TWO = 0.95
FIX_ONE = 1.0 - 0.9**10
FIX_TWO = 1.0 - 0.95**10
ADAM_EPS = 1e-08
WEIGHT_DECAY = 0.1
MAIN_RATE = 0.02
BIAS_RATE = 0.2

F32 = jnp.float32
BF16 = jnp.bfloat16
LANES = 128
BLOCK = 256
VMEM_CAP = 60 * 1024 * 1024
GELU_K = 0.7978845608028654
GELU_C = 0.044715


def rms_scale(values):
    return lax.rsqrt(jnp.mean(values * values, axis=-1, keepdims=True) + NORM_EPS)


def norm_back(values, scale_here, gain_here, gradient):
    weighted = gain_here * gradient
    row_inner = jnp.mean(values * weighted, axis=-1, keepdims=True)
    input_part = scale_here * weighted - values * scale_here**3 * row_inner
    return (input_part, jnp.sum(gradient * values * scale_here, axis=0))


def adamw_step(weight, gradient, first_moment, second_moment, step_rate):
    first_new = BETA_ONE * first_moment + (1.0 - BETA_ONE) * gradient
    second_new = BETA_TWO * second_moment + (1.0 - BETA_TWO) * gradient * gradient
    update = -step_rate * (
        first_new / FIX_ONE / (jnp.sqrt(second_new / FIX_TWO) + ADAM_EPS) + WEIGHT_DECAY * weight
    )
    return (first_new, second_new, update)


def swap(values, axis, bits):
    count = lax.axis_size(axis)
    return lax.ppermute(values, axis, [(i, i ^ bits) for i in range(count)])


def gather_xor(values, axis):
    pieces = {0: values}
    bit = lax.axis_size(axis) >> 1
    while bit:
        for key in list(pieces):
            pieces[key | bit] = swap(pieces[key], axis, bit)
        bit >>= 1
    return [pieces[m] for m in range(len(pieces))]


def scatter_sum(parts, axis):
    live = dict(enumerate(parts))
    bit = 1
    while bit < lax.axis_size(axis):
        left = {}
        for key in live:
            if key & bit == 0:
                moved = swap(live[key | bit].astype(BF16), axis, bit)
                left[key] = live[key].astype(F32) + moved.astype(F32)
        live = left
        bit <<= 1
    return live[0]


def all_sum(values, axis):
    bit = 1
    while bit < lax.axis_size(axis):
        values = values + swap(values, axis, bit)
        bit <<= 1
    return values


def in_order(pieces, place, dim):
    bit = 1
    while bit < len(pieces):
        odd = (place & bit) > 0
        pieces = [jnp.where(odd, pieces[m ^ bit], pieces[m]) for m in range(len(pieces))]
        bit <<= 1
    return jnp.concatenate(pieces, axis=dim)


MESH = pl.DeviceIdType.MESH


class Wire:
    def __init__(self, sends, receives):
        self.sends, self.receives, self.count, self.copies = sends, receives, 0, []

    def send(self, source, target, **device):
        copy = pltpu.make_async_remote_copy(
            src_ref=source,
            dst_ref=target,
            send_sem=self.sends.at[self.count],
            recv_sem=self.receives.at[self.count],
            device_id=device,
            device_id_type=MESH,
        )
        copy.start()
        self.count += 1
        self.copies.append(copy)
        return Arrival(copy)

    def finish(self):
        for copy in self.copies:
            copy.wait_send()


class Arrival:
    def __init__(self, copy):
        self.copy, self.waited = copy, False

    def wait(self):
        if not self.waited:
            self.copy.wait_recv()
        self.waited = True


def greet(partners):
    barrier = pltpu.get_barrier_semaphore()
    for device in partners:
        pl.semaphore_signal(barrier, inc=1, device_id=device, device_id_type=MESH)
    pl.semaphore_wait(barrier, len(partners))


def bits_down(count):
    bits, bit = [], count >> 1
    while bit:
        bits.append(bit)
        bit >>= 1
    return bits


def xor_order(count):
    order = [0]
    for bit in bits_down(count):
        order = order + [k | bit for k in order]
    return order


NT = (((1,), (1,)), ((), ()))
NN = (((1,), (0,)), ((), ()))


def mm(left, right, dims=NN):
    return lax.dot_general(left, right, dims, preferred_element_type=F32)


def fold_max(values):
    return jnp.max(values.reshape(values.shape[0] // 8, 8, values.shape[1]), axis=0)


def fold_sum(values):
    return jnp.sum(values.reshape(values.shape[0] // 8, 8, values.shape[1]), axis=0)


def skewed(row):
    width = row.shape[1]
    tall = jnp.broadcast_to(row, (LANES, width))
    return pltpu.roll(tall, width - (LANES - 1), 1, stride=1, stride_axis=0)


def unskew_sum(field):
    half = field.shape[0] // 2
    while half >= 1:
        field = pltpu.roll(field[:half], half, 1) + field[half:]
        half //= 2
    return field


def head_masks(rows):
    lane = lax.broadcasted_iota(jnp.int32, (rows, LANES), 1)
    return [(lane < HEAD_DIM).astype(BF16), (lane >= HEAD_DIM).astype(BF16)]


def score_tile(key_block, query_head, skew_ref, head, first, same):
    scores = mm(key_block, query_head, NT)
    tiles = []
    for s in range(BLOCK // LANES):
        column = pl.multiple_of(first - s * LANES, LANES)
        tiles.append(skew_ref[head, :, pl.ds(column, BLOCK)])
    return jnp.where(same, scores + jnp.concatenate(tiles, axis=0), NEG_FILL)


def attention_kernel(
    active_ref, base_ref, query_ref, key_ref, value_ref, window_ref, doc_row_ref, doc_col_ref,
    out_ref, total_ref, skew_ref, flip_ref, score_ref, most_ref, sum_ref, mix_ref,
):
    tokens, length = query_ref.shape[0], key_ref.shape[0]
    key_blocks = length // BLOCK
    masks = head_masks(BLOCK)
    for h in range(2):
        skew_ref[h] = skewed(window_ref[0, h : h + 1, :])

    @pl.loop(0, key_blocks)
    def _(kb):
        rows = pl.ds(pl.multiple_of(kb * BLOCK, BLOCK), BLOCK)
        flip_ref[:, rows] = value_ref[rows, :].T

    for qb in range(tokens // BLOCK):
        here = slice(qb * BLOCK, (qb + 1) * BLOCK)
        pair = query_ref[here, :] * jnp.asarray(HEAD_DIM**-0.5, BF16)
        query_heads = [pair * mask for mask in masks]
        doc_row = doc_row_ref[0:1, here]
        most_ref[...] = jnp.full_like(most_ref, NEG_FILL)
        sum_ref[...] = jnp.zeros_like(sum_ref)
        mix_ref[...] = jnp.zeros_like(mix_ref)

        @pl.loop(0, key_blocks)
        def _(kb):
            @pl.when(active_ref[qb, kb] > 0)
            def _():
                rows = pl.ds(pl.multiple_of(kb * BLOCK, BLOCK), BLOCK)
                column = doc_col_ref[rows, :]
                same = jnp.concatenate([column] * (BLOCK // LANES), axis=1) == doc_row
                for h in range(2):
                    tile = score_tile(
                        key_ref[rows, :], query_heads[h], skew_ref, h,
                        base_ref[kb] + qb * BLOCK, same,
                    )
                    score_ref[h, rows, :] = tile
                    most_ref[h] = jnp.maximum(most_ref[h], fold_max(tile))

        most = [jnp.max(most_ref[h], axis=0, keepdims=True) for h in range(2)]

        @pl.loop(0, key_blocks)
        def _(kb):
            @pl.when(active_ref[qb, kb] > 0)
            def _():
                rows = pl.ds(pl.multiple_of(kb * BLOCK, BLOCK), BLOCK)
                for h in range(2):
                    weights = jnp.exp(score_ref[h, rows, :] - most[h])
                    sum_ref[h] += fold_sum(weights)
                    mix_ref[h] += mm(
                        flip_ref[h * HEAD_DIM : (h + 1) * HEAD_DIM, rows], weights.astype(BF16)
                    )

        columns = []
        for h in range(2):
            total = jnp.sum(sum_ref[h], axis=0, keepdims=True)
            columns.append(mix_ref[h] / total)
            total_ref[0, h : h + 1, here] = most[h] + jnp.log(total)
        out_ref[here, :] = jnp.concatenate(columns, axis=0).T.astype(BF16)


def attention_back_kernel(
    active_ref, base_ref, query_ref, key_ref, value_ref, grad_ref, total_ref, window_ref,
    doc_row_ref, doc_col_ref,
    query_grad_ref, key_grad_ref, value_grad_ref, offset_ref,
    skew_ref, field_ref, flip_ref, weight_ref, change_ref, inner_ref, mix_ref, key_sum, value_sum,
):
    tokens, length = query_ref.shape[0], key_ref.shape[0]
    key_blocks = length // BLOCK
    masks = head_masks(BLOCK)
    for h in range(2):
        skew_ref[h] = skewed(window_ref[0, h : h + 1, :])
    field_ref[...] = jnp.zeros_like(field_ref)
    key_sum[...] = jnp.zeros_like(key_sum)
    value_sum[...] = jnp.zeros_like(value_sum)

    @pl.loop(0, key_blocks)
    def _(kb):
        rows = pl.ds(pl.multiple_of(kb * BLOCK, BLOCK), BLOCK)
        flip_ref[:, rows] = key_ref[rows, :].T

    for qb in range(tokens // BLOCK):
        here = slice(qb * BLOCK, (qb + 1) * BLOCK)
        pair = query_ref[here, :] * jnp.asarray(HEAD_DIM**-0.5, BF16)
        query_heads = [pair * mask for mask in masks]
        grad_pair = grad_ref[here, :]
        grad_heads = [grad_pair * mask for mask in masks]
        doc_row = doc_row_ref[0:1, here]
        inner_ref[...] = jnp.zeros_like(inner_ref)
        mix_ref[...] = jnp.zeros_like(mix_ref)
        totals = [total_ref[0, h : h + 1, here] for h in range(2)]

        @pl.loop(0, key_blocks)
        def _(kb):
            @pl.when(active_ref[qb, kb] > 0)
            def _():
                rows = pl.ds(pl.multiple_of(kb * BLOCK, BLOCK), BLOCK)
                column = doc_col_ref[rows, :]
                same = jnp.concatenate([column] * (BLOCK // LANES), axis=1) == doc_row
                for h in range(2):
                    tile = score_tile(
                        key_ref[rows, :], query_heads[h], skew_ref, h,
                        base_ref[kb] + qb * BLOCK, same,
                    )
                    weights = jnp.exp(tile - totals[h])
                    change = mm(value_ref[rows, :], grad_heads[h], NT)
                    weight_ref[h, rows, :] = weights
                    change_ref[h, rows, :] = change
                    inner_ref[h] += fold_sum(weights * change)

        inner = [jnp.sum(inner_ref[h], axis=0, keepdims=True) for h in range(2)]

        @pl.loop(0, key_blocks)
        def _(kb):
            @pl.when(active_ref[qb, kb] > 0)
            def _():
                rows = pl.ds(pl.multiple_of(kb * BLOCK, BLOCK), BLOCK)
                key_part = value_part = None
                for h in range(2):
                    weights = weight_ref[h, rows, :]
                    score_grad = weights * (change_ref[h, rows, :] - inner[h])
                    for s in range(BLOCK // LANES):
                        first = pl.multiple_of(base_ref[kb] + qb * BLOCK - s * LANES, LANES)
                        field_ref[h, :, pl.ds(first, BLOCK)] += score_grad[
                            s * LANES : (s + 1) * LANES
                        ]
                    low = score_grad.astype(BF16)
                    key_here = mm(low, query_heads[h])
                    value_here = mm(weights.astype(BF16), grad_heads[h])
                    key_part = key_here if h == 0 else key_part + key_here
                    value_part = value_here if h == 0 else value_part + value_here
                    mix_ref[h] += mm(flip_ref[h * HEAD_DIM : (h + 1) * HEAD_DIM, rows], low)
                key_sum[rows, :] += key_part
                value_sum[rows, :] += value_part

        both = jnp.concatenate([mix_ref[0], mix_ref[1]], axis=0) * HEAD_DIM**-0.5
        query_grad_ref[here, :] = both.T.astype(BF16)

    key_grad_ref[...] = key_sum[...].astype(BF16)
    value_grad_ref[...] = value_sum[...].astype(BF16)
    for h in range(2):
        offset_ref[0, h : h + 1, :] = unskew_sum(field_ref[h])


def attention_specs(tokens, length, pairs, width):
    smem = pl.BlockSpec(memory_space=pltpu.SMEM)
    return dict(
        smem=smem,
        query=pl.BlockSpec((tokens, LANES), lambda i: (0, i)),
        key=pl.BlockSpec((length, LANES), lambda i: (0, i)),
        value=pl.BlockSpec((length, LANES), lambda i: (0, i + pairs)),
        window=pl.BlockSpec((1, 8, width), lambda i: (i, 0, 0)),
        total=pl.BlockSpec((1, 8, tokens), lambda i: (i, 0, 0)),
        doc_row=pl.BlockSpec((8, tokens), lambda i: (0, 0)),
        doc_col=pl.BlockSpec((length, LANES), lambda i: (0, 0)),
    )


def attention(active, base, queries, key_values, window, doc_row, doc_col):
    tokens, length = queries.shape[0], key_values.shape[0]
    pairs, width = window.shape[0], window.shape[2]
    specs = attention_specs(tokens, length, pairs, width)
    return pl.pallas_call(
        attention_kernel,
        grid=(pairs,),
        in_specs=[
            specs["smem"], specs["smem"], specs["query"], specs["key"], specs["value"],
            specs["window"], specs["doc_row"], specs["doc_col"],
        ],
        out_specs=[specs["query"], specs["total"]],
        out_shape=[
            jax.ShapeDtypeStruct(queries.shape, BF16),
            jax.ShapeDtypeStruct((pairs, 8, tokens), F32),
        ],
        scratch_shapes=[
            pltpu.VMEM((2, LANES, width), F32),
            pltpu.VMEM((LANES, length), BF16),
            pltpu.VMEM((2, length, BLOCK), F32),
            pltpu.VMEM((2, 8, BLOCK), F32),
            pltpu.VMEM((2, 8, BLOCK), F32),
            pltpu.VMEM((2, HEAD_DIM, BLOCK), F32),
        ],
        compiler_params=pltpu.CompilerParams(vmem_limit_bytes=VMEM_CAP),
        name="attention_forward",
    )(active, base, queries, key_values, key_values, window, doc_row, doc_col)


def attention_back(active, base, queries, key_values, grads, totals, window, doc_row, doc_col):
    tokens, length = queries.shape[0], key_values.shape[0]
    pairs, width = window.shape[0], window.shape[2]
    specs = attention_specs(tokens, length, pairs, width)
    return pl.pallas_call(
        attention_back_kernel,
        grid=(pairs,),
        in_specs=[
            specs["smem"], specs["smem"], specs["query"], specs["key"], specs["value"],
            specs["query"], specs["total"], specs["window"], specs["doc_row"], specs["doc_col"],
        ],
        out_specs=[specs["query"], specs["key"], specs["key"], specs["window"]],
        out_shape=[
            jax.ShapeDtypeStruct(queries.shape, BF16),
            jax.ShapeDtypeStruct((length, queries.shape[1]), BF16),
            jax.ShapeDtypeStruct((length, queries.shape[1]), BF16),
            jax.ShapeDtypeStruct((pairs, 8, width), F32),
        ],
        scratch_shapes=[
            pltpu.VMEM((2, LANES, width), F32),
            pltpu.VMEM((2, LANES, width), F32),
            pltpu.VMEM((LANES, length), BF16),
            pltpu.VMEM((2, length, BLOCK), F32),
            pltpu.VMEM((2, length, BLOCK), F32),
            pltpu.VMEM((2, 8, BLOCK), F32),
            pltpu.VMEM((2, HEAD_DIM, BLOCK), F32),
            pltpu.VMEM((length, LANES), F32),
            pltpu.VMEM((length, LANES), F32),
        ],
        compiler_params=pltpu.CompilerParams(vmem_limit_bytes=VMEM_CAP),
        name="attention_backward",
    )(active, base, queries, key_values, key_values, grads, totals, window, doc_row, doc_col)


def start_kernel(
    experts, dp_count, ctx_count, pack_ref, hidden_ref, docs_ref,
    query_ref, pair_ref, normed_ref, weight_out, own_ref, lanes_ref, gains_ref, docs_out,
    weights, hidden, docs, sends, receives, out_sem,
):
    d, c = lax.axis_index("dp"), lax.axis_index("ctx")
    rows = pack_ref.shape[0]
    tokens, width = query_ref.shape
    greet(
        [{"ctx": c ^ m} for m in range(1, ctx_count)]
        + [{"dp": d ^ bit} for bit in bits_down(dp_count)]
    )
    wire = Wire(sends, receives)

    def shard(m, j):
        index = (d ^ m) * ctx_count + (c ^ j)
        return weights.at[pl.ds(pl.multiple_of(index * rows, rows), rows)]

    weights[pl.ds(pl.multiple_of((d * ctx_count + c) * rows, rows), rows), :] = pack_ref[...]
    docs_sent = [wire.send(docs_ref, docs.at[m], ctx=c ^ m) for m in range(1, ctx_count)]
    sides = [0]
    hidden_sent = {}
    for bit in bits_down(ctx_count)[:-1]:
        arrivals = [wire.send(shard(0, j), shard(0, j), ctx=c ^ bit) for j in sides]
        for m in [0] + list(hidden_sent):
            source = hidden_ref if m == 0 else hidden.at[m]
            if m:
                hidden_sent[m].wait()
            hidden_sent[m | bit] = wire.send(source, hidden.at[m | bit], ctx=c ^ bit)
        for copy in arrivals:
            copy.wait()
        sides = sides + [j | bit for j in sides]
    hidden_sent[1] = wire.send(hidden_ref, hidden.at[1], ctx=c ^ 1)
    groups, crossed = {}, []
    for m in xor_order(dp_count):
        if m:
            for copy in groups[m]:
                copy.wait()
        for bit in bits_down(dp_count):
            if m & (2 * bit - 1) == 0:
                groups[m | bit] = [
                    wire.send(shard(m, j), shard(m, j), dp=d ^ bit) for j in sides
                ]
        crossed += [wire.send(shard(m, j), shard(m, j), ctx=c ^ 1) for j in sides]
        if m == 0:
            for k in [k for k in hidden_sent if k > 1]:
                hidden_sent[k].wait()
                hidden_sent[k | 1] = wire.send(hidden.at[k], hidden.at[k | 1], ctx=c ^ 1)
    for copy in crossed:
        copy.wait()
    keep = pltpu.make_async_copy(weights.at[:, : 3 * width], weight_out, out_sem.at[0])
    keep.start()
    keep_own = pltpu.make_async_copy(weights.at[:, 3 * width + LANES :], own_ref, out_sem.at[1])
    keep_own.start()
    small = weights[:, 3 * width : 3 * width + LANES].astype(F32)
    lane = lax.broadcasted_iota(jnp.int32, small.shape, 1)
    lanes_ref[...] = jnp.where(lane < experts, small, 0.0).astype(BF16)
    gain_one = jnp.sum(jnp.where(lane == experts, small, 0.0), axis=1, keepdims=True)
    gain_two = jnp.sum(jnp.where(lane == experts + 1, small, 0.0), axis=1, keepdims=True)
    both = jnp.where(lane == 0, gain_one, jnp.where(lane == 1, gain_two, 0.0)).T
    gains_ref[...] = both[:8]
    gain = both[0:1]
    docs_out[0] = docs_ref[...]
    for m in range(ctx_count):
        if m:
            docs_sent[m - 1].wait()
            docs_out[m] = docs[m]
            hidden_sent[m].wait()
        values = (hidden[m] if m else hidden_ref[...]).astype(F32)
        scale = lax.rsqrt(jnp.mean(values * values, axis=-1, keepdims=True) + NORM_EPS)
        normed = (values * scale * gain).astype(BF16)
        pair_ref[m * tokens : (m + 1) * tokens, :] = mm(
            normed, weights[:, width : 3 * width]
        ).astype(BF16)
        if m == 0:
            normed_ref[...] = normed
            query_ref[...] = mm(normed, weights[:, :width]).astype(BF16)
    keep.wait()
    keep_own.wait()
    wire.finish()


def start(pack, hidden, docs, width, experts):
    tokens = hidden.shape[0]
    columns = pack.shape[1]
    dp_count, ctx_count = lax.axis_size("dp"), lax.axis_size("ctx")
    copies = 2 * (ctx_count - 1) + ctx_count // 2 + dp_count * ctx_count
    vmem = pl.BlockSpec(memory_space=pltpu.VMEM)
    hbm = pl.BlockSpec(memory_space=pl.ANY)
    return pl.pallas_call(
        functools.partial(start_kernel, experts, dp_count, ctx_count),
        in_specs=[vmem] * 3,
        out_specs=[vmem, vmem, vmem, hbm, hbm, vmem, vmem, vmem],
        out_shape=[
            jax.ShapeDtypeStruct((tokens, width), BF16),
            jax.ShapeDtypeStruct((tokens * ctx_count, 2 * width), BF16),
            jax.ShapeDtypeStruct((tokens, D), BF16),
            jax.ShapeDtypeStruct((D, 3 * width), BF16),
            jax.ShapeDtypeStruct((D, width), BF16),
            jax.ShapeDtypeStruct((D, LANES), BF16),
            jax.ShapeDtypeStruct((8, D), F32),
            jax.ShapeDtypeStruct((ctx_count, 8, tokens), jnp.int32),
        ],
        scratch_shapes=[
            pltpu.VMEM((D, columns), BF16),
            pltpu.VMEM((ctx_count, tokens, D), BF16),
            pltpu.VMEM((ctx_count, 8, tokens), jnp.int32),
            pltpu.SemaphoreType.DMA((copies,)),
            pltpu.SemaphoreType.DMA((copies,)),
            pltpu.SemaphoreType.DMA((2,)),
        ],
        compiler_params=pltpu.CompilerParams(
            vmem_limit_bytes=VMEM_CAP, collective_id=1, has_side_effects=True
        ),
        name="start",
    )(pack, hidden, docs)


def middle_kernel(shares, place_ref, *refs):
    attended, outs = refs[:shares], refs[shares : 2 * shares]
    (hidden_ref, gains_ref, lanes_ref, picker_ref,
     middle_ref, normed_ref, probs_ref, send_ref, weights, mixed) = refs[2 * shares :]
    share, experts = place_ref[2], place_ref[3]
    width = attended[0].shape[1]
    for m in range(shares):
        part = pl.ds(pl.multiple_of((share ^ m) * width, width), width)
        mixed[:, part] = attended[m][...]
        weights[:, part] = outs[m][...]
    middle = hidden_ref[...].astype(F32) + mm(mixed[...], weights[...], NT)
    middle_ref[...] = middle
    scale = lax.rsqrt(jnp.mean(middle * middle, axis=-1, keepdims=True) + NORM_EPS)
    normed = (middle * scale * gains_ref[1:2, :]).astype(BF16)
    normed_ref[...] = normed
    logits = mm(normed, lanes_ref[...])
    lane = lax.broadcasted_iota(jnp.int32, logits.shape, 1)
    logits = jnp.where(lane < experts, logits, NEG_FILL)
    powers = jnp.exp(logits - jnp.max(logits, axis=1, keepdims=True))
    probs_ref[...] = powers / jnp.sum(powers, axis=1, keepdims=True)
    slots = send_ref.shape[1]
    for m in range(send_ref.shape[0]):
        send_ref[m] = mm(picker_ref[m * slots : (m + 1) * slots, :], normed).astype(BF16)


def middle_step(places, attended, outs, hidden, gains, lanes, picker, blocks):
    shares, (tokens, width) = len(attended), attended[0].shape
    vmem = pl.BlockSpec(memory_space=pltpu.VMEM)
    return pl.pallas_call(
        functools.partial(middle_kernel, shares),
        in_specs=[pl.BlockSpec(memory_space=pltpu.SMEM)] + [vmem] * (2 * shares + 4),
        out_specs=[vmem] * 4,
        out_shape=[
            jax.ShapeDtypeStruct((tokens, D), F32),
            jax.ShapeDtypeStruct((tokens, D), BF16),
            jax.ShapeDtypeStruct((tokens, LANES), F32),
            jax.ShapeDtypeStruct((blocks, picker.shape[0] // blocks, D), BF16),
        ],
        scratch_shapes=[
            pltpu.VMEM((D, width * shares), BF16),
            pltpu.VMEM((tokens, width * shares), BF16),
        ],
        compiler_params=pltpu.CompilerParams(vmem_limit_bytes=VMEM_CAP),
        name="middle_step",
    )(places, *attended, *outs, hidden, gains, lanes, picker)


def return_kernel(shares, place_ref, *refs):
    parts = refs[:-6]
    picker_ref, probs_ref, lanes_ref, grad_ref, logit_ref, back = refs[-6:]
    share, experts = place_ref[2], place_ref[3]
    slots = parts[0].shape[0]
    width = grad_ref.shape[1]
    for m, part in enumerate(parts):
        back[m * slots : (m + 1) * slots, :] = part[...]
    returned = mm(picker_ref[...], back[...])
    tail = returned[:, width:]
    lane = lax.broadcasted_iota(jnp.int32, tail.shape, 1)
    step = LANES // (2 * shares)
    prob_grad = tail
    for k in range(1, 2 * shares):
        prob_grad = prob_grad + pltpu.roll(tail, LANES - k * step, 1)
    probs = probs_ref[...]
    prob_grad = jnp.where(lane < experts, prob_grad, 0.0)
    logit = probs * (prob_grad - jnp.sum(probs * prob_grad, axis=1, keepdims=True))
    logit_ref[...] = logit
    lanes = lanes_ref[pl.ds(pl.multiple_of(share * width, width), width), :]
    more = lax.dot_general(
        logit, lanes.astype(F32), NT, precision=lax.Precision.HIGHEST, preferred_element_type=F32
    )
    grad_ref[...] = (returned[:, :width] + more).astype(BF16)


def return_step(places, parts, picker_flip, probs, lanes, shares):
    tokens = picker_flip.shape[0]
    slots, columns = parts[0].shape
    vmem = pl.BlockSpec(memory_space=pltpu.VMEM)
    return pl.pallas_call(
        functools.partial(return_kernel, shares),
        in_specs=[pl.BlockSpec(memory_space=pltpu.SMEM)] + [vmem] * (len(parts) + 3),
        out_specs=[vmem] * 2,
        out_shape=[
            jax.ShapeDtypeStruct((tokens, columns - LANES), BF16),
            jax.ShapeDtypeStruct((tokens, LANES), F32),
        ],
        scratch_shapes=[pltpu.VMEM((slots * len(parts), columns), BF16)],
        compiler_params=pltpu.CompilerParams(vmem_limit_bytes=VMEM_CAP),
        name="return_step",
    )(places, *parts, picker_flip, probs, lanes)


def middle_back_kernel(shares, place_ref, *refs):
    halves = refs[:shares]
    (middle_ref, out_grad_ref, gains_ref, own_ref,
     grad_ref, low_ref, attended_ref, gain_ref, whole) = refs[shares:]
    share = place_ref[2]
    width = halves[0].shape[1]
    for m in range(shares):
        first = pl.multiple_of((share ^ m) * width, width)
        whole[:, pl.ds(first, width)] = halves[m][...]
    middle = middle_ref[...]
    gradient = whole[...].astype(F32)
    scale = lax.rsqrt(jnp.mean(middle * middle, axis=-1, keepdims=True) + NORM_EPS)
    weighted = gains_ref[1:2, :] * gradient
    inner = jnp.mean(middle * weighted, axis=-1, keepdims=True)
    part = scale * weighted - middle * (scale * scale * scale) * inner
    gain_ref[...] = fold_sum(gradient * middle * scale)
    total = out_grad_ref[...].astype(F32) + part
    grad_ref[...] = total
    low = total.astype(BF16)
    low_ref[...] = low
    attended_ref[...] = mm(low, own_ref[...]).astype(BF16)


def middle_back(places, halves, middle, out_grad, gains, own):
    shares, tokens = len(halves), middle.shape[0]
    vmem = pl.BlockSpec(memory_space=pltpu.VMEM)
    return pl.pallas_call(
        functools.partial(middle_back_kernel, shares),
        in_specs=[pl.BlockSpec(memory_space=pltpu.SMEM)] + [vmem] * (shares + 4),
        out_specs=[vmem] * 4,
        out_shape=[
            jax.ShapeDtypeStruct((tokens, D), F32),
            jax.ShapeDtypeStruct((tokens, D), BF16),
            jax.ShapeDtypeStruct((tokens, own.shape[1]), BF16),
            jax.ShapeDtypeStruct((8, D), F32),
        ],
        scratch_shapes=[pltpu.VMEM((tokens, D), BF16)],
        compiler_params=pltpu.CompilerParams(vmem_limit_bytes=VMEM_CAP),
        name="middle_back",
    )(places, *halves, middle, out_grad, gains, own)


def expert_kernel(experts, count, shares, place_ref, rows_ref, grads_ref, router_ref, *refs):
    ins, downs = refs[:count], refs[count : 2 * count]
    in_all, down_all, sems = refs[-3:]
    results = refs[-3 - 5 - 2 * shares : -3]
    rows_all, scaled_all, act_ref, gate_low_ref, up_low_ref = results[:5]
    row_parts, out_parts = results[5 : 5 + shares], results[5 + shares :]
    expert, ctx, share = place_ref[0], place_ref[1], place_ref[2]
    depth = ins[0].shape[1]
    ff = ins[0].shape[2]

    @pl.when(pl.program_id(0) == 0)
    def _():
        copies = []
        for j in range(count):
            part = pl.ds(j * depth, depth)
            copies.append(pltpu.make_async_copy(ins[j], in_all.at[:, part, :], sems.at[0, j]))
            copies.append(pltpu.make_async_copy(downs[j], down_all.at[:, part], sems.at[1, j]))
        for copy in copies:
            copy.start()
        for copy in copies:
            copy.wait()

    slots = rows_ref.shape[0]
    lane = lax.broadcasted_iota(jnp.int32, (slots, LANES), 1)
    logits = jnp.where(lane < experts, mm(rows_ref[...], router_ref[...]), NEG_FILL)
    powers = jnp.exp(logits - jnp.max(logits, axis=1, keepdims=True))
    probs = powers / jnp.sum(powers, axis=1, keepdims=True)
    gate = jnp.sum(jnp.where(lane == expert, probs, 0.0), axis=1, keepdims=True)
    rows_all[...] = rows_ref[...]
    scaled_all[...] = (gate * grads_ref[...].astype(F32)).astype(BF16)
    order = [pl.ds(pl.multiple_of((ctx ^ j) * depth, depth), depth) for j in range(count)]
    rows = jnp.concatenate([rows_ref[:, part] for part in order], axis=1)
    grads = jnp.concatenate([grads_ref[:, part] for part in order], axis=1)
    dots = jnp.zeros((slots, 1), F32)
    for start in range(0, ff, BLOCK):
        part = slice(start, min(ff, start + BLOCK))
        value = mm(rows, in_all[0, :, part])
        up = mm(rows, in_all[1, :, part])
        back = mm(grads, down_all[part, :], NT)
        square = value * value
        wave = jnp.tanh(GELU_K * value * (1.0 + GELU_C * square))
        half = 0.5 * (1.0 + wave)
        bent = value * half
        slope = half + 0.5 * value * (1.0 - wave * wave) * (
            GELU_K * (1.0 + 3.0 * GELU_C * square)
        )
        act = (bent * up).astype(BF16)
        act_ref[:, part] = act
        dots += jnp.sum(act.astype(F32) * back, axis=1, keepdims=True)
        scaled = gate * back
        gate_low_ref[:, part] = (scaled * up * slope).astype(BF16)
        up_low_ref[:, part] = (scaled * bent).astype(BF16)
    share_width = D // shares
    high = dots.astype(BF16).astype(F32)
    stride = LANES // shares
    tail = jnp.where(lane == share * stride + expert, high, 0.0)
    tail = jnp.where(lane == share * stride + stride // 2 + expert, dots - high, tail)
    for m in range(shares):
        for i in range(share_width // depth):
            piece = ((share ^ m) * (share_width // depth) + i) ^ ctx
            part = pl.ds(pl.multiple_of(piece * depth, depth), depth)
            spot = slice(i * depth, (i + 1) * depth)
            row = mm(gate_low_ref[...], in_all[0, part, :], NT)
            row += mm(up_low_ref[...], in_all[1, part, :], NT)
            row_parts[m][:, spot] = row.astype(BF16)
            out_parts[m][:, spot] = (gate * mm(act_ref[...], down_all[:, part])).astype(BF16)
        row_parts[m][:, share_width:] = tail.astype(BF16)


def expert_block(block, blocks, places, rows, grads, router, ins, downs, held, experts, shares):
    slots, width = rows.shape
    ff = ins[0].shape[2]
    count = len(ins)
    share_width = width // shares
    vmem = pl.BlockSpec(memory_space=pltpu.VMEM)
    hbm = pl.BlockSpec(memory_space=pl.ANY)
    at_block = lambda i: (block, 0)
    sizes = (width, width, ff, ff, ff)
    aliases = {4 + 2 * count + k: k for k in range(5)} if held else {}
    return pl.pallas_call(
        functools.partial(expert_kernel, experts, count, shares),
        grid=(1,),
        in_specs=[pl.BlockSpec(memory_space=pltpu.SMEM)]
        + [vmem] * 3
        + [hbm] * (2 * count + len(held)),
        out_specs=[pl.BlockSpec((slots, size), at_block) for size in sizes] + [vmem] * (2 * shares),
        out_shape=[jax.ShapeDtypeStruct((blocks * slots, size), BF16) for size in sizes]
        + [jax.ShapeDtypeStruct((slots, share_width + LANES), BF16)] * shares
        + [jax.ShapeDtypeStruct((slots, share_width), BF16)] * shares,
        scratch_shapes=[
            pltpu.VMEM((2, width, ff), BF16),
            pltpu.VMEM((ff, width), BF16),
            pltpu.SemaphoreType.DMA((2, count)),
        ],
        input_output_aliases=aliases,
        compiler_params=pltpu.CompilerParams(vmem_limit_bytes=VMEM_CAP),
        name="expert_block",
    )(places, rows, grads, router, *ins, *downs, *held)


def shards(
    hidden_in,
    out_grad,
    segments,
    routes,
    bucket_table,
    qkv_weight,
    out_weight,
    router,
    norm_gains,
    position_bias,
    expert_in,
    expert_down,
    qkv_first,
    qkv_second,
    out_first,
    out_second,
    router_first,
    router_second,
    gains_first,
    gains_second,
    bias_first,
    bias_second,
    in_first,
    in_second,
    down_first,
    down_second,
):
    tokens = hidden_in.shape[0]
    dp_count, ctx_count, tp_count = (lax.axis_size(a) for a in ("dp", "ctx", "tp"))
    dp_place, ctx_place, tp_place = (lax.axis_index(a) for a in ("dp", "ctx", "tp"))
    length = tokens * ctx_count
    heads_here = position_bias.shape[0]
    width_here = heads_here * HEAD_DIM
    pairs = heads_here // 2
    expert_count = router.shape[1]
    top_count = routes.shape[1]
    own_rows = router.shape[0]

    places = jnp.stack(
        [dp_place, ctx_place, tp_place, jnp.int32(expert_count)]
    ).astype(jnp.int32)
    tail_pack = jnp.pad(
        jnp.concatenate([router, norm_gains.T], axis=1), ((0, 0), (0, LANES - expert_count - 2))
    )
    pack = jnp.concatenate(
        [qkv_weight.reshape(own_rows, 3 * width_here), tail_pack, out_weight.T], axis=1
    )
    doc_row = jnp.broadcast_to(segments.reshape(1, tokens), (8, tokens))
    queries, key_values, normed_one, qkv_flat, out_own, lanes, gains, docs = start(
        pack, hidden_in, doc_row, width_here, expert_count
    )
    out_sides = gather_xor(out_own, "tp")
    docs_all = docs[:, 0].reshape(length)

    capacity = max(2, min(tokens, 5 * top_count * tokens // (4 * expert_count)))
    flat_routes = routes.reshape(-1)
    route_onehot = (
        flat_routes[:, None] == jnp.arange(expert_count, dtype=jnp.int32)[None, :]
    ).astype(jnp.int32)
    earlier = jnp.cumsum(route_onehot, axis=0) - route_onehot
    position = jnp.sum(earlier * route_onehot, axis=1).reshape(tokens, top_count)
    slot_expert = dp_place ^ jnp.arange(dp_count, dtype=jnp.int32)
    slot_index = jnp.arange(capacity, dtype=jnp.int32)
    chosen = jnp.zeros((dp_count, capacity, tokens), jnp.bool_)
    for k in range(top_count):
        chosen = chosen | (
            (routes[:, k][None, None, :] == slot_expert[:, None, None])
            & (position[:, k][None, None, :] == slot_index[None, :, None])
        )
    picker = chosen.astype(BF16).reshape(dp_count * capacity, tokens)
    chosen_flip = jnp.zeros((tokens, dp_count, capacity), jnp.bool_)
    for k in range(top_count):
        chosen_flip = chosen_flip | (
            (routes[:, k][:, None, None] == slot_expert[None, :, None])
            & (position[:, k][:, None, None] == slot_index[None, None, :])
        )
    picker_flip = chosen_flip.astype(BF16).reshape(tokens, dp_count * capacity)
    send_grads = mm(picker, out_grad).astype(BF16).reshape(dp_count, capacity, D)
    send_grads, expert_in_late, expert_down_late, _, _ = lax.optimization_barrier(
        (send_grads, expert_in[0], expert_down[0], queries, out_own)
    )
    arrived_grads = [send_grads[0]] + [swap(send_grads[m], "dp", m) for m in range(1, dp_count)]
    in_pieces = gather_xor(expert_in_late, "ctx")
    down_pieces = gather_xor(expert_down_late, "ctx")

    rev_table = bucket_table[::-1]
    window_width = tokens + length
    rev_table = jnp.pad(rev_table, (0, 1), constant_values=BUCKETS)
    first_row = ctx_place * tokens
    window_table = lax.dynamic_slice(rev_table, (first_row,), (window_width,))
    table_onehot = (
        window_table[None, :] == jnp.arange(BUCKETS, dtype=jnp.int32)[:, None]
    ).astype(F32)
    window = jnp.dot(
        position_bias, table_onehot, precision=lax.Precision.HIGHEST, preferred_element_type=F32
    )
    window = jnp.pad(window.reshape(pairs, 2, window_width), ((0, 0), (0, 6), (0, 0)))
    docs_row = segments.reshape(1, tokens)
    doc_col = jnp.broadcast_to(docs_all[:, None], (length, LANES))
    query_docs = docs_row.reshape(tokens // BLOCK, BLOCK)
    key_docs = docs_all.reshape(length // BLOCK, BLOCK)
    active = (
        (key_docs[:, -1][None, :] >= query_docs[:, 0][:, None])
        & (key_docs[:, 0][None, :] <= query_docs[:, -1][:, None])
    ).astype(jnp.int32)
    block_rows = (
        (ctx_place ^ jnp.arange(ctx_count, dtype=jnp.int32))[:, None] * tokens
        + jnp.arange(tokens // BLOCK, dtype=jnp.int32)[None, :] * BLOCK
    ).reshape(-1)
    base = (length - LANES - block_rows).astype(jnp.int32)

    attended, totals = attention(active, base, queries, key_values, window, doc_row, doc_col)
    middle, normed_two, probs, send_rows = middle_step(
        places, gather_xor(attended, "tp"), out_sides, hidden_in, gains, lanes, picker, dp_count
    )
    arrived_rows = [send_rows[0]] + [swap(send_rows[m], "dp", m) for m in range(1, dp_count)]

    held = ()
    row_sums, out_parts = [], []
    for m in range(dp_count):
        results = expert_block(
            m, dp_count, places, arrived_rows[m], arrived_grads[m], lanes,
            in_pieces, down_pieces, held, expert_count, tp_count,
        )
        held = results[:5]
        row_sums.append(scatter_sum(results[5 : 5 + tp_count], "tp").astype(BF16))
        out_parts.append(results[5 + tp_count :])
    back_rows = row_sums[:1] + [swap(row_sums[m], "dp", m) for m in range(1, dp_count)]
    held, _ = lax.optimization_barrier((held, row_sums))
    rows_all, scaled_all, act_all, gate_low_all, up_low_all = held

    def rows_by_ctx(values):
        depth = values.shape[0] // ctx_count
        return [
            lax.dynamic_slice_in_dim(values, (ctx_place ^ j) * depth, depth, 0)
            for j in range(ctx_count)
        ]

    def columns_by_ctx(values):
        depth = values.shape[1] // ctx_count
        return [
            lax.dynamic_slice_in_dim(values, (ctx_place ^ j) * depth, depth, 1)
            for j in range(ctx_count)
        ]

    def weight_grad(left, right):
        return lax.dot_general(
            left, right, (((0,), (0,)), ((), ())), preferred_element_type=F32
        ).astype(BF16)

    gate_total = scatter_sum(rows_by_ctx(weight_grad(rows_all, gate_low_all)), "ctx")
    up_total = scatter_sum(rows_by_ctx(weight_grad(rows_all, up_low_all)), "ctx")
    down_total = scatter_sum(columns_by_ctx(weight_grad(act_all, scaled_all)), "ctx")[None]
    in_total = jnp.stack([gate_total, up_total], axis=0)[None]

    grad_half, logit_grad = return_step(places, back_rows, picker_flip, probs, lanes, tp_count)
    middle_grad, middle_low, attended_grad, gain_two_grad = middle_back(
        places, gather_xor(grad_half, "tp"), middle, out_grad, gains, out_own
    )
    out_parts, _ = lax.optimization_barrier((out_parts, middle_grad))
    out_sums = [scatter_sum(parts, "tp").astype(BF16) for parts in out_parts]
    back_outs = out_sums[:1] + [swap(out_sums[m], "dp", m) for m in range(1, dp_count)]
    mixed_half = mm(picker_flip, jnp.concatenate(back_outs, axis=0)).astype(BF16)
    mixed = in_order(gather_xor(mixed_half, "tp"), tp_place, 1)
    output = middle + mixed.astype(F32)
    out_flip_grad = weight_grad(middle_low, attended)
    router_grad = lax.dot_general(
        normed_two.astype(F32), logit_grad, (((0,), (0,)), ((), ())),
        precision=lax.Precision.HIGHEST, preferred_element_type=F32,
    )[:, :expert_count]
    inputs = hidden_in.astype(F32)
    scale_one = rms_scale(inputs)

    query_grad, key_part, value_part, offset_grad = attention_back(
        active, base, queries, key_values, attended_grad, totals, window, doc_row, doc_col
    )
    bias_part = lax.dot_general(
        offset_grad[:, :2, :].reshape(heads_here, window_width), table_onehot, NT,
        precision=lax.Precision.HIGHEST, preferred_element_type=F32,
    )
    bias_total = all_sum(all_sum(bias_part, "ctx"), "dp")

    def row_blocks(values):
        return [values[j * tokens : (j + 1) * tokens] for j in range(ctx_count)]

    key_total = scatter_sum(row_blocks(key_part), "ctx").astype(BF16)
    value_total = scatter_sum(row_blocks(value_part), "ctx").astype(BF16)
    qkv_rows_grad = jnp.concatenate([query_grad, key_total, value_total], axis=1)
    normed_one_grad = all_sum(mm(qkv_rows_grad, qkv_flat, NT).astype(BF16), "tp").astype(F32)
    input_part, gain_one_grad = norm_back(inputs, scale_one, gains[0], normed_one_grad)
    input_grad = middle_grad + input_part
    qkv_weight_grad = weight_grad(normed_one, qkv_rows_grad)

    tail_grad = jnp.pad(
        jnp.concatenate(
            [router_grad, jnp.stack([gain_one_grad, jnp.sum(gain_two_grad, axis=0)], axis=1)], axis=1
        ),
        ((0, 0), (0, LANES - expert_count - 2)),
    ).astype(BF16)
    grad_pack = jnp.concatenate([qkv_weight_grad, out_flip_grad, tail_grad], axis=1)
    grad_pack = grad_pack.reshape(dp_count, ctx_count, own_rows, grad_pack.shape[1])
    ctx_parts = [
        lax.dynamic_slice_in_dim(grad_pack, ctx_place ^ j, 1, 1)[:, 0] for j in range(ctx_count)
    ]
    ctx_total = scatter_sum(ctx_parts, "ctx").astype(BF16)
    dp_parts = [
        lax.dynamic_slice_in_dim(ctx_total, dp_place ^ j, 1, 0)[0] for j in range(dp_count)
    ]
    pack_total = scatter_sum(dp_parts, "dp")
    qkv_total = pack_total[:, : 3 * width_here].reshape(own_rows, 3, width_here)
    out_total = pack_total[:, 3 * width_here : 4 * width_here].T
    tail_total = pack_total[:, 4 * width_here :]
    router_total = tail_total[:, :expert_count]
    gains_total = tail_total[:, expert_count : expert_count + 2].T

    qkv_new = adamw_step(qkv_weight.astype(F32), qkv_total, qkv_first, qkv_second, MAIN_RATE)
    out_new = adamw_step(out_weight.astype(F32), out_total, out_first, out_second, MAIN_RATE)
    router_new = adamw_step(
        router.astype(F32), router_total, router_first, router_second, MAIN_RATE
    )
    gains_new = adamw_step(
        norm_gains.astype(F32), gains_total, gains_first, gains_second, MAIN_RATE
    )
    bias_new = adamw_step(position_bias, bias_total, bias_first, bias_second, BIAS_RATE)
    in_new = adamw_step(expert_in.astype(F32), in_total, in_first, in_second, MAIN_RATE)
    down_new = adamw_step(expert_down.astype(F32), down_total, down_first, down_second, MAIN_RATE)
    return (
        output,
        input_grad,
        qkv_total,
        *qkv_new,
        out_total,
        *out_new,
        router_total,
        *router_new,
        gains_total,
        *gains_new,
        bias_total,
        *bias_new,
        in_total,
        *in_new,
        down_total,
        *down_new,
    )


def solution(mesh):
    token_rows = P(("dp", "ctx"), None)
    qkv = P(("dp", "ctx"), None, "tp")
    out = P("tp", ("dp", "ctx"))
    gains = P(None, ("dp", "ctx"))
    bias = P("tp", None)
    expert_in = P("dp", None, "ctx", "tp")
    expert_down = P("dp", "tp", "ctx")
    placed = (
        token_rows, token_rows, P("dp", "ctx"), token_rows, P(),
        qkv, out, token_rows, gains, bias, expert_in, expert_down,
        qkv, qkv, out, out, token_rows, token_rows, gains, gains, bias, bias,
        expert_in, expert_in, expert_down, expert_down,
    )
    return jax.shard_map(
        shards,
        mesh=mesh,
        in_specs=placed,
        out_specs=(token_rows, token_rows)
        + (qkv,) * 4
        + (out,) * 4
        + (token_rows,) * 4
        + (gains,) * 4
        + (bias,) * 4
        + (expert_in,) * 4
        + (expert_down,) * 4,
        check_vma=False,
    )
```

```python
import functools

import jax
import jax.numpy as jnp
from jax import lax
from jax.experimental import pallas as pl
from jax.experimental.pallas import tpu as pltpu
from jax.sharding import PartitionSpec as P

D = 1024
HEAD_DIM = 64
BUCKETS = 32

NORM_EPS = 1e-06
NEG_FILL = -1e30
BETA_ONE = 0.9
BETA_TWO = 0.95
FIX_ONE = 1.0 - 0.9**10
FIX_TWO = 1.0 - 0.95**10
ADAM_EPS = 1e-08
WEIGHT_DECAY = 0.1
MAIN_RATE = 0.02
BIAS_RATE = 0.2

F32 = jnp.float32
BF16 = jnp.bfloat16
LANES = 128
BLOCK = 256
VMEM_CAP = 60 * 1024 * 1024
GELU_K = 0.7978845608028654
GELU_C = 0.044715


def tree_sum(values):
    while len(values) > 1:
        values = [values[k] + values[k + 1] for k in range(0, len(values), 2)]
    return values[0]


def rms_scale(values):
    return lax.rsqrt(jnp.mean(values * values, axis=-1, keepdims=True) + NORM_EPS)


def norm_back(values, scale_here, gain_here, gradient):
    weighted = gain_here * gradient
    row_inner = jnp.mean(values * weighted, axis=-1, keepdims=True)
    input_part = scale_here * weighted - values * scale_here**3 * row_inner
    return (input_part, jnp.sum(gradient * values * scale_here, axis=0))


def adamw_step(weight, gradient, first_moment, second_moment, step_rate):
    first_new = BETA_ONE * first_moment + (1.0 - BETA_ONE) * gradient
    second_new = BETA_TWO * second_moment + (1.0 - BETA_TWO) * gradient * gradient
    update = -step_rate * (
        first_new / FIX_ONE / (jnp.sqrt(second_new / FIX_TWO) + ADAM_EPS) + WEIGHT_DECAY * weight
    )
    return (first_new, second_new, update)


def cost(micros):
    return pl.CostEstimate(flops=int(micros * 1.15e9), bytes_accessed=1 << 20, transcendentals=0)


def swap(values, axis, bits):
    count = lax.axis_size(axis)
    return lax.ppermute(values, axis, [(i, i ^ bits) for i in range(count)])


def gather_xor(values, axis):
    pieces = {0: values}
    bit = lax.axis_size(axis) >> 1
    while bit:
        for key in list(pieces):
            pieces[key | bit] = swap(pieces[key], axis, bit)
        bit >>= 1
    return [pieces[m] for m in range(len(pieces))]


def scatter_sum(parts, axis):
    live = dict(enumerate(parts))
    bit = 1
    while bit < lax.axis_size(axis):
        left = {}
        for key in live:
            if key & bit == 0:
                moved = swap(live[key | bit].astype(BF16), axis, bit)
                left[key] = live[key].astype(F32) + moved.astype(F32)
        live = left
        bit <<= 1
    return live[0]


def all_sum(values, axis):
    bit = 1
    while bit < lax.axis_size(axis):
        values = values + swap(values, axis, bit)
        bit <<= 1
    return values


def in_order(pieces, place, dim):
    bit = 1
    while bit < len(pieces):
        odd = (place & bit) > 0
        pieces = [jnp.where(odd, pieces[m ^ bit], pieces[m]) for m in range(len(pieces))]
        bit <<= 1
    return jnp.concatenate(pieces, axis=dim)


MESH = pl.DeviceIdType.MESH


class Wire:
    def __init__(self, sends, receives):
        self.sends, self.receives, self.count, self.copies = sends, receives, 0, []

    def send(self, source, target, **device):
        copy = pltpu.make_async_remote_copy(
            src_ref=source,
            dst_ref=target,
            send_sem=self.sends.at[self.count],
            recv_sem=self.receives.at[self.count],
            device_id=device,
            device_id_type=MESH,
        )
        copy.start()
        self.count += 1
        self.copies.append(Arrival(copy))
        return self.copies[-1]

    def finish(self):
        for copy in self.copies:
            copy.sent()


class Arrival:
    def __init__(self, copy):
        self.copy, self.waited, self.gone = copy, False, False

    def sent(self):
        if not self.gone:
            self.copy.wait_send()
        self.gone = True

    def wait(self):
        if not self.waited:
            self.copy.wait_recv()
        self.waited = True


def greet(partners):
    barrier = pltpu.get_barrier_semaphore()
    for device in partners:
        pl.semaphore_signal(barrier, inc=1, device_id=device, device_id_type=MESH)
    pl.semaphore_wait(barrier, len(partners))


def bits_down(count):
    bits, bit = [], count >> 1
    while bit:
        bits.append(bit)
        bit >>= 1
    return bits


def xor_order(count):
    order = [0]
    for bit in bits_down(count):
        order = order + [k | bit for k in order]
    return order


NT = (((1,), (1,)), ((), ()))
NN = (((1,), (0,)), ((), ()))


def mm(left, right, dims=NN):
    return lax.dot_general(left, right, dims, preferred_element_type=F32)


def fold_max(values):
    return jnp.max(values.reshape(values.shape[0] // 8, 8, values.shape[1]), axis=0)


def fold_sum(values):
    return jnp.sum(values.reshape(values.shape[0] // 8, 8, values.shape[1]), axis=0)


def skewed(row):
    width = row.shape[1]
    tall = jnp.broadcast_to(row, (LANES, width))
    return pltpu.roll(tall, width - (LANES - 1), 1, stride=1, stride_axis=0)


def unskew_sum(field):
    half = field.shape[0] // 2
    while half >= 1:
        field = pltpu.roll(field[:half], half, 1) + field[half:]
        half //= 2
    return field


def head_masks(rows):
    lane = lax.broadcasted_iota(jnp.int32, (rows, LANES), 1)
    return [(lane < HEAD_DIM).astype(BF16), (lane >= HEAD_DIM).astype(BF16)]


def score_tile(key_block, query_head, skew_ref, head, first, same):
    scores = mm(key_block, query_head, NT)
    tiles = []
    for s in range(BLOCK // LANES):
        column = pl.multiple_of(first - s * LANES, LANES)
        tiles.append(skew_ref[head, :, pl.ds(column, BLOCK)])
    return jnp.where(same, scores + jnp.concatenate(tiles, axis=0), NEG_FILL)


def attention_kernel(
    active_ref, base_ref, query_ref, key_ref, value_ref, window_ref, doc_row_ref, doc_col_ref,
    out_ref, total_ref, skew_ref, flip_ref, score_ref, most_ref, sum_ref, mix_ref,
):
    tokens, length = query_ref.shape[0], key_ref.shape[0]
    key_blocks = length // BLOCK
    masks = head_masks(BLOCK)
    for h in range(2):
        skew_ref[h] = skewed(window_ref[0, h : h + 1, :])

    @pl.loop(0, key_blocks)
    def _(kb):
        rows = pl.ds(pl.multiple_of(kb * BLOCK, BLOCK), BLOCK)
        flip_ref[:, rows] = value_ref[rows, :].T

    for qb in range(tokens // BLOCK):
        here = slice(qb * BLOCK, (qb + 1) * BLOCK)
        pair = query_ref[here, :] * jnp.asarray(HEAD_DIM**-0.5, BF16)
        query_heads = [pair * mask for mask in masks]
        doc_row = doc_row_ref[0:1, here]
        most_ref[...] = jnp.full_like(most_ref, NEG_FILL)
        sum_ref[...] = jnp.zeros_like(sum_ref)
        mix_ref[...] = jnp.zeros_like(mix_ref)

        @pl.loop(0, key_blocks)
        def _(kb):
            @pl.when(active_ref[qb, kb] > 0)
            def _():
                rows = pl.ds(pl.multiple_of(kb * BLOCK, BLOCK), BLOCK)
                column = doc_col_ref[rows, :]
                same = jnp.concatenate([column] * (BLOCK // LANES), axis=1) == doc_row
                for h in range(2):
                    tile = score_tile(
                        key_ref[rows, :], query_heads[h], skew_ref, h,
                        base_ref[kb] + qb * BLOCK, same,
                    )
                    score_ref[h, rows, :] = tile
                    most_ref[h] = jnp.maximum(most_ref[h], fold_max(tile))

        most = [jnp.max(most_ref[h], axis=0, keepdims=True) for h in range(2)]

        @pl.loop(0, key_blocks)
        def _(kb):
            @pl.when(active_ref[qb, kb] > 0)
            def _():
                rows = pl.ds(pl.multiple_of(kb * BLOCK, BLOCK), BLOCK)
                for h in range(2):
                    weights = jnp.exp(score_ref[h, rows, :] - most[h])
                    sum_ref[h] += fold_sum(weights)
                    mix_ref[h] += mm(
                        flip_ref[h * HEAD_DIM : (h + 1) * HEAD_DIM, rows], weights.astype(BF16)
                    )

        columns = []
        for h in range(2):
            total = jnp.sum(sum_ref[h], axis=0, keepdims=True)
            columns.append(mix_ref[h] / total)
            total_ref[0, h : h + 1, here] = most[h] + jnp.log(total)
        out_ref[here, :] = jnp.concatenate(columns, axis=0).T.astype(BF16)


def attention_back_kernel(
    active_ref, base_ref, query_ref, key_ref, value_ref, grad_ref, total_ref, window_ref,
    doc_row_ref, doc_col_ref,
    query_grad_ref, key_grad_ref, value_grad_ref, offset_ref,
    skew_ref, field_ref, flip_ref, weight_ref, change_ref, inner_ref, mix_ref, key_sum, value_sum,
):
    tokens, length = query_ref.shape[0], key_ref.shape[0]
    key_blocks = length // BLOCK
    masks = head_masks(BLOCK)
    for h in range(2):
        skew_ref[h] = skewed(window_ref[0, h : h + 1, :])
    field_ref[...] = jnp.zeros_like(field_ref)
    key_sum[...] = jnp.zeros_like(key_sum)
    value_sum[...] = jnp.zeros_like(value_sum)

    @pl.loop(0, key_blocks)
    def _(kb):
        rows = pl.ds(pl.multiple_of(kb * BLOCK, BLOCK), BLOCK)
        flip_ref[:, rows] = key_ref[rows, :].T

    for qb in range(tokens // BLOCK):
        here = slice(qb * BLOCK, (qb + 1) * BLOCK)
        pair = query_ref[here, :] * jnp.asarray(HEAD_DIM**-0.5, BF16)
        query_heads = [pair * mask for mask in masks]
        grad_pair = grad_ref[here, :]
        grad_heads = [grad_pair * mask for mask in masks]
        doc_row = doc_row_ref[0:1, here]
        inner_ref[...] = jnp.zeros_like(inner_ref)
        mix_ref[...] = jnp.zeros_like(mix_ref)
        totals = [total_ref[0, h : h + 1, here] for h in range(2)]

        @pl.loop(0, key_blocks)
        def _(kb):
            @pl.when(active_ref[qb, kb] > 0)
            def _():
                rows = pl.ds(pl.multiple_of(kb * BLOCK, BLOCK), BLOCK)
                column = doc_col_ref[rows, :]
                same = jnp.concatenate([column] * (BLOCK // LANES), axis=1) == doc_row
                for h in range(2):
                    tile = score_tile(
                        key_ref[rows, :], query_heads[h], skew_ref, h,
                        base_ref[kb] + qb * BLOCK, same,
                    )
                    weights = jnp.exp(tile - totals[h])
                    change = mm(value_ref[rows, :], grad_heads[h], NT)
                    weight_ref[h, rows, :] = weights
                    change_ref[h, rows, :] = change
                    inner_ref[h] += fold_sum(weights * change)

        inner = [jnp.sum(inner_ref[h], axis=0, keepdims=True) for h in range(2)]

        @pl.loop(0, key_blocks)
        def _(kb):
            @pl.when(active_ref[qb, kb] > 0)
            def _():
                rows = pl.ds(pl.multiple_of(kb * BLOCK, BLOCK), BLOCK)
                key_part = value_part = None
                for h in range(2):
                    weights = weight_ref[h, rows, :]
                    score_grad = weights * (change_ref[h, rows, :] - inner[h])
                    for s in range(BLOCK // LANES):
                        first = pl.multiple_of(base_ref[kb] + qb * BLOCK - s * LANES, LANES)
                        field_ref[h, :, pl.ds(first, BLOCK)] += score_grad[
                            s * LANES : (s + 1) * LANES
                        ]
                    low = score_grad.astype(BF16)
                    key_here = mm(low, query_heads[h])
                    value_here = mm(weights.astype(BF16), grad_heads[h])
                    key_part = key_here if h == 0 else key_part + key_here
                    value_part = value_here if h == 0 else value_part + value_here
                    mix_ref[h] += mm(flip_ref[h * HEAD_DIM : (h + 1) * HEAD_DIM, rows], low)
                key_sum[rows, :] += key_part
                value_sum[rows, :] += value_part

        both = jnp.concatenate([mix_ref[0], mix_ref[1]], axis=0) * HEAD_DIM**-0.5
        query_grad_ref[here, :] = both.T.astype(BF16)

    key_grad_ref[...] = key_sum[...].astype(BF16)
    value_grad_ref[...] = value_sum[...].astype(BF16)
    for h in range(2):
        offset_ref[0, h : h + 1, :] = unskew_sum(field_ref[h])


def attention_specs(tokens, length, pairs, width):
    smem = pl.BlockSpec(memory_space=pltpu.SMEM)
    return dict(
        smem=smem,
        query=pl.BlockSpec((tokens, LANES), lambda i: (0, i)),
        key=pl.BlockSpec((length, LANES), lambda i: (0, i)),
        value=pl.BlockSpec((length, LANES), lambda i: (0, i + pairs)),
        window=pl.BlockSpec((1, 8, width), lambda i: (i, 0, 0)),
        total=pl.BlockSpec((1, 8, tokens), lambda i: (i, 0, 0)),
        doc_row=pl.BlockSpec((8, tokens), lambda i: (0, 0)),
        doc_col=pl.BlockSpec((length, LANES), lambda i: (0, 0)),
    )


def attention(active, base, queries, key_values, window, doc_row, doc_col):
    tokens, length = queries.shape[0], key_values.shape[0]
    pairs, width = window.shape[0], window.shape[2]
    specs = attention_specs(tokens, length, pairs, width)
    return pl.pallas_call(
        attention_kernel,
        grid=(pairs,),
        in_specs=[
            specs["smem"], specs["smem"], specs["query"], specs["key"], specs["value"],
            specs["window"], specs["doc_row"], specs["doc_col"],
        ],
        out_specs=[specs["query"], specs["total"]],
        out_shape=[
            jax.ShapeDtypeStruct(queries.shape, BF16),
            jax.ShapeDtypeStruct((pairs, 8, tokens), F32),
        ],
        scratch_shapes=[
            pltpu.VMEM((2, LANES, width), F32),
            pltpu.VMEM((LANES, length), BF16),
            pltpu.VMEM((2, length, BLOCK), F32),
            pltpu.VMEM((2, 8, BLOCK), F32),
            pltpu.VMEM((2, 8, BLOCK), F32),
            pltpu.VMEM((2, HEAD_DIM, BLOCK), F32),
        ],
        compiler_params=pltpu.CompilerParams(vmem_limit_bytes=VMEM_CAP),
        cost_estimate=cost(25),
        name="attention_forward",
    )(active, base, queries, key_values, key_values, window, doc_row, doc_col)


def attention_back(active, base, queries, key_values, grads, totals, window, doc_row, doc_col):
    tokens, length = queries.shape[0], key_values.shape[0]
    pairs, width = window.shape[0], window.shape[2]
    specs = attention_specs(tokens, length, pairs, width)
    return pl.pallas_call(
        attention_back_kernel,
        grid=(pairs,),
        in_specs=[
            specs["smem"], specs["smem"], specs["query"], specs["key"], specs["value"],
            specs["query"], specs["total"], specs["window"], specs["doc_row"], specs["doc_col"],
        ],
        out_specs=[specs["query"], specs["key"], specs["key"], specs["window"]],
        out_shape=[
            jax.ShapeDtypeStruct(queries.shape, BF16),
            jax.ShapeDtypeStruct((length, queries.shape[1]), BF16),
            jax.ShapeDtypeStruct((length, queries.shape[1]), BF16),
            jax.ShapeDtypeStruct((pairs, 8, width), F32),
        ],
        scratch_shapes=[
            pltpu.VMEM((2, LANES, width), F32),
            pltpu.VMEM((2, LANES, width), F32),
            pltpu.VMEM((LANES, length), BF16),
            pltpu.VMEM((2, length, BLOCK), F32),
            pltpu.VMEM((2, length, BLOCK), F32),
            pltpu.VMEM((2, 8, BLOCK), F32),
            pltpu.VMEM((2, HEAD_DIM, BLOCK), F32),
            pltpu.VMEM((length, LANES), F32),
            pltpu.VMEM((length, LANES), F32),
        ],
        compiler_params=pltpu.CompilerParams(vmem_limit_bytes=VMEM_CAP),
        cost_estimate=cost(40),
        name="attention_backward",
    )(active, base, queries, key_values, key_values, grads, totals, window, doc_row, doc_col)


def start_kernel(
    experts, dp_count, ctx_count, pack_ref, hidden_ref, docs_ref,
    query_ref, pair_ref, normed_ref, weight_out, own_ref, lanes_ref, gains_ref, docs_out,
    weights, hidden, docs, sends, receives, out_sem,
):
    d, c = lax.axis_index("dp"), lax.axis_index("ctx")
    rows = pack_ref.shape[0]
    tokens, width = query_ref.shape
    greet(
        [{"ctx": c ^ m} for m in range(1, ctx_count)]
        + [{"dp": d ^ bit} for bit in bits_down(dp_count)]
    )
    wire = Wire(sends, receives)

    def shard(m, j):
        index = (d ^ m) * ctx_count + (c ^ j)
        return weights.at[pl.ds(pl.multiple_of(index * rows, rows), rows)]

    weights[pl.ds(pl.multiple_of((d * ctx_count + c) * rows, rows), rows), :] = pack_ref[...]
    docs_sent = [wire.send(docs_ref, docs.at[m], ctx=c ^ m) for m in range(1, ctx_count)]
    sides = [0]
    hidden_sent = {}
    for bit in bits_down(ctx_count)[:-1]:
        arrivals = [wire.send(shard(0, j), shard(0, j), ctx=c ^ bit) for j in sides]
        for m in [0] + list(hidden_sent):
            source = hidden_ref if m == 0 else hidden.at[m]
            if m:
                hidden_sent[m].wait()
            hidden_sent[m | bit] = wire.send(source, hidden.at[m | bit], ctx=c ^ bit)
        for copy in arrivals:
            copy.wait()
        sides = sides + [j | bit for j in sides]
    hidden_sent[1] = wire.send(hidden_ref, hidden.at[1], ctx=c ^ 1)
    groups, crossed = {}, []
    for m in xor_order(dp_count):
        if m:
            for copy in groups[m]:
                copy.wait()
        for bit in bits_down(dp_count):
            if m & (2 * bit - 1) == 0:
                groups[m | bit] = [
                    wire.send(shard(m, j), shard(m, j), dp=d ^ bit) for j in sides
                ]
        crossed += [wire.send(shard(m, j), shard(m, j), ctx=c ^ 1) for j in sides]
        if m == 0:
            for k in [k for k in hidden_sent if k > 1]:
                hidden_sent[k].wait()
                hidden_sent[k | 1] = wire.send(hidden.at[k], hidden.at[k | 1], ctx=c ^ 1)
    for copy in crossed:
        copy.wait()
    keep = pltpu.make_async_copy(weights.at[:, : 3 * width], weight_out, out_sem.at[0])
    keep.start()
    keep_own = pltpu.make_async_copy(weights.at[:, 3 * width + LANES :], own_ref, out_sem.at[1])
    keep_own.start()
    small = weights[:, 3 * width : 3 * width + LANES].astype(F32)
    lane = lax.broadcasted_iota(jnp.int32, small.shape, 1)
    lanes_ref[...] = jnp.where(lane < experts, small, 0.0).astype(BF16)
    gain_one = jnp.sum(jnp.where(lane == experts, small, 0.0), axis=1, keepdims=True)
    gain_two = jnp.sum(jnp.where(lane == experts + 1, small, 0.0), axis=1, keepdims=True)
    both = jnp.where(lane == 0, gain_one, jnp.where(lane == 1, gain_two, 0.0)).T
    gains_ref[...] = both[:8]
    gain = both[0:1]
    docs_out[0] = docs_ref[...]
    for m in range(ctx_count):
        if m:
            docs_sent[m - 1].wait()
            docs_out[m] = docs[m]
            hidden_sent[m].wait()
        values = (hidden[m] if m else hidden_ref[...]).astype(F32)
        scale = lax.rsqrt(jnp.mean(values * values, axis=-1, keepdims=True) + NORM_EPS)
        normed = (values * scale * gain).astype(BF16)
        pair_ref[m * tokens : (m + 1) * tokens, :] = mm(
            normed, weights[:, width : 3 * width]
        ).astype(BF16)
        if m == 0:
            normed_ref[...] = normed
            query_ref[...] = mm(normed, weights[:, :width]).astype(BF16)
    keep.wait()
    keep_own.wait()
    wire.finish()


def start(pack, hidden, docs, width, experts):
    tokens = hidden.shape[0]
    columns = pack.shape[1]
    dp_count, ctx_count = lax.axis_size("dp"), lax.axis_size("ctx")
    copies = 2 * (ctx_count - 1) + ctx_count // 2 + dp_count * ctx_count
    vmem = pl.BlockSpec(memory_space=pltpu.VMEM)
    hbm = pl.BlockSpec(memory_space=pl.ANY)
    return pl.pallas_call(
        functools.partial(start_kernel, experts, dp_count, ctx_count),
        in_specs=[vmem] * 3,
        out_specs=[vmem, vmem, vmem, hbm, hbm, vmem, vmem, vmem],
        out_shape=[
            jax.ShapeDtypeStruct((tokens, width), BF16),
            jax.ShapeDtypeStruct((tokens * ctx_count, 2 * width), BF16),
            jax.ShapeDtypeStruct((tokens, D), BF16),
            jax.ShapeDtypeStruct((D, 3 * width), BF16),
            jax.ShapeDtypeStruct((D, width), BF16),
            jax.ShapeDtypeStruct((D, LANES), BF16),
            jax.ShapeDtypeStruct((8, D), F32),
            jax.ShapeDtypeStruct((ctx_count, 8, tokens), jnp.int32),
        ],
        scratch_shapes=[
            pltpu.VMEM((D, columns), BF16),
            pltpu.VMEM((ctx_count, tokens, D), BF16),
            pltpu.VMEM((ctx_count, 8, tokens), jnp.int32),
            pltpu.SemaphoreType.DMA((copies,)),
            pltpu.SemaphoreType.DMA((copies,)),
            pltpu.SemaphoreType.DMA((2,)),
        ],
        compiler_params=pltpu.CompilerParams(
            vmem_limit_bytes=VMEM_CAP, collective_id=1, has_side_effects=True
        ),
        cost_estimate=cost(60),
        name="start",
    )(pack, hidden, docs)


TN = (((0,), (0,)), ((), ()))


def bent_parts(value):
    square = value * value
    wave = jnp.tanh(GELU_K * value * (1.0 + GELU_C * square))
    half = 0.5 * (1.0 + wave)
    slope = half + 0.5 * value * (1.0 - wave * wave) * (GELU_K * (1.0 + 3.0 * GELU_C * square))
    return value * half, slope


def expert_kernel(
    experts, dp_count, ctx_count, tp_count, attended_ref, hidden_ref, out_grad_ref, gains_ref,
    lanes_ref, picker_ref, *refs,
):
    d, c, t = lax.axis_index("dp"), lax.axis_index("ctx"), lax.axis_index("tp")
    outs, refs = refs[:tp_count], refs[tp_count:]
    grads, refs = refs[:dp_count], refs[dp_count:]
    ins, downs, refs = refs[:ctx_count], refs[ctx_count : 2 * ctx_count], refs[2 * ctx_count :]
    (middle_ref, normed_ref, logit_ref, grad_ref, low_ref, attended_grad_ref, gain_ref, out_parts,
     in_keep, down_keep, in_core, down_core,
     mixed, out_all, in_all, down_all, rows_all, scaled_all, act_all, gate_all, up_all, send_rows,
     row_parts, row_in, row_back, dot_parts, dot_in, dot_home, dot_back, probs, whole,
     sends, receives, in_sems, keep_sems) = refs
    tokens, width = attended_ref.shape
    share = D // tp_count
    slots = rows_all.shape[0] // dp_count
    depth, ff = ins[0].shape[1], ins[0].shape[2]
    shares = range(1, tp_count)
    order = [0] + list(range(2, dp_count)) + [1]

    local = []

    def load(source, target):
        copy = pltpu.make_async_copy(source, target, in_sems.at[len(local)])
        copy.start()
        local.append(copy)
        return copy

    out_copies = [
        load(outs[m], out_all.at[:, pl.ds(pl.multiple_of((t ^ m) * width, width), width)])
        for m in range(tp_count)
    ]
    weight_copies = []
    for j in range(ctx_count):
        part = slice(j * depth, (j + 1) * depth)
        weight_copies.append(load(ins[j], in_all.at[:, part, :]))
        weight_copies.append(load(downs[j], down_all.at[:, part]))
    for m in range(dp_count):
        weight_copies.append(load(grads[m], scaled_all.at[m * slots : (m + 1) * slots]))
    own_lanes = pl.ds(pl.multiple_of(t * width, width), width)
    mixed[:, own_lanes] = attended_ref[...]
    greet(
        [{"tp": t ^ k} for k in shares]
        + [{"dp": d ^ m} for m in range(1, dp_count)]
        + [{"ctx": c ^ 1}]
    )
    wire = Wire(sends, receives)
    arrivals = [wire.send(mixed.at[:, own_lanes], mixed.at[:, own_lanes], tp=t ^ k) for k in shares]
    for copy in out_copies:
        copy.wait()
    for copy in arrivals:
        copy.wait()
    middle = hidden_ref[...].astype(F32) + mm(mixed[...], out_all[...], NT)
    middle_ref[...] = middle
    scale = lax.rsqrt(jnp.mean(middle * middle, axis=-1, keepdims=True) + NORM_EPS)
    normed = (middle * scale * gains_ref[1:2, :]).astype(BF16)
    normed_ref[...] = normed
    own_share = pl.ds(pl.multiple_of(t * share, share), share)
    far = {}

    def block(m):
        return slice(m * slots, (m + 1) * slots)

    for m in order[1:] + [0]:
        picked = mm(picker_ref[:, block(m)], normed_ref[...], TN).astype(BF16)
        if m:
            send_rows[m - 1] = picked
            far[m] = wire.send(
                send_rows.at[m - 1, :, own_share], rows_all.at[block(m), own_share], dp=d ^ m
            )
        else:
            rows_all[block(0), :] = picked
    lane = lax.broadcasted_iota(jnp.int32, (tokens, LANES), 1)

    def router_probs(values):
        logits = mm(values, lanes_ref[...])
        where = lax.broadcasted_iota(jnp.int32, logits.shape, 1)
        logits = jnp.where(where < experts, logits, NEG_FILL)
        powers = jnp.exp(logits - jnp.max(logits, axis=1, keepdims=True))
        return where, powers / jnp.sum(powers, axis=1, keepdims=True)

    probs[...] = router_probs(normed_ref[...])[1]
    for copy in weight_copies:
        copy.wait()
    columns = [pl.ds(pl.multiple_of((c ^ j) * depth, depth), depth) for j in range(ctx_count)]
    spread, returned, dot_returned = {}, {}, {}

    def forward(m):
        far[m].wait()
        half = rows_all.at[block(m), own_share]
        spread[m] = [wire.send(half, half, tp=t ^ k) for k in shares]

    def experts_on(m, hook):
        here = block(m)
        where, chance = router_probs(rows_all[here, :])
        gate = jnp.sum(jnp.where(where == d, chance, 0.0), axis=1, keepdims=True)
        rows = jnp.concatenate([rows_all[here, part] for part in columns], axis=1)
        grad_rows = jnp.concatenate([scaled_all[here, part] for part in columns], axis=1)
        rows_all[here, :] = rows
        scaled_all[here, :] = (gate * grad_rows.astype(F32)).astype(BF16)
        dots = jnp.zeros((slots, LANES), F32)
        for first in range(0, ff, BLOCK):
            part = slice(first, min(ff, first + BLOCK))
            value = mm(rows, in_all[0, :, part])
            up = mm(rows, in_all[1, :, part])
            back = mm(grad_rows, down_all[part, :], NT)
            bent, slope = bent_parts(value)
            act = (bent * up).astype(BF16)
            act_all[here, part] = act
            dots += jnp.sum(act.astype(F32) * back, axis=1, keepdims=True)
            scaled = gate * back
            gate_all[here, part] = (scaled * up * slope).astype(BF16)
            up_all[here, part] = (scaled * bent).astype(BF16)
        if hook is not None:
            hook()
        dot_parts[m] = dots.T[:8]
        dot_returned[m] = [
            wire.send(dot_parts.at[m], dot_in.at[k - 1, m], tp=t ^ k) for k in shares
        ]
        for k in list(shares) + [0]:
            for i in range(share // depth):
                piece = ((t ^ k) * (share // depth) + i) ^ c
                part = pl.ds(pl.multiple_of(piece * depth, depth), depth)
                row = mm(gate_all[here, :], in_all[0, part, :], NT)
                row += mm(up_all[here, :], in_all[1, part, :], NT)
                row_parts[k, m, :, i * depth : (i + 1) * depth] = row.astype(BF16)
            if k:
                returned.setdefault(m, []).append(
                    wire.send(row_parts.at[k, m], row_in.at[k - 1, m], tp=t ^ k)
                )
        for k in range(tp_count):
            for i in range(share // depth):
                piece = ((t ^ k) * (share // depth) + i) ^ c
                part = pl.ds(pl.multiple_of(piece * depth, depth), depth)
                out_parts[k, m, :, i * depth : (i + 1) * depth] = (
                    gate * mm(act_all[here, :], down_all[:, part])
                ).astype(BF16)

    homeward = []

    def send_home(m):
        for copy in dot_returned[m]:
            copy.wait()
        dots = tree_sum([dot_parts[m]] + [dot_in[k - 1, m] for k in shares])
        total = row_parts[0, m].astype(F32)
        for k, copy in zip(shares, returned[m]):
            copy.wait()
            total = total + row_in[k - 1, m].astype(F32)
        if m:
            dot_home[m] = dots
            row_parts[0, m] = total.astype(BF16)
            homeward.append(wire.send(dot_home.at[m], dot_back.at[m], dp=d ^ m))
            homeward.append(wire.send(row_parts.at[0, m], row_back.at[block(m)], dp=d ^ m))
        else:
            dot_back[0] = dots
            row_back[block(0), :] = total.astype(BF16)

    for i, m in enumerate(order):
        for copy in spread.get(m, []):
            copy.wait()
            copy.sent()
        hook = functools.partial(forward, order[i + 1]) if i + 1 < len(order) else None
        experts_on(m, hook)
        if i:
            send_home(order[i - 1])

    def in_grads(j):
        part = slice(j * depth, (j + 1) * depth)
        for side, right in enumerate((gate_all, up_all)):
            in_all[side, part, :] = mm(rows_all[:, part], right[...], TN).astype(BF16)

    keeps = []

    def keep(source, target):
        copy = pltpu.make_async_copy(source, target, keep_sems.at[len(keeps)])
        copy.start()
        keeps.append(copy)

    near = []
    in_grads(1)
    send_home(order[-1])
    for j in range(1, ctx_count, 2):
        part = slice(j * depth, (j + 1) * depth)
        if j > 1:
            in_grads(j)
        near.append(wire.send(in_all.at[:, part, :], in_core.at[j // 2], ctx=c ^ 1))
    for first in range(0, ff, BLOCK):
        part = slice(first, min(ff, first + BLOCK))
        down_all[part, :] = mm(act_all[:, part], scaled_all[...], TN).astype(BF16)
    for j in range(ctx_count):
        part = slice(j * depth, (j + 1) * depth)
        if j % 2:
            near.append(wire.send(down_all.at[:, part], down_core.at[j // 2], ctx=c ^ 1))
        else:
            keep(down_all.at[:, part], down_keep.at[j // 2])
    for j in range(0, ctx_count, 2):
        in_grads(j)
        keep(in_all.at[:, j * depth : (j + 1) * depth, :], in_keep.at[j // 2])

    for copy in homeward:
        copy.wait()
    result = mm(picker_ref[...], row_back[...])
    prob_grad = jnp.zeros((tokens, LANES), F32)
    for m in range(dp_count):
        high = dot_back[m].astype(BF16)
        rest = dot_back[m] - high.astype(F32)
        middle_part = rest.astype(BF16)
        tiny = (rest - middle_part.astype(F32)).astype(BF16)
        total = mm(picker_ref[:, block(m)], high, NT)
        total += mm(picker_ref[:, block(m)], middle_part, NT)
        total += mm(picker_ref[:, block(m)], tiny, NT)
        prob_grad = jnp.where(lane == (d ^ m), total[:, 0:1], prob_grad)
    chance = probs[...]
    logit = chance * (prob_grad - jnp.sum(chance * prob_grad, axis=1, keepdims=True))
    logit_ref[...] = logit
    more = lax.dot_general(
        logit, lanes_ref[own_share, :].astype(F32), NT, precision=lax.Precision.HIGHEST,
        preferred_element_type=F32,
    )
    whole[:, own_share] = (result + more).astype(BF16)
    arrivals = [wire.send(whole.at[:, own_share], whole.at[:, own_share], tp=t ^ k) for k in shares]
    for copy in arrivals:
        copy.wait()
    middle = middle_ref[...]
    gradient = whole[...].astype(F32)
    scale = lax.rsqrt(jnp.mean(middle * middle, axis=-1, keepdims=True) + NORM_EPS)
    weighted = gains_ref[1:2, :] * gradient
    inner = jnp.mean(middle * weighted, axis=-1, keepdims=True)
    gain_ref[...] = fold_sum(gradient * middle * scale)
    total = out_grad_ref[...].astype(F32) + (
        scale * weighted - middle * (scale * scale * scale) * inner
    )
    grad_ref[...] = total
    low_ref[...] = total.astype(BF16)
    attended_grad_ref[...] = mm(low_ref[...], out_all[:, own_lanes]).astype(BF16)
    for copy in keeps:
        copy.wait()
    for copy in near:
        copy.wait()
    wire.finish()


def expert_step(
    attended, hidden, out_grad, gains, lanes, picker_flip, outs, grads, ins, downs, experts
):
    dp_count, ctx_count, tp_count = (lax.axis_size(a) for a in ("dp", "ctx", "tp"))
    tokens, width = attended.shape
    slots = grads[0].shape[0]
    share = D // tp_count
    depth, ff = ins[0].shape[1], ins[0].shape[2]
    all_slots = dp_count * slots
    half = ctx_count // 2
    others = tp_count - 1
    copies = others * (2 + 3 * dp_count) + 3 * dp_count + 2 * half
    vmem = pl.BlockSpec(memory_space=pltpu.VMEM)
    hbm = pl.BlockSpec(memory_space=pl.ANY)
    shape = jax.ShapeDtypeStruct
    return pl.pallas_call(
        functools.partial(expert_kernel, experts, dp_count, ctx_count, tp_count),
        in_specs=[vmem] * 6 + [hbm] * (tp_count + dp_count + 2 * ctx_count),
        out_specs=[vmem] * 8 + [hbm] * 4,
        out_shape=[
            shape((tokens, D), F32),
            shape((tokens, D), BF16),
            shape((tokens, LANES), F32),
            shape((tokens, D), F32),
            shape((tokens, D), BF16),
            shape((tokens, width), BF16),
            shape((8, D), F32),
            shape((tp_count, dp_count, slots, share), BF16),
            shape((half, 2, depth, ff), BF16),
            shape((half, ff, depth), BF16),
            shape((half, 2, depth, ff), BF16),
            shape((half, ff, depth), BF16),
        ],
        scratch_shapes=[
            pltpu.VMEM((tokens, tp_count * width), BF16),
            pltpu.VMEM((D, tp_count * width), BF16),
            pltpu.VMEM((2, D, ff), BF16),
            pltpu.VMEM((ff, D), BF16),
            pltpu.VMEM((all_slots, D), BF16),
            pltpu.VMEM((all_slots, D), BF16),
            pltpu.VMEM((all_slots, ff), BF16),
            pltpu.VMEM((all_slots, ff), BF16),
            pltpu.VMEM((all_slots, ff), BF16),
            pltpu.VMEM((dp_count - 1, slots, D), BF16),
            pltpu.VMEM((tp_count, dp_count, slots, share), BF16),
            pltpu.VMEM((others, dp_count, slots, share), BF16),
            pltpu.VMEM((all_slots, share), BF16),
            pltpu.VMEM((dp_count, 8, slots), F32),
            pltpu.VMEM((others, dp_count, 8, slots), F32),
            pltpu.VMEM((dp_count, 8, slots), F32),
            pltpu.VMEM((dp_count, 8, slots), F32),
            pltpu.VMEM((tokens, LANES), F32),
            pltpu.VMEM((tokens, D), BF16),
            pltpu.SemaphoreType.DMA((copies,)),
            pltpu.SemaphoreType.DMA((copies,)),
            pltpu.SemaphoreType.DMA((tp_count + 2 * ctx_count + dp_count,)),
            pltpu.SemaphoreType.DMA((ctx_count,)),
        ],
        compiler_params=pltpu.CompilerParams(
            vmem_limit_bytes=VMEM_CAP, collective_id=3, has_side_effects=True
        ),
        cost_estimate=cost(120),
        name="expert_step",
    )(attended, hidden, out_grad, gains, lanes, picker_flip, *outs, *grads, *ins, *downs)


def final_kernel(
    experts, dp_count, ctx_count, tp_count,
    query_grad_ref, key_ref, value_ref, normed_ref, weight_ref, low_ref, attended_ref,
    normed_two_ref, logit_ref, hidden_ref, gains_ref, gain_two_ref, middle_grad_ref,
    input_grad_ref, first_ref, second_ref,
    key_in, send_far, far_in, first_all, second_all, first_core, second_core, first_sum,
    second_sum, first_dp, second_dp, first_x, second_x, rows_all, token_grad, token_in,
    gain_send, gain_in, sends, receives,
):
    d, c, t = lax.axis_index("dp"), lax.axis_index("ctx"), lax.axis_index("tp")
    tokens, width = query_grad_ref.shape
    dp_bits = bits_down(dp_count)[::-1]
    far_bits = bits_down(ctx_count)[:-1][::-1]
    far = list(range(0, ctx_count, 2))
    greet(
        [{"ctx": c ^ bit} for bit in bits_down(ctx_count)]
        + [{"dp": d ^ bit} for bit in dp_bits]
        + [{"tp": t ^ bit} for bit in bits_down(tp_count)]
    )
    wire = Wire(sends, receives)

    near = []
    for k in far[::-1]:
        rows = slice((k + 1) * tokens, (k + 2) * tokens)
        for side, ref in enumerate((key_ref, value_ref)):
            near.append(wire.send(ref.at[rows], key_in.at[side, k // 2], ctx=c ^ 1))

    def split(values):
        return values.astype(BF16).reshape(dp_count, ctx_count, -1, values.shape[1])

    first_all[:, :, :, :width] = split(mm(normed_ref[...], query_grad_ref[...], TN))
    first_all[:, :, :, width:] = split(mm(low_ref[...], attended_ref[...], TN))

    def cross(whole, landed):
        return [wire.send(whole.at[:, c ^ (k + 1)], landed.at[k // 2], ctx=c ^ 1) for k in far]

    def add_core(whole, landed, total, copies):
        for k, copy in zip(far, copies):
            copy.wait()
            own = whole[:, pl.ds(c ^ k, 1)][:, 0]
            total[k // 2] = (own.astype(F32) + landed[k // 2].astype(F32)).astype(BF16)

    first_crossed = cross(first_all, first_core)
    for copy in near:
        copy.wait()
    for k in far:
        rows = slice(k * tokens, (k + 1) * tokens)
        for side, ref in enumerate((key_ref, value_ref)):
            send_far[side, k // 2] = (
                ref[rows, :].astype(F32) + key_in[side, k // 2].astype(F32)
            ).astype(BF16)
    assert len(far_bits) == 1
    far_copies = [
        wire.send(send_far.at[side, 1], far_in.at[side], ctx=c ^ 2) for side in range(2)
    ]

    def dp_send(total, landed, level, bit, sides):
        copies = []
        for m in range(bit, dp_count, 2 * bit):
            for k in sides:
                spot = landed.at[level, k, d ^ m]
                copies.append((m ^ bit, k, wire.send(total.at[k, d ^ m], spot, dp=d ^ bit)))
        return copies

    def dp_add(total, landed, level, copies):
        for m, k, copy in copies:
            copy.wait()
            own = total[k, pl.ds(d ^ m, 1)][0]
            other = landed[level, k, pl.ds(d ^ m, 1)][0]
            total[k, pl.ds(d ^ m, 1)] = (own.astype(F32) + other.astype(F32)).astype(BF16)[None]

    add_core(first_all, first_core, first_sum, first_crossed)
    moving = dp_send(first_sum, first_dp, 0, dp_bits[0], range(len(far)))
    token_grad[...] = mm(query_grad_ref[...], weight_ref[:, :width], NT)
    logit = logit_ref[...]
    logit_high = logit.astype(BF16)
    logit_rest = logit - logit_high.astype(F32)
    logit_low = logit_rest.astype(BF16)
    logit_tiny = (logit_rest - logit_low.astype(F32)).astype(BF16)
    router_grad = mm(normed_two_ref[...], logit_high, TN)
    router_grad += mm(normed_two_ref[...], logit_low, TN)
    router_grad += mm(normed_two_ref[...], logit_tiny, TN)
    rows_all[:, :width] = query_grad_ref[...]
    for level, bit in enumerate(dp_bits):
        dp_add(first_sum, first_dp, level, moving)
        if level + 1 < len(dp_bits):
            moving = dp_send(
                first_sum, first_dp, level + 1, dp_bits[level + 1], range(len(far))
            )
    first_far = wire.send(first_sum.at[1, d], first_x, ctx=c ^ 2)

    for side in range(2):
        far_copies[side].wait()
        rows_all[:, (side + 1) * width : (side + 2) * width] = (
            send_far[side, 0].astype(F32) + far_in[side].astype(F32)
        ).astype(BF16)
    part = token_grad[...] + mm(rows_all[:, width:], weight_ref[:, width:], NT)
    part_low = part.astype(BF16)
    inputs = hidden_ref[...].astype(F32)
    scale = lax.rsqrt(jnp.mean(inputs * inputs, axis=-1, keepdims=True) + NORM_EPS)
    gain_send[0] = fold_sum(part_low.astype(F32) * inputs * scale)
    token_in[0] = part_low
    gain_total = gain_send[0]
    gain_copies, token_copies = [], []
    tp_bits = bits_down(tp_count)[::-1]
    gain_copies.append(wire.send(gain_send.at[0], gain_in.at[0], tp=t ^ tp_bits[0]))
    token_copies.append(wire.send(token_in.at[0], token_in.at[1], tp=t ^ tp_bits[0]))
    second_all[:, :, :, : 2 * width] = split(mm(normed_ref[...], rows_all[:, width:], TN))
    for level, bit in enumerate(tp_bits):
        if level:
            gain_send[level] = gain_total
            gain_copies.append(wire.send(gain_send.at[level], gain_in.at[level], tp=t ^ bit))
        gain_copies[level].wait()
        gain_total = gain_total + gain_in[level]
    gain_one = jnp.sum(gain_total, axis=0, keepdims=True)
    gain_two = jnp.sum(gain_two_ref[...], axis=0, keepdims=True)
    row = lax.broadcasted_iota(jnp.int32, (LANES, D), 0)
    gain_rows = jnp.where(row == experts, gain_one, jnp.where(row == experts + 1, gain_two, 0.0))
    second_all[:, :, :, 2 * width :] = split(router_grad + gain_rows.T)
    second_crossed = cross(second_all, second_core)

    add_core(second_all, second_core, second_sum, second_crossed)
    second_far = wire.send(second_sum.at[1], second_x, ctx=c ^ 2)
    total = part_low.astype(F32)
    for level, bit in enumerate(tp_bits):
        if level:
            token_in[2 * level] = total.astype(BF16)
            total = token_in[2 * level].astype(F32)
            token_copies.append(
                wire.send(token_in.at[2 * level], token_in.at[2 * level + 1], tp=t ^ bit)
            )
        token_copies[level].wait()
        total = total + token_in[2 * level + 1].astype(F32)
    weighted = gains_ref[0:1, :] * total
    inner = jnp.mean(inputs * weighted, axis=-1, keepdims=True)
    input_grad_ref[...] = (
        middle_grad_ref[...] + scale * weighted - inputs * (scale * scale * scale) * inner
    )
    first_far.wait()
    first_ref[...] = first_sum[0, pl.ds(d, 1)][0].astype(F32) + first_x[...].astype(F32)
    second_far.wait()
    second_sum[0] = (second_sum[0].astype(F32) + second_x[...].astype(F32)).astype(BF16)
    for level, bit in enumerate(dp_bits):
        moving = dp_send(second_sum, second_dp, level, bit, [0])
        dp_add(second_sum, second_dp, level, moving)
    second_ref[...] = second_sum[0, pl.ds(d, 1)][0].astype(F32)
    wire.finish()


def final_step(
    query_grad, key_part, value_part, normed, weight, low, attended, normed_two, logit, hidden,
    gains, gain_two, middle_grad, experts,
):
    tokens, width = query_grad.shape
    dp_count, ctx_count, tp_count = (lax.axis_size(a) for a in ("dp", "ctx", "tp"))
    rows = D // (dp_count * ctx_count)
    half = ctx_count // 2
    levels = len(bits_down(dp_count))
    tp_levels = len(bits_down(tp_count))
    one, two = 2 * width, 2 * width + LANES
    copies = 4 * half + 2 * half + 4 + 2 * tp_levels + (half + 1) * dp_count + 2
    vmem = pl.BlockSpec(memory_space=pltpu.VMEM)
    return pl.pallas_call(
        functools.partial(final_kernel, experts, dp_count, ctx_count, tp_count),
        in_specs=[vmem] * 13,
        out_specs=[vmem] * 3,
        out_shape=[
            jax.ShapeDtypeStruct((tokens, D), F32),
            jax.ShapeDtypeStruct((rows, one), F32),
            jax.ShapeDtypeStruct((rows, two), F32),
        ],
        scratch_shapes=[
            pltpu.VMEM((2, half, tokens, width), BF16),
            pltpu.VMEM((2, half, tokens, width), BF16),
            pltpu.VMEM((2, tokens, width), BF16),
            pltpu.VMEM((dp_count, ctx_count, rows, one), BF16),
            pltpu.VMEM((dp_count, ctx_count, rows, two), BF16),
            pltpu.VMEM((half, dp_count, rows, one), BF16),
            pltpu.VMEM((half, dp_count, rows, two), BF16),
            pltpu.VMEM((half, dp_count, rows, one), BF16),
            pltpu.VMEM((half, dp_count, rows, two), BF16),
            pltpu.VMEM((levels, half, dp_count, rows, one), BF16),
            pltpu.VMEM((levels, 1, dp_count, rows, two), BF16),
            pltpu.VMEM((rows, one), BF16),
            pltpu.VMEM((dp_count, rows, two), BF16),
            pltpu.VMEM((tokens, 3 * width), BF16),
            pltpu.VMEM((tokens, D), F32),
            pltpu.VMEM((2 * tp_levels, tokens, D), BF16),
            pltpu.VMEM((tp_levels, 8, D), F32),
            pltpu.VMEM((tp_levels, 8, D), F32),
            pltpu.SemaphoreType.DMA((copies,)),
            pltpu.SemaphoreType.DMA((copies,)),
        ],
        compiler_params=pltpu.CompilerParams(
            vmem_limit_bytes=VMEM_CAP, collective_id=2, has_side_effects=True
        ),
        cost_estimate=cost(87),
        name="final_step",
    )(
        query_grad, key_part, value_part, normed, weight, low, attended, normed_two, logit,
        hidden, gains, gain_two, middle_grad,
    )


def shards(
    hidden_in,
    out_grad,
    segments,
    routes,
    bucket_table,
    qkv_weight,
    out_weight,
    router,
    norm_gains,
    position_bias,
    expert_in,
    expert_down,
    qkv_first,
    qkv_second,
    out_first,
    out_second,
    router_first,
    router_second,
    gains_first,
    gains_second,
    bias_first,
    bias_second,
    in_first,
    in_second,
    down_first,
    down_second,
):
    tokens = hidden_in.shape[0]
    dp_count, ctx_count, tp_count = (lax.axis_size(a) for a in ("dp", "ctx", "tp"))
    dp_place, ctx_place, tp_place = (lax.axis_index(a) for a in ("dp", "ctx", "tp"))
    length = tokens * ctx_count
    heads_here = position_bias.shape[0]
    width_here = heads_here * HEAD_DIM
    pairs = heads_here // 2
    expert_count = router.shape[1]
    top_count = routes.shape[1]
    own_rows = router.shape[0]

    places = jnp.stack(
        [dp_place, ctx_place, tp_place, jnp.int32(expert_count)]
    ).astype(jnp.int32)
    tail_pack = jnp.pad(
        jnp.concatenate([router, norm_gains.T], axis=1), ((0, 0), (0, LANES - expert_count - 2))
    )
    pack = jnp.concatenate(
        [qkv_weight.reshape(own_rows, 3 * width_here), tail_pack, out_weight.T], axis=1
    )
    doc_row = jnp.broadcast_to(segments.reshape(1, tokens), (8, tokens))
    queries, key_values, normed_one, qkv_flat, out_own, lanes, gains, docs = start(
        pack, hidden_in, doc_row, width_here, expert_count
    )
    out_sides = gather_xor(out_own, "tp")
    docs_all = docs[:, 0].reshape(length)

    capacity = max(2, min(tokens, 5 * top_count * tokens // (4 * expert_count)))
    flat_routes = routes.reshape(-1)
    route_onehot = (
        flat_routes[:, None] == jnp.arange(expert_count, dtype=jnp.int32)[None, :]
    ).astype(jnp.int32)
    earlier = jnp.cumsum(route_onehot, axis=0) - route_onehot
    position = jnp.sum(earlier * route_onehot, axis=1).reshape(tokens, top_count)
    slot_expert = dp_place ^ jnp.arange(dp_count, dtype=jnp.int32)
    slot_index = jnp.arange(capacity, dtype=jnp.int32)
    chosen = jnp.zeros((dp_count, capacity, tokens), jnp.bool_)
    for k in range(top_count):
        chosen = chosen | (
            (routes[:, k][None, None, :] == slot_expert[:, None, None])
            & (position[:, k][None, None, :] == slot_index[None, :, None])
        )
    picker = chosen.astype(BF16).reshape(dp_count * capacity, tokens)
    chosen_flip = jnp.zeros((tokens, dp_count, capacity), jnp.bool_)
    for k in range(top_count):
        chosen_flip = chosen_flip | (
            (routes[:, k][:, None, None] == slot_expert[None, :, None])
            & (position[:, k][:, None, None] == slot_index[None, None, :])
        )
    picker_flip = chosen_flip.astype(BF16).reshape(tokens, dp_count * capacity)
    send_grads = mm(picker, out_grad).astype(BF16).reshape(dp_count, capacity, D)
    send_grads, expert_in_late, expert_down_late, _, _ = lax.optimization_barrier(
        (send_grads, expert_in[0], expert_down[0], queries, out_own)
    )
    arrived_grads = [send_grads[0]] + [swap(send_grads[m], "dp", m) for m in range(1, dp_count)]
    in_pieces = gather_xor(expert_in_late, "ctx")
    down_pieces = gather_xor(expert_down_late, "ctx")

    rev_table = bucket_table[::-1]
    window_width = tokens + length
    rev_table = jnp.pad(rev_table, (0, 1), constant_values=BUCKETS)
    first_row = ctx_place * tokens
    window_table = lax.dynamic_slice(rev_table, (first_row,), (window_width,))
    table_onehot = (
        window_table[None, :] == jnp.arange(BUCKETS, dtype=jnp.int32)[:, None]
    ).astype(F32)
    window = jnp.dot(
        position_bias, table_onehot, precision=lax.Precision.HIGHEST, preferred_element_type=F32
    )
    window = jnp.pad(window.reshape(pairs, 2, window_width), ((0, 0), (0, 6), (0, 0)))
    docs_row = segments.reshape(1, tokens)
    doc_col = jnp.broadcast_to(docs_all[:, None], (length, LANES))
    query_docs = docs_row.reshape(tokens // BLOCK, BLOCK)
    key_docs = docs_all.reshape(length // BLOCK, BLOCK)
    active = (
        (key_docs[:, -1][None, :] >= query_docs[:, 0][:, None])
        & (key_docs[:, 0][None, :] <= query_docs[:, -1][:, None])
    ).astype(jnp.int32)
    block_rows = (
        (ctx_place ^ jnp.arange(ctx_count, dtype=jnp.int32))[:, None] * tokens
        + jnp.arange(tokens // BLOCK, dtype=jnp.int32)[None, :] * BLOCK
    ).reshape(-1)
    base = (length - LANES - block_rows).astype(jnp.int32)

    attended, totals = attention(active, base, queries, key_values, window, doc_row, doc_col)
    (middle, normed_two, logit_grad, middle_grad, middle_low, attended_grad, gain_two_grad,
     out_parts, in_keep, down_keep, in_core, down_core) = expert_step(
        attended, hidden_in, out_grad, gains, lanes, picker_flip, out_sides, arrived_grads,
        in_pieces, down_pieces, expert_count,
    )

    def add_cores(kept, arrived, k):
        return kept[k].astype(F32) + arrived[k].astype(F32)

    in_far = [swap(add_cores(in_keep, in_core, 1).astype(BF16), "ctx", 2)]
    down_far = [swap(add_cores(down_keep, down_core, 1).astype(BF16), "ctx", 2)]
    out_far = [swap(out_parts[k], "tp", k) for k in range(1, tp_count)]
    query_grad, key_part, value_part, offset_grad = attention_back(
        active, base, queries, key_values, attended_grad, totals, window, doc_row, doc_col
    )
    bias_part = lax.dot_general(
        offset_grad[:, :2, :].reshape(heads_here, window_width), table_onehot, NT,
        precision=lax.Precision.HIGHEST, preferred_element_type=F32,
    )
    bias_total = all_sum(all_sum(bias_part, "ctx"), "dp")

    query_grad, in_far, down_far, out_far = lax.optimization_barrier(
        (query_grad, in_far, down_far, out_far)
    )
    in_total = (add_cores(in_keep, in_core, 0) + in_far[0].astype(F32))[None]
    down_total = (add_cores(down_keep, down_core, 0) + down_far[0].astype(F32))[None]
    out_sum = tree_sum([part.astype(F32) for part in [out_parts[0]] + out_far]).astype(BF16)
    back_outs = [out_sum[0]] + [swap(out_sum[m], "dp", m) for m in range(1, dp_count)]
    mixed_half = mm(picker_flip, jnp.concatenate(back_outs, axis=0)).astype(BF16)
    mixed = in_order(gather_xor(mixed_half, "tp"), tp_place, 1)
    output = middle + mixed.astype(F32)
    input_grad, first_total, second_total = final_step(
        query_grad, key_part, value_part, normed_one, qkv_flat, middle_low, attended, normed_two,
        logit_grad, hidden_in, gains, gain_two_grad, middle_grad, expert_count,
    )
    qkv_total = jnp.concatenate(
        [first_total[:, :width_here], second_total[:, : 2 * width_here]], axis=1
    ).reshape(own_rows, 3, width_here)
    out_total = first_total[:, width_here:].T
    tail_total = second_total[:, 2 * width_here :]
    router_total = tail_total[:, :expert_count]
    gains_total = tail_total[:, expert_count : expert_count + 2].T

    qkv_new = adamw_step(qkv_weight.astype(F32), qkv_total, qkv_first, qkv_second, MAIN_RATE)
    out_new = adamw_step(out_weight.astype(F32), out_total, out_first, out_second, MAIN_RATE)
    router_new = adamw_step(
        router.astype(F32), router_total, router_first, router_second, MAIN_RATE
    )
    gains_new = adamw_step(
        norm_gains.astype(F32), gains_total, gains_first, gains_second, MAIN_RATE
    )
    bias_new = adamw_step(position_bias, bias_total, bias_first, bias_second, BIAS_RATE)
    in_new = adamw_step(expert_in.astype(F32), in_total, in_first, in_second, MAIN_RATE)
    down_new = adamw_step(expert_down.astype(F32), down_total, down_first, down_second, MAIN_RATE)
    return (
        output,
        input_grad,
        qkv_total,
        *qkv_new,
        out_total,
        *out_new,
        router_total,
        *router_new,
        gains_total,
        *gains_new,
        bias_total,
        *bias_new,
        in_total,
        *in_new,
        down_total,
        *down_new,
    )


def solution(mesh):
    token_rows = P(("dp", "ctx"), None)
    qkv = P(("dp", "ctx"), None, "tp")
    out = P("tp", ("dp", "ctx"))
    gains = P(None, ("dp", "ctx"))
    bias = P("tp", None)
    expert_in = P("dp", None, "ctx", "tp")
    expert_down = P("dp", "tp", "ctx")
    placed = (
        token_rows, token_rows, P("dp", "ctx"), token_rows, P(),
        qkv, out, token_rows, gains, bias, expert_in, expert_down,
        qkv, qkv, out, out, token_rows, token_rows, gains, gains, bias, bias,
        expert_in, expert_in, expert_down, expert_down,
    )
    return jax.shard_map(
        shards,
        mesh=mesh,
        in_specs=placed,
        out_specs=(token_rows, token_rows)
        + (qkv,) * 4
        + (out,) * 4
        + (token_rows,) * 4
        + (gains,) * 4
        + (bias,) * 4
        + (expert_in,) * 4
        + (expert_down,) * 4,
        check_vma=False,
    )
```

```python
import functools

import jax
import jax.numpy as jnp
from jax import lax
from jax.experimental import pallas as pl
from jax.experimental.pallas import tpu as pltpu
from jax.sharding import PartitionSpec as P

D = 1024
HEAD_DIM = 64
BUCKETS = 32

NORM_EPS = 1e-06
NEG_FILL = -1e30
BETA_ONE = 0.9
BETA_TWO = 0.95
FIX_ONE = 1.0 - 0.9**10
FIX_TWO = 1.0 - 0.95**10
ADAM_EPS = 1e-08
WEIGHT_DECAY = 0.1
MAIN_RATE = 0.02
BIAS_RATE = 0.2

F32 = jnp.float32
BF16 = jnp.bfloat16
LANES = 128
BLOCK = 256
VMEM_CAP = 60 * 1024 * 1024
GELU_K = 0.7978845608028654
GELU_C = 0.044715


def tree_sum(values):
    while len(values) > 1:
        values = [values[k] + values[k + 1] for k in range(0, len(values), 2)]
    return values[0]


def rms_scale(values):
    return lax.rsqrt(jnp.mean(values * values, axis=-1, keepdims=True) + NORM_EPS)


def norm_back(values, scale_here, gain_here, gradient):
    weighted = gain_here * gradient
    row_inner = jnp.mean(values * weighted, axis=-1, keepdims=True)
    input_part = scale_here * weighted - values * scale_here**3 * row_inner
    return (input_part, jnp.sum(gradient * values * scale_here, axis=0))


def adamw_step(weight, gradient, first_moment, second_moment, step_rate):
    first_new = BETA_ONE * first_moment + (1.0 - BETA_ONE) * gradient
    second_new = BETA_TWO * second_moment + (1.0 - BETA_TWO) * gradient * gradient
    update = -step_rate * (
        first_new / FIX_ONE / (jnp.sqrt(second_new / FIX_TWO) + ADAM_EPS) + WEIGHT_DECAY * weight
    )
    return (first_new, second_new, update)


def cost(micros):
    return pl.CostEstimate(flops=int(micros * 1.15e9), bytes_accessed=1 << 20, transcendentals=0)


def swap(values, axis, bits):
    count = lax.axis_size(axis)
    return lax.ppermute(values, axis, [(i, i ^ bits) for i in range(count)])


def gather_xor(values, axis):
    pieces = {0: values}
    bit = lax.axis_size(axis) >> 1
    while bit:
        for key in list(pieces):
            pieces[key | bit] = swap(pieces[key], axis, bit)
        bit >>= 1
    return [pieces[m] for m in range(len(pieces))]


def scatter_sum(parts, axis):
    live = dict(enumerate(parts))
    bit = 1
    while bit < lax.axis_size(axis):
        left = {}
        for key in live:
            if key & bit == 0:
                moved = swap(live[key | bit].astype(BF16), axis, bit)
                left[key] = live[key].astype(F32) + moved.astype(F32)
        live = left
        bit <<= 1
    return live[0]


def all_sum(values, axis):
    bit = 1
    while bit < lax.axis_size(axis):
        values = values + swap(values, axis, bit)
        bit <<= 1
    return values


def in_order(pieces, place, dim):
    bit = 1
    while bit < len(pieces):
        odd = (place & bit) > 0
        pieces = [jnp.where(odd, pieces[m ^ bit], pieces[m]) for m in range(len(pieces))]
        bit <<= 1
    return jnp.concatenate(pieces, axis=dim)


MESH = pl.DeviceIdType.MESH


class Wire:
    def __init__(self, sends, receives):
        self.sends, self.receives, self.count, self.copies = sends, receives, 0, []

    def send(self, source, target, **device):
        copy = pltpu.make_async_remote_copy(
            src_ref=source,
            dst_ref=target,
            send_sem=self.sends.at[self.count],
            recv_sem=self.receives.at[self.count],
            device_id=device,
            device_id_type=MESH,
        )
        copy.start()
        self.count += 1
        self.copies.append(Arrival(copy))
        return self.copies[-1]

    def finish(self):
        for copy in self.copies:
            copy.sent()


class Arrival:
    def __init__(self, copy):
        self.copy, self.waited, self.gone = copy, False, False

    def sent(self):
        if not self.gone:
            self.copy.wait_send()
        self.gone = True

    def wait(self):
        if not self.waited:
            self.copy.wait_recv()
        self.waited = True


def greet(partners):
    barrier = pltpu.get_barrier_semaphore()
    for device in partners:
        pl.semaphore_signal(barrier, inc=1, device_id=device, device_id_type=MESH)
    pl.semaphore_wait(barrier, len(partners))


def bits_down(count):
    bits, bit = [], count >> 1
    while bit:
        bits.append(bit)
        bit >>= 1
    return bits


def xor_order(count):
    order = [0]
    for bit in bits_down(count):
        order = order + [k | bit for k in order]
    return order


NT = (((1,), (1,)), ((), ()))
NN = (((1,), (0,)), ((), ()))
TN = (((0,), (0,)), ((), ()))


def mm(left, right, dims=NN):
    return lax.dot_general(left, right, dims, preferred_element_type=F32)


def fold_max(values):
    return jnp.max(values.reshape(values.shape[0] // 8, 8, values.shape[1]), axis=0)


def fold_sum(values):
    return jnp.sum(values.reshape(values.shape[0] // 8, 8, values.shape[1]), axis=0)


def skewed(row):
    width = row.shape[1]
    tall = jnp.broadcast_to(row, (LANES, width))
    return pltpu.roll(tall, width - (LANES - 1), 1, stride=1, stride_axis=0)


def unskew_sum(field):
    half = field.shape[0] // 2
    while half >= 1:
        field = pltpu.roll(field[:half], half, 1) + field[half:]
        half //= 2
    return field


def head_masks(rows):
    lane = lax.broadcasted_iota(jnp.int32, (rows, LANES), 1)
    return [(lane < HEAD_DIM).astype(BF16), (lane >= HEAD_DIM).astype(BF16)]


def score_tile(key_block, query_head, skew_ref, head, first, same):
    scores = mm(key_block, query_head, NT)
    tiles = []
    for s in range(BLOCK // LANES):
        column = pl.multiple_of(first - s * LANES, LANES)
        tiles.append(skew_ref[head, :, pl.ds(column, BLOCK)])
    return jnp.where(same, scores + jnp.concatenate(tiles, axis=0), NEG_FILL)


def bucket_lanes(table_ref):
    row = lax.broadcasted_iota(jnp.int32, (BUCKETS, table_ref.shape[1]), 0)
    return (row == table_ref[0:1, :]).astype(F32)


def spread_bias(bias_ref, table_ref, skew_ref, first=0):
    rows = bias_ref[pl.ds((pl.program_id(0) + first) * 2, 2), :]
    window = jnp.dot(
        jnp.concatenate([rows] * 4, axis=0), bucket_lanes(table_ref),
        precision=lax.Precision.HIGHEST, preferred_element_type=F32,
    )
    for h in range(2):
        skew_ref[h] = skewed(window[h : h + 1, :])


def attention_kernel(
    first, info_ref, query_ref, key_ref, value_ref, bias_ref, table_ref, doc_row_ref,
    doc_col_ref, *refs,
):
    out_ref, total_ref, skew_ref, flip_ref, score_ref, most_ref, sum_ref, mix_ref = refs[-8:]
    tokens, length = query_ref.shape[0], key_ref.shape[0]
    key_blocks, query_blocks = length // BLOCK, tokens // BLOCK
    masks = head_masks(BLOCK)
    spread_bias(bias_ref, table_ref, skew_ref, first)

    @pl.loop(0, key_blocks)
    def _(kb):
        rows = pl.ds(pl.multiple_of(kb * BLOCK, BLOCK), BLOCK)
        flip_ref[:, rows] = value_ref[rows, :].T

    for qb in range(query_blocks):
        here = slice(qb * BLOCK, (qb + 1) * BLOCK)
        pair = query_ref[here, :] * jnp.asarray(HEAD_DIM**-0.5, BF16)
        query_heads = [pair * mask for mask in masks]
        doc_row = doc_row_ref[0:1, here]
        most_ref[...] = jnp.full_like(most_ref, NEG_FILL)
        sum_ref[...] = jnp.zeros_like(sum_ref)
        mix_ref[...] = jnp.zeros_like(mix_ref)

        @pl.loop(0, key_blocks)
        def _(kb):
            @pl.when(info_ref[qb, kb] > 0)
            def _():
                rows = pl.ds(pl.multiple_of(kb * BLOCK, BLOCK), BLOCK)
                column = doc_col_ref[rows, :]
                same = jnp.concatenate([column] * (BLOCK // LANES), axis=1) == doc_row
                for h in range(2):
                    tile = score_tile(
                        key_ref[rows, :], query_heads[h], skew_ref, h,
                        info_ref[query_blocks, kb] + qb * BLOCK, same,
                    )
                    score_ref[h, rows, :] = tile
                    most_ref[h] = jnp.maximum(most_ref[h], fold_max(tile))

        most = [jnp.max(most_ref[h], axis=0, keepdims=True) for h in range(2)]

        @pl.loop(0, key_blocks)
        def _(kb):
            @pl.when(info_ref[qb, kb] > 0)
            def _():
                rows = pl.ds(pl.multiple_of(kb * BLOCK, BLOCK), BLOCK)
                for h in range(2):
                    weights = jnp.exp(score_ref[h, rows, :] - most[h])
                    sum_ref[h] += fold_sum(weights)
                    mix_ref[h] += mm(
                        flip_ref[h * HEAD_DIM : (h + 1) * HEAD_DIM, rows], weights.astype(BF16)
                    )

        columns = []
        for h in range(2):
            total = jnp.sum(sum_ref[h], axis=0, keepdims=True)
            columns.append(mix_ref[h] / total)
            total_ref[0, h : h + 1, here] = most[h] + jnp.log(total)
        out_ref[here, :] = jnp.concatenate(columns, axis=0).T.astype(BF16)


def attention_back_kernel(
    info_ref, query_ref, key_ref, value_ref, grad_ref, total_ref, bias_ref, table_ref,
    doc_row_ref, doc_col_ref,
    query_grad_ref, key_grad_ref, value_grad_ref, bias_grad_ref,
    skew_ref, field_ref, flip_ref, weight_ref, change_ref, inner_ref, mix_ref, key_sum, value_sum,
):
    tokens, length = query_ref.shape[0], key_ref.shape[0]
    key_blocks, query_blocks = length // BLOCK, tokens // BLOCK
    masks = head_masks(BLOCK)
    spread_bias(bias_ref, table_ref, skew_ref)
    field_ref[...] = jnp.zeros_like(field_ref)
    key_sum[...] = jnp.zeros_like(key_sum)
    value_sum[...] = jnp.zeros_like(value_sum)

    @pl.loop(0, key_blocks)
    def _(kb):
        rows = pl.ds(pl.multiple_of(kb * BLOCK, BLOCK), BLOCK)
        flip_ref[:, rows] = key_ref[rows, :].T

    for qb in range(query_blocks):
        here = slice(qb * BLOCK, (qb + 1) * BLOCK)
        pair = query_ref[here, :] * jnp.asarray(HEAD_DIM**-0.5, BF16)
        query_heads = [pair * mask for mask in masks]
        grad_pair = grad_ref[here, :]
        grad_heads = [grad_pair * mask for mask in masks]
        doc_row = doc_row_ref[0:1, here]
        inner_ref[...] = jnp.zeros_like(inner_ref)
        mix_ref[...] = jnp.zeros_like(mix_ref)
        totals = [total_ref[0, h : h + 1, here] for h in range(2)]

        @pl.loop(0, key_blocks)
        def _(kb):
            @pl.when(info_ref[qb, kb] > 0)
            def _():
                rows = pl.ds(pl.multiple_of(kb * BLOCK, BLOCK), BLOCK)
                column = doc_col_ref[rows, :]
                same = jnp.concatenate([column] * (BLOCK // LANES), axis=1) == doc_row
                for h in range(2):
                    tile = score_tile(
                        key_ref[rows, :], query_heads[h], skew_ref, h,
                        info_ref[query_blocks, kb] + qb * BLOCK, same,
                    )
                    weights = jnp.exp(tile - totals[h])
                    change = mm(value_ref[rows, :], grad_heads[h], NT)
                    weight_ref[h, rows, :] = weights
                    change_ref[h, rows, :] = change
                    inner_ref[h] += fold_sum(weights * change)

        inner = [jnp.sum(inner_ref[h], axis=0, keepdims=True) for h in range(2)]

        @pl.loop(0, key_blocks)
        def _(kb):
            @pl.when(info_ref[qb, kb] > 0)
            def _():
                rows = pl.ds(pl.multiple_of(kb * BLOCK, BLOCK), BLOCK)
                key_part = value_part = None
                for h in range(2):
                    weights = weight_ref[h, rows, :]
                    score_grad = weights * (change_ref[h, rows, :] - inner[h])
                    for s in range(BLOCK // LANES):
                        first = pl.multiple_of(info_ref[query_blocks, kb] + qb * BLOCK - s * LANES, LANES)
                        field_ref[h, :, pl.ds(first, BLOCK)] += score_grad[
                            s * LANES : (s + 1) * LANES
                        ]
                    low = score_grad.astype(BF16)
                    key_here = mm(low, query_heads[h])
                    value_here = mm(weights.astype(BF16), grad_heads[h])
                    key_part = key_here if h == 0 else key_part + key_here
                    value_part = value_here if h == 0 else value_part + value_here
                    mix_ref[h] += mm(flip_ref[h * HEAD_DIM : (h + 1) * HEAD_DIM, rows], low)
                key_sum[rows, :] += key_part
                value_sum[rows, :] += value_part

        both = jnp.concatenate([mix_ref[0], mix_ref[1]], axis=0) * HEAD_DIM**-0.5
        query_grad_ref[here, :] = both.T.astype(BF16)

    key_grad_ref[...] = key_sum[...].astype(BF16)
    value_grad_ref[...] = value_sum[...].astype(BF16)
    offsets = jnp.concatenate([unskew_sum(field_ref[h]) for h in range(2)] * 4, axis=0)
    bias_grad_ref[0] = lax.dot_general(
        offsets, bucket_lanes(table_ref), NT, precision=lax.Precision.HIGHEST,
        preferred_element_type=F32,
    )


def attention_specs(tokens, length, pairs, heads, width, first=0):
    smem = pl.BlockSpec(memory_space=pltpu.SMEM)
    return dict(
        info=smem,
        query=pl.BlockSpec((tokens, LANES), lambda i: (0, i + first)),
        key=pl.BlockSpec((length, LANES), lambda i: (0, i + first)),
        value=pl.BlockSpec((length, LANES), lambda i: (0, i + first + pairs)),
        bias=pl.BlockSpec((heads, BUCKETS), lambda i: (0, 0)),
        table=pl.BlockSpec((8, width), lambda i: (0, 0)),
        total=pl.BlockSpec((1, 8, tokens), lambda i: (i + first, 0, 0)),
        bias_grad=pl.BlockSpec((1, 8, BUCKETS), lambda i: (i, 0, 0)),
        doc_row=pl.BlockSpec((8, tokens), lambda i: (0, 0)),
        doc_col=pl.BlockSpec((length, LANES), lambda i: (0, 0)),
    )


def attention(info, queries, key_values, bias, table, doc_row, doc_col, first, count, held):
    tokens, length = queries.shape[0], key_values.shape[0]
    pairs, width = bias.shape[0] // 2, table.shape[1]
    specs = attention_specs(tokens, length, pairs, bias.shape[0], width, first)
    return pl.pallas_call(
        functools.partial(attention_kernel, first),
        grid=(count,),
        in_specs=[
            specs["info"], specs["query"], specs["key"], specs["value"], specs["bias"],
            specs["table"], specs["doc_row"], specs["doc_col"],
        ]
        + [pl.BlockSpec(memory_space=pl.ANY)] * len(held),
        out_specs=[pl.BlockSpec((tokens, LANES), lambda i: (0, i)), specs["total"]],
        out_shape=[
            jax.ShapeDtypeStruct((tokens, count * LANES), BF16),
            jax.ShapeDtypeStruct((pairs, 8, tokens), F32),
        ],
        scratch_shapes=[
            pltpu.VMEM((2, LANES, width), F32),
            pltpu.VMEM((LANES, length), BF16),
            pltpu.VMEM((2, length, BLOCK), F32),
            pltpu.VMEM((2, 8, BLOCK), F32),
            pltpu.VMEM((2, 8, BLOCK), F32),
            pltpu.VMEM((2, HEAD_DIM, BLOCK), F32),
        ],
        input_output_aliases={8: 1} if held else {},
        compiler_params=pltpu.CompilerParams(vmem_limit_bytes=VMEM_CAP),
        cost_estimate=cost(13),
        name="attention_forward",
    )(info, queries, key_values, key_values, bias, table, doc_row, doc_col, *held)


def attention_back(info, queries, key_values, grads, totals, bias, table, doc_row, doc_col):
    tokens, length = queries.shape[0], key_values.shape[0]
    pairs, width = bias.shape[0] // 2, table.shape[1]
    specs = attention_specs(tokens, length, pairs, bias.shape[0], width)
    return pl.pallas_call(
        attention_back_kernel,
        grid=(pairs,),
        in_specs=[
            specs["info"], specs["query"], specs["key"], specs["value"], specs["query"],
            specs["total"], specs["bias"], specs["table"], specs["doc_row"], specs["doc_col"],
        ],
        out_specs=[specs["query"], specs["key"], specs["key"], specs["bias_grad"]],
        out_shape=[
            jax.ShapeDtypeStruct(queries.shape, BF16),
            jax.ShapeDtypeStruct((length, queries.shape[1]), BF16),
            jax.ShapeDtypeStruct((length, queries.shape[1]), BF16),
            jax.ShapeDtypeStruct((pairs, 8, BUCKETS), F32),
        ],
        scratch_shapes=[
            pltpu.VMEM((2, LANES, width), F32),
            pltpu.VMEM((2, LANES, width), F32),
            pltpu.VMEM((LANES, length), BF16),
            pltpu.VMEM((2, length, BLOCK), F32),
            pltpu.VMEM((2, length, BLOCK), F32),
            pltpu.VMEM((2, 8, BLOCK), F32),
            pltpu.VMEM((2, HEAD_DIM, BLOCK), F32),
            pltpu.VMEM((length, LANES), F32),
            pltpu.VMEM((length, LANES), F32),
        ],
        compiler_params=pltpu.CompilerParams(vmem_limit_bytes=VMEM_CAP),
        cost_estimate=cost(40),
        name="attention_backward",
    )(info, queries, key_values, key_values, grads, totals, bias, table, doc_row, doc_col)


def start_kernel(
    experts, dp_count, ctx_count, tp_count, pack_ref, hidden_ref, docs_ref, routes_ref,
    out_grad_ref, expert_ref,
    query_ref, pair_ref, normed_ref, weight_out, own_ref, lanes_ref, gains_ref, info_ref,
    column_ref, picker_ref, grads_own_ref, grads_ref, expert_land,
    weights, hidden, docs, sends, receives, out_sem,
):
    d, c, t = lax.axis_index("dp"), lax.axis_index("ctx"), lax.axis_index("tp")
    rows = pack_ref.shape[0]
    tokens, width = query_ref.shape
    first_part = slice(0, 3 * width + LANES)
    second_part = slice(3 * width + LANES, 4 * width + LANES)
    weights[pl.ds(pl.multiple_of((d * ctx_count + c) * rows, rows), rows), :] = pack_ref[...]
    greet(
        [{"ctx": c ^ m} for m in range(1, ctx_count)]
        + [{"dp": d ^ bit} for bit in bits_down(dp_count)]
        + [{"tp": t ^ k} for k in range(1, tp_count)]
    )
    wire = Wire(sends, receives)
    share = grads_ref.shape[2]
    own_share = pl.ds(pl.multiple_of(t * share, share), share)

    def send_shard(m, j, part, **device):
        index = (d ^ m) * ctx_count + (c ^ j)
        shard = weights.at[pl.ds(pl.multiple_of(index * rows, rows), rows), part]
        return wire.send(shard, shard, **device)

    docs_sent = [wire.send(docs_ref, docs.at[m], ctx=c ^ m) for m in range(1, ctx_count)]
    sides, sides_far = [0], []
    parts = (first_part, second_part)
    arrivals = {part: [] for part in range(2)}
    hidden_sent, expert_sent = {}, {}
    for bit in bits_down(ctx_count)[:-1]:
        arrivals = {
            k: [send_shard(0, j, part, ctx=c ^ bit) for j in sides]
            for k, part in enumerate(parts)
        }
        assert bit == 2
        half = hidden_ref.at[:, own_share]
        hidden_sent[2] = wire.send(half, hidden.at[2, :, own_share], ctx=c ^ 2)
        for m in [0] + list(expert_sent):
            if m:
                expert_sent[m].wait()
            source = expert_land.at[m - 1] if m else expert_ref
            expert_sent[m | bit] = wire.send(source, expert_land.at[(m | bit) - 1], ctx=c ^ bit)
        for copy in arrivals[0]:
            copy.wait()
        sides_far = sides + [j | bit for j in sides]
        if bit != 2:
            for copy in arrivals[1]:
                copy.wait()
        sides = sides_far
    hidden_sent[1] = wire.send(hidden_ref, hidden.at[1], ctx=c ^ 1)

    order = xor_order(dp_count)
    groups = [{}, {}]
    crossed = [[], []]

    def onward(k, m):
        for copy in groups[k].get(m, []):
            copy.wait()
        for bit in bits_down(dp_count):
            if m & (2 * bit - 1) == 0:
                groups[k][m | bit] = [send_shard(m, j, parts[k], dp=d ^ bit) for j in sides]
        crossed[k] += [send_shard(m, j, parts[k], ctx=c ^ 1) for j in sides]

    onward(0, 0)
    for copy in arrivals[1]:
        copy.wait()
    onward(1, 0)
    expert_sent[1] = wire.send(expert_ref, expert_land.at[0], ctx=c ^ 1)

    lane = lax.broadcasted_iota(jnp.int32, (tokens, LANES), 1)
    tops = [routes_ref[:, k : k + 1] for k in range(routes_ref.shape[1])]
    named = jnp.zeros((tokens, LANES), F32)
    for top in tops:
        named = jnp.where(lane == top, 1.0, named)
    row_index = lax.broadcasted_iota(jnp.int32, (tokens, tokens), 0)
    column_index = lax.broadcasted_iota(jnp.int32, (tokens, tokens), 1)
    before = jnp.where(column_index < row_index, 1.0, 0.0).astype(BF16)
    earlier = mm(before, named.astype(BF16))
    slots = grads_own_ref.shape[0]
    column = lax.broadcasted_iota(jnp.int32, picker_ref.shape, 1)
    picker = jnp.zeros(picker_ref.shape, F32)
    for top in tops:
        place = jnp.sum(jnp.where(lane == top, earlier, 0.0), axis=1, keepdims=True)
        place = place.astype(jnp.int32)
        target = jnp.where(place < slots, (top ^ d) * slots + place, -1)
        picker = jnp.where(column == target, 1.0, picker)
    picker_ref[...] = picker.astype(BF16)
    hidden_sent[2].wait()
    half = hidden.at[2, :, own_share]
    spread = [wire.send(half, half, tp=t ^ k) for k in range(1, tp_count)]
    for m in range(dp_count):
        chosen = picker_ref[:, m * slots : (m + 1) * slots]
        if m:
            grads_ref[m - 1] = mm(chosen, out_grad_ref[:, own_share], TN).astype(BF16)
        else:
            grads_own_ref[...] = mm(chosen, out_grad_ref[...], TN).astype(BF16)

    key_blocks, query_blocks = tokens // BLOCK, tokens // BLOCK
    where = lax.broadcasted_iota(jnp.int32, info_ref.shape, 1)
    which = lax.broadcasted_iota(jnp.int32, info_ref.shape, 0)
    info = jnp.zeros(info_ref.shape, jnp.int32)
    for m in range(ctx_count):
        if m:
            docs_sent[m - 1].wait()
        row = docs[m] if m else docs_ref[...]
        tall = jnp.broadcast_to(row[0:1, :].astype(F32), (LANES, tokens))
        column_ref[m * tokens : (m + 1) * tokens, :] = tall.T.astype(jnp.int32)
        for k in range(key_blocks):
            spot = m * key_blocks + k
            low = row[0:1, k * BLOCK : k * BLOCK + 1]
            high = row[0:1, (k + 1) * BLOCK - 1 : (k + 1) * BLOCK]
            for q in range(query_blocks):
                query_low = docs_ref[0:1, q * BLOCK : q * BLOCK + 1]
                query_high = docs_ref[0:1, (q + 1) * BLOCK - 1 : (q + 1) * BLOCK]
                meets = ((high >= query_low) & (low <= query_high)).astype(jnp.int32)
                info = jnp.where((where == spot) & (which == q), meets, info)
            base = (ctx_count * tokens - LANES) - ((c ^ m) * tokens + k * BLOCK)
            info = jnp.where((where == spot) & (which == query_blocks), base, info)
    info_ref[...] = info

    for m in order[1:]:
        onward(0, m)
    for copy in spread:
        copy.wait()
    hidden_sent[3] = wire.send(hidden.at[2], hidden.at[3], ctx=c ^ 1)
    for copy in crossed[0]:
        copy.wait()
    keep = pltpu.make_async_copy(weights.at[:, : 3 * width], weight_out, out_sem.at[0])
    keep.start()
    small = weights[:, 3 * width : 3 * width + LANES].astype(F32)
    lane = lax.broadcasted_iota(jnp.int32, small.shape, 1)
    lanes_ref[...] = jnp.where(lane < experts, small, 0.0).astype(BF16)
    gain_one = jnp.sum(jnp.where(lane == experts, small, 0.0), axis=1, keepdims=True)
    gain_two = jnp.sum(jnp.where(lane == experts + 1, small, 0.0), axis=1, keepdims=True)
    both = jnp.where(lane == 0, gain_one, jnp.where(lane == 1, gain_two, 0.0)).T
    gains_ref[...] = both[:8]
    gain = both[0:1]
    for m in range(ctx_count):
        if m:
            hidden_sent[m].wait()
        values = (hidden[m] if m else hidden_ref[...]).astype(F32)
        scale = lax.rsqrt(jnp.mean(values * values, axis=-1, keepdims=True) + NORM_EPS)
        normed = (values * scale * gain).astype(BF16)
        pair_ref[m * tokens : (m + 1) * tokens, :] = mm(
            normed, weights[:, width : 3 * width]
        ).astype(BF16)
        if m == 0:
            normed_ref[...] = normed
            query_ref[...] = mm(normed, weights[:, :width]).astype(BF16)
            for n in order[1:]:
                onward(1, n)
    for copy in crossed[1]:
        copy.wait()
    keep_own = pltpu.make_async_copy(weights.at[:, second_part], own_ref, out_sem.at[1])
    keep_own.start()
    for k in [k for k in expert_sent if k > 1]:
        expert_sent[k].wait()
        expert_sent[k | 1] = wire.send(expert_land.at[k - 1], expert_land.at[k], ctx=c ^ 1)
    for k in range(1, ctx_count):
        expert_sent[k].wait()
    keep.wait()
    keep_own.wait()
    wire.finish()


def start(pack, hidden, docs, routes, out_grad, expert, width, experts, slots):
    tokens = hidden.shape[0]
    columns = pack.shape[1]
    dp_count, ctx_count, tp_count = (lax.axis_size(a) for a in ("dp", "ctx", "tp"))
    copies = 4 * (ctx_count - 1) + ctx_count + 2 * dp_count * ctx_count + tp_count
    vmem = pl.BlockSpec(memory_space=pltpu.VMEM)
    hbm = pl.BlockSpec(memory_space=pl.ANY)
    shape = jax.ShapeDtypeStruct
    return pl.pallas_call(
        functools.partial(start_kernel, experts, dp_count, ctx_count, tp_count),
        in_specs=[vmem] * 5 + [hbm],
        out_specs=[vmem] * 3 + [hbm] * 2 + [vmem] * 7 + [hbm],
        out_shape=[
            shape((tokens, width), BF16),
            shape((tokens * ctx_count, 2 * width), BF16),
            shape((tokens, D), BF16),
            shape((D, 3 * width), BF16),
            shape((D, width), BF16),
            shape((D, LANES), BF16),
            shape((8, D), F32),
            shape((8, LANES), jnp.int32),
            shape((tokens * ctx_count, LANES), jnp.int32),
            shape((tokens, dp_count * slots), BF16),
            shape((slots, D), BF16),
            shape((dp_count - 1, slots, D // tp_count), BF16),
            shape((ctx_count - 1,) + expert.shape, BF16),
        ],
        scratch_shapes=[
            pltpu.VMEM((D, columns), BF16),
            pltpu.VMEM((ctx_count, tokens, D), BF16),
            pltpu.VMEM((ctx_count, 8, tokens), jnp.int32),
            pltpu.SemaphoreType.DMA((copies,)),
            pltpu.SemaphoreType.DMA((copies,)),
            pltpu.SemaphoreType.DMA((2,)),
        ],
        compiler_params=pltpu.CompilerParams(
            vmem_limit_bytes=VMEM_CAP, collective_id=1, has_side_effects=True
        ),
        cost_estimate=cost(60),
        name="start",
    )(pack, hidden, docs, routes, out_grad, expert)


def bent_parts(value):
    square = value * value
    wave = jnp.tanh(GELU_K * value * (1.0 + GELU_C * square))
    half = 0.5 * (1.0 + wave)
    slope = half + 0.5 * value * (1.0 - wave * wave) * (GELU_K * (1.0 + 3.0 * GELU_C * square))
    return value * half, slope


def expert_kernel(
    experts, dp_count, ctx_count, tp_count, attended_ref, hidden_ref, out_grad_ref, gains_ref,
    lanes_ref, picker_ref, *refs,
):
    d, c, t = lax.axis_index("dp"), lax.axis_index("ctx"), lax.axis_index("tp")
    firsts, refs = refs[:tp_count], refs[tp_count:]
    outs, refs = refs[:tp_count], refs[tp_count:]
    grads, refs = refs[:dp_count], refs[dp_count:]
    in_own, in_land, refs = refs[0], refs[1], refs[2:]
    ins = [in_own] + [in_land.at[j] for j in range(ctx_count - 1)]
    downs, refs = refs[:ctx_count], refs[ctx_count:]
    (middle_ref, normed_ref, logit_ref, grad_ref, low_ref, attended_grad_ref, gain_ref, out_parts,
     attended_out, in_keep, down_keep, in_core, down_core,
     mixed, out_all, in_all, down_all, rows_all, scaled_all, act_all, gate_all, up_all, send_rows,
     row_parts, row_in, row_back, dot_parts, dot_in, dot_home, dot_back, probs, whole,
     sends, receives, in_sems, keep_sems) = refs
    tokens, second_width = attended_ref.shape
    first_width = firsts[0].shape[1]
    width = first_width + second_width
    share = D // tp_count
    slots = rows_all.shape[0] // dp_count
    depth, ff = in_own.shape[1], in_own.shape[2]
    shares = range(1, tp_count)
    order = [0] + list(range(2, dp_count)) + [1]

    local = []

    def load(source, target):
        copy = pltpu.make_async_copy(source, target, in_sems.at[len(local)])
        copy.start()
        local.append(copy)
        return copy

    out_copies = [
        load(outs[m], out_all.at[:, pl.ds(pl.multiple_of((t ^ m) * width, width), width)])
        for m in range(tp_count)
    ]
    weight_copies = []
    for j in range(ctx_count):
        part = slice(j * depth, (j + 1) * depth)
        weight_copies.append(load(ins[j], in_all.at[:, part, :]))
        weight_copies.append(load(downs[j], down_all.at[:, part]))
    own_share = pl.ds(pl.multiple_of(t * share, share), share)
    weight_copies.append(load(grads[0], scaled_all.at[:slots]))
    grad_copies = [
        load(grads[m], scaled_all.at[m * slots : (m + 1) * slots, own_share])
        for m in range(1, dp_count)
    ]
    own_lanes = pl.ds(pl.multiple_of(t * width, width), width)
    second_lanes = pl.ds(pl.multiple_of(t * width + first_width, LANES), second_width)
    mixed[:, second_lanes] = attended_ref[...]
    for m in range(tp_count):
        start = pl.multiple_of((t ^ m) * width, width)
        mixed[:, pl.ds(start, first_width)] = firsts[m][...]
    attended_out[...] = mixed[:, own_lanes]
    greet(
        [{"tp": t ^ k} for k in shares]
        + [{"dp": d ^ m} for m in range(1, dp_count)]
        + [{"ctx": c ^ 1}]
    )
    wire = Wire(sends, receives)
    second_part = mixed.at[:, second_lanes]
    arrivals = [wire.send(second_part, second_part, tp=t ^ k) for k in shares]
    spread, returned, dot_returned = {}, {}, {}
    for m, copy in zip(range(1, dp_count), grad_copies):
        copy.wait()
        half = scaled_all.at[m * slots : (m + 1) * slots, own_share]
        spread[m] = [wire.send(half, half, tp=t ^ k) for k in shares]
    for copy in out_copies:
        copy.wait()
    for copy in arrivals:
        copy.wait()
    middle = hidden_ref[...].astype(F32) + mm(mixed[...], out_all[...], NT)
    middle_ref[...] = middle
    scale = lax.rsqrt(jnp.mean(middle * middle, axis=-1, keepdims=True) + NORM_EPS)
    normed = (middle * scale * gains_ref[1:2, :]).astype(BF16)
    normed_ref[...] = normed
    far = {}

    def block(m):
        return slice(m * slots, (m + 1) * slots)

    for m in order[1:] + [0]:
        picked = mm(picker_ref[:, block(m)], normed_ref[...], TN).astype(BF16)
        if m:
            send_rows[m - 1] = picked
            far[m] = wire.send(
                send_rows.at[m - 1, :, own_share], rows_all.at[block(m), own_share], dp=d ^ m
            )
        else:
            rows_all[block(0), :] = picked
    lane = lax.broadcasted_iota(jnp.int32, (tokens, LANES), 1)

    def router_probs(values):
        logits = mm(values, lanes_ref[...])
        where = lax.broadcasted_iota(jnp.int32, logits.shape, 1)
        logits = jnp.where(where < experts, logits, NEG_FILL)
        powers = jnp.exp(logits - jnp.max(logits, axis=1, keepdims=True))
        return where, powers / jnp.sum(powers, axis=1, keepdims=True)

    probs[...] = router_probs(normed_ref[...])[1]
    for copy in weight_copies:
        copy.wait()
    columns = [pl.ds(pl.multiple_of((c ^ j) * depth, depth), depth) for j in range(ctx_count)]

    def forward(m):
        far[m].wait()
        half = rows_all.at[block(m), own_share]
        spread[m] += [wire.send(half, half, tp=t ^ k) for k in shares]

    def experts_on(m, hook):
        here = block(m)
        where, chance = router_probs(rows_all[here, :])
        gate = jnp.sum(jnp.where(where == d, chance, 0.0), axis=1, keepdims=True)
        rows = jnp.concatenate([rows_all[here, part] for part in columns], axis=1)
        grad_rows = jnp.concatenate([scaled_all[here, part] for part in columns], axis=1)
        rows_all[here, :] = rows
        scaled_all[here, :] = (gate * grad_rows.astype(F32)).astype(BF16)
        dots = jnp.zeros((slots, LANES), F32)
        for first in range(0, ff, BLOCK):
            part = slice(first, min(ff, first + BLOCK))
            value = mm(rows, in_all[0, :, part])
            up = mm(rows, in_all[1, :, part])
            back = mm(grad_rows, down_all[part, :], NT)
            bent, slope = bent_parts(value)
            act = (bent * up).astype(BF16)
            act_all[here, part] = act
            dots += jnp.sum(act.astype(F32) * back, axis=1, keepdims=True)
            scaled = gate * back
            gate_all[here, part] = (scaled * up * slope).astype(BF16)
            up_all[here, part] = (scaled * bent).astype(BF16)
        if hook is not None:
            hook()
        dot_parts[m] = dots.T[:8]
        dot_returned[m] = [
            wire.send(dot_parts.at[m], dot_in.at[k - 1, m], tp=t ^ k) for k in shares
        ]
        for k in list(shares) + [0]:
            for i in range(share // depth):
                piece = ((t ^ k) * (share // depth) + i) ^ c
                part = pl.ds(pl.multiple_of(piece * depth, depth), depth)
                row = mm(gate_all[here, :], in_all[0, part, :], NT)
                row += mm(up_all[here, :], in_all[1, part, :], NT)
                row_parts[k, m, :, i * depth : (i + 1) * depth] = row.astype(BF16)
            if k:
                returned.setdefault(m, []).append(
                    wire.send(row_parts.at[k, m], row_in.at[k - 1, m], tp=t ^ k)
                )
        for k in range(tp_count):
            for i in range(share // depth):
                piece = ((t ^ k) * (share // depth) + i) ^ c
                part = pl.ds(pl.multiple_of(piece * depth, depth), depth)
                out_parts[k, m, :, i * depth : (i + 1) * depth] = (
                    gate * mm(act_all[here, :], down_all[:, part])
                ).astype(BF16)

    homeward = []

    def send_home(m):
        for copy in dot_returned[m]:
            copy.wait()
        dots = tree_sum([dot_parts[m]] + [dot_in[k - 1, m] for k in shares])
        total = row_parts[0, m].astype(F32)
        for k, copy in zip(shares, returned[m]):
            copy.wait()
            total = total + row_in[k - 1, m].astype(F32)
        if m:
            dot_home[m] = dots
            row_parts[0, m] = total.astype(BF16)
            homeward.append(wire.send(dot_home.at[m], dot_back.at[m], dp=d ^ m))
            homeward.append(wire.send(row_parts.at[0, m], row_back.at[block(m)], dp=d ^ m))
        else:
            dot_back[0] = dots
            row_back[block(0), :] = total.astype(BF16)

    for i, m in enumerate(order):
        for copy in spread.get(m, []):
            copy.wait()
            copy.sent()
        hook = functools.partial(forward, order[i + 1]) if i + 1 < len(order) else None
        experts_on(m, hook)
        if i:
            send_home(order[i - 1])

    def in_grads(j):
        part = slice(j * depth, (j + 1) * depth)
        for side, right in enumerate((gate_all, up_all)):
            in_all[side, part, :] = mm(rows_all[:, part], right[...], TN).astype(BF16)

    keeps = []

    def keep(source, target):
        copy = pltpu.make_async_copy(source, target, keep_sems.at[len(keeps)])
        copy.start()
        keeps.append(copy)

    near = []
    in_grads(1)
    send_home(order[-1])
    for j in range(1, ctx_count, 2):
        part = slice(j * depth, (j + 1) * depth)
        if j > 1:
            in_grads(j)
        near.append(wire.send(in_all.at[:, part, :], in_core.at[j // 2], ctx=c ^ 1))
    for first in range(0, ff, BLOCK):
        part = slice(first, min(ff, first + BLOCK))
        down_all[part, :] = mm(act_all[:, part], scaled_all[...], TN).astype(BF16)
    for j in range(ctx_count):
        part = slice(j * depth, (j + 1) * depth)
        if j % 2:
            near.append(wire.send(down_all.at[:, part], down_core.at[j // 2], ctx=c ^ 1))
        else:
            keep(down_all.at[:, part], down_keep.at[j // 2])
    for j in range(0, ctx_count, 2):
        in_grads(j)
        keep(in_all.at[:, j * depth : (j + 1) * depth, :], in_keep.at[j // 2])

    for copy in homeward:
        copy.wait()
    result = mm(picker_ref[...], row_back[...])
    prob_grad = jnp.zeros((tokens, LANES), F32)
    for m in range(dp_count):
        high = dot_back[m].astype(BF16)
        rest = dot_back[m] - high.astype(F32)
        middle_part = rest.astype(BF16)
        tiny = (rest - middle_part.astype(F32)).astype(BF16)
        total = mm(picker_ref[:, block(m)], high, NT)
        total += mm(picker_ref[:, block(m)], middle_part, NT)
        total += mm(picker_ref[:, block(m)], tiny, NT)
        prob_grad = jnp.where(lane == (d ^ m), total[:, 0:1], prob_grad)
    chance = probs[...]
    logit = chance * (prob_grad - jnp.sum(chance * prob_grad, axis=1, keepdims=True))
    logit_ref[...] = logit
    more = lax.dot_general(
        logit, lanes_ref[own_share, :].astype(F32), NT, precision=lax.Precision.HIGHEST,
        preferred_element_type=F32,
    )
    whole[:, own_share] = (result + more).astype(BF16)
    arrivals = [wire.send(whole.at[:, own_share], whole.at[:, own_share], tp=t ^ k) for k in shares]
    for copy in arrivals:
        copy.wait()
    middle = middle_ref[...]
    gradient = whole[...].astype(F32)
    scale = lax.rsqrt(jnp.mean(middle * middle, axis=-1, keepdims=True) + NORM_EPS)
    weighted = gains_ref[1:2, :] * gradient
    inner = jnp.mean(middle * weighted, axis=-1, keepdims=True)
    gain_ref[...] = fold_sum(gradient * middle * scale)
    total = out_grad_ref[...].astype(F32) + (
        scale * weighted - middle * (scale * scale * scale) * inner
    )
    grad_ref[...] = total
    low_ref[...] = total.astype(BF16)
    attended_grad_ref[...] = mm(low_ref[...], out_all[:, own_lanes]).astype(BF16)
    for copy in keeps:
        copy.wait()
    for copy in near:
        copy.wait()
    wire.finish()


def expert_step(
    firsts, attended, hidden, out_grad, gains, lanes, picker_flip, outs, grads, expert, expert_land,
    downs, experts,
):
    dp_count, ctx_count, tp_count = (lax.axis_size(a) for a in ("dp", "ctx", "tp"))
    tokens, width = attended.shape[0], firsts[0].shape[1] + attended.shape[1]
    slots = grads[0].shape[0]
    share = D // tp_count
    depth, ff = expert.shape[1], expert.shape[2]
    all_slots = dp_count * slots
    half = ctx_count // 2
    others = tp_count - 1
    copies = others * (2 + 4 * dp_count) + 3 * dp_count + 2 * half
    vmem = pl.BlockSpec(memory_space=pltpu.VMEM)
    hbm = pl.BlockSpec(memory_space=pl.ANY)
    shape = jax.ShapeDtypeStruct
    return pl.pallas_call(
        functools.partial(expert_kernel, experts, dp_count, ctx_count, tp_count),
        in_specs=[vmem] * (6 + tp_count) + [hbm] * (tp_count + dp_count + 2 + ctx_count),
        out_specs=[vmem] * 9 + [hbm] * 4,
        out_shape=[
            shape((tokens, D), F32),
            shape((tokens, D), BF16),
            shape((tokens, LANES), F32),
            shape((tokens, D), F32),
            shape((tokens, D), BF16),
            shape((tokens, width), BF16),
            shape((8, D), F32),
            shape((tp_count, dp_count, slots, share), BF16),
            shape((tokens, width), BF16),
            shape((half, 2, depth, ff), BF16),
            shape((half, ff, depth), BF16),
            shape((half, 2, depth, ff), BF16),
            shape((half, ff, depth), BF16),
        ],
        scratch_shapes=[
            pltpu.VMEM((tokens, tp_count * width), BF16),
            pltpu.VMEM((D, tp_count * width), BF16),
            pltpu.VMEM((2, D, ff), BF16),
            pltpu.VMEM((ff, D), BF16),
            pltpu.VMEM((all_slots, D), BF16),
            pltpu.VMEM((all_slots, D), BF16),
            pltpu.VMEM((all_slots, ff), BF16),
            pltpu.VMEM((all_slots, ff), BF16),
            pltpu.VMEM((all_slots, ff), BF16),
            pltpu.VMEM((dp_count - 1, slots, D), BF16),
            pltpu.VMEM((tp_count, dp_count, slots, share), BF16),
            pltpu.VMEM((others, dp_count, slots, share), BF16),
            pltpu.VMEM((all_slots, share), BF16),
            pltpu.VMEM((dp_count, 8, slots), F32),
            pltpu.VMEM((others, dp_count, 8, slots), F32),
            pltpu.VMEM((dp_count, 8, slots), F32),
            pltpu.VMEM((dp_count, 8, slots), F32),
            pltpu.VMEM((tokens, LANES), F32),
            pltpu.VMEM((tokens, D), BF16),
            pltpu.SemaphoreType.DMA((copies,)),
            pltpu.SemaphoreType.DMA((copies,)),
            pltpu.SemaphoreType.DMA((tp_count + 2 * ctx_count + dp_count,)),
            pltpu.SemaphoreType.DMA((ctx_count,)),
        ],
        compiler_params=pltpu.CompilerParams(
            vmem_limit_bytes=VMEM_CAP, collective_id=3, has_side_effects=True
        ),
        cost_estimate=cost(120),
        name="expert_step",
    )(
        attended, hidden, out_grad, gains, lanes, picker_flip, *firsts, *outs, *grads, expert,
        expert_land, *downs,
    )


def final_kernel(
    experts, dp_count, ctx_count, tp_count,
    query_grad_ref, key_ref, value_ref, normed_ref, weight_ref, low_ref, attended_ref,
    normed_two_ref, logit_ref, hidden_ref, gains_ref, gain_two_ref, middle_grad_ref, middle_ref,
    picker_ref, bias_ref, *refs,
):
    outs, refs = refs[:tp_count], refs[tp_count:]
    (input_grad_ref, output_ref, bias_out_ref, first_ref, second_ref, tail_ref, out_sum, out_back,
     mixed, bias_send, bias_in,
    key_in, send_far, far_in, first_all, second_all, first_core, second_core, first_sum,
    second_sum, first_dp, second_dp, first_x, second_x, rows_all, token_grad, token_in,
    gain_send, gain_in, sends, receives) = refs
    d, c, t = lax.axis_index("dp"), lax.axis_index("ctx"), lax.axis_index("tp")
    tokens, width = query_grad_ref.shape
    dp_bits = bits_down(dp_count)[::-1]
    far_bits = bits_down(ctx_count)[:-1][::-1]
    far = list(range(0, ctx_count, 2))
    greet(
        [{"ctx": c ^ bit} for bit in bits_down(ctx_count)]
        + [{"dp": d ^ m} for m in range(1, dp_count)]
        + [{"tp": t ^ k} for k in range(1, tp_count)]
    )
    wire = Wire(sends, receives)

    bias_steps = [{"ctx": c ^ bit} for bit in bits_down(ctx_count)[::-1]]
    bias_steps += [{"dp": d ^ bit} for bit in dp_bits]
    bias_total, bias_copies = [bias_ref[...]], []

    def bias_begin():
        level = len(bias_copies)
        bias_send[level] = bias_total[-1]
        bias_copies.append(
            wire.send(bias_send.at[level], bias_in.at[level], **bias_steps[level])
        )

    def bias_end():
        level = len(bias_copies) - 1
        bias_copies[level].wait()
        bias_total.append(bias_total[-1] + bias_in[level])

    bias_begin()

    slots, share = out_sum.shape[1], out_sum.shape[2]
    own_share = pl.ds(pl.multiple_of(t * share, share), share)
    out_home = []
    for m in list(range(2, dp_count)) + [1, 0]:
        total = tree_sum([out[m].astype(F32) for out in outs]).astype(BF16)
        if m:
            out_sum[m - 1] = total
            out_home.append(
                wire.send(
                    out_sum.at[m - 1], out_back.at[m * slots : (m + 1) * slots], dp=d ^ m
                )
            )
        else:
            out_back[:slots, :] = total

    near = []
    for k in far[::-1]:
        rows = slice((k + 1) * tokens, (k + 2) * tokens)
        for side, ref in enumerate((key_ref, value_ref)):
            near.append(wire.send(ref.at[rows], key_in.at[side, k // 2], ctx=c ^ 1))

    def split(values):
        return values.astype(BF16).reshape(dp_count, ctx_count, -1, values.shape[1])

    def cross(whole, landed):
        return [wire.send(whole.at[:, c ^ (k + 1)], landed.at[k // 2], ctx=c ^ 1) for k in far]

    def add_core(whole, landed, total, copies):
        for k, copy in zip(far, copies):
            copy.wait()
            own = whole[:, pl.ds(c ^ k, 1)][:, 0]
            total[k // 2] = (own.astype(F32) + landed[k // 2].astype(F32)).astype(BF16)

    def dp_send(total, landed, level, sides):
        copies, bit = [], dp_bits[level]
        for m in range(bit, dp_count, 2 * bit):
            for k in sides:
                spot = landed.at[level, k, d ^ m]
                copies.append((m ^ bit, k, wire.send(total.at[k, d ^ m], spot, dp=d ^ bit)))
        return copies

    def dp_add(total, landed, level, copies):
        for m, k, copy in copies:
            copy.wait()
            own = total[k, pl.ds(d ^ m, 1)][0]
            other = landed[level, k, pl.ds(d ^ m, 1)][0]
            total[k, pl.ds(d ^ m, 1)] = (own.astype(F32) + other.astype(F32)).astype(BF16)[None]

    for copy in near:
        copy.wait()
    for k in far[::-1]:
        rows = slice(k * tokens, (k + 1) * tokens)
        for side, ref in enumerate((key_ref, value_ref)):
            send_far[side, k // 2] = (
                ref[rows, :].astype(F32) + key_in[side, k // 2].astype(F32)
            ).astype(BF16)
    assert len(far_bits) == 1
    far_copies = [
        wire.send(send_far.at[side, 1], far_in.at[side], ctx=c ^ 2) for side in range(2)
    ]

    first_all[:, :, :, :width] = split(mm(normed_ref[...], query_grad_ref[...], TN))
    first_all[:, :, :, width:] = split(mm(low_ref[...], attended_ref[...], TN))
    first_crossed = cross(first_all, first_core)
    bias_end()
    bias_begin()
    token_grad[...] = mm(query_grad_ref[...], weight_ref[:, :width], NT)
    add_core(first_all, first_core, first_sum, first_crossed)
    bias_end()
    bias_begin()
    first_moving = dp_send(first_sum, first_dp, 0, range(len(far)))
    logit = logit_ref[...]
    logit_high = logit.astype(BF16)
    logit_rest = logit - logit_high.astype(F32)
    logit_low = logit_rest.astype(BF16)
    logit_tiny = (logit_rest - logit_low.astype(F32)).astype(BF16)
    router_grad = mm(normed_two_ref[...], logit_high, TN)
    router_grad += mm(normed_two_ref[...], logit_low, TN)
    router_grad += mm(normed_two_ref[...], logit_tiny, TN)
    rows_all[:, :width] = query_grad_ref[...]

    for side in range(2):
        far_copies[side].wait()
        rows_all[:, (side + 1) * width : (side + 2) * width] = (
            send_far[side, 0].astype(F32) + far_in[side].astype(F32)
        ).astype(BF16)
    part = token_grad[...] + mm(rows_all[:, width:], weight_ref[:, width:], NT)
    part_low = part.astype(BF16)
    inputs = hidden_ref[...].astype(F32)
    scale = lax.rsqrt(jnp.mean(inputs * inputs, axis=-1, keepdims=True) + NORM_EPS)
    gain_send[0] = fold_sum(part_low.astype(F32) * inputs * scale)
    token_in[0] = part_low
    gain_total = gain_send[0]
    gain_copies, token_copies = [], []
    tp_bits = bits_down(tp_count)[::-1]
    gain_copies.append(wire.send(gain_send.at[0], gain_in.at[0], tp=t ^ tp_bits[0]))
    token_copies.append(wire.send(token_in.at[0], token_in.at[1], tp=t ^ tp_bits[0]))
    second_all[:, :, :, : 2 * width] = split(mm(normed_ref[...], rows_all[:, width:], TN))
    for level, bit in enumerate(tp_bits):
        if level:
            gain_send[level] = gain_total
            gain_copies.append(wire.send(gain_send.at[level], gain_in.at[level], tp=t ^ bit))
        gain_copies[level].wait()
        gain_total = gain_total + gain_in[level]
    gain_one = jnp.sum(gain_total, axis=0, keepdims=True)
    gain_two = jnp.sum(gain_two_ref[...], axis=0, keepdims=True)
    row = lax.broadcasted_iota(jnp.int32, (LANES, D), 0)
    gain_rows = jnp.where(row == experts, gain_one, jnp.where(row == experts + 1, gain_two, 0.0))
    second_all[:, :, :, 2 * width :] = split(router_grad + gain_rows.T)
    second_crossed = cross(second_all, second_core)

    add_core(second_all, second_core, second_sum, second_crossed)
    second_far = wire.send(second_sum.at[1], second_x, ctx=c ^ 2)
    for copy in out_home:
        copy.wait()
    mixed[:, own_share] = mm(picker_ref[...], out_back[...]).astype(BF16)
    mixed_part = mixed.at[:, own_share]
    mixed_copies = [wire.send(mixed_part, mixed_part, tp=t ^ k) for k in range(1, tp_count)]
    first_far, second_moving = None, None
    for level in range(len(dp_bits)):
        dp_add(first_sum, first_dp, level, first_moving)
        bias_end()
        if level + 1 < len(dp_bits):
            bias_begin()
            first_moving = dp_send(first_sum, first_dp, level + 1, range(len(far)))
        else:
            first_far = wire.send(first_sum.at[1, d], first_x, ctx=c ^ 2)
        if level == 0:
            second_far.wait()
            second_sum[0] = (second_sum[0].astype(F32) + second_x[...].astype(F32)).astype(BF16)
        else:
            dp_add(second_sum, second_dp, level - 1, second_moving)
        second_moving = dp_send(second_sum, second_dp, level, [0])
    total = part_low.astype(F32)
    for level, bit in enumerate(tp_bits):
        if level:
            token_in[2 * level] = total.astype(BF16)
            total = token_in[2 * level].astype(F32)
            token_copies.append(
                wire.send(token_in.at[2 * level], token_in.at[2 * level + 1], tp=t ^ bit)
            )
        token_copies[level].wait()
        total = total + token_in[2 * level + 1].astype(F32)
    weighted = gains_ref[0:1, :] * total
    inner = jnp.mean(inputs * weighted, axis=-1, keepdims=True)
    input_grad_ref[...] = (
        middle_grad_ref[...] + scale * weighted - inputs * (scale * scale * scale) * inner
    )
    for copy in mixed_copies:
        copy.wait()
    output_ref[...] = middle_ref[...] + mixed[...].astype(F32)
    bias_out_ref[...] = bias_total[-1]
    first_far.wait()
    first_ref[...] = first_sum[0, pl.ds(d, 1)][0].astype(F32) + first_x[...].astype(F32)
    dp_add(second_sum, second_dp, len(dp_bits) - 1, second_moving)
    result = second_sum[0, pl.ds(d, 1)][0].astype(F32)
    second_ref[...] = result[:, : 2 * width]
    rest = jnp.zeros((LANES - result.shape[0], LANES), F32)
    tail_ref[...] = jnp.concatenate([result[:, 2 * width :], rest], axis=0).T
    wire.finish()


def final_step(
    query_grad, key_part, value_part, normed, weight, low, attended, normed_two, logit, hidden,
    gains, gain_two, middle_grad, middle, picker, bias, outs, experts,
):
    tokens, width = query_grad.shape
    slots, share = outs[0].shape[1:]
    dp_count, ctx_count, tp_count = (lax.axis_size(a) for a in ("dp", "ctx", "tp"))
    rows = D // (dp_count * ctx_count)
    half = ctx_count // 2
    levels = len(bits_down(dp_count))
    tp_levels = len(bits_down(tp_count))
    one, two = 2 * width, 2 * width + LANES
    copies = 6 * half + 8 + 3 * tp_count + (half + 2) * dp_count + 2 * ctx_count
    vmem = pl.BlockSpec(memory_space=pltpu.VMEM)
    return pl.pallas_call(
        functools.partial(final_kernel, experts, dp_count, ctx_count, tp_count),
        in_specs=[vmem] * (16 + tp_count),
        out_specs=[vmem] * 6,
        out_shape=[
            jax.ShapeDtypeStruct((tokens, D), F32),
            jax.ShapeDtypeStruct((tokens, D), F32),
            jax.ShapeDtypeStruct(bias.shape, F32),
            jax.ShapeDtypeStruct((rows, one), F32),
            jax.ShapeDtypeStruct((rows, 2 * width), F32),
            jax.ShapeDtypeStruct((LANES, LANES), F32),
        ],
        scratch_shapes=[
            pltpu.VMEM((dp_count - 1, slots, share), BF16),
            pltpu.VMEM((dp_count * slots, share), BF16),
            pltpu.VMEM((tokens, D), BF16),
            pltpu.VMEM((levels + ctx_count.bit_length() - 1,) + bias.shape, F32),
            pltpu.VMEM((levels + ctx_count.bit_length() - 1,) + bias.shape, F32),
            pltpu.VMEM((2, half, tokens, width), BF16),
            pltpu.VMEM((2, half, tokens, width), BF16),
            pltpu.VMEM((2, tokens, width), BF16),
            pltpu.VMEM((dp_count, ctx_count, rows, one), BF16),
            pltpu.VMEM((dp_count, ctx_count, rows, two), BF16),
            pltpu.VMEM((half, dp_count, rows, one), BF16),
            pltpu.VMEM((half, dp_count, rows, two), BF16),
            pltpu.VMEM((half, dp_count, rows, one), BF16),
            pltpu.VMEM((half, dp_count, rows, two), BF16),
            pltpu.VMEM((levels, half, dp_count, rows, one), BF16),
            pltpu.VMEM((levels, 1, dp_count, rows, two), BF16),
            pltpu.VMEM((rows, one), BF16),
            pltpu.VMEM((dp_count, rows, two), BF16),
            pltpu.VMEM((tokens, 3 * width), BF16),
            pltpu.VMEM((tokens, D), F32),
            pltpu.VMEM((2 * tp_levels, tokens, D), BF16),
            pltpu.VMEM((tp_levels, 8, D), F32),
            pltpu.VMEM((tp_levels, 8, D), F32),
            pltpu.SemaphoreType.DMA((copies,)),
            pltpu.SemaphoreType.DMA((copies,)),
        ],
        compiler_params=pltpu.CompilerParams(
            vmem_limit_bytes=VMEM_CAP, collective_id=2, has_side_effects=True
        ),
        cost_estimate=cost(87),
        name="final_step",
    )(
        query_grad, key_part, value_part, normed, weight, low, attended, normed_two, logit,
        hidden, gains, gain_two, middle_grad, middle, picker, bias, *outs,
    )


def adam_kernel(*refs):
    weight, first, second = refs[:3]
    parts, outs = refs[3:-4], refs[-4:]
    gradient = parts[0][...].astype(F32) + parts[1][...].astype(F32) + parts[2][...].astype(F32)
    first_new = BETA_ONE * first[...] + (1.0 - BETA_ONE) * gradient
    second_new = BETA_TWO * second[...] + (1.0 - BETA_TWO) * gradient * gradient
    outs[0][...] = gradient
    outs[1][...] = first_new
    outs[2][...] = second_new
    outs[3][...] = -MAIN_RATE * (
        first_new / FIX_ONE / (jnp.sqrt(second_new / FIX_TWO) + ADAM_EPS)
        + WEIGHT_DECAY * weight[...].astype(F32)
    )


def adam(weight, first, second, kept, arrived, far):
    count, rows, columns = weight.shape
    step = 64
    plain = pl.BlockSpec((1, step, columns), lambda i, j: (i, j, 0))
    held = pl.BlockSpec((None, 1, step, columns), lambda i, j: (0, i, j, 0))
    shape = jax.ShapeDtypeStruct(weight.shape, F32)
    return pl.pallas_call(
        adam_kernel,
        grid=(count, rows // step),
        in_specs=[plain] * 3 + [held] * 2 + [plain],
        out_specs=[plain] * 4,
        out_shape=[shape] * 4,
        compiler_params=pltpu.CompilerParams(vmem_limit_bytes=VMEM_CAP),
        cost_estimate=cost(5),
        name="adam",
    )(weight, first, second, kept, arrived, far)


def shards(
    hidden_in,
    out_grad,
    segments,
    routes,
    bucket_table,
    qkv_weight,
    out_weight,
    router,
    norm_gains,
    position_bias,
    expert_in,
    expert_down,
    qkv_first,
    qkv_second,
    out_first,
    out_second,
    router_first,
    router_second,
    gains_first,
    gains_second,
    bias_first,
    bias_second,
    in_first,
    in_second,
    down_first,
    down_second,
):
    tokens = hidden_in.shape[0]
    dp_count, ctx_count, tp_count = (lax.axis_size(a) for a in ("dp", "ctx", "tp"))
    dp_place, ctx_place, tp_place = (lax.axis_index(a) for a in ("dp", "ctx", "tp"))
    length = tokens * ctx_count
    heads_here = position_bias.shape[0]
    width_here = heads_here * HEAD_DIM
    pairs = heads_here // 2
    expert_count = router.shape[1]
    top_count = routes.shape[1]
    own_rows = router.shape[0]

    tail_pack = jnp.pad(
        jnp.concatenate([router, norm_gains.T], axis=1), ((0, 0), (0, LANES - expert_count - 2))
    )
    pack = jnp.concatenate(
        [qkv_weight.reshape(own_rows, 3 * width_here), tail_pack, out_weight.T], axis=1
    )
    doc_row = jnp.broadcast_to(segments.reshape(1, tokens), (8, tokens))
    capacity = max(2, min(tokens, 5 * top_count * tokens // (4 * expert_count)))
    window_width = tokens + length
    table = jnp.pad(bucket_table[::-1], (0, 1), constant_values=BUCKETS)
    table = lax.dynamic_slice(table, (ctx_place * tokens,), (window_width,))
    table = jnp.broadcast_to(table[None], (8, window_width))
    (queries, key_values, normed_one, qkv_flat, out_own, lanes, gains, info, doc_col,
     picker_flip, grads_own, grads_half, expert_land) = start(
        pack, hidden_in, doc_row, routes, out_grad, expert_in[0], width_here, expert_count,
        capacity,
    )
    down_late, _ = lax.optimization_barrier((expert_down[0], gains))
    out_sides = gather_xor(out_own, "tp")
    arrived_grads = [grads_own] + [swap(grads_half[m - 1], "dp", m) for m in range(1, dp_count)]
    down_pieces = gather_xor(down_late, "ctx")
    half = pairs // 2
    attended_first, totals = attention(
        info, queries, key_values, position_bias, table, doc_row, doc_col, 0, half, ()
    )
    first_sides = gather_xor(attended_first, "tp")
    attended_second, totals = attention(
        info, queries, key_values, position_bias, table, doc_row, doc_col, half, pairs - half,
        (totals,),
    )
    (middle, normed_two, logit_grad, middle_grad, middle_low, attended_grad, gain_two_grad,
     out_parts, attended, in_keep, down_keep, in_core, down_core) = expert_step(
        first_sides, attended_second, hidden_in, out_grad, gains, lanes, picker_flip, out_sides,
        arrived_grads, expert_in[0], expert_land, down_pieces, expert_count,
    )

    def add_cores(kept, arrived, k):
        return kept[k].astype(F32) + arrived[k].astype(F32)

    in_far = [swap(add_cores(in_keep, in_core, 1).astype(BF16), "ctx", 2)]
    down_far = [swap(add_cores(down_keep, down_core, 1).astype(BF16), "ctx", 2)]
    out_far = [swap(out_parts[k], "tp", k) for k in range(1, tp_count)]
    query_grad, key_part, value_part, bias_part = attention_back(
        info, queries, key_values, attended_grad, totals, position_bias, table, doc_row, doc_col
    )
    query_grad, in_far, down_far, out_far = lax.optimization_barrier(
        (query_grad, in_far, down_far, out_far)
    )
    input_grad, output, bias_total, first_total, second_total, tail_total = final_step(
        query_grad, key_part, value_part, normed_one, qkv_flat, middle_low, attended, normed_two,
        logit_grad, hidden_in, gains, gain_two_grad, middle_grad, middle, picker_flip, bias_part,
        [out_parts[0]] + out_far, expert_count,
    )
    bias_total = bias_total[:, :2].reshape(heads_here, BUCKETS)
    qkv_total = jnp.concatenate(
        [first_total[:, :width_here], second_total], axis=1
    ).reshape(own_rows, 3, width_here)
    out_total = first_total[:, width_here:].T
    router_total = tail_total[:expert_count, :own_rows].T
    gains_total = tail_total[expert_count : expert_count + 2, :own_rows]

    qkv_new = adamw_step(qkv_weight.astype(F32), qkv_total, qkv_first, qkv_second, MAIN_RATE)
    out_new = adamw_step(out_weight.astype(F32), out_total, out_first, out_second, MAIN_RATE)
    router_new = adamw_step(
        router.astype(F32), router_total, router_first, router_second, MAIN_RATE
    )
    gains_new = adamw_step(
        norm_gains.astype(F32), gains_total, gains_first, gains_second, MAIN_RATE
    )
    bias_new = adamw_step(position_bias, bias_total, bias_first, bias_second, BIAS_RATE)
    in_new = [
        values[None]
        for values in adam(
            expert_in[0], in_first[0], in_second[0], in_keep, in_core, in_far[0]
        )
    ]
    down_new = adam(
        expert_down, down_first, down_second, down_keep[:, None], down_core[:, None],
        down_far[0][None],
    )
    return (
        output,
        input_grad,
        qkv_total,
        *qkv_new,
        out_total,
        *out_new,
        router_total,
        *router_new,
        gains_total,
        *gains_new,
        bias_total,
        *bias_new,
        *in_new,
        *down_new,
    )


def solution(mesh):
    token_rows = P(("dp", "ctx"), None)
    qkv = P(("dp", "ctx"), None, "tp")
    out = P("tp", ("dp", "ctx"))
    gains = P(None, ("dp", "ctx"))
    bias = P("tp", None)
    expert_in = P("dp", None, "ctx", "tp")
    expert_down = P("dp", "tp", "ctx")
    placed = (
        token_rows, token_rows, P("dp", "ctx"), token_rows, P(),
        qkv, out, token_rows, gains, bias, expert_in, expert_down,
        qkv, qkv, out, out, token_rows, token_rows, gains, gains, bias, bias,
        expert_in, expert_in, expert_down, expert_down,
    )
    return jax.shard_map(
        shards,
        mesh=mesh,
        in_specs=placed,
        out_specs=(token_rows, token_rows)
        + (qkv,) * 4
        + (out,) * 4
        + (token_rows,) * 4
        + (gains,) * 4
        + (bias,) * 4
        + (expert_in,) * 4
        + (expert_down,) * 4,
        check_vma=False,
    )
```

```python
import functools

import jax
import jax.numpy as jnp
from jax import lax
from jax.experimental import pallas as pl
from jax.experimental.pallas import tpu as pltpu
from jax.sharding import PartitionSpec as P

D = 1024
HEAD_DIM = 64
BUCKETS = 32

NORM_EPS = 1e-06
NEG_FILL = -1e30
BETA_ONE = 0.9
BETA_TWO = 0.95
FIX_ONE = 1.0 - 0.9**10
FIX_TWO = 1.0 - 0.95**10
ADAM_EPS = 1e-08
WEIGHT_DECAY = 0.1
MAIN_RATE = 0.02
BIAS_RATE = 0.2

F32 = jnp.float32
BF16 = jnp.bfloat16
LANES = 128
BLOCK = 256
VMEM_CAP = 60 * 1024 * 1024
GELU_K = 0.7978845608028654
GELU_C = 0.044715


def tree_sum(values):
    while len(values) > 1:
        values = [values[k] + values[k + 1] for k in range(0, len(values), 2)]
    return values[0]


def rms_scale(values):
    return lax.rsqrt(jnp.mean(values * values, axis=-1, keepdims=True) + NORM_EPS)


def norm_back(values, scale_here, gain_here, gradient):
    weighted = gain_here * gradient
    row_inner = jnp.mean(values * weighted, axis=-1, keepdims=True)
    input_part = scale_here * weighted - values * scale_here**3 * row_inner
    return (input_part, jnp.sum(gradient * values * scale_here, axis=0))


def adamw_step(weight, gradient, first_moment, second_moment, step_rate):
    first_new = BETA_ONE * first_moment + (1.0 - BETA_ONE) * gradient
    second_new = BETA_TWO * second_moment + (1.0 - BETA_TWO) * gradient * gradient
    update = -step_rate * (
        first_new / FIX_ONE / (jnp.sqrt(second_new / FIX_TWO) + ADAM_EPS) + WEIGHT_DECAY * weight
    )
    return (first_new, second_new, update)


def cost(micros):
    return pl.CostEstimate(flops=int(micros * 1.15e9), bytes_accessed=1 << 20, transcendentals=0)


def swap(values, axis, bits):
    count = lax.axis_size(axis)
    return lax.ppermute(values, axis, [(i, i ^ bits) for i in range(count)])


def gather_xor(values, axis):
    pieces = {0: values}
    bit = lax.axis_size(axis) >> 1
    while bit:
        for key in list(pieces):
            pieces[key | bit] = swap(pieces[key], axis, bit)
        bit >>= 1
    return [pieces[m] for m in range(len(pieces))]


def scatter_sum(parts, axis):
    live = dict(enumerate(parts))
    bit = 1
    while bit < lax.axis_size(axis):
        left = {}
        for key in live:
            if key & bit == 0:
                moved = swap(live[key | bit].astype(BF16), axis, bit)
                left[key] = live[key].astype(F32) + moved.astype(F32)
        live = left
        bit <<= 1
    return live[0]


def all_sum(values, axis):
    bit = 1
    while bit < lax.axis_size(axis):
        values = values + swap(values, axis, bit)
        bit <<= 1
    return values


def in_order(pieces, place, dim):
    bit = 1
    while bit < len(pieces):
        odd = (place & bit) > 0
        pieces = [jnp.where(odd, pieces[m ^ bit], pieces[m]) for m in range(len(pieces))]
        bit <<= 1
    return jnp.concatenate(pieces, axis=dim)


MESH = pl.DeviceIdType.MESH


class Wire:
    def __init__(self, sends, receives):
        self.sends, self.receives, self.count, self.copies = sends, receives, 0, []

    def send(self, source, target, **device):
        copy = pltpu.make_async_remote_copy(
            src_ref=source,
            dst_ref=target,
            send_sem=self.sends.at[self.count],
            recv_sem=self.receives.at[self.count],
            device_id=device,
            device_id_type=MESH,
        )
        copy.start()
        self.count += 1
        self.copies.append(Arrival(copy))
        return self.copies[-1]

    def finish(self):
        for copy in self.copies:
            copy.sent()


class Arrival:
    def __init__(self, copy):
        self.copy, self.waited, self.gone = copy, False, False

    def sent(self):
        if not self.gone:
            self.copy.wait_send()
        self.gone = True

    def wait(self):
        if not self.waited:
            self.copy.wait_recv()
        self.waited = True


def greet(partners):
    barrier = pltpu.get_barrier_semaphore()
    for device in partners:
        pl.semaphore_signal(barrier, inc=1, device_id=device, device_id_type=MESH)
    pl.semaphore_wait(barrier, len(partners))


def bits_down(count):
    bits, bit = [], count >> 1
    while bit:
        bits.append(bit)
        bit >>= 1
    return bits


def xor_order(count):
    order = [0]
    for bit in bits_down(count):
        order = order + [k | bit for k in order]
    return order


NT = (((1,), (1,)), ((), ()))
NN = (((1,), (0,)), ((), ()))
TN = (((0,), (0,)), ((), ()))


def mm(left, right, dims=NN):
    return lax.dot_general(left, right, dims, preferred_element_type=F32)


def fold_max(values):
    return jnp.max(values.reshape(values.shape[0] // 8, 8, values.shape[1]), axis=0)


def fold_sum(values):
    return jnp.sum(values.reshape(values.shape[0] // 8, 8, values.shape[1]), axis=0)


def skewed(row):
    width = row.shape[1]
    tall = jnp.broadcast_to(row, (LANES, width))
    return pltpu.roll(tall, width - (LANES - 1), 1, stride=1, stride_axis=0)


def unskew_sum(field):
    half = field.shape[0] // 2
    while half >= 1:
        field = pltpu.roll(field[:half], half, 1) + field[half:]
        half //= 2
    return field


def head_masks(rows):
    lane = lax.broadcasted_iota(jnp.int32, (rows, LANES), 1)
    return [(lane < HEAD_DIM).astype(BF16), (lane >= HEAD_DIM).astype(BF16)]


def score_tile(key_block, query_head, skew_ref, head, first, same):
    scores = mm(key_block, query_head, NT)
    tiles = []
    for s in range(BLOCK // LANES):
        column = pl.multiple_of(first - s * LANES, LANES)
        tiles.append(skew_ref[head, :, pl.ds(column, BLOCK)])
    return jnp.where(same, scores + jnp.concatenate(tiles, axis=0), NEG_FILL)


def bucket_lanes(table_ref):
    row = lax.broadcasted_iota(jnp.int32, (BUCKETS, table_ref.shape[1]), 0)
    return (row == table_ref[0:1, :]).astype(F32)


def spread_bias(bias_ref, table_ref, skew_ref, first=0):
    rows = bias_ref[pl.ds((pl.program_id(0) + first) * 2, 2), :]
    window = jnp.dot(
        jnp.concatenate([rows] * 4, axis=0), bucket_lanes(table_ref),
        precision=lax.Precision.HIGHEST, preferred_element_type=F32,
    )
    for h in range(2):
        skew_ref[h] = skewed(window[h : h + 1, :])


def over_blocks(info_ref, qb, query_blocks, step):
    @pl.loop(0, info_ref[query_blocks + qb, 0])
    def _(i):
        blocks = [info_ref[qb, 2 * i + k] for k in range(2)]
        step(
            [pl.ds(pl.multiple_of(kb * BLOCK, BLOCK), BLOCK) for kb in blocks],
            [info_ref[2 * query_blocks, kb] + qb * BLOCK for kb in blocks],
        )


def attention_kernel(
    first, info_ref, query_ref, key_ref, value_ref, bias_ref, table_ref, doc_row_ref,
    doc_col_ref, *refs,
):
    out_ref, total_ref, skew_ref, flip_ref, score_ref, most_ref, sum_ref, mix_ref = refs[-8:]
    tokens, length = query_ref.shape[0], key_ref.shape[0]
    key_blocks, query_blocks = length // BLOCK, tokens // BLOCK
    masks = head_masks(BLOCK)
    spread_bias(bias_ref, table_ref, skew_ref, first)

    @pl.loop(0, key_blocks)
    def _(kb):
        rows = pl.ds(pl.multiple_of(kb * BLOCK, BLOCK), BLOCK)
        flip_ref[:, rows] = value_ref[rows, :].T

    for qb in range(query_blocks):
        here = slice(qb * BLOCK, (qb + 1) * BLOCK)
        pair = query_ref[here, :] * jnp.asarray(HEAD_DIM**-0.5, BF16)
        query_heads = [pair * mask for mask in masks]
        doc_row = doc_row_ref[0:1, here]
        most_ref[...] = jnp.full_like(most_ref, NEG_FILL)
        sum_ref[...] = jnp.zeros_like(sum_ref)
        mix_ref[...] = jnp.zeros_like(mix_ref)

        def scores(spans, firsts):
            for rows, first_column in zip(spans, firsts):
                column = doc_col_ref[rows, :]
                same = jnp.concatenate([column] * (BLOCK // LANES), axis=1) == doc_row
                for h in range(2):
                    tile = score_tile(
                        key_ref[rows, :], query_heads[h], skew_ref, h, first_column, same
                    )
                    score_ref[h, rows, :] = tile
                    most_ref[h] = jnp.maximum(most_ref[h], fold_max(tile))

        over_blocks(info_ref, qb, query_blocks, scores)
        most = [jnp.max(most_ref[h], axis=0, keepdims=True) for h in range(2)]

        def mixes(spans, firsts):
            for h in range(2):
                heads = slice(h * HEAD_DIM, (h + 1) * HEAD_DIM)
                total, mix = sum_ref[h], mix_ref[h]
                for rows in spans:
                    weights = jnp.exp(score_ref[h, rows, :] - most[h])
                    total += fold_sum(weights)
                    mix += mm(flip_ref[heads, rows], weights.astype(BF16))
                sum_ref[h] = total
                mix_ref[h] = mix

        over_blocks(info_ref, qb, query_blocks, mixes)
        columns = []
        for h in range(2):
            total = jnp.sum(sum_ref[h], axis=0, keepdims=True)
            columns.append(mix_ref[h] / total)
            total_ref[0, h : h + 1, here] = most[h] + jnp.log(total)
        out_ref[here, :] = jnp.concatenate(columns, axis=0).T.astype(BF16)


def attention_back_kernel(
    info_ref, query_ref, key_ref, value_ref, grad_ref, total_ref, bias_ref, table_ref,
    doc_row_ref, doc_col_ref,
    query_grad_ref, key_grad_ref, value_grad_ref, bias_grad_ref,
    skew_ref, field_ref, flip_ref, weight_ref, change_ref, inner_ref, mix_ref, key_sum, value_sum,
):
    tokens, length = query_ref.shape[0], key_ref.shape[0]
    key_blocks, query_blocks = length // BLOCK, tokens // BLOCK
    masks = head_masks(BLOCK)
    spread_bias(bias_ref, table_ref, skew_ref)
    field_ref[...] = jnp.zeros_like(field_ref)
    key_sum[...] = jnp.zeros_like(key_sum)
    value_sum[...] = jnp.zeros_like(value_sum)

    @pl.loop(0, key_blocks)
    def _(kb):
        rows = pl.ds(pl.multiple_of(kb * BLOCK, BLOCK), BLOCK)
        flip_ref[:, rows] = key_ref[rows, :].T

    for qb in range(query_blocks):
        here = slice(qb * BLOCK, (qb + 1) * BLOCK)
        pair = query_ref[here, :] * jnp.asarray(HEAD_DIM**-0.5, BF16)
        query_heads = [pair * mask for mask in masks]
        grad_pair = grad_ref[here, :]
        grad_heads = [grad_pair * mask for mask in masks]
        doc_row = doc_row_ref[0:1, here]
        inner_ref[...] = jnp.zeros_like(inner_ref)
        mix_ref[...] = jnp.zeros_like(mix_ref)
        totals = [total_ref[0, h : h + 1, here] for h in range(2)]

        def changes(spans, firsts):
            for rows, first_column in zip(spans, firsts):
                column = doc_col_ref[rows, :]
                same = jnp.concatenate([column] * (BLOCK // LANES), axis=1) == doc_row
                for h in range(2):
                    tile = score_tile(
                        key_ref[rows, :], query_heads[h], skew_ref, h, first_column, same
                    )
                    weights = jnp.exp(tile - totals[h])
                    change = mm(value_ref[rows, :], grad_heads[h], NT)
                    weight_ref[h, rows, :] = weights
                    change_ref[h, rows, :] = change
                    inner_ref[h] += fold_sum(weights * change)

        over_blocks(info_ref, qb, query_blocks, changes)
        inner = [jnp.sum(inner_ref[h], axis=0, keepdims=True) for h in range(2)]

        def gradients(spans, firsts):
            mixes = [mix_ref[h] for h in range(2)]
            for rows, first_column in zip(spans, firsts):
                key_part = value_part = None
                for h in range(2):
                    weights = weight_ref[h, rows, :]
                    score_grad = weights * (change_ref[h, rows, :] - inner[h])
                    for s in range(BLOCK // LANES):
                        first = pl.multiple_of(first_column - s * LANES, LANES)
                        field_ref[h, :, pl.ds(first, BLOCK)] += score_grad[
                            s * LANES : (s + 1) * LANES
                        ]
                    low = score_grad.astype(BF16)
                    key_here = mm(low, query_heads[h])
                    value_here = mm(weights.astype(BF16), grad_heads[h])
                    key_part = key_here if h == 0 else key_part + key_here
                    value_part = value_here if h == 0 else value_part + value_here
                    heads = slice(h * HEAD_DIM, (h + 1) * HEAD_DIM)
                    mixes[h] += mm(flip_ref[heads, rows], low)
                key_sum[rows, :] += key_part
                value_sum[rows, :] += value_part
            for h in range(2):
                mix_ref[h] = mixes[h]

        over_blocks(info_ref, qb, query_blocks, gradients)
        both = jnp.concatenate([mix_ref[0], mix_ref[1]], axis=0) * HEAD_DIM**-0.5
        query_grad_ref[here, :] = both.T.astype(BF16)

    key_grad_ref[...] = key_sum[...].astype(BF16)
    value_grad_ref[...] = value_sum[...].astype(BF16)
    offsets = jnp.concatenate([unskew_sum(field_ref[h]) for h in range(2)] * 4, axis=0)
    bias_grad_ref[0] = lax.dot_general(
        offsets, bucket_lanes(table_ref), NT, precision=lax.Precision.HIGHEST,
        preferred_element_type=F32,
    )


def attention_specs(tokens, length, pairs, heads, width, first=0):
    smem = pl.BlockSpec(memory_space=pltpu.SMEM)
    return dict(
        info=smem,
        query=pl.BlockSpec((tokens, LANES), lambda i: (0, i + first)),
        key=pl.BlockSpec((length, LANES), lambda i: (0, i + first)),
        value=pl.BlockSpec((length, LANES), lambda i: (0, i + first + pairs)),
        bias=pl.BlockSpec((heads, BUCKETS), lambda i: (0, 0)),
        table=pl.BlockSpec((8, width), lambda i: (0, 0)),
        total=pl.BlockSpec((1, 8, tokens), lambda i: (i + first, 0, 0)),
        bias_grad=pl.BlockSpec((1, 8, BUCKETS), lambda i: (i, 0, 0)),
        doc_row=pl.BlockSpec((8, tokens), lambda i: (0, 0)),
        doc_col=pl.BlockSpec((length, LANES), lambda i: (0, 0)),
    )


def attention(info, queries, key_values, bias, table, doc_row, doc_col, first, count, held):
    tokens, length = queries.shape[0], key_values.shape[0]
    pairs, width = bias.shape[0] // 2, table.shape[1]
    specs = attention_specs(tokens, length, pairs, bias.shape[0], width, first)
    return pl.pallas_call(
        functools.partial(attention_kernel, first),
        grid=(count,),
        in_specs=[
            specs["info"], specs["query"], specs["key"], specs["value"], specs["bias"],
            specs["table"], specs["doc_row"], specs["doc_col"],
        ]
        + [pl.BlockSpec(memory_space=pl.ANY)] * len(held),
        out_specs=[pl.BlockSpec((tokens, LANES), lambda i: (0, i)), specs["total"]],
        out_shape=[
            jax.ShapeDtypeStruct((tokens, count * LANES), BF16),
            jax.ShapeDtypeStruct((pairs, 8, tokens), F32),
        ],
        scratch_shapes=[
            pltpu.VMEM((2, LANES, width), F32),
            pltpu.VMEM((LANES, length), BF16),
            pltpu.VMEM((2, length, BLOCK), F32),
            pltpu.VMEM((2, 8, BLOCK), F32),
            pltpu.VMEM((2, 8, BLOCK), F32),
            pltpu.VMEM((2, HEAD_DIM, BLOCK), F32),
        ],
        input_output_aliases={8: 1} if held else {},
        compiler_params=pltpu.CompilerParams(vmem_limit_bytes=VMEM_CAP),
        cost_estimate=cost(5),
        name="attention_forward",
    )(info, queries, key_values, key_values, bias, table, doc_row, doc_col, *held)


def attention_back(info, queries, key_values, grads, totals, bias, table, doc_row, doc_col):
    tokens, length = queries.shape[0], key_values.shape[0]
    pairs, width = bias.shape[0] // 2, table.shape[1]
    specs = attention_specs(tokens, length, pairs, bias.shape[0], width)
    return pl.pallas_call(
        attention_back_kernel,
        grid=(pairs,),
        in_specs=[
            specs["info"], specs["query"], specs["key"], specs["value"], specs["query"],
            specs["total"], specs["bias"], specs["table"], specs["doc_row"], specs["doc_col"],
        ],
        out_specs=[specs["query"], specs["key"], specs["key"], specs["bias_grad"]],
        out_shape=[
            jax.ShapeDtypeStruct(queries.shape, BF16),
            jax.ShapeDtypeStruct((length, queries.shape[1]), BF16),
            jax.ShapeDtypeStruct((length, queries.shape[1]), BF16),
            jax.ShapeDtypeStruct((pairs, 8, BUCKETS), F32),
        ],
        scratch_shapes=[
            pltpu.VMEM((2, LANES, width), F32),
            pltpu.VMEM((2, LANES, width), F32),
            pltpu.VMEM((LANES, length), BF16),
            pltpu.VMEM((2, length, BLOCK), F32),
            pltpu.VMEM((2, length, BLOCK), F32),
            pltpu.VMEM((2, 8, BLOCK), F32),
            pltpu.VMEM((2, HEAD_DIM, BLOCK), F32),
            pltpu.VMEM((length, LANES), F32),
            pltpu.VMEM((length, LANES), F32),
        ],
        compiler_params=pltpu.CompilerParams(vmem_limit_bytes=VMEM_CAP),
        cost_estimate=cost(40),
        name="attention_backward",
    )(info, queries, key_values, key_values, grads, totals, bias, table, doc_row, doc_col)


def start_kernel(
    experts, dp_count, ctx_count, tp_count, qkv_ref, out_flip_ref, router_ref, gain_pair_ref,
    hidden_ref, segments_ref, routes_ref, out_grad_ref, expert_ref,
    query_ref, pair_ref, normed_flip_ref, weight_out, own_ref, lanes_ref, gains_ref, info_ref,
    row_ref, column_ref, picker_ref, picker_rows_ref, grads_own_ref, grads_ref, early_land,
    expert_land,
    weights, out_all, hidden, docs, docs_ref, flip, sends, receives, out_sem,
):
    d, c, t = lax.axis_index("dp"), lax.axis_index("ctx"), lax.axis_index("tp")
    rows = out_flip_ref.shape[0]
    tokens, width = query_ref.shape
    early = early_blocks(dp_count)
    own_rows = pl.ds(pl.multiple_of((d * ctx_count + c) * rows, rows), rows)
    own_lanes = pl.ds(pl.multiple_of(t * width, width), width)
    for part in range(3):
        weights[own_rows, part * width : (part + 1) * width] = qkv_ref[part]
    out_all[own_rows, own_lanes] = out_flip_ref[...]
    flip[...] = jnp.zeros_like(flip)
    flip[:experts, :rows] = router_ref[...].astype(F32)
    flip[experts : experts + 2, :rows] = gain_pair_ref[...].astype(F32)
    weights[own_rows, 3 * width :] = flip[:, :LANES].T[:rows].astype(BF16)
    docs_ref[...] = jnp.broadcast_to(segments_ref[...], docs_ref.shape)
    row_ref[...] = docs_ref[...]
    greet(
        [{"ctx": c ^ m} for m in range(1, ctx_count)]
        + [{"dp": d ^ m} for m in sorted(set(bits_down(dp_count) + early))]
        + [{"tp": t ^ k} for k in range(1, tp_count)]
    )
    wire = Wire(sends, receives)
    share = grads_ref.shape[2]
    own_share = pl.ds(pl.multiple_of(t * share, share), share)

    def send_shard(m, j, part, lanes=own_lanes, **device):
        index = (d ^ m) * ctx_count + (c ^ j)
        here = pl.ds(pl.multiple_of(index * rows, rows), rows)
        shard = out_all.at[here, lanes] if part else weights.at[here]
        return wire.send(shard, shard, **device)

    docs_sent = [wire.send(docs_ref, docs.at[m], ctx=c ^ m) for m in range(1, ctx_count)]
    sides, sides_far = [0], []
    parts = (0, 1)
    arrivals = {part: [] for part in range(2)}
    hidden_sent, expert_sent = {}, {}
    for bit in bits_down(ctx_count)[:-1]:
        arrivals = {
            k: [send_shard(0, j, part, ctx=c ^ bit) for j in sides]
            for k, part in enumerate(parts)
        }
        assert bit == 2
        half = hidden_ref.at[:, own_share]
        hidden_sent[2] = wire.send(half, hidden.at[2, :, own_share], ctx=c ^ 2)
        for m in [0] + list(expert_sent):
            if m:
                expert_sent[m].wait()
            source = expert_land.at[m - 1] if m else expert_ref
            expert_sent[m | bit] = wire.send(source, expert_land.at[(m | bit) - 1], ctx=c ^ bit)
        for copy in arrivals[0]:
            copy.wait()
        sides_far = sides + [j | bit for j in sides]
        if bit != 2:
            for copy in arrivals[1]:
                copy.wait()
        sides = sides_far
    hidden_sent[1] = wire.send(hidden_ref, hidden.at[1], ctx=c ^ 1)

    order = xor_order(dp_count)
    groups = [{}, {}]
    crossed, beside = [[], []], []

    def onward(k, m):
        for copy in groups[k].get(m, []):
            copy.wait()
        for bit in bits_down(dp_count):
            if m & (2 * bit - 1) == 0:
                groups[k][m | bit] = [send_shard(m, j, parts[k], dp=d ^ bit) for j in sides]
        crossed[k] += [send_shard(m, j, parts[k], ctx=c ^ 1) for j in sides]
        if k:
            for other in range(1, tp_count):
                beside.append(
                    (m, other, [send_shard(m, j, 1, tp=t ^ other) for j in sides])
                )

    onward(0, 0)
    for copy in arrivals[1]:
        copy.wait()
    onward(1, 0)
    expert_sent[1] = wire.send(expert_ref, expert_land.at[0], ctx=c ^ 1)

    lane = lax.broadcasted_iota(jnp.int32, (tokens, LANES), 1)
    flip[:8, :] = jnp.zeros((8, tokens), F32)
    flip[: routes_ref.shape[0], :] = routes_ref[...].astype(F32)
    routes = flip[...].T
    tops = [routes[:, k : k + 1].astype(jnp.int32) for k in range(routes_ref.shape[0])]
    named = jnp.zeros((tokens, LANES), F32)
    for top in tops:
        named = jnp.where(lane == top, 1.0, named)
    row_index = lax.broadcasted_iota(jnp.int32, (tokens, tokens), 0)
    column_index = lax.broadcasted_iota(jnp.int32, (tokens, tokens), 1)
    before = jnp.where(column_index < row_index, 1.0, 0.0).astype(BF16)
    earlier = mm(before, named.astype(BF16))
    slots = grads_own_ref.shape[0]
    column = lax.broadcasted_iota(jnp.int32, picker_ref.shape, 1)
    picker = jnp.zeros(picker_ref.shape, F32)
    for top in tops:
        place = jnp.sum(jnp.where(lane == top, earlier, 0.0), axis=1, keepdims=True)
        place = place.astype(jnp.int32)
        target = jnp.where(place < slots, (top ^ d) * slots + place, -1)
        picker = jnp.where(column == target, 1.0, picker)
    picker_ref[...] = picker.astype(BF16)
    picker_rows_ref[...] = picker_ref[...].T
    hidden_sent[2].wait()
    half = hidden.at[2, :, own_share]
    spread = [wire.send(half, half, tp=t ^ k) for k in range(1, tp_count)]
    for m in range(dp_count):
        chosen = picker_rows_ref[m * slots : (m + 1) * slots, :]
        if m:
            grads_ref[m - 1] = mm(chosen, out_grad_ref[:, own_share]).astype(BF16)
        else:
            grads_own_ref[...] = mm(chosen, out_grad_ref[...]).astype(BF16)

    key_blocks, query_blocks = tokens // BLOCK, tokens // BLOCK
    where = lax.broadcasted_iota(jnp.int32, info_ref.shape, 1)
    which = lax.broadcasted_iota(jnp.int32, info_ref.shape, 0)
    info = jnp.zeros(info_ref.shape, jnp.int32)
    met = [[] for _ in range(query_blocks)]
    for m in range(ctx_count):
        if m:
            docs_sent[m - 1].wait()
        row = docs[m] if m else docs_ref[...]
        tall = jnp.broadcast_to(row[0:1, :].astype(F32), (LANES, tokens))
        column_ref[m * tokens : (m + 1) * tokens, :] = tall.T.astype(jnp.int32)
        for k in range(key_blocks):
            spot = m * key_blocks + k
            low = row[0:1, k * BLOCK : k * BLOCK + 1]
            high = row[0:1, (k + 1) * BLOCK - 1 : (k + 1) * BLOCK]
            for q in range(query_blocks):
                query_low = docs_ref[0:1, q * BLOCK : q * BLOCK + 1]
                query_high = docs_ref[0:1, (q + 1) * BLOCK - 1 : (q + 1) * BLOCK]
                meets = ((high >= query_low) & (low <= query_high)).astype(jnp.int32)
                met[q].append(meets)
            base = (ctx_count * tokens - LANES) - ((c ^ m) * tokens + k * BLOCK)
            info = jnp.where((where == spot) & (which == 2 * query_blocks), base, info)
    for q in range(query_blocks):
        count = sum(met[q][1:], met[q][0])
        inside, outside = jnp.zeros_like(count), count
        for spot, meets in enumerate(met[q]):
            place = jnp.where(meets > 0, inside, outside)
            info = jnp.where((where == place) & (which == q), spot, info)
            inside, outside = inside + meets, outside + (1 - meets)
        steps = lax.shift_right_logical(count + 1, 1)
        info = jnp.where(which == query_blocks + q, steps, info)
    info_ref[...] = info

    early_copies = []
    for i, m in enumerate(order[1:]):
        onward(0, m)
        onward(1, m)
        if i == 0:
            early_copies = [
                wire.send(grads_ref.at[n - 1], early_land.at[k], dp=d ^ n)
                for k, n in enumerate(early)
            ]
    for copy in spread:
        copy.wait()
    hidden_sent[3] = wire.send(hidden.at[2], hidden.at[3], ctx=c ^ 1)
    for copy in crossed[0]:
        copy.wait()
    keep = pltpu.make_async_copy(weights.at[:, : 3 * width], weight_out, out_sem.at[0])
    keep.start()
    small = weights[:, 3 * width : 3 * width + LANES].astype(F32)
    lane = lax.broadcasted_iota(jnp.int32, small.shape, 1)
    lanes_ref[...] = jnp.where(lane < experts, small, 0.0).astype(BF16)
    gain_one = jnp.sum(jnp.where(lane == experts, small, 0.0), axis=1, keepdims=True)
    gain_two = jnp.sum(jnp.where(lane == experts + 1, small, 0.0), axis=1, keepdims=True)
    both = jnp.where(lane == 0, gain_one, jnp.where(lane == 1, gain_two, 0.0)).T
    gains_ref[...] = both[:8]
    gain = both[0:1]
    for m in range(ctx_count):
        if m:
            hidden_sent[m].wait()
        values = (hidden[m] if m else hidden_ref[...]).astype(F32)
        scale = lax.rsqrt(jnp.mean(values * values, axis=-1, keepdims=True) + NORM_EPS)
        normed = (values * scale * gain).astype(BF16)
        pair_ref[m * tokens : (m + 1) * tokens, :] = mm(
            normed, weights[:, width : 3 * width]
        ).astype(BF16)
        if m == 0:
            normed_flip_ref[...] = normed.T
            query_ref[...] = mm(normed, weights[:, :width]).astype(BF16)
            for n, other, copies in beside:
                for copy in copies:
                    copy.wait()
                lanes = pl.ds(pl.multiple_of((t ^ other) * width, width), width)
                crossed[1] += [send_shard(n, j, 1, lanes, ctx=c ^ 1) for j in sides]
    for copy in crossed[1]:
        copy.wait()
    keep_own = pltpu.make_async_copy(out_all, own_ref, out_sem.at[1])
    keep_own.start()
    for k in [k for k in expert_sent if k > 1]:
        expert_sent[k].wait()
        expert_sent[k | 1] = wire.send(expert_land.at[k - 1], expert_land.at[k], ctx=c ^ 1)
    for k in range(1, ctx_count):
        expert_sent[k].wait()
    for copy in early_copies:
        copy.wait()
    keep.wait()
    keep_own.wait()
    wire.finish()


def early_blocks(dp_count):
    return list(range(2, dp_count))[:1]


def start(qkv, out_flip, router, gain_pair, hidden, segments, routes, out_grad, expert, slots):
    tokens, (experts, _), width = hidden.shape[0], router.shape, qkv.shape[2]
    columns = 4 * width + LANES
    dp_count, ctx_count, tp_count = (lax.axis_size(a) for a in ("dp", "ctx", "tp"))
    copies = 5 * ctx_count + (2 + tp_count) * dp_count * ctx_count + tp_count + dp_count + 1
    vmem = pl.BlockSpec(memory_space=pltpu.VMEM)
    hbm = pl.BlockSpec(memory_space=pl.ANY)
    shape = jax.ShapeDtypeStruct
    return pl.pallas_call(
        functools.partial(start_kernel, experts, dp_count, ctx_count, tp_count),
        in_specs=[vmem] * 8 + [hbm],
        out_specs=[vmem] * 3 + [hbm] * 2 + [vmem] * 9 + [hbm] * 2,
        out_shape=[
            shape((tokens, width), BF16),
            shape((tokens * ctx_count, 2 * width), BF16),
            shape((D, tokens), BF16),
            shape((D, 3 * width), BF16),
            shape((D, tp_count * width), BF16),
            shape((D, LANES), BF16),
            shape((8, D), F32),
            shape((8, LANES), jnp.int32),
            shape((8, tokens), jnp.int32),
            shape((tokens * ctx_count, LANES), jnp.int32),
            shape((tokens, dp_count * slots), BF16),
            shape((dp_count * slots, tokens), BF16),
            shape((slots, D), BF16),
            shape((dp_count - 1, slots, D // tp_count), BF16),
            shape((len(early_blocks(dp_count)), slots, D // tp_count), BF16),
            shape((ctx_count - 1,) + expert.shape, BF16),
        ],
        scratch_shapes=[
            pltpu.VMEM((D, columns - width), BF16),
            pltpu.VMEM((D, tp_count * width), BF16),
            pltpu.VMEM((ctx_count, tokens, D), BF16),
            pltpu.VMEM((ctx_count, 8, tokens), jnp.int32),
            pltpu.VMEM((8, tokens), jnp.int32),
            pltpu.VMEM((LANES, tokens), F32),
            pltpu.SemaphoreType.DMA((copies,)),
            pltpu.SemaphoreType.DMA((copies,)),
            pltpu.SemaphoreType.DMA((2,)),
        ],
        compiler_params=pltpu.CompilerParams(
            vmem_limit_bytes=VMEM_CAP, collective_id=1, has_side_effects=True
        ),
        cost_estimate=cost(60),
        name="start",
    )(qkv, out_flip, router, gain_pair, hidden, segments, routes, out_grad, expert)


def bent_parts(value):
    square = value * value
    wave = jnp.tanh(GELU_K * value * (1.0 + GELU_C * square))
    half = 0.5 * (1.0 + wave)
    slope = half + 0.5 * value * (1.0 - wave * wave) * (GELU_K * (1.0 + 3.0 * GELU_C * square))
    return value * half, slope


def expert_kernel(
    experts, dp_count, ctx_count, tp_count, attended_ref, hidden_ref, out_grad_ref, gains_ref,
    lanes_ref, picker_ref, picker_rows_ref, *refs,
):
    d, c, t = lax.axis_index("dp"), lax.axis_index("ctx"), lax.axis_index("tp")
    firsts, refs = refs[:tp_count], refs[tp_count:]
    out_ref, grads_own, refs = refs[0], refs[1], refs[2:]
    grads_land, refs = refs[: dp_count - 1], refs[dp_count - 1 :]
    in_own, in_land, refs = refs[0], refs[1], refs[2:]
    ins = [in_own] + [in_land.at[j] for j in range(ctx_count - 1)]
    down_own, refs = refs[0], refs[1:]
    middle_ref, router_grad_ref, grad_ref, low_ref, attended_grad_ref, gain_ref = refs[:6]
    out_parts, refs = refs[6 : 6 + tp_count], refs[6 + tp_count :]
    (attended_out, in_keep, in_core, in_sum, down_keep, down_core, down_far,
     mixed, out_all, in_all, down_all, rows_all, scaled_all, act_all, gate_all, up_all, send_rows,
     row_parts, row_in, row_back, dot_parts, dot_in, dot_home, dot_back, probs, whole,
     normed_flip, in_land_far, down_land_far,
     sends, receives, in_sems, keep_sems) = refs
    tokens, second_width = attended_ref.shape
    first_width = firsts[0].shape[1]
    width = first_width + second_width
    share = D // tp_count
    slots = rows_all.shape[0] // dp_count
    depth, ff = in_own.shape[1], in_own.shape[2]
    shares = range(1, tp_count)
    order = [0] + list(range(2, dp_count)) + [1]

    local = []

    def load(source, target):
        copy = pltpu.make_async_copy(source, target, in_sems.at[len(local)])
        copy.start()
        local.append(copy)
        return copy

    out_copies = [load(out_ref, out_all)]
    weight_copies, down_parts = [], []
    for j in range(ctx_count):
        part = slice(j * depth, (j + 1) * depth)
        weight_copies.append(load(ins[j], in_all.at[:, part, :]))
        down_parts.append(down_all.at[:, part])
    weight_copies.append(load(down_own, down_parts[0]))
    own_share = pl.ds(pl.multiple_of(t * share, share), share)
    weight_copies.append(load(grads_own, scaled_all.at[:slots]))
    grad_copies = [
        load(grads_land[m - 1], scaled_all.at[m * slots : (m + 1) * slots, own_share])
        for m in range(1, dp_count)
    ]
    own_lanes = pl.ds(pl.multiple_of(t * width, width), width)
    second_lanes = pl.ds(pl.multiple_of(t * width + first_width, LANES), second_width)
    mixed[:, second_lanes] = attended_ref[...]
    for m in range(tp_count):
        start = pl.multiple_of((t ^ m) * width, width)
        mixed[:, pl.ds(start, first_width)] = firsts[m][...]
    attended_out[...] = mixed[:, own_lanes]
    greet(
        [{"tp": t ^ k} for k in shares]
        + [{"dp": d ^ m} for m in range(1, dp_count)]
        + [{"ctx": c ^ 1}, {"ctx": c ^ 2}]
    )
    wire = Wire(sends, receives)
    assert ctx_count == 4
    downs = {j: wire.send(down_own, down_parts[j], ctx=c ^ j) for j in (2, 1)}
    second_part = mixed.at[:, second_lanes]
    arrivals = [wire.send(second_part, second_part, tp=t ^ k) for k in shares]
    spread, returned, dot_returned = {}, {}, {}
    for copy in grad_copies:
        copy.wait()

    def spread_grads(m):
        half = scaled_all.at[m * slots : (m + 1) * slots, own_share]
        spread[m] = [wire.send(half, half, tp=t ^ k) for k in shares]

    for m in order[1:]:
        spread_grads(m)
    for copy in out_copies:
        copy.wait()
    for copy in arrivals:
        copy.wait()
    middle = hidden_ref[...].astype(F32) + mm(mixed[...], out_all[...], NT)
    middle_ref[...] = middle
    scale = lax.rsqrt(jnp.mean(middle * middle, axis=-1, keepdims=True) + NORM_EPS)
    normed = (middle * scale * gains_ref[1:2, :]).astype(BF16)
    far = {}

    def block(m):
        return slice(m * slots, (m + 1) * slots)

    for m in order[1:] + [0]:
        picked = mm(picker_rows_ref[block(m), :], normed).astype(BF16)
        if m:
            send_rows[m - 1] = picked
            far[m] = wire.send(
                send_rows.at[m - 1, :, own_share], rows_all.at[block(m), own_share], dp=d ^ m
            )
        else:
            rows_all[block(0), :] = picked
    lane = lax.broadcasted_iota(jnp.int32, (tokens, LANES), 1)

    def router_probs(values):
        logits = mm(values, lanes_ref[...])
        where = lax.broadcasted_iota(jnp.int32, logits.shape, 1)
        logits = jnp.where(where < experts, logits, NEG_FILL)
        powers = jnp.exp(logits - jnp.max(logits, axis=1, keepdims=True))
        return where, powers / jnp.sum(powers, axis=1, keepdims=True)

    probs[...] = router_probs(normed)[1]
    normed_flip[...] = normed.T
    for copy in weight_copies:
        copy.wait()
    downs[2].wait()
    downs[3] = wire.send(down_parts[2], down_parts[3], ctx=c ^ 1)
    downs[1].wait()
    downs[3].wait()
    columns = [pl.ds(pl.multiple_of((c ^ j) * depth, depth), depth) for j in range(ctx_count)]

    def forward(m):
        far[m].wait()
        half = rows_all.at[block(m), own_share]
        spread[m] += [wire.send(half, half, tp=t ^ k) for k in shares]

    def experts_on(m, hook):
        here = block(m)
        where, chance = router_probs(rows_all[here, :])
        gate = jnp.sum(jnp.where(where == d, chance, 0.0), axis=1, keepdims=True)
        rows = jnp.concatenate([rows_all[here, part] for part in columns], axis=1)
        grad_rows = jnp.concatenate([scaled_all[here, part] for part in columns], axis=1)
        rows_all[here, :] = rows
        scaled_all[here, :] = (gate * grad_rows.astype(F32)).astype(BF16)
        dots = jnp.zeros((slots, LANES), F32)
        for first in range(0, ff, BLOCK):
            part = slice(first, min(ff, first + BLOCK))
            value = mm(rows, in_all[0, :, part])
            up = mm(rows, in_all[1, :, part])
            back = mm(grad_rows, down_all[part, :], NT)
            bent, slope = bent_parts(value)
            act = (bent * up).astype(BF16)
            act_all[here, part] = act
            dots += jnp.sum(act.astype(F32) * back, axis=1, keepdims=True)
            scaled = gate * back
            gate_all[here, part] = (scaled * up * slope).astype(BF16)
            up_all[here, part] = (scaled * bent).astype(BF16)
        if hook is not None:
            hook()
        dot_parts[m] = dots.T[:8]
        dot_returned[m] = [
            wire.send(dot_parts.at[m], dot_in.at[k - 1, m], tp=t ^ k) for k in shares
        ]
        for k in list(shares) + [0]:
            for i in range(share // depth):
                piece = ((t ^ k) * (share // depth) + i) ^ c
                part = pl.ds(pl.multiple_of(piece * depth, depth), depth)
                row = mm(gate_all[here, :], in_all[0, part, :], NT)
                row += mm(up_all[here, :], in_all[1, part, :], NT)
                row_parts[k, m, :, i * depth : (i + 1) * depth] = row.astype(BF16)
            if k:
                returned.setdefault(m, []).append(
                    wire.send(row_parts.at[k, m], row_in.at[k - 1, m], tp=t ^ k)
                )
        for k in range(tp_count):
            for i in range(share // depth):
                piece = ((t ^ k) * (share // depth) + i) ^ c
                part = pl.ds(pl.multiple_of(piece * depth, depth), depth)
                out_parts[k][m, :, i * depth : (i + 1) * depth] = (
                    gate * mm(act_all[here, :], down_all[:, part])
                ).astype(BF16)

    homeward = []

    def send_home(m):
        for copy in dot_returned[m]:
            copy.wait()
        dots = tree_sum([dot_parts[m]] + [dot_in[k - 1, m] for k in shares])
        total = row_parts[0, m].astype(F32)
        for k, copy in zip(shares, returned[m]):
            copy.wait()
            total = total + row_in[k - 1, m].astype(F32)
        if m:
            dot_home[m] = dots
            row_parts[0, m] = total.astype(BF16)
            homeward.append(wire.send(dot_home.at[m], dot_back.at[m], dp=d ^ m))
            homeward.append(wire.send(row_parts.at[0, m], row_back.at[block(m)], dp=d ^ m))
        else:
            dot_back[0] = dots
            row_back[block(0), :] = total.astype(BF16)

    for i, m in enumerate(order):
        for copy in spread.get(m, []):
            copy.wait()
            copy.sent()
        hook = functools.partial(forward, order[i + 1]) if i + 1 < len(order) else None
        experts_on(m, hook)
        if i:
            send_home(order[i - 1])

    def in_grads(j):
        part = slice(j * depth, (j + 1) * depth)
        for side, right in enumerate((gate_all, up_all)):
            in_all[side, part, :] = mm(rows_all[:, part], right[...], TN).astype(BF16)

    keeps = []

    def keep(source, target):
        copy = pltpu.make_async_copy(source, target, keep_sems.at[len(keeps)])
        copy.start()
        keeps.append(copy)

    def part_of(j):
        return slice(j * depth, (j + 1) * depth)

    downs[3].sent()
    for first in range(0, ff, BLOCK):
        part = slice(first, min(ff, first + BLOCK))
        down_all[part, :] = mm(act_all[:, part], scaled_all[...], TN).astype(BF16)
    near = [
        wire.send(down_parts[3], down_land_far, ctx=c ^ 1),
        wire.send(down_parts[1], down_core, ctx=c ^ 1),
    ]
    keep(down_parts[0], down_keep)
    send_home(order[-1])
    in_grads(3)
    near.append(wire.send(in_all.at[:, part_of(3), :], in_land_far, ctx=c ^ 1))
    near[0].wait()
    down_all[:, part_of(2)] = (
        down_all[:, part_of(2)].astype(F32) + down_land_far[...].astype(F32)
    ).astype(BF16)
    near.append(wire.send(down_parts[2], down_far, ctx=c ^ 2))
    in_grads(1)
    near.append(wire.send(in_all.at[:, part_of(1), :], in_core, ctx=c ^ 1))
    in_grads(2)
    near[2].wait()
    for side in range(2):
        in_all[side, part_of(2), :] = (
            in_all[side, part_of(2), :].astype(F32) + in_land_far[side].astype(F32)
        ).astype(BF16)
    keep(in_all.at[:, part_of(2), :], in_sum)
    in_grads(0)
    keep(in_all.at[:, part_of(0), :], in_keep)

    for copy in homeward:
        copy.wait()
    result = mm(picker_ref[...], row_back[...])
    prob_grad = jnp.zeros((tokens, LANES), F32)
    for m in range(dp_count):
        high = dot_back[m].astype(BF16)
        rest = dot_back[m] - high.astype(F32)
        middle_part = rest.astype(BF16)
        tiny = (rest - middle_part.astype(F32)).astype(BF16)
        total = mm(picker_ref[:, block(m)], high, NT)
        total += mm(picker_ref[:, block(m)], middle_part, NT)
        total += mm(picker_ref[:, block(m)], tiny, NT)
        prob_grad = jnp.where(lane == (d ^ m), total[:, 0:1], prob_grad)
    chance = probs[...]
    logit = chance * (prob_grad - jnp.sum(chance * prob_grad, axis=1, keepdims=True))
    more = lax.dot_general(
        logit, lanes_ref[own_share, :].astype(F32), NT, precision=lax.Precision.HIGHEST,
        preferred_element_type=F32,
    )
    whole[:, own_share] = (result + more).astype(BF16)
    arrivals = [wire.send(whole.at[:, own_share], whole.at[:, own_share], tp=t ^ k) for k in shares]
    logit_high = logit.astype(BF16)
    logit_rest = logit - logit_high.astype(F32)
    logit_low = logit_rest.astype(BF16)
    logit_tiny = (logit_rest - logit_low.astype(F32)).astype(BF16)
    router_grad = mm(normed_flip[...], logit_high)
    router_grad += mm(normed_flip[...], logit_low)
    router_grad += mm(normed_flip[...], logit_tiny)
    router_grad_ref[...] = router_grad
    for copy in arrivals:
        copy.wait()
    middle = middle_ref[...]
    gradient = whole[...].astype(F32)
    scale = lax.rsqrt(jnp.mean(middle * middle, axis=-1, keepdims=True) + NORM_EPS)
    weighted = gains_ref[1:2, :] * gradient
    inner = jnp.mean(middle * weighted, axis=-1, keepdims=True)
    gain_ref[...] = fold_sum(gradient * middle * scale)
    total = out_grad_ref[...].astype(F32) + (
        scale * weighted - middle * (scale * scale * scale) * inner
    )
    grad_ref[...] = total
    low_ref[...] = total.astype(BF16)
    attended_grad_ref[...] = mm(low_ref[...], out_all[:, own_lanes]).astype(BF16)
    for copy in keeps:
        copy.wait()
    for copy in near:
        copy.wait()
    wire.finish()


def expert_step(
    firsts, attended, hidden, out_grad, gains, lanes, picker_flip, picker_rows, out, grads_own,
    grads, expert, expert_land, down, experts,
):
    dp_count, ctx_count, tp_count = (lax.axis_size(a) for a in ("dp", "ctx", "tp"))
    tokens, width = attended.shape[0], firsts[0].shape[1] + attended.shape[1]
    slots = grads_own.shape[0]
    share = D // tp_count
    depth, ff = expert.shape[1], expert.shape[2]
    all_slots = dp_count * slots
    others = tp_count - 1
    copies = others * (2 + 4 * dp_count) + 3 * dp_count + 8
    vmem = pl.BlockSpec(memory_space=pltpu.VMEM)
    hbm = pl.BlockSpec(memory_space=pl.ANY)
    shape = jax.ShapeDtypeStruct
    return pl.pallas_call(
        functools.partial(expert_kernel, experts, dp_count, ctx_count, tp_count),
        in_specs=[vmem] * (7 + tp_count) + [hbm] * (4 + dp_count),
        out_specs=[vmem] * (7 + tp_count) + [hbm] * 6,
        out_shape=[
            shape((tokens, D), F32),
            shape((D, LANES), F32),
            shape((tokens, D), F32),
            shape((tokens, D), BF16),
            shape((tokens, width), BF16),
            shape((8, D), F32),
        ]
        + [shape((dp_count, slots, share), BF16)] * tp_count
        + [shape((tokens, width), BF16)]
        + [shape((2, depth, ff), BF16)] * 3
        + [shape((ff, depth), BF16)] * 3,
        scratch_shapes=[
            pltpu.VMEM((tokens, tp_count * width), BF16),
            pltpu.VMEM((D, tp_count * width), BF16),
            pltpu.VMEM((2, D, ff), BF16),
            pltpu.VMEM((ff, D), BF16),
            pltpu.VMEM((all_slots, D), BF16),
            pltpu.VMEM((all_slots, D), BF16),
            pltpu.VMEM((all_slots, ff), BF16),
            pltpu.VMEM((all_slots, ff), BF16),
            pltpu.VMEM((all_slots, ff), BF16),
            pltpu.VMEM((dp_count - 1, slots, D), BF16),
            pltpu.VMEM((tp_count, dp_count, slots, share), BF16),
            pltpu.VMEM((others, dp_count, slots, share), BF16),
            pltpu.VMEM((all_slots, share), BF16),
            pltpu.VMEM((dp_count, 8, slots), F32),
            pltpu.VMEM((others, dp_count, 8, slots), F32),
            pltpu.VMEM((dp_count, 8, slots), F32),
            pltpu.VMEM((dp_count, 8, slots), F32),
            pltpu.VMEM((tokens, LANES), F32),
            pltpu.VMEM((tokens, D), BF16),
            pltpu.VMEM((D, tokens), BF16),
            pltpu.VMEM((2, depth, ff), BF16),
            pltpu.VMEM((ff, depth), BF16),
            pltpu.SemaphoreType.DMA((copies,)),
            pltpu.SemaphoreType.DMA((copies,)),
            pltpu.SemaphoreType.DMA((2 + ctx_count + dp_count,)),
            pltpu.SemaphoreType.DMA((3,)),
        ],
        compiler_params=pltpu.CompilerParams(
            vmem_limit_bytes=VMEM_CAP, collective_id=3, has_side_effects=True
        ),
        cost_estimate=cost(120),
        name="expert_step",
    )(
        attended, hidden, out_grad, gains, lanes, picker_flip, picker_rows, *firsts, out,
        grads_own, *grads, expert, expert_land, down,
    )


def final_kernel(
    experts, dp_count, ctx_count, tp_count,
    query_grad_ref, key_ref, value_ref, normed_ref, weight_ref, low_ref, attended_ref,
    router_grad_ref, hidden_ref, gains_ref, gain_two_ref, middle_grad_ref, middle_ref,
    picker_ref, bias_ref, *refs,
):
    outs, refs = refs[:tp_count], refs[tp_count:]
    (input_grad_ref, output_ref, bias_out_ref, first_ref, second_ref, tail_ref, out_sum, out_back,
     mixed, bias_send, bias_in,
    key_in, send_far, far_in, first_all, second_all, first_core, second_core, first_sum,
    second_sum, first_dp, second_dp, first_x, second_x, rows_all, token_grad, token_in,
    gain_send, gain_in, sends, receives) = refs
    d, c, t = lax.axis_index("dp"), lax.axis_index("ctx"), lax.axis_index("tp")
    tokens, width = query_grad_ref.shape
    dp_bits = bits_down(dp_count)[::-1]
    far_bits = bits_down(ctx_count)[:-1][::-1]
    far = list(range(0, ctx_count, 2))
    greet(
        [{"ctx": c ^ bit} for bit in bits_down(ctx_count)]
        + [{"dp": d ^ m} for m in range(1, dp_count)]
        + [{"tp": t ^ k} for k in range(1, tp_count)]
    )
    wire = Wire(sends, receives)

    bias_steps = [{"ctx": c ^ bit} for bit in bits_down(ctx_count)[::-1]]
    bias_steps += [{"dp": d ^ bit} for bit in dp_bits]
    bias_total, bias_copies = [bias_ref[...]], []

    def bias_begin():
        level = len(bias_copies)
        bias_send[level] = bias_total[-1]
        bias_copies.append(
            wire.send(bias_send.at[level], bias_in.at[level], **bias_steps[level])
        )

    def bias_end():
        level = len(bias_copies) - 1
        bias_copies[level].wait()
        bias_total.append(bias_total[-1] + bias_in[level])

    bias_begin()

    slots, share = out_sum.shape[1], out_sum.shape[2]
    own_share = pl.ds(pl.multiple_of(t * share, share), share)
    out_home = []
    for m in list(range(2, dp_count)) + [1, 0]:
        total = tree_sum([out[m].astype(F32) for out in outs]).astype(BF16)
        if m:
            out_sum[m - 1] = total
            out_home.append(
                wire.send(
                    out_sum.at[m - 1], out_back.at[m * slots : (m + 1) * slots], dp=d ^ m
                )
            )
        else:
            out_back[:slots, :] = total

    near = []
    for k in far[::-1]:
        rows = slice((k + 1) * tokens, (k + 2) * tokens)
        for side, ref in enumerate((key_ref, value_ref)):
            near.append(wire.send(ref.at[rows], key_in.at[side, k // 2], ctx=c ^ 1))

    def split(values):
        return values.astype(BF16).reshape(dp_count, ctx_count, -1, values.shape[1])

    def cross(whole, landed):
        return [wire.send(whole.at[:, c ^ (k + 1)], landed.at[k // 2], ctx=c ^ 1) for k in far]

    def add_core(whole, landed, total, copies):
        for k, copy in zip(far, copies):
            copy.wait()
            own = whole[:, pl.ds(c ^ k, 1)][:, 0]
            total[k // 2] = (own.astype(F32) + landed[k // 2].astype(F32)).astype(BF16)

    def dp_send(total, landed, level, sides):
        copies, bit = [], dp_bits[level]
        for m in range(bit, dp_count, 2 * bit):
            for k in sides:
                spot = landed.at[level, k, d ^ m]
                copies.append((m ^ bit, k, wire.send(total.at[k, d ^ m], spot, dp=d ^ bit)))
        return copies

    def dp_add(total, landed, level, copies):
        for m, k, copy in copies:
            copy.wait()
            own = total[k, pl.ds(d ^ m, 1)][0]
            other = landed[level, k, pl.ds(d ^ m, 1)][0]
            total[k, pl.ds(d ^ m, 1)] = (own.astype(F32) + other.astype(F32)).astype(BF16)[None]

    for copy in near:
        copy.wait()
    for k in far[::-1]:
        rows = slice(k * tokens, (k + 1) * tokens)
        for side, ref in enumerate((key_ref, value_ref)):
            send_far[side, k // 2] = (
                ref[rows, :].astype(F32) + key_in[side, k // 2].astype(F32)
            ).astype(BF16)
    assert len(far_bits) == 1
    far_copies = [
        wire.send(send_far.at[side, 1], far_in.at[side], ctx=c ^ 2) for side in range(2)
    ]

    first_all[:, :, :, :width] = split(mm(normed_ref[...], query_grad_ref[...]))
    first_all[:, :, :, width:] = split(mm(low_ref[...], attended_ref[...], TN))
    first_crossed = cross(first_all, first_core)
    bias_end()
    bias_begin()
    token_grad[...] = mm(query_grad_ref[...], weight_ref[:, :width], NT)
    add_core(first_all, first_core, first_sum, first_crossed)
    bias_end()
    bias_begin()
    first_moving = dp_send(first_sum, first_dp, 0, range(len(far)))
    rows_all[:, :width] = query_grad_ref[...]

    for side in range(2):
        far_copies[side].wait()
        rows_all[:, (side + 1) * width : (side + 2) * width] = (
            send_far[side, 0].astype(F32) + far_in[side].astype(F32)
        ).astype(BF16)
    part = token_grad[...] + mm(rows_all[:, width:], weight_ref[:, width:], NT)
    part_low = part.astype(BF16)
    inputs = hidden_ref[...].astype(F32)
    scale = lax.rsqrt(jnp.mean(inputs * inputs, axis=-1, keepdims=True) + NORM_EPS)
    gain_send[0] = fold_sum(part_low.astype(F32) * inputs * scale)
    token_in[0] = part_low
    gain_total = gain_send[0]
    gain_copies, token_copies = [], []
    tp_bits = bits_down(tp_count)[::-1]
    gain_copies.append(wire.send(gain_send.at[0], gain_in.at[0], tp=t ^ tp_bits[0]))
    token_copies.append(wire.send(token_in.at[0], token_in.at[1], tp=t ^ tp_bits[0]))
    second_all[:, :, :, : 2 * width] = split(mm(normed_ref[...], rows_all[:, width:]))
    for level, bit in enumerate(tp_bits):
        if level:
            gain_send[level] = gain_total
            gain_copies.append(wire.send(gain_send.at[level], gain_in.at[level], tp=t ^ bit))
        gain_copies[level].wait()
        gain_total = gain_total + gain_in[level]
    gain_one = jnp.sum(gain_total, axis=0, keepdims=True)
    gain_two = jnp.sum(gain_two_ref[...], axis=0, keepdims=True)
    row = lax.broadcasted_iota(jnp.int32, (LANES, D), 0)
    gain_rows = jnp.where(row == experts, gain_one, jnp.where(row == experts + 1, gain_two, 0.0))
    second_all[:, :, :, 2 * width :] = split(router_grad_ref[...] + gain_rows.T)
    second_crossed = cross(second_all, second_core)

    add_core(second_all, second_core, second_sum, second_crossed)
    second_far = wire.send(second_sum.at[1], second_x, ctx=c ^ 2)
    for copy in out_home:
        copy.wait()
    mixed[:, own_share] = mm(picker_ref[...], out_back[...]).astype(BF16)
    mixed_part = mixed.at[:, own_share]
    mixed_copies = [wire.send(mixed_part, mixed_part, tp=t ^ k) for k in range(1, tp_count)]
    first_far, second_moving = None, None
    for level in range(len(dp_bits)):
        dp_add(first_sum, first_dp, level, first_moving)
        bias_end()
        if level + 1 < len(dp_bits):
            bias_begin()
            first_moving = dp_send(first_sum, first_dp, level + 1, range(len(far)))
        else:
            first_far = wire.send(first_sum.at[1, d], first_x, ctx=c ^ 2)
        if level == 0:
            second_far.wait()
            second_sum[0] = (second_sum[0].astype(F32) + second_x[...].astype(F32)).astype(BF16)
        else:
            dp_add(second_sum, second_dp, level - 1, second_moving)
        second_moving = dp_send(second_sum, second_dp, level, [0])
    total = part_low.astype(F32)
    for level, bit in enumerate(tp_bits):
        if level:
            token_in[2 * level] = total.astype(BF16)
            total = token_in[2 * level].astype(F32)
            token_copies.append(
                wire.send(token_in.at[2 * level], token_in.at[2 * level + 1], tp=t ^ bit)
            )
        token_copies[level].wait()
        total = total + token_in[2 * level + 1].astype(F32)
    weighted = gains_ref[0:1, :] * total
    inner = jnp.mean(inputs * weighted, axis=-1, keepdims=True)
    input_grad_ref[...] = (
        middle_grad_ref[...] + scale * weighted - inputs * (scale * scale * scale) * inner
    )
    for copy in mixed_copies:
        copy.wait()
    output_ref[...] = middle_ref[...] + mixed[...].astype(F32)
    bias_out_ref[...] = bias_total[-1]
    first_far.wait()
    first_ref[...] = first_sum[0, pl.ds(d, 1)][0].astype(F32) + first_x[...].astype(F32)
    dp_add(second_sum, second_dp, len(dp_bits) - 1, second_moving)
    result = second_sum[0, pl.ds(d, 1)][0].astype(F32)
    second_ref[...] = result[:, : 2 * width]
    rest = jnp.zeros((LANES - result.shape[0], LANES), F32)
    tail_ref[...] = jnp.concatenate([result[:, 2 * width :], rest], axis=0).T
    wire.finish()


def final_step(
    query_grad, key_part, value_part, normed, weight, low, attended, router_grad, hidden,
    gains, gain_two, middle_grad, middle, picker, bias, outs, experts,
):
    tokens, width = query_grad.shape
    slots, share = outs[0].shape[1:]
    dp_count, ctx_count, tp_count = (lax.axis_size(a) for a in ("dp", "ctx", "tp"))
    rows = D // (dp_count * ctx_count)
    half = ctx_count // 2
    levels = len(bits_down(dp_count))
    tp_levels = len(bits_down(tp_count))
    one, two = 2 * width, 2 * width + LANES
    copies = 6 * half + 8 + 3 * tp_count + (half + 2) * dp_count + 2 * ctx_count
    vmem = pl.BlockSpec(memory_space=pltpu.VMEM)
    return pl.pallas_call(
        functools.partial(final_kernel, experts, dp_count, ctx_count, tp_count),
        in_specs=[vmem] * (15 + tp_count),
        out_specs=[vmem] * 6,
        out_shape=[
            jax.ShapeDtypeStruct((tokens, D), F32),
            jax.ShapeDtypeStruct((tokens, D), F32),
            jax.ShapeDtypeStruct(bias.shape, F32),
            jax.ShapeDtypeStruct((rows, one), F32),
            jax.ShapeDtypeStruct((rows, 2 * width), F32),
            jax.ShapeDtypeStruct((LANES, LANES), F32),
        ],
        scratch_shapes=[
            pltpu.VMEM((dp_count - 1, slots, share), BF16),
            pltpu.VMEM((dp_count * slots, share), BF16),
            pltpu.VMEM((tokens, D), BF16),
            pltpu.VMEM((levels + ctx_count.bit_length() - 1,) + bias.shape, F32),
            pltpu.VMEM((levels + ctx_count.bit_length() - 1,) + bias.shape, F32),
            pltpu.VMEM((2, half, tokens, width), BF16),
            pltpu.VMEM((2, half, tokens, width), BF16),
            pltpu.VMEM((2, tokens, width), BF16),
            pltpu.VMEM((dp_count, ctx_count, rows, one), BF16),
            pltpu.VMEM((dp_count, ctx_count, rows, two), BF16),
            pltpu.VMEM((half, dp_count, rows, one), BF16),
            pltpu.VMEM((half, dp_count, rows, two), BF16),
            pltpu.VMEM((half, dp_count, rows, one), BF16),
            pltpu.VMEM((half, dp_count, rows, two), BF16),
            pltpu.VMEM((levels, half, dp_count, rows, one), BF16),
            pltpu.VMEM((levels, 1, dp_count, rows, two), BF16),
            pltpu.VMEM((rows, one), BF16),
            pltpu.VMEM((dp_count, rows, two), BF16),
            pltpu.VMEM((tokens, 3 * width), BF16),
            pltpu.VMEM((tokens, D), F32),
            pltpu.VMEM((2 * tp_levels, tokens, D), BF16),
            pltpu.VMEM((tp_levels, 8, D), F32),
            pltpu.VMEM((tp_levels, 8, D), F32),
            pltpu.SemaphoreType.DMA((copies,)),
            pltpu.SemaphoreType.DMA((copies,)),
        ],
        compiler_params=pltpu.CompilerParams(
            vmem_limit_bytes=VMEM_CAP, collective_id=2, has_side_effects=True
        ),
        cost_estimate=cost(87),
        name="final_step",
    )(
        query_grad, key_part, value_part, normed, weight, low, attended, router_grad,
        hidden, gains, gain_two, middle_grad, middle, picker, bias, *outs,
    )


def adam_kernel(*refs):
    weight, first, second = refs[:3]
    parts, outs = refs[3:-4], refs[-4:]
    gradient = parts[0][...].astype(F32) + parts[1][...].astype(F32) + parts[2][...].astype(F32)
    first_new = BETA_ONE * first[...] + (1.0 - BETA_ONE) * gradient
    second_new = BETA_TWO * second[...] + (1.0 - BETA_TWO) * gradient * gradient
    outs[0][...] = gradient
    outs[1][...] = first_new
    outs[2][...] = second_new
    outs[3][...] = -MAIN_RATE * (
        first_new * (1.0 / FIX_ONE) / (jnp.sqrt(second_new * (1.0 / FIX_TWO)) + ADAM_EPS)
        + WEIGHT_DECAY * weight[...].astype(F32)
    )


def adam(weight, first, second, kept, arrived, far):
    count, rows, columns = weight.shape
    step = max(size for size in range(16, rows + 1, 16) if rows % size == 0 and size * columns <= 1 << 17)
    plain = pl.BlockSpec((1, step, columns), lambda i, j: (i, j, 0))
    shape = jax.ShapeDtypeStruct(weight.shape, F32)
    return pl.pallas_call(
        adam_kernel,
        grid=(count, rows // step),
        in_specs=[plain] * 6,
        out_specs=[plain] * 4,
        out_shape=[shape] * 4,
        compiler_params=pltpu.CompilerParams(vmem_limit_bytes=VMEM_CAP),
        cost_estimate=cost(5),
        name="adam",
    )(weight, first, second, kept, arrived, far)


def small_adam_kernel(experts, pairs, *refs):
    first_ref, second_ref, tail_ref, bias_ref = refs[:4]
    inputs, outs = refs[4:19], refs[19:]

    def step(k, gradient, part, rate):
        weight, first, second = (ref[part].astype(F32) for ref in inputs[3 * k : 3 * k + 3])
        first_new = BETA_ONE * first + (1.0 - BETA_ONE) * gradient
        second_new = BETA_TWO * second + (1.0 - BETA_TWO) * gradient * gradient
        update = -rate * (
            first_new * (1.0 / FIX_ONE) / (jnp.sqrt(second_new * (1.0 / FIX_TWO)) + ADAM_EPS)
            + WEIGHT_DECAY * weight
        )
        for out, values in zip(
            outs[4 * k : 4 * k + 4], (gradient, first_new, second_new, update)
        ):
            out[part] = values

    rows, width = inputs[3].shape
    whole = slice(None)
    step(0, first_ref[:, :width], 0, MAIN_RATE)
    step(0, second_ref[:, :width], 1, MAIN_RATE)
    step(0, second_ref[:, width:], 2, MAIN_RATE)
    step(1, first_ref[:, width:], whole, MAIN_RATE)
    step(2, tail_ref[:experts, :rows], whole, MAIN_RATE)
    step(3, tail_ref[experts : experts + 2, :rows], whole, MAIN_RATE)
    bias = jnp.concatenate([bias_ref[p, :2] for p in range(pairs)], axis=0)
    step(4, bias, whole, BIAS_RATE)


def small_adam(first_total, second_total, tail_total, bias_total, triples, experts):
    flat = [array for triple in triples for array in triple]
    vmem = pl.BlockSpec(memory_space=pltpu.VMEM)
    results = pl.pallas_call(
        functools.partial(small_adam_kernel, experts, bias_total.shape[0]),
        in_specs=[vmem] * (4 + len(flat)),
        out_specs=[vmem] * (4 * len(triples)),
        out_shape=[
            jax.ShapeDtypeStruct(triple[0].shape, F32) for triple in triples for _ in range(4)
        ],
        compiler_params=pltpu.CompilerParams(vmem_limit_bytes=VMEM_CAP),
        cost_estimate=cost(2),
        name="small_adam",
    )(first_total, second_total, tail_total, bias_total, *flat)
    return [results[4 * k : 4 * k + 4] for k in range(len(triples))]


def shards(
    hidden_in,
    out_grad,
    segments,
    routes,
    bucket_table,
    qkv_weight,
    out_weight,
    router,
    norm_gains,
    position_bias,
    expert_in,
    expert_down,
    qkv_first,
    qkv_second,
    out_first,
    out_second,
    router_first,
    router_second,
    gains_first,
    gains_second,
    bias_first,
    bias_second,
    in_first,
    in_second,
    down_first,
    down_second,
):
    tokens = hidden_in.shape[0]
    dp_count, ctx_count, tp_count = (lax.axis_size(a) for a in ("dp", "ctx", "tp"))
    dp_place, ctx_place, tp_place = (lax.axis_index(a) for a in ("dp", "ctx", "tp"))
    length = tokens * ctx_count
    heads_here = position_bias.shape[0]
    width_here = heads_here * HEAD_DIM
    pairs = heads_here // 2
    expert_count = router.shape[1]
    top_count = routes.shape[1]
    own_rows = router.shape[0]

    capacity = max(2, min(tokens, 5 * top_count * tokens // (4 * expert_count)))
    window_width = tokens + length
    table = jnp.pad(bucket_table[::-1], (0, 1), constant_values=BUCKETS)
    table = lax.dynamic_slice(table, (ctx_place * tokens,), (window_width,))
    table = jnp.broadcast_to(table[None], (8, window_width))
    qkv_view = [array.transpose(1, 0, 2) for array in (qkv_weight, qkv_first, qkv_second)]
    out_view = [array.T for array in (out_weight, out_first, out_second)]
    router_view = [array.T for array in (router, router_first, router_second)]
    (queries, key_values, normed_flip, qkv_flat, out_own, lanes, gains, info, doc_row, doc_col,
     picker_flip, picker_rows, grads_own, grads_half, early_land, expert_land) = start(
        qkv_view[0], out_view[0], router_view[0], norm_gains, hidden_in, segments, routes.T,
        out_grad, expert_in[0], capacity,
    )
    early = early_blocks(dp_count)
    arrived = [
        early_land[early.index(m)] if m in early else swap(grads_half[m - 1], "dp", m)
        for m in range(1, dp_count)
    ]
    half = pairs // 2
    attended_first, totals = attention(
        info, queries, key_values, position_bias, table, doc_row, doc_col, 0, half, ()
    )
    first_sides = gather_xor(attended_first, "tp")
    attended_second, totals = attention(
        info, queries, key_values, position_bias, table, doc_row, doc_col, half, pairs - half,
        (totals,),
    )
    results = expert_step(
        first_sides, attended_second, hidden_in, out_grad, gains, lanes, picker_flip, picker_rows,
        out_own, grads_own, arrived, expert_in[0], expert_land, expert_down[0], expert_count,
    )
    middle, router_grad, middle_grad, middle_low, attended_grad, gain_two_grad = results[:6]
    out_parts, results = results[6 : 6 + tp_count], results[6 + tp_count :]
    attended, in_keep, in_core, in_sum, down_keep, down_core, down_far = results

    in_far = swap(in_sum, "ctx", 2)
    out_far = [swap(out_parts[k], "tp", k) for k in range(1, tp_count)]
    query_grad, key_part, value_part, bias_part = attention_back(
        info, queries, key_values, attended_grad, totals, position_bias, table, doc_row, doc_col
    )
    query_grad, in_far, out_far = lax.optimization_barrier((query_grad, in_far, out_far))
    input_grad, output, bias_total, first_total, second_total, tail_total = final_step(
        query_grad, key_part, value_part, normed_flip, qkv_flat, middle_low, attended,
        router_grad, hidden_in, gains, gain_two_grad, middle_grad, middle, picker_flip, bias_part,
        [out_parts[0]] + out_far, expert_count,
    )
    qkv_all, out_new, router_new, gains_new, bias_new = small_adam(
        first_total, second_total, tail_total, bias_total,
        [
            qkv_view,
            out_view,
            router_view,
            (norm_gains, gains_first, gains_second),
            (position_bias, bias_first, bias_second),
        ],
        expert_count,
    )
    in_new = [
        values[None]
        for values in adam(
            expert_in[0], in_first[0], in_second[0], in_keep, in_core, in_far
        )
    ]
    down_new = adam(
        expert_down, down_first, down_second, down_keep[None], down_core[None], down_far[None]
    )
    return (
        output,
        input_grad,
        *[array.transpose(1, 0, 2) for array in qkv_all],
        *[array.T for array in out_new],
        *[array.T for array in router_new],
        *gains_new,
        *bias_new,
        *in_new,
        *down_new,
    )


def solution(mesh):
    token_rows = P(("dp", "ctx"), None)
    qkv = P(("dp", "ctx"), None, "tp")
    out = P("tp", ("dp", "ctx"))
    gains = P(None, ("dp", "ctx"))
    bias = P("tp", None)
    expert_in = P("dp", None, "ctx", "tp")
    expert_down = P("dp", "tp", "ctx")
    placed = (
        token_rows, token_rows, P("dp", "ctx"), token_rows, P(),
        qkv, out, token_rows, gains, bias, expert_in, expert_down,
        qkv, qkv, out, out, token_rows, token_rows, gains, gains, bias, bias,
        expert_in, expert_in, expert_down, expert_down,
    )
    return jax.shard_map(
        shards,
        mesh=mesh,
        in_specs=placed,
        out_specs=(token_rows, token_rows)
        + (qkv,) * 4
        + (out,) * 4
        + (token_rows,) * 4
        + (gains,) * 4
        + (bias,) * 4
        + (expert_in,) * 4
        + (expert_down,) * 4,
        check_vma=False,
    )
```

```python
import functools

import jax
import jax.numpy as jnp
from jax import lax
from jax.experimental import pallas as pl
from jax.experimental.pallas import tpu as pltpu
from jax.sharding import PartitionSpec as P

D = 1024
HEAD_DIM = 64
BUCKETS = 32

NORM_EPS = 1e-06
NEG_FILL = -1e30
BETA_ONE = 0.9
BETA_TWO = 0.95
FIX_ONE = 1.0 - 0.9**10
FIX_TWO = 1.0 - 0.95**10
ADAM_EPS = 1e-08
WEIGHT_DECAY = 0.1
MAIN_RATE = 0.02
BIAS_RATE = 0.2

F32 = jnp.float32
BF16 = jnp.bfloat16
LANES = 128
BLOCK = 256
VMEM_CAP = 60 * 1024 * 1024
GELU_K = 0.7978845608028654
GELU_C = 0.044715


def tree_sum(values):
    while len(values) > 1:
        values = [values[k] + values[k + 1] for k in range(0, len(values), 2)]
    return values[0]


def rms_scale(values):
    return lax.rsqrt(jnp.mean(values * values, axis=-1, keepdims=True) + NORM_EPS)


def norm_back(values, scale_here, gain_here, gradient):
    weighted = gain_here * gradient
    row_inner = jnp.mean(values * weighted, axis=-1, keepdims=True)
    input_part = scale_here * weighted - values * scale_here**3 * row_inner
    return (input_part, jnp.sum(gradient * values * scale_here, axis=0))


def adamw_step(weight, gradient, first_moment, second_moment, step_rate):
    first_new = BETA_ONE * first_moment + (1.0 - BETA_ONE) * gradient
    second_new = BETA_TWO * second_moment + (1.0 - BETA_TWO) * gradient * gradient
    update = -step_rate * (
        first_new / FIX_ONE / (jnp.sqrt(second_new / FIX_TWO) + ADAM_EPS) + WEIGHT_DECAY * weight
    )
    return (first_new, second_new, update)


def cost(micros):
    return pl.CostEstimate(flops=int(micros * 1.15e9), bytes_accessed=1 << 20, transcendentals=0)


def swap(values, axis, bits):
    count = lax.axis_size(axis)
    return lax.ppermute(values, axis, [(i, i ^ bits) for i in range(count)])


def gather_xor(values, axis):
    pieces = {0: values}
    bit = lax.axis_size(axis) >> 1
    while bit:
        for key in list(pieces):
            pieces[key | bit] = swap(pieces[key], axis, bit)
        bit >>= 1
    return [pieces[m] for m in range(len(pieces))]


def scatter_sum(parts, axis):
    live = dict(enumerate(parts))
    bit = 1
    while bit < lax.axis_size(axis):
        left = {}
        for key in live:
            if key & bit == 0:
                moved = swap(live[key | bit].astype(BF16), axis, bit)
                left[key] = live[key].astype(F32) + moved.astype(F32)
        live = left
        bit <<= 1
    return live[0]


def all_sum(values, axis):
    bit = 1
    while bit < lax.axis_size(axis):
        values = values + swap(values, axis, bit)
        bit <<= 1
    return values


def in_order(pieces, place, dim):
    bit = 1
    while bit < len(pieces):
        odd = (place & bit) > 0
        pieces = [jnp.where(odd, pieces[m ^ bit], pieces[m]) for m in range(len(pieces))]
        bit <<= 1
    return jnp.concatenate(pieces, axis=dim)


MESH = pl.DeviceIdType.MESH


class Wire:
    def __init__(self, sends, receives):
        self.sends, self.receives, self.count, self.copies = sends, receives, 0, []

    def send(self, source, target, **device):
        copy = pltpu.make_async_remote_copy(
            src_ref=source,
            dst_ref=target,
            send_sem=self.sends.at[self.count],
            recv_sem=self.receives.at[self.count],
            device_id=device,
            device_id_type=MESH,
        )
        copy.start()
        self.count += 1
        self.copies.append(Arrival(copy))
        return self.copies[-1]

    def finish(self):
        for copy in self.copies:
            copy.sent()


class Arrival:
    def __init__(self, copy):
        self.copy, self.waited, self.gone = copy, False, False

    def sent(self):
        if not self.gone:
            self.copy.wait_send()
        self.gone = True

    def wait(self):
        if not self.waited:
            self.copy.wait_recv()
        self.waited = True


def greet(partners):
    barrier = pltpu.get_barrier_semaphore()
    for device in partners:
        pl.semaphore_signal(barrier, inc=1, device_id=device, device_id_type=MESH)
    pl.semaphore_wait(barrier, len(partners))


def bits_down(count):
    bits, bit = [], count >> 1
    while bit:
        bits.append(bit)
        bit >>= 1
    return bits


def xor_order(count):
    order = [0]
    for bit in bits_down(count):
        order = order + [k | bit for k in order]
    return order


NT = (((1,), (1,)), ((), ()))
NN = (((1,), (0,)), ((), ()))
TN = (((0,), (0,)), ((), ()))


def mm(left, right, dims=NN):
    return lax.dot_general(left, right, dims, preferred_element_type=F32)


def fold_max(values):
    return jnp.max(values.reshape(values.shape[0] // 8, 8, values.shape[1]), axis=0)


def fold_sum(values):
    return jnp.sum(values.reshape(values.shape[0] // 8, 8, values.shape[1]), axis=0)


def skewed(row):
    width = row.shape[1]
    tall = jnp.broadcast_to(row, (LANES, width))
    return pltpu.roll(tall, width - (LANES - 1), 1, stride=1, stride_axis=0)


def unskew_sum(field):
    half = field.shape[0] // 2
    while half >= 1:
        field = pltpu.roll(field[:half], half, 1) + field[half:]
        half //= 2
    return field


def head_masks(rows):
    lane = lax.broadcasted_iota(jnp.int32, (rows, LANES), 1)
    return [(lane < HEAD_DIM).astype(BF16), (lane >= HEAD_DIM).astype(BF16)]


def score_tile(key_block, query_head, skew_ref, head, first, same):
    scores = mm(key_block, query_head, NT)
    tiles = []
    for s in range(BLOCK // LANES):
        column = pl.multiple_of(first - s * LANES, LANES)
        tiles.append(skew_ref[head, :, pl.ds(column, BLOCK)])
    return jnp.where(same, scores + jnp.concatenate(tiles, axis=0), NEG_FILL)


def bucket_lanes(table_ref):
    row = lax.broadcasted_iota(jnp.int32, (BUCKETS, table_ref.shape[1]), 0)
    return (row == table_ref[0:1, :]).astype(F32)


def spread_bias(bias_ref, table_ref, skew_ref, first=0):
    rows = bias_ref[pl.ds((pl.program_id(0) + first) * 2, 2), :]
    window = jnp.dot(
        jnp.concatenate([rows] * 4, axis=0), bucket_lanes(table_ref),
        precision=lax.Precision.HIGHEST, preferred_element_type=F32,
    )
    for h in range(2):
        skew_ref[h] = skewed(window[h : h + 1, :])


def over_blocks(info_ref, qb, query_blocks, step):
    @pl.loop(0, info_ref[query_blocks + qb, 0])
    def _(i):
        blocks = [info_ref[qb, 2 * i + k] for k in range(2)]
        step(
            [pl.ds(pl.multiple_of(kb * BLOCK, BLOCK), BLOCK) for kb in blocks],
            [info_ref[2 * query_blocks, kb] + qb * BLOCK for kb in blocks],
        )


def attention_kernel(
    first, info_ref, query_ref, key_ref, value_ref, bias_ref, table_ref, doc_row_ref,
    doc_col_ref, *refs,
):
    out_ref, total_ref, skew_ref, flip_ref, score_ref, most_ref, sum_ref, mix_ref = refs[-8:]
    tokens, length = query_ref.shape[0], key_ref.shape[0]
    key_blocks, query_blocks = length // BLOCK, tokens // BLOCK
    masks = head_masks(BLOCK)
    spread_bias(bias_ref, table_ref, skew_ref, first)

    @pl.loop(0, key_blocks)
    def _(kb):
        rows = pl.ds(pl.multiple_of(kb * BLOCK, BLOCK), BLOCK)
        flip_ref[:, rows] = value_ref[rows, :].T

    for qb in range(query_blocks):
        here = slice(qb * BLOCK, (qb + 1) * BLOCK)
        pair = query_ref[here, :] * jnp.asarray(HEAD_DIM**-0.5, BF16)
        query_heads = [pair * mask for mask in masks]
        doc_row = doc_row_ref[0:1, here]
        most_ref[...] = jnp.full_like(most_ref, NEG_FILL)
        sum_ref[...] = jnp.zeros_like(sum_ref)
        mix_ref[...] = jnp.zeros_like(mix_ref)

        def scores(spans, firsts):
            for rows, first_column in zip(spans, firsts):
                column = doc_col_ref[rows, :]
                same = jnp.concatenate([column] * (BLOCK // LANES), axis=1) == doc_row
                for h in range(2):
                    tile = score_tile(
                        key_ref[rows, :], query_heads[h], skew_ref, h, first_column, same
                    )
                    score_ref[h, rows, :] = tile
                    most_ref[h] = jnp.maximum(most_ref[h], fold_max(tile))

        over_blocks(info_ref, qb, query_blocks, scores)
        most = [jnp.max(most_ref[h], axis=0, keepdims=True) for h in range(2)]

        def mixes(spans, firsts):
            for h in range(2):
                heads = slice(h * HEAD_DIM, (h + 1) * HEAD_DIM)
                total, mix = sum_ref[h], mix_ref[h]
                for rows in spans:
                    weights = jnp.exp(score_ref[h, rows, :] - most[h])
                    total += fold_sum(weights)
                    mix += mm(flip_ref[heads, rows], weights.astype(BF16))
                sum_ref[h] = total
                mix_ref[h] = mix

        over_blocks(info_ref, qb, query_blocks, mixes)
        columns = []
        for h in range(2):
            total = jnp.sum(sum_ref[h], axis=0, keepdims=True)
            columns.append(mix_ref[h] / total)
            total_ref[0, h : h + 1, here] = most[h] + jnp.log(total)
        out_ref[here, :] = jnp.concatenate(columns, axis=0).T.astype(BF16)


def attention_back_kernel(
    info_ref, query_ref, key_ref, value_ref, grad_ref, total_ref, bias_ref, table_ref,
    doc_row_ref, doc_col_ref,
    query_grad_ref, key_grad_ref, value_grad_ref, bias_grad_ref,
    skew_ref, field_ref, flip_ref, weight_ref, change_ref, inner_ref, mix_ref, key_sum, value_sum,
):
    tokens, length = query_ref.shape[0], key_ref.shape[0]
    key_blocks, query_blocks = length // BLOCK, tokens // BLOCK
    masks = head_masks(BLOCK)
    spread_bias(bias_ref, table_ref, skew_ref)
    field_ref[...] = jnp.zeros_like(field_ref)
    key_sum[...] = jnp.zeros_like(key_sum)
    value_sum[...] = jnp.zeros_like(value_sum)

    @pl.loop(0, key_blocks)
    def _(kb):
        rows = pl.ds(pl.multiple_of(kb * BLOCK, BLOCK), BLOCK)
        flip_ref[:, rows] = key_ref[rows, :].T

    for qb in range(query_blocks):
        here = slice(qb * BLOCK, (qb + 1) * BLOCK)
        pair = query_ref[here, :] * jnp.asarray(HEAD_DIM**-0.5, BF16)
        query_heads = [pair * mask for mask in masks]
        grad_pair = grad_ref[here, :]
        grad_heads = [grad_pair * mask for mask in masks]
        doc_row = doc_row_ref[0:1, here]
        inner_ref[...] = jnp.zeros_like(inner_ref)
        mix_ref[...] = jnp.zeros_like(mix_ref)
        totals = [total_ref[0, h : h + 1, here] for h in range(2)]

        def changes(spans, firsts):
            for rows, first_column in zip(spans, firsts):
                column = doc_col_ref[rows, :]
                same = jnp.concatenate([column] * (BLOCK // LANES), axis=1) == doc_row
                for h in range(2):
                    tile = score_tile(
                        key_ref[rows, :], query_heads[h], skew_ref, h, first_column, same
                    )
                    weights = jnp.exp(tile - totals[h])
                    change = mm(value_ref[rows, :], grad_heads[h], NT)
                    weight_ref[h, rows, :] = weights
                    change_ref[h, rows, :] = change
                    inner_ref[h] += fold_sum(weights * change)

        over_blocks(info_ref, qb, query_blocks, changes)
        inner = [jnp.sum(inner_ref[h], axis=0, keepdims=True) for h in range(2)]

        def gradients(spans, firsts):
            mixes = [mix_ref[h] for h in range(2)]
            for rows, first_column in zip(spans, firsts):
                key_part = value_part = None
                for h in range(2):
                    weights = weight_ref[h, rows, :]
                    score_grad = weights * (change_ref[h, rows, :] - inner[h])
                    for s in range(BLOCK // LANES):
                        first = pl.multiple_of(first_column - s * LANES, LANES)
                        field_ref[h, :, pl.ds(first, BLOCK)] += score_grad[
                            s * LANES : (s + 1) * LANES
                        ]
                    low = score_grad.astype(BF16)
                    key_here = mm(low, query_heads[h])
                    value_here = mm(weights.astype(BF16), grad_heads[h])
                    key_part = key_here if h == 0 else key_part + key_here
                    value_part = value_here if h == 0 else value_part + value_here
                    heads = slice(h * HEAD_DIM, (h + 1) * HEAD_DIM)
                    mixes[h] += mm(flip_ref[heads, rows], low)
                key_sum[rows, :] += key_part
                value_sum[rows, :] += value_part
            for h in range(2):
                mix_ref[h] = mixes[h]

        over_blocks(info_ref, qb, query_blocks, gradients)
        both = jnp.concatenate([mix_ref[0], mix_ref[1]], axis=0) * HEAD_DIM**-0.5
        query_grad_ref[here, :] = both.T.astype(BF16)

    key_grad_ref[...] = key_sum[...].astype(BF16)
    value_grad_ref[...] = value_sum[...].astype(BF16)
    offsets = jnp.concatenate([unskew_sum(field_ref[h]) for h in range(2)] * 4, axis=0)
    bias_grad_ref[0] = lax.dot_general(
        offsets, bucket_lanes(table_ref), NT, precision=lax.Precision.HIGHEST,
        preferred_element_type=F32,
    )


def attention_specs(tokens, length, pairs, heads, width, first=0):
    smem = pl.BlockSpec(memory_space=pltpu.SMEM)
    return dict(
        info=smem,
        query=pl.BlockSpec((tokens, LANES), lambda i: (0, i + first)),
        key=pl.BlockSpec((length, LANES), lambda i: (0, i + first)),
        value=pl.BlockSpec((length, LANES), lambda i: (0, i + first + pairs)),
        bias=pl.BlockSpec((heads, BUCKETS), lambda i: (0, 0)),
        table=pl.BlockSpec((8, width), lambda i: (0, 0)),
        total=pl.BlockSpec((1, 8, tokens), lambda i: (i + first, 0, 0)),
        bias_grad=pl.BlockSpec((1, 8, BUCKETS), lambda i: (i, 0, 0)),
        doc_row=pl.BlockSpec((8, tokens), lambda i: (0, 0)),
        doc_col=pl.BlockSpec((length, LANES), lambda i: (0, 0)),
    )


def attention(info, queries, key_values, bias, table, doc_row, doc_col, first, count, held):
    tokens, length = queries.shape[0], key_values.shape[0]
    pairs, width = bias.shape[0] // 2, table.shape[1]
    specs = attention_specs(tokens, length, pairs, bias.shape[0], width, first)
    return pl.pallas_call(
        functools.partial(attention_kernel, first),
        grid=(count,),
        in_specs=[
            specs["info"], specs["query"], specs["key"], specs["value"], specs["bias"],
            specs["table"], specs["doc_row"], specs["doc_col"],
        ]
        + [pl.BlockSpec(memory_space=pl.ANY)] * len(held),
        out_specs=[pl.BlockSpec((tokens, LANES), lambda i: (0, i)), specs["total"]],
        out_shape=[
            jax.ShapeDtypeStruct((tokens, count * LANES), BF16),
            jax.ShapeDtypeStruct((pairs, 8, tokens), F32),
        ],
        scratch_shapes=[
            pltpu.VMEM((2, LANES, width), F32),
            pltpu.VMEM((LANES, length), BF16),
            pltpu.VMEM((2, length, BLOCK), F32),
            pltpu.VMEM((2, 8, BLOCK), F32),
            pltpu.VMEM((2, 8, BLOCK), F32),
            pltpu.VMEM((2, HEAD_DIM, BLOCK), F32),
        ],
        input_output_aliases={8: 1} if held else {},
        compiler_params=pltpu.CompilerParams(vmem_limit_bytes=VMEM_CAP),
        cost_estimate=cost(5),
        name="attention_forward",
    )(info, queries, key_values, key_values, bias, table, doc_row, doc_col, *held)


def attention_back(info, queries, key_values, grads, totals, bias, table, doc_row, doc_col):
    tokens, length = queries.shape[0], key_values.shape[0]
    pairs, width = bias.shape[0] // 2, table.shape[1]
    specs = attention_specs(tokens, length, pairs, bias.shape[0], width)
    return pl.pallas_call(
        attention_back_kernel,
        grid=(pairs,),
        in_specs=[
            specs["info"], specs["query"], specs["key"], specs["value"], specs["query"],
            specs["total"], specs["bias"], specs["table"], specs["doc_row"], specs["doc_col"],
        ],
        out_specs=[specs["query"], specs["key"], specs["key"], specs["bias_grad"]],
        out_shape=[
            jax.ShapeDtypeStruct(queries.shape, BF16),
            jax.ShapeDtypeStruct((length, queries.shape[1]), BF16),
            jax.ShapeDtypeStruct((length, queries.shape[1]), BF16),
            jax.ShapeDtypeStruct((pairs, 8, BUCKETS), F32),
        ],
        scratch_shapes=[
            pltpu.VMEM((2, LANES, width), F32),
            pltpu.VMEM((2, LANES, width), F32),
            pltpu.VMEM((LANES, length), BF16),
            pltpu.VMEM((2, length, BLOCK), F32),
            pltpu.VMEM((2, length, BLOCK), F32),
            pltpu.VMEM((2, 8, BLOCK), F32),
            pltpu.VMEM((2, HEAD_DIM, BLOCK), F32),
            pltpu.VMEM((length, LANES), F32),
            pltpu.VMEM((length, LANES), F32),
        ],
        compiler_params=pltpu.CompilerParams(vmem_limit_bytes=VMEM_CAP),
        cost_estimate=cost(40),
        name="attention_backward",
    )(info, queries, key_values, key_values, grads, totals, bias, table, doc_row, doc_col)


def start_kernel(
    experts, dp_count, ctx_count, tp_count, qkv_ref, out_flip_ref, router_ref, gain_pair_ref,
    hidden_ref, segments_ref, routes_ref, out_grad_ref, expert_ref,
    query_ref, pair_ref, normed_flip_ref, weight_out, own_ref, lanes_ref, gains_ref, info_ref,
    row_ref, column_ref, picker_ref, picker_rows_ref, grads_own_ref, grads_ref, early_land,
    expert_land,
    weights, out_all, hidden, docs, docs_ref, flip, sends, receives, out_sem,
):
    d, c, t = lax.axis_index("dp"), lax.axis_index("ctx"), lax.axis_index("tp")
    rows = out_flip_ref.shape[0]
    tokens, width = query_ref.shape
    early = early_blocks(dp_count)
    own_rows = pl.ds(pl.multiple_of((d * ctx_count + c) * rows, rows), rows)
    own_lanes = pl.ds(pl.multiple_of(t * width, width), width)
    for part in range(3):
        weights[own_rows, part * width : (part + 1) * width] = qkv_ref[part]
    out_all[own_rows, own_lanes] = out_flip_ref[...]
    flip[...] = jnp.zeros_like(flip)
    flip[:experts, :rows] = router_ref[...].astype(F32)
    flip[experts : experts + 2, :rows] = gain_pair_ref[...].astype(F32)
    weights[own_rows, 3 * width :] = flip[:, :LANES].T[:rows].astype(BF16)
    docs_ref[...] = jnp.broadcast_to(segments_ref[...], docs_ref.shape)
    row_ref[...] = docs_ref[...]
    greet(
        [{"ctx": c ^ m} for m in range(1, ctx_count)]
        + [{"dp": d ^ m} for m in sorted(set(bits_down(dp_count) + early))]
        + [{"tp": t ^ k} for k in range(1, tp_count)]
    )
    wire = Wire(sends, receives)
    share = grads_ref.shape[2]
    own_share = pl.ds(pl.multiple_of(t * share, share), share)

    def send_shard(m, j, part, lanes=own_lanes, **device):
        index = (d ^ m) * ctx_count + (c ^ j)
        here = pl.ds(pl.multiple_of(index * rows, rows), rows)
        shard = out_all.at[here, lanes] if part else weights.at[here]
        return wire.send(shard, shard, **device)

    docs_sent = [wire.send(docs_ref, docs.at[m], ctx=c ^ m) for m in range(1, ctx_count)]
    sides, sides_far = [0], []
    parts = (0, 1)
    arrivals = {part: [] for part in range(2)}
    hidden_sent, expert_sent = {}, {}
    for bit in bits_down(ctx_count)[:-1]:
        arrivals = {
            k: [send_shard(0, j, part, ctx=c ^ bit) for j in sides]
            for k, part in enumerate(parts)
        }
        assert bit == 2
        half = hidden_ref.at[:, own_share]
        hidden_sent[2] = wire.send(half, hidden.at[2, :, own_share], ctx=c ^ 2)
        for m in [0] + list(expert_sent):
            if m:
                expert_sent[m].wait()
            source = expert_land.at[m - 1] if m else expert_ref
            expert_sent[m | bit] = wire.send(source, expert_land.at[(m | bit) - 1], ctx=c ^ bit)
        for copy in arrivals[0]:
            copy.wait()
        sides_far = sides + [j | bit for j in sides]
        if bit != 2:
            for copy in arrivals[1]:
                copy.wait()
        sides = sides_far
    hidden_sent[1] = wire.send(hidden_ref, hidden.at[1], ctx=c ^ 1)

    order = xor_order(dp_count)
    groups = [{}, {}]
    crossed, beside = [[], []], []

    def onward(k, m):
        for copy in groups[k].get(m, []):
            copy.wait()
        for bit in bits_down(dp_count):
            if m & (2 * bit - 1) == 0:
                groups[k][m | bit] = [send_shard(m, j, parts[k], dp=d ^ bit) for j in sides]
        crossed[k] += [send_shard(m, j, parts[k], ctx=c ^ 1) for j in sides]
        if k:
            for other in range(1, tp_count):
                beside.append(
                    (m, other, [send_shard(m, j, 1, tp=t ^ other) for j in sides])
                )

    onward(0, 0)
    expert_sent[1] = wire.send(expert_ref, expert_land.at[0], ctx=c ^ 1)

    lane = lax.broadcasted_iota(jnp.int32, (tokens, LANES), 1)
    flip[:8, :] = jnp.zeros((8, tokens), F32)
    flip[: routes_ref.shape[0], :] = routes_ref[...].astype(F32)
    routes = flip[...].T
    tops = [routes[:, k : k + 1].astype(jnp.int32) for k in range(routes_ref.shape[0])]
    named = jnp.zeros((tokens, LANES), F32)
    for top in tops:
        named = jnp.where(lane == top, 1.0, named)
    row_index = lax.broadcasted_iota(jnp.int32, (tokens, tokens), 0)
    column_index = lax.broadcasted_iota(jnp.int32, (tokens, tokens), 1)
    before = jnp.where(column_index < row_index, 1.0, 0.0).astype(BF16)
    earlier = mm(before, named.astype(BF16))
    slots = grads_own_ref.shape[0]
    column = lax.broadcasted_iota(jnp.int32, picker_ref.shape, 1)
    picker = jnp.zeros(picker_ref.shape, F32)
    for top in tops:
        place = jnp.sum(jnp.where(lane == top, earlier, 0.0), axis=1, keepdims=True)
        place = place.astype(jnp.int32)
        target = jnp.where(place < slots, (top ^ d) * slots + place, -1)
        picker = jnp.where(column == target, 1.0, picker)
    picker_ref[...] = picker.astype(BF16)
    picker_rows_ref[...] = picker_ref[...].T
    hidden_sent[2].wait()
    half = hidden.at[2, :, own_share]
    spread = [wire.send(half, half, tp=t ^ k) for k in range(1, tp_count)]
    for m in range(dp_count):
        chosen = picker_rows_ref[m * slots : (m + 1) * slots, :]
        if m:
            grads_ref[m - 1] = mm(chosen, out_grad_ref[:, own_share]).astype(BF16)
        else:
            grads_own_ref[...] = mm(chosen, out_grad_ref[...]).astype(BF16)

    key_blocks, query_blocks = tokens // BLOCK, tokens // BLOCK
    where = lax.broadcasted_iota(jnp.int32, info_ref.shape, 1)
    which = lax.broadcasted_iota(jnp.int32, info_ref.shape, 0)
    info = jnp.zeros(info_ref.shape, jnp.int32)
    met = [[] for _ in range(query_blocks)]
    for m in range(ctx_count):
        if m:
            docs_sent[m - 1].wait()
        row = docs[m] if m else docs_ref[...]
        tall = jnp.broadcast_to(row[0:1, :].astype(F32), (LANES, tokens))
        column_ref[m * tokens : (m + 1) * tokens, :] = tall.T.astype(jnp.int32)
        for k in range(key_blocks):
            spot = m * key_blocks + k
            low = row[0:1, k * BLOCK : k * BLOCK + 1]
            high = row[0:1, (k + 1) * BLOCK - 1 : (k + 1) * BLOCK]
            for q in range(query_blocks):
                query_low = docs_ref[0:1, q * BLOCK : q * BLOCK + 1]
                query_high = docs_ref[0:1, (q + 1) * BLOCK - 1 : (q + 1) * BLOCK]
                meets = ((high >= query_low) & (low <= query_high)).astype(jnp.int32)
                met[q].append(meets)
            base = (ctx_count * tokens - LANES) - ((c ^ m) * tokens + k * BLOCK)
            info = jnp.where((where == spot) & (which == 2 * query_blocks), base, info)
    for q in range(query_blocks):
        count = sum(met[q][1:], met[q][0])
        inside, outside = jnp.zeros_like(count), count
        for spot, meets in enumerate(met[q]):
            place = jnp.where(meets > 0, inside, outside)
            info = jnp.where((where == place) & (which == q), spot, info)
            inside, outside = inside + meets, outside + (1 - meets)
        steps = lax.shift_right_logical(count + 1, 1)
        info = jnp.where(which == query_blocks + q, steps, info)
    info_ref[...] = info

    early_copies = []
    for i, m in enumerate(order[1:]):
        onward(0, m)
        if i == 0:
            for copy in arrivals[1]:
                copy.wait()
            onward(1, 0)
    for i, m in enumerate(order[1:]):
        onward(1, m)
        if i == 0:
            early_copies = [
                wire.send(grads_ref.at[n - 1], early_land.at[k], dp=d ^ n)
                for k, n in enumerate(early)
            ]
    for copy in spread:
        copy.wait()
    hidden_sent[3] = wire.send(hidden.at[2], hidden.at[3], ctx=c ^ 1)
    for copy in crossed[0]:
        copy.wait()
    keep = pltpu.make_async_copy(weights.at[:, : 3 * width], weight_out, out_sem.at[0])
    keep.start()
    small = weights[:, 3 * width : 3 * width + LANES].astype(F32)
    lane = lax.broadcasted_iota(jnp.int32, small.shape, 1)
    lanes_ref[...] = jnp.where(lane < experts, small, 0.0).astype(BF16)
    gain_one = jnp.sum(jnp.where(lane == experts, small, 0.0), axis=1, keepdims=True)
    gain_two = jnp.sum(jnp.where(lane == experts + 1, small, 0.0), axis=1, keepdims=True)
    both = jnp.where(lane == 0, gain_one, jnp.where(lane == 1, gain_two, 0.0)).T
    gains_ref[...] = both[:8]
    gain = both[0:1]
    for m in range(ctx_count):
        if m:
            hidden_sent[m].wait()
        values = (hidden[m] if m else hidden_ref[...]).astype(F32)
        scale = lax.rsqrt(jnp.mean(values * values, axis=-1, keepdims=True) + NORM_EPS)
        normed = (values * scale * gain).astype(BF16)
        pair_ref[m * tokens : (m + 1) * tokens, :] = mm(
            normed, weights[:, width : 3 * width]
        ).astype(BF16)
        if m == 0:
            normed_flip_ref[...] = normed.T
            query_ref[...] = mm(normed, weights[:, :width]).astype(BF16)
            for n, other, copies in beside:
                for copy in copies:
                    copy.wait()
                lanes = pl.ds(pl.multiple_of((t ^ other) * width, width), width)
                crossed[1] += [send_shard(n, j, 1, lanes, ctx=c ^ 1) for j in sides]
    for copy in crossed[1]:
        copy.wait()
    keep_own = pltpu.make_async_copy(out_all, own_ref, out_sem.at[1])
    keep_own.start()
    for k in [k for k in expert_sent if k > 1]:
        expert_sent[k].wait()
        expert_sent[k | 1] = wire.send(expert_land.at[k - 1], expert_land.at[k], ctx=c ^ 1)
    for k in range(1, ctx_count):
        expert_sent[k].wait()
    for copy in early_copies:
        copy.wait()
    keep.wait()
    keep_own.wait()
    wire.finish()


def early_blocks(dp_count):
    return list(range(2, dp_count))[:1]


def start(qkv, out_flip, router, gain_pair, hidden, segments, routes, out_grad, expert, slots):
    tokens, (experts, _), width = hidden.shape[0], router.shape, qkv.shape[2]
    columns = 4 * width + LANES
    dp_count, ctx_count, tp_count = (lax.axis_size(a) for a in ("dp", "ctx", "tp"))
    copies = 5 * ctx_count + (2 + tp_count) * dp_count * ctx_count + tp_count + dp_count + 1
    vmem = pl.BlockSpec(memory_space=pltpu.VMEM)
    hbm = pl.BlockSpec(memory_space=pl.ANY)
    shape = jax.ShapeDtypeStruct
    return pl.pallas_call(
        functools.partial(start_kernel, experts, dp_count, ctx_count, tp_count),
        in_specs=[vmem] * 8 + [hbm],
        out_specs=[vmem] * 3 + [hbm] * 2 + [vmem] * 9 + [hbm] * 2,
        out_shape=[
            shape((tokens, width), BF16),
            shape((tokens * ctx_count, 2 * width), BF16),
            shape((D, tokens), BF16),
            shape((D, 3 * width), BF16),
            shape((D, tp_count * width), BF16),
            shape((D, LANES), BF16),
            shape((8, D), F32),
            shape((8, LANES), jnp.int32),
            shape((8, tokens), jnp.int32),
            shape((tokens * ctx_count, LANES), jnp.int32),
            shape((tokens, dp_count * slots), BF16),
            shape((dp_count * slots, tokens), BF16),
            shape((slots, D), BF16),
            shape((dp_count - 1, slots, D // tp_count), BF16),
            shape((len(early_blocks(dp_count)), slots, D // tp_count), BF16),
            shape((ctx_count - 1,) + expert.shape, BF16),
        ],
        scratch_shapes=[
            pltpu.VMEM((D, columns - width), BF16),
            pltpu.VMEM((D, tp_count * width), BF16),
            pltpu.VMEM((ctx_count, tokens, D), BF16),
            pltpu.VMEM((ctx_count, 8, tokens), jnp.int32),
            pltpu.VMEM((8, tokens), jnp.int32),
            pltpu.VMEM((LANES, tokens), F32),
            pltpu.SemaphoreType.DMA((copies,)),
            pltpu.SemaphoreType.DMA((copies,)),
            pltpu.SemaphoreType.DMA((2,)),
        ],
        compiler_params=pltpu.CompilerParams(
            vmem_limit_bytes=VMEM_CAP, collective_id=1, has_side_effects=True
        ),
        cost_estimate=cost(60),
        name="start",
    )(qkv, out_flip, router, gain_pair, hidden, segments, routes, out_grad, expert)


def bent_parts(value):
    square = value * value
    wave = jnp.tanh(GELU_K * value * (1.0 + GELU_C * square))
    half = 0.5 * (1.0 + wave)
    slope = half + 0.5 * value * (1.0 - wave * wave) * (GELU_K * (1.0 + 3.0 * GELU_C * square))
    return value * half, slope


def expert_kernel(
    experts, dp_count, ctx_count, tp_count, attended_ref, gains_ref, lanes_ref, hidden_hbm,
    out_grad_hbm, picker_hbm, picker_rows_hbm, *refs,
):
    d, c, t = lax.axis_index("dp"), lax.axis_index("ctx"), lax.axis_index("tp")
    firsts, refs = refs[:tp_count], refs[tp_count:]
    out_ref, grads_own, refs = refs[0], refs[1], refs[2:]
    grads_land, refs = refs[: dp_count - 1], refs[dp_count - 1 :]
    in_own, in_land, refs = refs[0], refs[1], refs[2:]
    ins = [in_own] + [in_land.at[j] for j in range(ctx_count - 1)]
    down_own, refs = refs[0], refs[1:]
    middle_ref, router_grad_ref, grad_ref, low_ref, attended_grad_ref, gain_ref = refs[:6]
    out_sums, refs = refs[6 : 4 + dp_count], refs[4 + dp_count :]
    near_parts, refs = refs[:tp_count], refs[tp_count:]
    (attended_out, in_keep, in_core, in_sum, down_keep, down_core, down_far,
     mixed, out_all, in_all, down_all, rows_all, scaled_all, act_all, gate_all, up_all, send_rows,
     row_parts, row_in, row_back, dot_parts, dot_in, dot_home, dot_back, probs, whole,
     normed_flip, in_land_far, down_land_far, out_parts, out_in, hidden_ref, out_grad_ref,
     picker_ref, picker_rows_ref, sends, receives, in_sems, keep_sems) = refs
    tokens, second_width = attended_ref.shape
    first_width = firsts[0].shape[1]
    width = first_width + second_width
    share = D // tp_count
    slots = rows_all.shape[0] // dp_count
    depth, ff = in_own.shape[1], in_own.shape[2]
    shares = range(1, tp_count)
    order = [0] + list(range(2, dp_count)) + [1]

    local = []

    def load(source, target):
        copy = pltpu.make_async_copy(source, target, in_sems.at[len(local)])
        copy.start()
        local.append(copy)
        return copy

    out_copies = [
        load(out_ref, out_all),
        load(hidden_hbm, hidden_ref),
        load(picker_rows_hbm, picker_rows_ref),
    ]
    weight_copies, down_parts = [], []
    for j in range(ctx_count):
        part = slice(j * depth, (j + 1) * depth)
        weight_copies.append(load(ins[j], in_all.at[:, part, :]))
        down_parts.append(down_all.at[:, part])
    weight_copies.append(load(down_own, down_parts[0]))
    weight_copies.append(load(picker_hbm, picker_ref))
    weight_copies.append(load(out_grad_hbm, out_grad_ref))
    own_share = pl.ds(pl.multiple_of(t * share, share), share)
    weight_copies.append(load(grads_own, scaled_all.at[:slots]))
    grad_copies = [
        load(grads_land[m - 1], scaled_all.at[m * slots : (m + 1) * slots, own_share])
        for m in range(1, dp_count)
    ]
    own_lanes = pl.ds(pl.multiple_of(t * width, width), width)
    second_lanes = pl.ds(pl.multiple_of(t * width + first_width, LANES), second_width)
    mixed[:, second_lanes] = attended_ref[...]
    for m in range(tp_count):
        start = pl.multiple_of((t ^ m) * width, width)
        mixed[:, pl.ds(start, first_width)] = firsts[m][...]
    attended_out[...] = mixed[:, own_lanes]
    greet(
        [{"tp": t ^ k} for k in shares]
        + [{"dp": d ^ m} for m in range(1, dp_count)]
        + [{"ctx": c ^ 1}, {"ctx": c ^ 2}]
    )
    wire = Wire(sends, receives)
    assert ctx_count == 4
    downs = {j: wire.send(down_own, down_parts[j], ctx=c ^ j) for j in (2, 1)}
    second_part = mixed.at[:, second_lanes]
    arrivals = [wire.send(second_part, second_part, tp=t ^ k) for k in shares]
    spread, returned, dot_returned = {}, {}, {}
    for copy in grad_copies:
        copy.wait()

    def spread_grads(m):
        half = scaled_all.at[m * slots : (m + 1) * slots, own_share]
        spread[m] = [wire.send(half, half, tp=t ^ k) for k in shares]

    for m in order[1:]:
        spread_grads(m)
    for copy in out_copies:
        copy.wait()
    for copy in arrivals:
        copy.wait()
    middle = hidden_ref[...].astype(F32) + mm(mixed[...], out_all[...], NT)
    middle_ref[...] = middle
    scale = lax.rsqrt(jnp.mean(middle * middle, axis=-1, keepdims=True) + NORM_EPS)
    normed = (middle * scale * gains_ref[1:2, :]).astype(BF16)
    far = {}

    def block(m):
        return slice(m * slots, (m + 1) * slots)

    for m in order[1:] + [0]:
        picked = mm(picker_rows_ref[block(m), :], normed).astype(BF16)
        if m:
            send_rows[m - 1] = picked
            far[m] = wire.send(
                send_rows.at[m - 1, :, own_share], rows_all.at[block(m), own_share], dp=d ^ m
            )
        else:
            rows_all[block(0), :] = picked
    lane = lax.broadcasted_iota(jnp.int32, (tokens, LANES), 1)

    def router_probs(values):
        logits = mm(values, lanes_ref[...])
        where = lax.broadcasted_iota(jnp.int32, logits.shape, 1)
        logits = jnp.where(where < experts, logits, NEG_FILL)
        powers = jnp.exp(logits - jnp.max(logits, axis=1, keepdims=True))
        return where, powers / jnp.sum(powers, axis=1, keepdims=True)

    probs[...] = router_probs(normed)[1]
    normed_flip[...] = normed.T
    for copy in weight_copies:
        copy.wait()
    downs[2].wait()
    downs[3] = wire.send(down_parts[2], down_parts[3], ctx=c ^ 1)
    downs[1].wait()
    downs[3].wait()
    columns = [pl.ds(pl.multiple_of((c ^ j) * depth, depth), depth) for j in range(ctx_count)]

    gates = {}

    def forward(m):
        far[m].wait()
        half = rows_all.at[block(m), own_share]
        spread[m] += [wire.send(half, half, tp=t ^ k) for k in shares]

    def experts_on(m, hook):
        here = block(m)
        where, chance = router_probs(rows_all[here, :])
        gate = jnp.sum(jnp.where(where == d, chance, 0.0), axis=1, keepdims=True)
        rows = jnp.concatenate([rows_all[here, part] for part in columns], axis=1)
        grad_rows = jnp.concatenate([scaled_all[here, part] for part in columns], axis=1)
        rows_all[here, :] = rows
        scaled_all[here, :] = (gate * grad_rows.astype(F32)).astype(BF16)
        dots = jnp.zeros((slots, LANES), F32)
        for first in range(0, ff, BLOCK):
            part = slice(first, min(ff, first + BLOCK))
            value = mm(rows, in_all[0, :, part])
            up = mm(rows, in_all[1, :, part])
            back = mm(grad_rows, down_all[part, :], NT)
            bent, slope = bent_parts(value)
            act = (bent * up).astype(BF16)
            act_all[here, part] = act
            dots += jnp.sum(act.astype(F32) * back, axis=1, keepdims=True)
            scaled = gate * back
            gate_all[here, part] = (scaled * up * slope).astype(BF16)
            up_all[here, part] = (scaled * bent).astype(BF16)
        if hook is not None:
            hook()
        dot_parts[m] = dots.T[:8]
        dot_returned[m] = [
            wire.send(dot_parts.at[m], dot_in.at[k - 1, m], tp=t ^ k) for k in shares
        ]
        for k in list(shares) + [0]:
            for i in range(share // depth):
                piece = ((t ^ k) * (share // depth) + i) ^ c
                part = pl.ds(pl.multiple_of(piece * depth, depth), depth)
                row = mm(gate_all[here, :], in_all[0, part, :], NT)
                row += mm(up_all[here, :], in_all[1, part, :], NT)
                row_parts[k, m, :, i * depth : (i + 1) * depth] = row.astype(BF16)
            if k:
                returned.setdefault(m, []).append(
                    wire.send(row_parts.at[k, m], row_in.at[k - 1, m], tp=t ^ k)
                )
        gates[m] = gate

    def outputs_of(m):
        here = block(m)
        for k in range(tp_count):
            for i in range(share // depth):
                piece = ((t ^ k) * (share // depth) + i) ^ c
                part = pl.ds(pl.multiple_of(piece * depth, depth), depth)
                out_parts[k, m, :, i * depth : (i + 1) * depth] = (
                    gates[m] * mm(act_all[here, :], down_all[:, part])
                ).astype(BF16)

    homeward = []

    def send_home(m):
        for copy in dot_returned[m]:
            copy.wait()
        dots = tree_sum([dot_parts[m]] + [dot_in[k - 1, m] for k in shares])
        total = row_parts[0, m].astype(F32)
        for k, copy in zip(shares, returned[m]):
            copy.wait()
            total = total + row_in[k - 1, m].astype(F32)
        if m:
            dot_home[m] = dots
            row_parts[0, m] = total.astype(BF16)
            homeward.append(wire.send(dot_home.at[m], dot_back.at[m], dp=d ^ m))
            homeward.append(wire.send(row_parts.at[0, m], row_back.at[block(m)], dp=d ^ m))
        else:
            dot_back[0] = dots
            row_back[block(0), :] = total.astype(BF16)

    for i, m in enumerate(order):
        for copy in spread.get(m, []):
            copy.wait()
            copy.sent()
        hook = functools.partial(forward, order[i + 1]) if i + 1 < len(order) else None
        experts_on(m, hook)
        if i:
            send_home(order[i - 1])

    def in_grads(j):
        part = slice(j * depth, (j + 1) * depth)
        for side, right in enumerate((gate_all, up_all)):
            in_all[side, part, :] = mm(rows_all[:, part], right[...], TN).astype(BF16)

    keeps = []

    def keep(source, target):
        copy = pltpu.make_async_copy(source, target, keep_sems.at[len(keeps)])
        copy.start()
        keeps.append(copy)

    def part_of(j):
        return slice(j * depth, (j + 1) * depth)

    for m in order:
        outputs_of(m)
    out_copies = [
        wire.send(out_parts.at[k, m], out_in.at[k - 1, m], tp=t ^ k)
        for m in order[1:-1]
        for k in shares
    ]
    for k in range(tp_count):
        near_parts[k][...] = out_parts[k, :2]
    downs[3].sent()
    for first in range(0, ff, BLOCK):
        part = slice(first, min(ff, first + BLOCK))
        down_all[part, :] = mm(act_all[:, part], scaled_all[...], TN).astype(BF16)
    near = [
        wire.send(down_parts[3], down_land_far, ctx=c ^ 1),
        wire.send(down_parts[1], down_core, ctx=c ^ 1),
    ]
    keep(down_parts[0], down_keep)
    send_home(order[-1])
    in_grads(3)
    near.append(wire.send(in_all.at[:, part_of(3), :], in_land_far, ctx=c ^ 1))
    near[0].wait()
    down_all[:, part_of(2)] = (
        down_all[:, part_of(2)].astype(F32) + down_land_far[...].astype(F32)
    ).astype(BF16)
    near.append(wire.send(down_parts[2], down_far, ctx=c ^ 2))
    in_grads(1)
    near.append(wire.send(in_all.at[:, part_of(1), :], in_core, ctx=c ^ 1))
    in_grads(2)
    near[2].wait()
    for side in range(2):
        in_all[side, part_of(2), :] = (
            in_all[side, part_of(2), :].astype(F32) + in_land_far[side].astype(F32)
        ).astype(BF16)
    keep(in_all.at[:, part_of(2), :], in_sum)
    in_grads(0)
    keep(in_all.at[:, part_of(0), :], in_keep)

    for copy in homeward:
        copy.wait()
    result = mm(picker_ref[...], row_back[...])
    prob_grad = jnp.zeros((tokens, LANES), F32)
    for m in range(dp_count):
        high = dot_back[m].astype(BF16)
        rest = dot_back[m] - high.astype(F32)
        middle_part = rest.astype(BF16)
        tiny = (rest - middle_part.astype(F32)).astype(BF16)
        total = mm(picker_ref[:, block(m)], high, NT)
        total += mm(picker_ref[:, block(m)], middle_part, NT)
        total += mm(picker_ref[:, block(m)], tiny, NT)
        prob_grad = jnp.where(lane == (d ^ m), total[:, 0:1], prob_grad)
    chance = probs[...]
    logit = chance * (prob_grad - jnp.sum(chance * prob_grad, axis=1, keepdims=True))
    more = lax.dot_general(
        logit, lanes_ref[own_share, :].astype(F32), NT, precision=lax.Precision.HIGHEST,
        preferred_element_type=F32,
    )
    whole[:, own_share] = (result + more).astype(BF16)
    arrivals = [wire.send(whole.at[:, own_share], whole.at[:, own_share], tp=t ^ k) for k in shares]
    logit_high = logit.astype(BF16)
    logit_rest = logit - logit_high.astype(F32)
    logit_low = logit_rest.astype(BF16)
    logit_tiny = (logit_rest - logit_low.astype(F32)).astype(BF16)
    router_grad = mm(normed_flip[...], logit_high)
    router_grad += mm(normed_flip[...], logit_low)
    router_grad += mm(normed_flip[...], logit_tiny)
    router_grad_ref[...] = router_grad
    for copy in out_copies:
        copy.wait()
    for m in range(2, dp_count):
        parts = [out_parts[0, m]] + [out_in[k - 1, m] for k in shares]
        out_sums[m - 2][...] = tree_sum([part.astype(F32) for part in parts]).astype(BF16)
    for copy in arrivals:
        copy.wait()
    middle = middle_ref[...]
    gradient = whole[...].astype(F32)
    scale = lax.rsqrt(jnp.mean(middle * middle, axis=-1, keepdims=True) + NORM_EPS)
    weighted = gains_ref[1:2, :] * gradient
    inner = jnp.mean(middle * weighted, axis=-1, keepdims=True)
    gain_ref[...] = fold_sum(gradient * middle * scale)
    total = out_grad_ref[...].astype(F32) + (
        scale * weighted - middle * (scale * scale * scale) * inner
    )
    grad_ref[...] = total
    low_ref[...] = total.astype(BF16)
    attended_grad_ref[...] = mm(low_ref[...], out_all[:, own_lanes]).astype(BF16)
    for copy in keeps:
        copy.wait()
    for copy in near:
        copy.wait()
    wire.finish()


def expert_step(
    firsts, attended, hidden, out_grad, gains, lanes, picker_flip, picker_rows, out, grads_own,
    grads, expert, expert_land, down, experts,
):
    dp_count, ctx_count, tp_count = (lax.axis_size(a) for a in ("dp", "ctx", "tp"))
    tokens, width = attended.shape[0], firsts[0].shape[1] + attended.shape[1]
    slots = grads_own.shape[0]
    share = D // tp_count
    depth, ff = expert.shape[1], expert.shape[2]
    all_slots = dp_count * slots
    others = tp_count - 1
    copies = others * (2 + 5 * dp_count) + 3 * dp_count + 8
    vmem = pl.BlockSpec(memory_space=pltpu.VMEM)
    hbm = pl.BlockSpec(memory_space=pl.ANY)
    shape = jax.ShapeDtypeStruct
    return pl.pallas_call(
        functools.partial(expert_kernel, experts, dp_count, ctx_count, tp_count),
        in_specs=[vmem] * 3 + [hbm] * 4 + [vmem] * tp_count + [hbm] * (4 + dp_count),
        out_specs=[vmem] * (5 + dp_count + tp_count) + [hbm] * 6,
        out_shape=[
            shape((tokens, D), F32),
            shape((D, LANES), F32),
            shape((tokens, D), F32),
            shape((tokens, D), BF16),
            shape((tokens, width), BF16),
            shape((8, D), F32),
        ]
        + [shape((slots, share), BF16)] * (dp_count - 2)
        + [shape((2, slots, share), BF16)] * tp_count
        + [shape((tokens, width), BF16)]
        + [shape((2, depth, ff), BF16)] * 3
        + [shape((ff, depth), BF16)] * 3,
        scratch_shapes=[
            pltpu.VMEM((tokens, tp_count * width), BF16),
            pltpu.VMEM((D, tp_count * width), BF16),
            pltpu.VMEM((2, D, ff), BF16),
            pltpu.VMEM((ff, D), BF16),
            pltpu.VMEM((all_slots, D), BF16),
            pltpu.VMEM((all_slots, D), BF16),
            pltpu.VMEM((all_slots, ff), BF16),
            pltpu.VMEM((all_slots, ff), BF16),
            pltpu.VMEM((all_slots, ff), BF16),
            pltpu.VMEM((dp_count - 1, slots, D), BF16),
            pltpu.VMEM((tp_count, dp_count, slots, share), BF16),
            pltpu.VMEM((others, dp_count, slots, share), BF16),
            pltpu.VMEM((all_slots, share), BF16),
            pltpu.VMEM((dp_count, 8, slots), F32),
            pltpu.VMEM((others, dp_count, 8, slots), F32),
            pltpu.VMEM((dp_count, 8, slots), F32),
            pltpu.VMEM((dp_count, 8, slots), F32),
            pltpu.VMEM((tokens, LANES), F32),
            pltpu.VMEM((tokens, D), BF16),
            pltpu.VMEM((D, tokens), BF16),
            pltpu.VMEM((2, depth, ff), BF16),
            pltpu.VMEM((ff, depth), BF16),
            pltpu.VMEM((tp_count, dp_count, slots, share), BF16),
            pltpu.VMEM((others, dp_count, slots, share), BF16),
            pltpu.VMEM((tokens, D), BF16),
            pltpu.VMEM((tokens, D), BF16),
            pltpu.VMEM((tokens, all_slots), BF16),
            pltpu.VMEM((all_slots, tokens), BF16),
            pltpu.SemaphoreType.DMA((copies,)),
            pltpu.SemaphoreType.DMA((copies,)),
            pltpu.SemaphoreType.DMA((6 + ctx_count + dp_count,)),
            pltpu.SemaphoreType.DMA((3,)),
        ],
        compiler_params=pltpu.CompilerParams(
            vmem_limit_bytes=VMEM_CAP, collective_id=3, has_side_effects=True
        ),
        cost_estimate=cost(120),
        name="expert_step",
    )(
        attended, gains, lanes, hidden, out_grad, picker_flip, picker_rows, *firsts, out,
        grads_own, *grads, expert, expert_land, down,
    )


def final_kernel(
    experts, dp_count, ctx_count, tp_count,
    key_ref, value_ref, gains_ref, gain_two_ref, bias_ref, *refs,
):
    late, refs = refs[:10], refs[10:]
    near_outs, refs = refs[:tp_count], refs[tp_count:]
    far_outs, refs = refs[: dp_count - 2], refs[dp_count - 2 :]
    (input_grad_ref, output_ref, bias_out_ref, first_ref, second_ref, tail_ref, out_back,
     mixed, bias_send, bias_in, near_in, far_send, far_in, rows_all, token_grad, token_in,
     gain_send, gain_in, out_send) = refs[:19]
    first, value, key = (refs[19 + 5 * k : 24 + 5 * k] for k in range(3))
    targets, refs = refs[34:44], refs[44:]
    (query_grad_ref, normed_ref, low_ref, attended_ref, weight_ref, hidden_ref,
     router_grad_ref, picker_ref, middle_ref, middle_grad_ref) = targets
    near_land, (sends, receives, late_sems, near_sems) = refs[:tp_count], refs[tp_count:]
    loads = [
        pltpu.make_async_copy(source, target, late_sems.at[k])
        for k, (source, target) in enumerate(zip(late, targets))
    ]
    near_loads = [
        pltpu.make_async_copy(source, target, near_sems.at[k])
        for k, (source, target) in enumerate(zip(near_outs, near_land))
    ]
    d, c, t = lax.axis_index("dp"), lax.axis_index("ctx"), lax.axis_index("tp")
    tokens, width = query_grad_ref.shape
    dp_bits = bits_down(dp_count)[::-1]
    assert ctx_count == 4
    halves = (0, 1)
    greet(
        [{"ctx": c ^ 1}, {"ctx": c ^ 2}]
        + [{"dp": d ^ bit} for bit in dp_bits]
        + [{"tp": t ^ k} for k in range(1, tp_count)]
    )
    wire = Wire(sends, receives)

    bias_steps = [{"ctx": c ^ 1}, {"ctx": c ^ 2}] + [{"dp": d ^ bit} for bit in dp_bits]
    bias_total, bias_copies = [bias_ref[...]], []

    def bias_begin():
        level = len(bias_copies)
        bias_send[level] = bias_total[-1]
        bias_copies.append(
            wire.send(bias_send.at[level], bias_in.at[level], **bias_steps[level])
        )

    def bias_end():
        level = len(bias_copies) - 1
        bias_copies[level].wait()
        bias_total.append(bias_total[-1] + bias_in[level])

    def split(values):
        return values.astype(BF16).reshape(dp_count, ctx_count, -1, values.shape[1])

    def cross(part):
        return [
            wire.send(part[0].at[:, c ^ (2 * k + 1)], part[1].at[k], ctx=c ^ 1) for k in halves
        ]

    def add_core(part, copies):
        for k, copy in zip(halves, copies):
            copy.wait()
            own = part[0][:, pl.ds(c ^ (2 * k), 1)][:, 0]
            part[2][k] = (own.astype(F32) + part[1][k].astype(F32)).astype(BF16)

    def dp_send(part, level, sides):
        copies, bit = [], dp_bits[level]
        for m in range(bit, dp_count, 2 * bit):
            for k in sides:
                spot = part[3].at[level, k, d ^ m]
                copies.append((m ^ bit, k, wire.send(part[2].at[k, d ^ m], spot, dp=d ^ bit)))
        return copies

    def dp_add(part, level, copies):
        for m, k, copy in copies:
            copy.wait()
            own = part[2][k, pl.ds(d ^ m, 1)][0]
            other = part[3][level, k, pl.ds(d ^ m, 1)][0]
            part[2][k, pl.ds(d ^ m, 1)] = (own.astype(F32) + other.astype(F32)).astype(BF16)[None]

    def x_send(part):
        return wire.send(part[2].at[1], part[4], ctx=c ^ 2)

    def x_add(part, copy):
        copy.wait()
        part[2][0] = (part[2][0].astype(F32) + part[4][...].astype(F32)).astype(BF16)

    bias_begin()
    sources = (value_ref, key_ref)
    near = [
        [
            wire.send(ref.at[(2 * k + 1) * tokens : (2 * k + 2) * tokens], near_in.at[side, k],
                      ctx=c ^ 1)
            for k in (1, 0)
        ]
        for side, ref in enumerate(sources)
    ]
    slots, share = out_send.shape
    far_loads = [
        pltpu.make_async_copy(
            source, out_back.at[(k + 2) * slots : (k + 3) * slots], near_sems.at[tp_count + k]
        )
        for k, source in enumerate(far_outs)
    ]
    for copy in near_loads + loads + far_loads:
        copy.start()
    for copy in near_loads:
        copy.wait()
    sums = [tree_sum([land[m].astype(F32) for land in near_land]) for m in range(2)]
    out_back[:slots, :] = sums[0].astype(BF16)
    out_send[...] = sums[1].astype(BF16)
    out_home = wire.send(out_send, out_back.at[slots : 2 * slots], dp=d ^ 1)
    far_copies = []
    for side, ref in enumerate(sources):
        for k, copy in zip((1, 0), near[side]):
            copy.wait()
            rows = slice(2 * k * tokens, (2 * k + 1) * tokens)
            far_send[side, k] = (
                ref[rows, :].astype(F32) + near_in[side, k].astype(F32)
            ).astype(BF16)
            if k:
                if side == 0:
                    bias_end()
                    bias_begin()
                far_copies.append(wire.send(far_send.at[side, 1], far_in.at[side], ctx=c ^ 2))

    for copy in loads[:5]:
        copy.wait()
    first[0][:, :, :, :width] = split(mm(normed_ref[...], query_grad_ref[...]))
    first[0][:, :, :, width:] = split(mm(low_ref[...], attended_ref[...], TN))
    first_crossed = cross(first)
    token_grad[...] = mm(query_grad_ref[...], weight_ref[:, :width], NT)
    add_core(first, first_crossed)
    bias_end()
    bias_begin()
    first_moving = dp_send(first, 0, halves)
    for copy in loads[5:]:
        copy.wait()
    out_home.wait()
    for copy in far_loads:
        copy.wait()
    own_share = pl.ds(pl.multiple_of(t * share, share), share)
    mixed[:, own_share] = mm(picker_ref[...], out_back[...]).astype(BF16)
    mixed_part = mixed.at[:, own_share]
    mixed_copies = [wire.send(mixed_part, mixed_part, tp=t ^ k) for k in range(1, tp_count)]

    def land(side, columns):
        far_copies[side].wait()
        rows_all[:, columns] = (
            far_send[side, 0].astype(F32) + far_in[side].astype(F32)
        ).astype(BF16)

    key_columns, value_columns = slice(width, 2 * width), slice(2 * width, 3 * width)
    land(0, value_columns)
    value[0][...] = split(mm(normed_ref[...], rows_all[:, value_columns]))
    value_crossed = cross(value)
    token_grad[...] += mm(rows_all[:, value_columns], weight_ref[:, value_columns], NT)
    add_core(value, value_crossed)
    value_far = x_send(value)
    inputs = hidden_ref[...].astype(F32)
    scale = lax.rsqrt(jnp.mean(inputs * inputs, axis=-1, keepdims=True) + NORM_EPS)

    land(1, key_columns)
    part = token_grad[...] + mm(rows_all[:, key_columns], weight_ref[:, key_columns], NT)
    part_low = part.astype(BF16)
    gain_send[0] = fold_sum(part_low.astype(F32) * inputs * scale)
    token_in[0] = part_low
    gain_total = gain_send[0]
    gain_copies, token_copies = [], []
    tp_bits = bits_down(tp_count)[::-1]
    gain_copies.append(wire.send(gain_send.at[0], gain_in.at[0], tp=t ^ tp_bits[0]))
    token_copies.append(wire.send(token_in.at[0], token_in.at[1], tp=t ^ tp_bits[0]))
    key[0][:, :, :, :width] = split(mm(normed_ref[...], rows_all[:, key_columns]))
    for level, bit in enumerate(tp_bits):
        if level:
            gain_send[level] = gain_total
            gain_copies.append(wire.send(gain_send.at[level], gain_in.at[level], tp=t ^ bit))
        gain_copies[level].wait()
        gain_total = gain_total + gain_in[level]
    gain_one = jnp.sum(gain_total, axis=0, keepdims=True)
    gain_two = jnp.sum(gain_two_ref[...], axis=0, keepdims=True)
    row = lax.broadcasted_iota(jnp.int32, (LANES, D), 0)
    gain_rows = jnp.where(row == experts, gain_one, jnp.where(row == experts + 1, gain_two, 0.0))
    key[0][:, :, :, width:] = split(router_grad_ref[...] + gain_rows.T)
    key_crossed = cross(key)
    add_core(key, key_crossed)
    key_far = x_send(key)

    moving = {}
    first_far = None
    for level in range(len(dp_bits)):
        dp_add(first, level, first_moving)
        bias_end()
        if level + 1 < len(dp_bits):
            bias_begin()
            first_moving = dp_send(first, level + 1, halves)
        else:
            first_far = wire.send(first[2].at[1, d], first[4], ctx=c ^ 2)
        for name, weights, copy in (("value", value, value_far), ("key", key, key_far)):
            if level == 0:
                x_add(weights, copy)
            else:
                dp_add(weights, level - 1, moving[name])
            moving[name] = dp_send(weights, level, [0])
    total = part_low.astype(F32)
    for level, bit in enumerate(tp_bits):
        if level:
            token_in[2 * level] = total.astype(BF16)
            total = token_in[2 * level].astype(F32)
            token_copies.append(
                wire.send(token_in.at[2 * level], token_in.at[2 * level + 1], tp=t ^ bit)
            )
        token_copies[level].wait()
        total = total + token_in[2 * level + 1].astype(F32)
    weighted = gains_ref[0:1, :] * total
    inner = jnp.mean(inputs * weighted, axis=-1, keepdims=True)
    input_grad_ref[...] = (
        middle_grad_ref[...] + scale * weighted - inputs * (scale * scale * scale) * inner
    )
    bias_out_ref[...] = bias_total[-1]
    first_far.wait()
    first_ref[...] = first[2][0, pl.ds(d, 1)][0].astype(F32) + first[4][...].astype(F32)
    last = len(dp_bits) - 1
    dp_add(value, last, moving["value"])
    second_ref[:, width:] = value[2][0, pl.ds(d, 1)][0].astype(F32)
    dp_add(key, last, moving["key"])
    result = key[2][0, pl.ds(d, 1)][0].astype(F32)
    second_ref[:, :width] = result[:, :width]
    rest = jnp.zeros((LANES - result.shape[0], LANES), F32)
    tail_ref[...] = jnp.concatenate([result[:, width:], rest], axis=0).T
    for copy in mixed_copies:
        copy.wait()
    output_ref[...] = middle_ref[...] + mixed[...].astype(F32)
    wire.finish()


def final_step(
    query_grad, key_part, value_part, normed, weight, low, attended, router_grad, hidden,
    gains, gain_two, middle_grad, middle, picker, bias, outs, experts,
):
    tokens, width = query_grad.shape
    slots, share = outs[0].shape[1:]
    dp_count, ctx_count, tp_count = (lax.axis_size(a) for a in ("dp", "ctx", "tp"))
    rows = D // (dp_count * ctx_count)
    levels = len(bits_down(dp_count))
    tp_levels = len(bits_down(tp_count))
    copies = 7 + 2 + levels + 3 * 2 + 4 * dp_count + 3 + 2 * tp_levels + tp_count
    hbm = pl.BlockSpec(memory_space=pl.ANY)
    vmem = pl.BlockSpec(memory_space=pltpu.VMEM)
    shape = jax.ShapeDtypeStruct

    late = (
        query_grad, normed, low, attended, weight, hidden, router_grad, picker, middle,
        middle_grad,
    )

    def buffers(columns, far_shape, sides):
        return [
            pltpu.VMEM((dp_count, ctx_count, rows, columns), BF16),
            pltpu.VMEM((2, dp_count, rows, columns), BF16),
            pltpu.VMEM((2, dp_count, rows, columns), BF16),
            pltpu.VMEM((levels, sides, dp_count, rows, columns), BF16),
            pltpu.VMEM(far_shape + (columns,), BF16),
        ]

    return pl.pallas_call(
        functools.partial(final_kernel, experts, dp_count, ctx_count, tp_count),
        in_specs=[vmem] * 5 + [hbm] * (10 + len(outs)),
        out_specs=[vmem] * 6,
        out_shape=[
            shape((tokens, D), F32),
            shape((tokens, D), F32),
            shape(bias.shape, F32),
            shape((rows, 2 * width), F32),
            shape((rows, 2 * width), F32),
            shape((LANES, LANES), F32),
        ],
        scratch_shapes=[
            pltpu.VMEM((dp_count * slots, share), BF16),
            pltpu.VMEM((tokens, D), BF16),
            pltpu.VMEM((2 + levels,) + bias.shape, F32),
            pltpu.VMEM((2 + levels,) + bias.shape, F32),
            pltpu.VMEM((2, 2, tokens, width), BF16),
            pltpu.VMEM((2, 2, tokens, width), BF16),
            pltpu.VMEM((2, tokens, width), BF16),
            pltpu.VMEM((tokens, 3 * width), BF16),
            pltpu.VMEM((tokens, D), F32),
            pltpu.VMEM((2 * tp_levels, tokens, D), BF16),
            pltpu.VMEM((tp_levels, 8, D), F32),
            pltpu.VMEM((tp_levels, 8, D), F32),
            pltpu.VMEM((slots, share), BF16),
        ]
        + buffers(2 * width, (rows,), 2)
        + buffers(width, (dp_count, rows), 1)
        + buffers(width + LANES, (dp_count, rows), 1)
        + [pltpu.VMEM(array.shape, array.dtype) for array in late]
        + [pltpu.VMEM((2, slots, share), BF16)] * tp_count
        + [
            pltpu.SemaphoreType.DMA((copies,)),
            pltpu.SemaphoreType.DMA((copies,)),
            pltpu.SemaphoreType.DMA((10,)),
            pltpu.SemaphoreType.DMA((tp_count + dp_count,)),
        ],
        compiler_params=pltpu.CompilerParams(
            vmem_limit_bytes=VMEM_CAP, collective_id=2, has_side_effects=True
        ),
        cost_estimate=cost(87),
        name="final_step",
    )(key_part, value_part, gains, gain_two, bias, *late, *outs)


def adam_kernel(*refs):
    weight, first, second = refs[:3]
    parts, outs = refs[3:-4], refs[-4:]
    gradient = parts[0][...].astype(F32) + parts[1][...].astype(F32) + parts[2][...].astype(F32)
    first_new = BETA_ONE * first[...] + (1.0 - BETA_ONE) * gradient
    second_new = BETA_TWO * second[...] + (1.0 - BETA_TWO) * gradient * gradient
    outs[0][...] = gradient
    outs[1][...] = first_new
    outs[2][...] = second_new
    outs[3][...] = -MAIN_RATE * (
        first_new * (1.0 / FIX_ONE) / (jnp.sqrt(second_new * (1.0 / FIX_TWO)) + ADAM_EPS)
        + WEIGHT_DECAY * weight[...].astype(F32)
    )


def adam(weight, first, second, kept, arrived, far):
    count, rows, columns = weight.shape
    sizes = [size for size in range(16, rows + 1, 16) if rows % size == 0]
    step = max(k for k in sizes if k * columns <= 400000 and count * rows >= 2 * k)
    plain = pl.BlockSpec((1, step, columns), lambda i, j: (i, j, 0))
    shape = jax.ShapeDtypeStruct(weight.shape, F32)
    return pl.pallas_call(
        adam_kernel,
        grid=(count, rows // step),
        in_specs=[plain] * 6,
        out_specs=[plain] * 4,
        out_shape=[shape] * 4,
        compiler_params=pltpu.CompilerParams(vmem_limit_bytes=VMEM_CAP),
        cost_estimate=cost(5),
        name="adam",
    )(weight, first, second, kept, arrived, far)


def small_adam_kernel(experts, pairs, *refs):
    first_ref, second_ref, tail_ref, bias_ref = refs[:4]
    inputs, outs = refs[4:19], refs[19:]

    def step(k, gradient, part, rate):
        weight, first, second = (ref[part].astype(F32) for ref in inputs[3 * k : 3 * k + 3])
        first_new = BETA_ONE * first + (1.0 - BETA_ONE) * gradient
        second_new = BETA_TWO * second + (1.0 - BETA_TWO) * gradient * gradient
        update = -rate * (
            first_new * (1.0 / FIX_ONE) / (jnp.sqrt(second_new * (1.0 / FIX_TWO)) + ADAM_EPS)
            + WEIGHT_DECAY * weight
        )
        for out, values in zip(
            outs[4 * k : 4 * k + 4], (gradient, first_new, second_new, update)
        ):
            out[part] = values

    rows, width = inputs[3].shape
    whole = slice(None)
    step(0, first_ref[:, :width], 0, MAIN_RATE)
    step(0, second_ref[:, :width], 1, MAIN_RATE)
    step(0, second_ref[:, width:], 2, MAIN_RATE)
    step(1, first_ref[:, width:], whole, MAIN_RATE)
    step(2, tail_ref[:experts, :rows], whole, MAIN_RATE)
    step(3, tail_ref[experts : experts + 2, :rows], whole, MAIN_RATE)
    bias = jnp.concatenate([bias_ref[p, :2] for p in range(pairs)], axis=0)
    step(4, bias, whole, BIAS_RATE)


def small_adam(first_total, second_total, tail_total, bias_total, triples, experts):
    flat = [array for triple in triples for array in triple]
    vmem = pl.BlockSpec(memory_space=pltpu.VMEM)
    results = pl.pallas_call(
        functools.partial(small_adam_kernel, experts, bias_total.shape[0]),
        in_specs=[vmem] * (4 + len(flat)),
        out_specs=[vmem] * (4 * len(triples)),
        out_shape=[
            jax.ShapeDtypeStruct(triple[0].shape, F32) for triple in triples for _ in range(4)
        ],
        compiler_params=pltpu.CompilerParams(vmem_limit_bytes=VMEM_CAP),
        cost_estimate=cost(2),
        name="small_adam",
    )(first_total, second_total, tail_total, bias_total, *flat)
    return [results[4 * k : 4 * k + 4] for k in range(len(triples))]


def shards(
    hidden_in,
    out_grad,
    segments,
    routes,
    bucket_table,
    qkv_weight,
    out_weight,
    router,
    norm_gains,
    position_bias,
    expert_in,
    expert_down,
    qkv_first,
    qkv_second,
    out_first,
    out_second,
    router_first,
    router_second,
    gains_first,
    gains_second,
    bias_first,
    bias_second,
    in_first,
    in_second,
    down_first,
    down_second,
):
    tokens = hidden_in.shape[0]
    dp_count, ctx_count, tp_count = (lax.axis_size(a) for a in ("dp", "ctx", "tp"))
    dp_place, ctx_place, tp_place = (lax.axis_index(a) for a in ("dp", "ctx", "tp"))
    length = tokens * ctx_count
    heads_here = position_bias.shape[0]
    width_here = heads_here * HEAD_DIM
    pairs = heads_here // 2
    expert_count = router.shape[1]
    top_count = routes.shape[1]
    own_rows = router.shape[0]

    capacity = max(2, min(tokens, 5 * top_count * tokens // (4 * expert_count)))
    window_width = tokens + length
    table = jnp.pad(bucket_table[::-1], (0, 1), constant_values=BUCKETS)
    table = lax.dynamic_slice(table, (ctx_place * tokens,), (window_width,))
    table = jnp.broadcast_to(table[None], (8, window_width))
    qkv_view = [array.transpose(1, 0, 2) for array in (qkv_weight, qkv_first, qkv_second)]
    out_view = [array.T for array in (out_weight, out_first, out_second)]
    router_view = [array.T for array in (router, router_first, router_second)]
    (queries, key_values, normed_flip, qkv_flat, out_own, lanes, gains, info, doc_row, doc_col,
     picker_flip, picker_rows, grads_own, grads_half, early_land, expert_land) = start(
        qkv_view[0], out_view[0], router_view[0], norm_gains, hidden_in, segments, routes.T,
        out_grad, expert_in[0], capacity,
    )
    early = early_blocks(dp_count)
    arrived = [
        early_land[early.index(m)] if m in early else swap(grads_half[m - 1], "dp", m)
        for m in range(1, dp_count)
    ]
    half = pairs // 2
    attended_first, totals = attention(
        info, queries, key_values, position_bias, table, doc_row, doc_col, 0, half, ()
    )
    first_sides = gather_xor(attended_first, "tp")
    attended_second, totals = attention(
        info, queries, key_values, position_bias, table, doc_row, doc_col, half, pairs - half,
        (totals,),
    )
    results = expert_step(
        first_sides, attended_second, hidden_in, out_grad, gains, lanes, picker_flip, picker_rows,
        out_own, grads_own, arrived, expert_in[0], expert_land, expert_down[0], expert_count,
    )
    middle, router_grad, middle_grad, middle_low, attended_grad, gain_two_grad = results[:6]
    out_sums, results = results[6 : 4 + dp_count], results[4 + dp_count :]
    near_parts, results = results[:tp_count], results[tp_count:]
    attended, in_keep, in_core, in_sum, down_keep, down_core, down_far = results

    in_far = swap(in_sum, "ctx", 2)
    out_far = [swap(near_parts[k], "tp", k) for k in range(1, tp_count)]
    out_far += [swap(out_sums[m - 2], "dp", m) for m in range(2, dp_count)]
    query_grad, key_part, value_part, bias_part = attention_back(
        info, queries, key_values, attended_grad, totals, position_bias, table, doc_row, doc_col
    )
    query_grad, in_far, out_far = lax.optimization_barrier((query_grad, in_far, out_far))
    input_grad, output, bias_total, first_total, second_total, tail_total = final_step(
        query_grad, key_part, value_part, normed_flip, qkv_flat, middle_low, attended,
        router_grad, hidden_in, gains, gain_two_grad, middle_grad, middle, picker_flip, bias_part,
        [near_parts[0]] + out_far, expert_count,
    )
    qkv_all, out_new, router_new, gains_new, bias_new = small_adam(
        first_total, second_total, tail_total, bias_total,
        [
            qkv_view,
            out_view,
            router_view,
            (norm_gains, gains_first, gains_second),
            (position_bias, bias_first, bias_second),
        ],
        expert_count,
    )
    in_new = [
        values[None]
        for values in adam(
            expert_in[0], in_first[0], in_second[0], in_keep, in_core, in_far
        )
    ]
    down_new = adam(
        expert_down, down_first, down_second, down_keep[None], down_core[None], down_far[None]
    )
    return (
        output,
        input_grad,
        *[array.transpose(1, 0, 2) for array in qkv_all],
        *[array.T for array in out_new],
        *[array.T for array in router_new],
        *gains_new,
        *bias_new,
        *in_new,
        *down_new,
    )


def solution(mesh):
    token_rows = P(("dp", "ctx"), None)
    qkv = P(("dp", "ctx"), None, "tp")
    out = P("tp", ("dp", "ctx"))
    gains = P(None, ("dp", "ctx"))
    bias = P("tp", None)
    expert_in = P("dp", None, "ctx", "tp")
    expert_down = P("dp", "tp", "ctx")
    placed = (
        token_rows, token_rows, P("dp", "ctx"), token_rows, P(),
        qkv, out, token_rows, gains, bias, expert_in, expert_down,
        qkv, qkv, out, out, token_rows, token_rows, gains, gains, bias, bias,
        expert_in, expert_in, expert_down, expert_down,
    )
    return jax.shard_map(
        shards,
        mesh=mesh,
        in_specs=placed,
        out_specs=(token_rows, token_rows)
        + (qkv,) * 4
        + (out,) * 4
        + (token_rows,) * 4
        + (gains,) * 4
        + (bias,) * 4
        + (expert_in,) * 4
        + (expert_down,) * 4,
        check_vma=False,
    )
```

```python
import functools

import jax
import jax.numpy as jnp
from jax import lax
from jax.experimental import pallas as pl
from jax.experimental.pallas import tpu as pltpu
from jax.sharding import PartitionSpec as P

D = 1024
HEAD_DIM = 64
BUCKETS = 32

NORM_EPS = 1e-06
NEG_FILL = -1e30
BETA_ONE = 0.9
BETA_TWO = 0.95
FIX_ONE = 1.0 - 0.9**10
FIX_TWO = 1.0 - 0.95**10
ADAM_EPS = 1e-08
WEIGHT_DECAY = 0.1
MAIN_RATE = 0.02
BIAS_RATE = 0.2

F32 = jnp.float32
BF16 = jnp.bfloat16
LANES = 128
BLOCK = 256
FF_STEP = 256
VMEM_CAP = 60 * 1024 * 1024
GELU_K = 0.7978845608028654
GELU_C = 0.044715


def tree_sum(values):
    while len(values) > 1:
        values = [values[k] + values[k + 1] for k in range(0, len(values), 2)]
    return values[0]


def rms_scale(values):
    return lax.rsqrt(jnp.mean(values * values, axis=-1, keepdims=True) + NORM_EPS)


def norm_back(values, scale_here, gain_here, gradient):
    weighted = gain_here * gradient
    row_inner = jnp.mean(values * weighted, axis=-1, keepdims=True)
    input_part = scale_here * weighted - values * scale_here**3 * row_inner
    return (input_part, jnp.sum(gradient * values * scale_here, axis=0))


def adamw_step(weight, gradient, first_moment, second_moment, step_rate):
    first_new = BETA_ONE * first_moment + (1.0 - BETA_ONE) * gradient
    second_new = BETA_TWO * second_moment + (1.0 - BETA_TWO) * gradient * gradient
    update = -step_rate * (
        first_new / FIX_ONE / (jnp.sqrt(second_new / FIX_TWO) + ADAM_EPS) + WEIGHT_DECAY * weight
    )
    return (first_new, second_new, update)


def cost(micros):
    return pl.CostEstimate(flops=int(micros * 1.15e9), bytes_accessed=1 << 20, transcendentals=0)


def swap(values, axis, bits):
    count = lax.axis_size(axis)
    return lax.ppermute(values, axis, [(i, i ^ bits) for i in range(count)])


def gather_xor(values, axis):
    pieces = {0: values}
    bit = lax.axis_size(axis) >> 1
    while bit:
        for key in list(pieces):
            pieces[key | bit] = swap(pieces[key], axis, bit)
        bit >>= 1
    return [pieces[m] for m in range(len(pieces))]


def scatter_sum(parts, axis):
    live = dict(enumerate(parts))
    bit = 1
    while bit < lax.axis_size(axis):
        left = {}
        for key in live:
            if key & bit == 0:
                moved = swap(live[key | bit].astype(BF16), axis, bit)
                left[key] = live[key].astype(F32) + moved.astype(F32)
        live = left
        bit <<= 1
    return live[0]


def all_sum(values, axis):
    bit = 1
    while bit < lax.axis_size(axis):
        values = values + swap(values, axis, bit)
        bit <<= 1
    return values


def in_order(pieces, place, dim):
    bit = 1
    while bit < len(pieces):
        odd = (place & bit) > 0
        pieces = [jnp.where(odd, pieces[m ^ bit], pieces[m]) for m in range(len(pieces))]
        bit <<= 1
    return jnp.concatenate(pieces, axis=dim)


MESH = pl.DeviceIdType.MESH


class Wire:
    def __init__(self, sends, receives):
        self.sends, self.receives, self.count, self.copies = sends, receives, 0, []

    def send(self, source, target, **device):
        copy = pltpu.make_async_remote_copy(
            src_ref=source,
            dst_ref=target,
            send_sem=self.sends.at[self.count],
            recv_sem=self.receives.at[self.count],
            device_id=device,
            device_id_type=MESH,
        )
        copy.start()
        self.count += 1
        self.copies.append(Arrival(copy))
        return self.copies[-1]

    def finish(self):
        for copy in self.copies:
            copy.sent()


class Arrival:
    def __init__(self, copy):
        self.copy, self.waited, self.gone = copy, False, False

    def sent(self):
        if not self.gone:
            self.copy.wait_send()
        self.gone = True

    def wait(self):
        if not self.waited:
            self.copy.wait_recv()
        self.waited = True


def greet(partners):
    barrier = pltpu.get_barrier_semaphore()
    for device in partners:
        pl.semaphore_signal(barrier, inc=1, device_id=device, device_id_type=MESH)
    pl.semaphore_wait(barrier, len(partners))


def bits_down(count):
    bits, bit = [], count >> 1
    while bit:
        bits.append(bit)
        bit >>= 1
    return bits


def xor_order(count):
    order = [0]
    for bit in bits_down(count):
        order = order + [k | bit for k in order]
    return order


NT = (((1,), (1,)), ((), ()))
NN = (((1,), (0,)), ((), ()))
TN = (((0,), (0,)), ((), ()))


def mm(left, right, dims=NN):
    return lax.dot_general(left, right, dims, preferred_element_type=F32)


def fold_max(values):
    return jnp.max(values.reshape(values.shape[0] // 8, 8, values.shape[1]), axis=0)


def fold_sum(values):
    return jnp.sum(values.reshape(values.shape[0] // 8, 8, values.shape[1]), axis=0)


def skewed(row):
    width = row.shape[1]
    tall = jnp.broadcast_to(row, (LANES, width))
    return pltpu.roll(tall, width - (LANES - 1), 1, stride=1, stride_axis=0)


def unskew_sum(field):
    half = field.shape[0] // 2
    while half >= 1:
        field = pltpu.roll(field[:half], half, 1) + field[half:]
        half //= 2
    return field


def head_masks(rows):
    lane = lax.broadcasted_iota(jnp.int32, (rows, LANES), 1)
    return [(lane < HEAD_DIM).astype(BF16), (lane >= HEAD_DIM).astype(BF16)]


def score_tile(key_block, query_head, skew_ref, head, first, same):
    scores = mm(key_block, query_head, NT)
    tiles = []
    for s in range(BLOCK // LANES):
        column = pl.multiple_of(first - s * LANES, LANES)
        tiles.append(skew_ref[head, :, pl.ds(column, BLOCK)])
    return jnp.where(same, scores + jnp.concatenate(tiles, axis=0), NEG_FILL)


def bucket_lanes(table_ref):
    row = lax.broadcasted_iota(jnp.int32, (BUCKETS, table_ref.shape[1]), 0)
    return (row == table_ref[0:1, :]).astype(F32)


def spread_bias(bias_ref, table_ref, skew_ref, first=0):
    rows = bias_ref[pl.ds((pl.program_id(0) + first) * 2, 2), :]
    window = jnp.dot(
        jnp.concatenate([rows] * 4, axis=0), bucket_lanes(table_ref),
        precision=lax.Precision.HIGHEST, preferred_element_type=F32,
    )
    for h in range(2):
        skew_ref[h] = skewed(window[h : h + 1, :])


def over_blocks(info_ref, qb, query_blocks, step):
    @pl.loop(0, info_ref[query_blocks + qb, 0])
    def _(i):
        blocks = [info_ref[qb, 2 * i + k] for k in range(2)]
        step(
            [pl.ds(pl.multiple_of(kb * BLOCK, BLOCK), BLOCK) for kb in blocks],
            [info_ref[2 * query_blocks, kb] + qb * BLOCK for kb in blocks],
        )


def attention_kernel(
    first, info_ref, query_ref, key_ref, value_ref, bias_ref, table_ref, doc_row_ref,
    doc_col_ref, *refs,
):
    out_ref, total_ref, skew_ref, flip_ref, score_ref, most_ref, sum_ref, mix_ref = refs[-8:]
    tokens, length = query_ref.shape[0], key_ref.shape[0]
    key_blocks, query_blocks = length // BLOCK, tokens // BLOCK
    masks = head_masks(BLOCK)
    spread_bias(bias_ref, table_ref, skew_ref, first)

    @pl.loop(0, key_blocks)
    def _(kb):
        rows = pl.ds(pl.multiple_of(kb * BLOCK, BLOCK), BLOCK)
        flip_ref[:, rows] = value_ref[rows, :].T

    for qb in range(query_blocks):
        here = slice(qb * BLOCK, (qb + 1) * BLOCK)
        pair = query_ref[here, :] * jnp.asarray(HEAD_DIM**-0.5, BF16)
        query_heads = [pair * mask for mask in masks]
        doc_row = doc_row_ref[0:1, here]
        most_ref[...] = jnp.full_like(most_ref, NEG_FILL)
        sum_ref[...] = jnp.zeros_like(sum_ref)
        mix_ref[...] = jnp.zeros_like(mix_ref)

        def scores(spans, firsts):
            for rows, first_column in zip(spans, firsts):
                column = doc_col_ref[rows, :]
                same = jnp.concatenate([column] * (BLOCK // LANES), axis=1) == doc_row
                for h in range(2):
                    tile = score_tile(
                        key_ref[rows, :], query_heads[h], skew_ref, h, first_column, same
                    )
                    score_ref[h, rows, :] = tile
                    most_ref[h] = jnp.maximum(most_ref[h], fold_max(tile))

        over_blocks(info_ref, qb, query_blocks, scores)
        most = [jnp.max(most_ref[h], axis=0, keepdims=True) for h in range(2)]

        def mixes(spans, firsts):
            for h in range(2):
                heads = slice(h * HEAD_DIM, (h + 1) * HEAD_DIM)
                total, mix = sum_ref[h], mix_ref[h]
                for rows in spans:
                    weights = jnp.exp(score_ref[h, rows, :] - most[h])
                    total += fold_sum(weights)
                    mix += mm(flip_ref[heads, rows], weights.astype(BF16))
                sum_ref[h] = total
                mix_ref[h] = mix

        over_blocks(info_ref, qb, query_blocks, mixes)
        columns = []
        for h in range(2):
            total = jnp.sum(sum_ref[h], axis=0, keepdims=True)
            columns.append(mix_ref[h] / total)
            total_ref[0, h : h + 1, here] = most[h] + jnp.log(total)
        out_ref[here, :] = jnp.concatenate(columns, axis=0).T.astype(BF16)


def attention_back_kernel(
    info_ref, query_ref, key_ref, value_ref, grad_ref, total_ref, bias_ref, table_ref,
    doc_row_ref, doc_col_ref,
    query_grad_ref, key_grad_ref, value_grad_ref, bias_grad_ref,
    skew_ref, field_ref, flip_ref, weight_ref, change_ref, inner_ref, mix_ref, key_sum, value_sum,
):
    tokens, length = query_ref.shape[0], key_ref.shape[0]
    key_blocks, query_blocks = length // BLOCK, tokens // BLOCK
    masks = head_masks(BLOCK)
    spread_bias(bias_ref, table_ref, skew_ref)
    field_ref[...] = jnp.zeros_like(field_ref)
    key_sum[...] = jnp.zeros_like(key_sum)
    value_sum[...] = jnp.zeros_like(value_sum)

    @pl.loop(0, key_blocks)
    def _(kb):
        rows = pl.ds(pl.multiple_of(kb * BLOCK, BLOCK), BLOCK)
        flip_ref[:, rows] = key_ref[rows, :].T

    for qb in range(query_blocks):
        here = slice(qb * BLOCK, (qb + 1) * BLOCK)
        pair = query_ref[here, :] * jnp.asarray(HEAD_DIM**-0.5, BF16)
        query_heads = [pair * mask for mask in masks]
        grad_pair = grad_ref[here, :]
        grad_heads = [grad_pair * mask for mask in masks]
        doc_row = doc_row_ref[0:1, here]
        inner_ref[...] = jnp.zeros_like(inner_ref)
        mix_ref[...] = jnp.zeros_like(mix_ref)
        totals = [total_ref[0, h : h + 1, here] for h in range(2)]

        def changes(spans, firsts):
            for rows, first_column in zip(spans, firsts):
                column = doc_col_ref[rows, :]
                same = jnp.concatenate([column] * (BLOCK // LANES), axis=1) == doc_row
                for h in range(2):
                    tile = score_tile(
                        key_ref[rows, :], query_heads[h], skew_ref, h, first_column, same
                    )
                    weights = jnp.exp(tile - totals[h])
                    change = mm(value_ref[rows, :], grad_heads[h], NT)
                    weight_ref[h, rows, :] = weights
                    change_ref[h, rows, :] = change
                    inner_ref[h] += fold_sum(weights * change)

        over_blocks(info_ref, qb, query_blocks, changes)
        inner = [jnp.sum(inner_ref[h], axis=0, keepdims=True) for h in range(2)]

        def gradients(spans, firsts):
            mixes = [mix_ref[h] for h in range(2)]
            for rows, first_column in zip(spans, firsts):
                key_part = value_part = None
                for h in range(2):
                    weights = weight_ref[h, rows, :]
                    score_grad = weights * (change_ref[h, rows, :] - inner[h])
                    for s in range(BLOCK // LANES):
                        first = pl.multiple_of(first_column - s * LANES, LANES)
                        field_ref[h, :, pl.ds(first, BLOCK)] += score_grad[
                            s * LANES : (s + 1) * LANES
                        ]
                    low = score_grad.astype(BF16)
                    key_here = mm(low, query_heads[h])
                    value_here = mm(weights.astype(BF16), grad_heads[h])
                    key_part = key_here if h == 0 else key_part + key_here
                    value_part = value_here if h == 0 else value_part + value_here
                    heads = slice(h * HEAD_DIM, (h + 1) * HEAD_DIM)
                    mixes[h] += mm(flip_ref[heads, rows], low)
                key_sum[rows, :] += key_part
                value_sum[rows, :] += value_part
            for h in range(2):
                mix_ref[h] = mixes[h]

        over_blocks(info_ref, qb, query_blocks, gradients)
        both = jnp.concatenate([mix_ref[0], mix_ref[1]], axis=0) * HEAD_DIM**-0.5
        query_grad_ref[here, :] = both.T.astype(BF16)

    key_grad_ref[...] = key_sum[...].astype(BF16)
    value_grad_ref[...] = value_sum[...].astype(BF16)
    offsets = jnp.concatenate([unskew_sum(field_ref[h]) for h in range(2)] * 4, axis=0)
    bias_grad_ref[0] = lax.dot_general(
        offsets, bucket_lanes(table_ref), NT, precision=lax.Precision.HIGHEST,
        preferred_element_type=F32,
    )


def attention_specs(tokens, length, pairs, heads, width, first=0):
    smem = pl.BlockSpec(memory_space=pltpu.SMEM)
    return dict(
        info=smem,
        query=pl.BlockSpec((tokens, LANES), lambda i: (0, i + first)),
        key=pl.BlockSpec((length, LANES), lambda i: (0, i + first)),
        value=pl.BlockSpec((length, LANES), lambda i: (0, i + first + pairs)),
        bias=pl.BlockSpec((heads, BUCKETS), lambda i: (0, 0)),
        table=pl.BlockSpec((8, width), lambda i: (0, 0)),
        total=pl.BlockSpec((1, 8, tokens), lambda i: (i + first, 0, 0)),
        bias_grad=pl.BlockSpec((1, 8, BUCKETS), lambda i: (i, 0, 0)),
        doc_row=pl.BlockSpec((8, tokens), lambda i: (0, 0)),
        doc_col=pl.BlockSpec((length, LANES), lambda i: (0, 0)),
    )


def attention(info, queries, key_values, bias, table, doc_row, doc_col, first, count, held):
    tokens, length = queries.shape[0], key_values.shape[0]
    pairs, width = bias.shape[0] // 2, table.shape[1]
    specs = attention_specs(tokens, length, pairs, bias.shape[0], width, first)
    return pl.pallas_call(
        functools.partial(attention_kernel, first),
        grid=(count,),
        in_specs=[
            specs["info"], specs["query"], specs["key"], specs["value"], specs["bias"],
            specs["table"], specs["doc_row"], specs["doc_col"],
        ]
        + [pl.BlockSpec(memory_space=pl.ANY)] * len(held),
        out_specs=[pl.BlockSpec((tokens, LANES), lambda i: (0, i)), specs["total"]],
        out_shape=[
            jax.ShapeDtypeStruct((tokens, count * LANES), BF16),
            jax.ShapeDtypeStruct((pairs, 8, tokens), F32),
        ],
        scratch_shapes=[
            pltpu.VMEM((2, LANES, width), F32),
            pltpu.VMEM((LANES, length), BF16),
            pltpu.VMEM((2, length, BLOCK), F32),
            pltpu.VMEM((2, 8, BLOCK), F32),
            pltpu.VMEM((2, 8, BLOCK), F32),
            pltpu.VMEM((2, HEAD_DIM, BLOCK), F32),
        ],
        input_output_aliases={8: 1} if held else {},
        compiler_params=pltpu.CompilerParams(vmem_limit_bytes=VMEM_CAP),
        cost_estimate=cost(5),
        name="attention_forward",
    )(info, queries, key_values, key_values, bias, table, doc_row, doc_col, *held)


def attention_back(info, queries, key_values, grads, totals, bias, table, doc_row, doc_col):
    tokens, length = queries.shape[0], key_values.shape[0]
    pairs, width = bias.shape[0] // 2, table.shape[1]
    specs = attention_specs(tokens, length, pairs, bias.shape[0], width)
    return pl.pallas_call(
        attention_back_kernel,
        grid=(pairs,),
        in_specs=[
            specs["info"], specs["query"], specs["key"], specs["value"], specs["query"],
            specs["total"], specs["bias"], specs["table"], specs["doc_row"], specs["doc_col"],
        ],
        out_specs=[specs["query"], specs["key"], specs["key"], specs["bias_grad"]],
        out_shape=[
            jax.ShapeDtypeStruct(queries.shape, BF16),
            jax.ShapeDtypeStruct((length, queries.shape[1]), BF16),
            jax.ShapeDtypeStruct((length, queries.shape[1]), BF16),
            jax.ShapeDtypeStruct((pairs, 8, BUCKETS), F32),
        ],
        scratch_shapes=[
            pltpu.VMEM((2, LANES, width), F32),
            pltpu.VMEM((2, LANES, width), F32),
            pltpu.VMEM((LANES, length), BF16),
            pltpu.VMEM((2, length, BLOCK), F32),
            pltpu.VMEM((2, length, BLOCK), F32),
            pltpu.VMEM((2, 8, BLOCK), F32),
            pltpu.VMEM((2, HEAD_DIM, BLOCK), F32),
            pltpu.VMEM((length, LANES), F32),
            pltpu.VMEM((length, LANES), F32),
        ],
        compiler_params=pltpu.CompilerParams(vmem_limit_bytes=VMEM_CAP),
        cost_estimate=cost(40),
        name="attention_backward",
    )(info, queries, key_values, key_values, grads, totals, bias, table, doc_row, doc_col)


def start_kernel(
    experts, dp_count, ctx_count, tp_count, qkv_ref, out_flip_ref, router_ref, gain_pair_ref,
    hidden_ref, segments_ref, routes_ref, out_grad_hbm, expert_ref,
    query_ref, pair_out, normed_flip_ref, weight_out, own_ref, lanes_ref, gains_ref, info_ref,
    row_ref, column_out, picker_out, picker_rows_out, grads_own_out, grads_out, early_land,
    expert_land,
    weights, out_all, hidden, docs, docs_ref, flip, pair_ref, column_ref, picker_ref,
    picker_rows_ref, grads_own_ref, grads_ref, out_grad_ref, sends, receives, out_sem, in_sem,
):
    d, c, t = lax.axis_index("dp"), lax.axis_index("ctx"), lax.axis_index("tp")
    rows = out_flip_ref.shape[0]
    tokens, width = query_ref.shape
    early = early_blocks(dp_count)
    out_grad_load = pltpu.make_async_copy(out_grad_hbm, out_grad_ref, in_sem)
    out_grad_load.start()
    stores = []

    def store(source, target):
        copy = pltpu.make_async_copy(source, target, out_sem.at[len(stores)])
        copy.start()
        stores.append(copy)

    own_rows = pl.ds(pl.multiple_of((d * ctx_count + c) * rows, rows), rows)
    own_lanes = pl.ds(pl.multiple_of(t * width, width), width)
    for part in range(3):
        weights[own_rows, part * width : (part + 1) * width] = qkv_ref[part]
    out_all[own_rows, own_lanes] = out_flip_ref[...]
    flip[...] = jnp.zeros_like(flip)
    flip[:experts, :rows] = router_ref[...].astype(F32)
    flip[experts : experts + 2, :rows] = gain_pair_ref[...].astype(F32)
    weights[own_rows, 3 * width :] = flip[:, :LANES].T[:rows].astype(BF16)
    docs_ref[...] = jnp.broadcast_to(segments_ref[...], docs_ref.shape)
    row_ref[...] = docs_ref[...]
    greet(
        [{"ctx": c ^ m} for m in range(1, ctx_count)]
        + [{"dp": d ^ m} for m in sorted(set(bits_down(dp_count) + early))]
        + [{"tp": t ^ k} for k in range(1, tp_count)]
    )
    wire = Wire(sends, receives)
    share = grads_ref.shape[2]
    own_share = pl.ds(pl.multiple_of(t * share, share), share)

    def send_shard(m, j, part, lanes=own_lanes, **device):
        index = (d ^ m) * ctx_count + (c ^ j)
        here = pl.ds(pl.multiple_of(index * rows, rows), rows)
        shard = out_all.at[here, lanes] if part else weights.at[here]
        return wire.send(shard, shard, **device)

    docs_sent = [wire.send(docs_ref, docs.at[m], ctx=c ^ m) for m in range(1, ctx_count)]
    sides, sides_far = [0], []
    parts = (0, 1)
    arrivals = {part: [] for part in range(2)}
    hidden_sent, expert_sent = {}, {}
    for bit in bits_down(ctx_count)[:-1]:
        arrivals = {
            k: [send_shard(0, j, part, ctx=c ^ bit) for j in sides]
            for k, part in enumerate(parts)
        }
        assert bit == 2
        half = hidden_ref.at[:, own_share]
        hidden_sent[2] = wire.send(half, hidden.at[2, :, own_share], ctx=c ^ 2)
        for m in [0] + list(expert_sent):
            if m:
                expert_sent[m].wait()
            source = expert_land.at[m - 1] if m else expert_ref
            expert_sent[m | bit] = wire.send(source, expert_land.at[(m | bit) - 1], ctx=c ^ bit)
        for copy in arrivals[0]:
            copy.wait()
        sides_far = sides + [j | bit for j in sides]
        if bit != 2:
            for copy in arrivals[1]:
                copy.wait()
        sides = sides_far
    hidden_sent[1] = wire.send(hidden_ref, hidden.at[1], ctx=c ^ 1)

    order = xor_order(dp_count)
    groups = [{}, {}]
    crossed, beside = [[], []], []

    def onward(k, m):
        for copy in groups[k].get(m, []):
            copy.wait()
        for bit in bits_down(dp_count):
            if m & (2 * bit - 1) == 0:
                groups[k][m | bit] = [send_shard(m, j, parts[k], dp=d ^ bit) for j in sides]
        crossed[k] += [send_shard(m, j, parts[k], ctx=c ^ 1) for j in sides]
        if k:
            for other in range(1, tp_count):
                beside.append(
                    (m, other, [send_shard(m, j, 1, tp=t ^ other) for j in sides])
                )

    onward(0, 0)
    expert_sent[1] = wire.send(expert_ref, expert_land.at[0], ctx=c ^ 1)

    lane = lax.broadcasted_iota(jnp.int32, (tokens, LANES), 1)
    flip[:8, :] = jnp.zeros((8, tokens), F32)
    flip[: routes_ref.shape[0], :] = routes_ref[...].astype(F32)
    routes = flip[...].T
    tops = [routes[:, k : k + 1].astype(jnp.int32) for k in range(routes_ref.shape[0])]
    named = jnp.zeros((tokens, LANES), F32)
    for top in tops:
        named = jnp.where(lane == top, 1.0, named)
    row_index = lax.broadcasted_iota(jnp.int32, (tokens, tokens), 0)
    column_index = lax.broadcasted_iota(jnp.int32, (tokens, tokens), 1)
    before = jnp.where(column_index < row_index, 1.0, 0.0).astype(BF16)
    earlier = mm(before, named.astype(BF16))
    slots = grads_own_ref.shape[0]
    column = lax.broadcasted_iota(jnp.int32, picker_ref.shape, 1)
    picker = jnp.zeros(picker_ref.shape, F32)
    for top in tops:
        place = jnp.sum(jnp.where(lane == top, earlier, 0.0), axis=1, keepdims=True)
        place = place.astype(jnp.int32)
        target = jnp.where(place < slots, (top ^ d) * slots + place, -1)
        picker = jnp.where(column == target, 1.0, picker)
    picker_ref[...] = picker.astype(BF16)
    picker_rows_ref[...] = picker_ref[...].T
    hidden_sent[2].wait()
    half = hidden.at[2, :, own_share]
    spread = [wire.send(half, half, tp=t ^ k) for k in range(1, tp_count)]
    out_grad_load.wait()
    for m in range(dp_count):
        chosen = picker_rows_ref[m * slots : (m + 1) * slots, :]
        if m:
            grads_ref[m - 1] = mm(chosen, out_grad_ref[:, own_share]).astype(BF16)
        else:
            grads_own_ref[...] = mm(chosen, out_grad_ref[...]).astype(BF16)

    store(picker_ref, picker_out)
    store(picker_rows_ref, picker_rows_out)
    store(grads_own_ref, grads_own_out)
    store(grads_ref, grads_out)

    key_blocks, query_blocks = tokens // BLOCK, tokens // BLOCK
    where = lax.broadcasted_iota(jnp.int32, info_ref.shape, 1)
    which = lax.broadcasted_iota(jnp.int32, info_ref.shape, 0)
    info = jnp.zeros(info_ref.shape, jnp.int32)
    met = [[] for _ in range(query_blocks)]
    for m in range(ctx_count):
        if m:
            docs_sent[m - 1].wait()
        row = docs[m] if m else docs_ref[...]
        tall = jnp.broadcast_to(row[0:1, :].astype(F32), (LANES, tokens))
        column_ref[m * tokens : (m + 1) * tokens, :] = tall.T.astype(jnp.int32)
        for k in range(key_blocks):
            spot = m * key_blocks + k
            low = row[0:1, k * BLOCK : k * BLOCK + 1]
            high = row[0:1, (k + 1) * BLOCK - 1 : (k + 1) * BLOCK]
            for q in range(query_blocks):
                query_low = docs_ref[0:1, q * BLOCK : q * BLOCK + 1]
                query_high = docs_ref[0:1, (q + 1) * BLOCK - 1 : (q + 1) * BLOCK]
                meets = ((high >= query_low) & (low <= query_high)).astype(jnp.int32)
                met[q].append(meets)
            base = (ctx_count * tokens - LANES) - ((c ^ m) * tokens + k * BLOCK)
            info = jnp.where((where == spot) & (which == 2 * query_blocks), base, info)
    for q in range(query_blocks):
        count = sum(met[q][1:], met[q][0])
        inside, outside = jnp.zeros_like(count), count
        for spot, meets in enumerate(met[q]):
            place = jnp.where(meets > 0, inside, outside)
            info = jnp.where((where == place) & (which == q), spot, info)
            inside, outside = inside + meets, outside + (1 - meets)
        steps = lax.shift_right_logical(count + 1, 1)
        info = jnp.where(which == query_blocks + q, steps, info)
    info_ref[...] = info
    store(column_ref, column_out)

    early_copies = []
    for i, m in enumerate(order[1:]):
        onward(0, m)
        if i == 0:
            for copy in arrivals[1]:
                copy.wait()
            onward(1, 0)
    for i, m in enumerate(order[1:]):
        onward(1, m)
        if i == 0:
            early_copies = [
                wire.send(grads_ref.at[n - 1], early_land.at[k], dp=d ^ n)
                for k, n in enumerate(early)
            ]
    for copy in spread:
        copy.wait()
    hidden_sent[3] = wire.send(hidden.at[2], hidden.at[3], ctx=c ^ 1)
    for copy in crossed[0]:
        copy.wait()
    store(weights.at[:, : 3 * width], weight_out)
    small = weights[:, 3 * width : 3 * width + LANES].astype(F32)
    lane = lax.broadcasted_iota(jnp.int32, small.shape, 1)
    lanes_ref[...] = jnp.where(lane < experts, small, 0.0).astype(BF16)
    gain_one = jnp.sum(jnp.where(lane == experts, small, 0.0), axis=1, keepdims=True)
    gain_two = jnp.sum(jnp.where(lane == experts + 1, small, 0.0), axis=1, keepdims=True)
    both = jnp.where(lane == 0, gain_one, jnp.where(lane == 1, gain_two, 0.0)).T
    gains_ref[...] = both[:8]
    gain = both[0:1]
    for m in range(ctx_count):
        if m:
            hidden_sent[m].wait()
        values = (hidden[m] if m else hidden_ref[...]).astype(F32)
        scale = lax.rsqrt(jnp.mean(values * values, axis=-1, keepdims=True) + NORM_EPS)
        normed = (values * scale * gain).astype(BF16)
        pair_ref[m * tokens : (m + 1) * tokens, :] = mm(
            normed, weights[:, width : 3 * width]
        ).astype(BF16)
        here = pl.ds(m * tokens, tokens)
        store(pair_ref.at[here], pair_out.at[here])
        if m == 0:
            normed_flip_ref[...] = normed.T
            query_ref[...] = mm(normed, weights[:, :width]).astype(BF16)
            for n, other, copies in beside:
                for copy in copies:
                    copy.wait()
                lanes = pl.ds(pl.multiple_of((t ^ other) * width, width), width)
                crossed[1] += [send_shard(n, j, 1, lanes, ctx=c ^ 1) for j in sides]
    for copy in crossed[1]:
        copy.wait()
    store(out_all, own_ref)
    for k in [k for k in expert_sent if k > 1]:
        expert_sent[k].wait()
        expert_sent[k | 1] = wire.send(expert_land.at[k - 1], expert_land.at[k], ctx=c ^ 1)
    for k in range(1, ctx_count):
        expert_sent[k].wait()
    for copy in early_copies:
        copy.wait()
    for copy in stores:
        copy.wait()
    wire.finish()


def early_blocks(dp_count):
    return list(range(2, dp_count))[:1]


def start(qkv, out_flip, router, gain_pair, hidden, segments, routes, out_grad, expert, slots):
    tokens, (experts, _), width = hidden.shape[0], router.shape, qkv.shape[2]
    columns = 4 * width + LANES
    dp_count, ctx_count, tp_count = (lax.axis_size(a) for a in ("dp", "ctx", "tp"))
    copies = 5 * ctx_count + (2 + tp_count) * dp_count * ctx_count + tp_count + dp_count + 1
    vmem = pl.BlockSpec(memory_space=pltpu.VMEM)
    hbm = pl.BlockSpec(memory_space=pl.ANY)
    shape = jax.ShapeDtypeStruct
    return pl.pallas_call(
        functools.partial(start_kernel, experts, dp_count, ctx_count, tp_count),
        in_specs=[vmem] * 7 + [hbm] * 2,
        out_specs=[vmem, hbm, vmem] + [hbm] * 2 + [vmem] * 4 + [hbm] * 7,
        out_shape=[
            shape((tokens, width), BF16),
            shape((tokens * ctx_count, 2 * width), BF16),
            shape((D, tokens), BF16),
            shape((D, 3 * width), BF16),
            shape((D, tp_count * width), BF16),
            shape((D, LANES), BF16),
            shape((8, D), F32),
            shape((8, LANES), jnp.int32),
            shape((8, tokens), jnp.int32),
            shape((tokens * ctx_count, LANES), jnp.int32),
            shape((tokens, dp_count * slots), BF16),
            shape((dp_count * slots, tokens), BF16),
            shape((slots, D), BF16),
            shape((dp_count - 1, slots, D // tp_count), BF16),
            shape((len(early_blocks(dp_count)), slots, D // tp_count), BF16),
            shape((ctx_count - 1,) + expert.shape, BF16),
        ],
        scratch_shapes=[
            pltpu.VMEM((D, columns - width), BF16),
            pltpu.VMEM((D, tp_count * width), BF16),
            pltpu.VMEM((ctx_count, tokens, D), BF16),
            pltpu.VMEM((ctx_count, 8, tokens), jnp.int32),
            pltpu.VMEM((8, tokens), jnp.int32),
            pltpu.VMEM((LANES, tokens), F32),
            pltpu.VMEM((tokens * ctx_count, 2 * width), BF16),
            pltpu.VMEM((tokens * ctx_count, LANES), jnp.int32),
            pltpu.VMEM((tokens, dp_count * slots), BF16),
            pltpu.VMEM((dp_count * slots, tokens), BF16),
            pltpu.VMEM((slots, D), BF16),
            pltpu.VMEM((dp_count - 1, slots, D // tp_count), BF16),
            pltpu.VMEM((tokens, D), BF16),
            pltpu.SemaphoreType.DMA((copies,)),
            pltpu.SemaphoreType.DMA((copies,)),
            pltpu.SemaphoreType.DMA((7 + ctx_count,)),
            pltpu.SemaphoreType.DMA(()),
        ],
        compiler_params=pltpu.CompilerParams(
            vmem_limit_bytes=VMEM_CAP, collective_id=1, has_side_effects=True
        ),
        cost_estimate=cost(60),
        name="start",
    )(qkv, out_flip, router, gain_pair, hidden, segments, routes, out_grad, expert)


def bent_parts(value):
    square = value * value
    wave = jnp.tanh(GELU_K * value * (1.0 + GELU_C * square))
    half = 0.5 * (1.0 + wave)
    slope = half + 0.5 * value * (1.0 - wave * wave) * (GELU_K * (1.0 + 3.0 * GELU_C * square))
    return value * half, slope


def expert_kernel(
    experts, dp_count, ctx_count, tp_count, attended_ref, gains_ref, lanes_ref, hidden_hbm,
    out_grad_hbm, picker_hbm, picker_rows_hbm, *refs,
):
    d, c, t = lax.axis_index("dp"), lax.axis_index("ctx"), lax.axis_index("tp")
    firsts, refs = refs[:tp_count], refs[tp_count:]
    out_ref, grads_own, refs = refs[0], refs[1], refs[2:]
    grads_land, refs = refs[: dp_count - 1], refs[dp_count - 1 :]
    in_own, in_land, refs = refs[0], refs[1], refs[2:]
    ins = [in_own] + [in_land.at[j] for j in range(ctx_count - 1)]
    down_own, refs = refs[0], refs[1:]
    middle_out, router_grad_ref, grad_ref, low_ref, attended_grad_ref, gain_ref = refs[:6]
    out_sums, refs = refs[6 : 4 + dp_count], refs[4 + dp_count :]
    near_parts, refs = refs[:tp_count], refs[tp_count:]
    (attended_out, in_keep, in_core, in_sum, down_keep, down_core, down_far,
     mixed, out_all, in_all, down_all, rows_all, scaled_all, act_all, gate_all, up_all, send_rows,
     row_parts, row_in, row_back, dot_parts, dot_in, dot_home, dot_back, probs, whole,
     normed_flip, in_land_far, down_land_far, out_parts, out_in, hidden_ref, out_grad_ref,
     picker_ref, picker_rows_ref, middle_ref, sends, receives, in_sems, keep_sems) = refs
    tokens, second_width = attended_ref.shape
    first_width = firsts[0].shape[1]
    width = first_width + second_width
    share = D // tp_count
    slots = rows_all.shape[0] // dp_count
    depth, ff = in_own.shape[1], in_own.shape[2]
    shares = range(1, tp_count)
    order = [0] + list(range(2, dp_count)) + [1]

    local = []

    def load(source, target):
        copy = pltpu.make_async_copy(source, target, in_sems.at[len(local)])
        copy.start()
        local.append(copy)
        return copy

    keeps = []

    def keep(source, target):
        copy = pltpu.make_async_copy(source, target, keep_sems.at[len(keeps)])
        copy.start()
        keeps.append(copy)

    out_copies = [
        load(out_ref, out_all),
        load(hidden_hbm, hidden_ref),
        load(picker_rows_hbm, picker_rows_ref),
    ]
    weight_copies, down_parts = [], []
    for j in range(ctx_count):
        part = slice(j * depth, (j + 1) * depth)
        weight_copies.append(load(ins[j], in_all.at[:, part, :]))
        down_parts.append(down_all.at[:, part])
    weight_copies.append(load(down_own, down_parts[0]))
    weight_copies.append(load(picker_hbm, picker_ref))
    weight_copies.append(load(out_grad_hbm, out_grad_ref))
    own_share = pl.ds(pl.multiple_of(t * share, share), share)
    weight_copies.append(load(grads_own, scaled_all.at[:slots]))
    grad_copies = [
        load(grads_land[m - 1], scaled_all.at[m * slots : (m + 1) * slots, own_share])
        for m in range(1, dp_count)
    ]
    own_lanes = pl.ds(pl.multiple_of(t * width, width), width)
    second_lanes = pl.ds(pl.multiple_of(t * width + first_width, LANES), second_width)
    mixed[:, second_lanes] = attended_ref[...]
    for m in range(tp_count):
        start = pl.multiple_of((t ^ m) * width, width)
        mixed[:, pl.ds(start, first_width)] = firsts[m][...]
    keep(mixed.at[:, own_lanes], attended_out)
    greet(
        [{"tp": t ^ k} for k in shares]
        + [{"dp": d ^ m} for m in range(1, dp_count)]
        + [{"ctx": c ^ 1}, {"ctx": c ^ 2}]
    )
    wire = Wire(sends, receives)
    assert ctx_count == 4
    downs = {j: wire.send(down_own, down_parts[j], ctx=c ^ j) for j in (2, 1)}
    second_part = mixed.at[:, second_lanes]
    arrivals = [wire.send(second_part, second_part, tp=t ^ k) for k in shares]
    spread, returned, dot_returned = {}, {}, {}
    for copy in grad_copies:
        copy.wait()

    def spread_grads(m):
        half = scaled_all.at[m * slots : (m + 1) * slots, own_share]
        spread[m] = [wire.send(half, half, tp=t ^ k) for k in shares]

    for m in order[1:]:
        spread_grads(m)
    for copy in out_copies:
        copy.wait()
    for copy in arrivals:
        copy.wait()
    middle = hidden_ref[...].astype(F32) + mm(mixed[...], out_all[...], NT)
    middle_ref[...] = middle
    keep(middle_ref, middle_out)
    scale = lax.rsqrt(jnp.mean(middle * middle, axis=-1, keepdims=True) + NORM_EPS)
    normed = (middle * scale * gains_ref[1:2, :]).astype(BF16)
    far = {}
    cut = slots // 2 if slots % 32 == 0 else slots

    def block(m):
        return slice(m * slots, (m + 1) * slots)

    def pieces(m):
        return [slice(m * slots + k, m * slots + k + cut) for k in range(0, slots, cut)]

    for m in order[1:] + [0]:
        picked = mm(picker_rows_ref[block(m), :], normed).astype(BF16)
        if m:
            send_rows[m - 1] = picked
            far[m] = [
                wire.send(
                    send_rows.at[m - 1, here, own_share], rows_all.at[there, own_share], dp=d ^ m
                )
                for here, there in zip(pieces(0), pieces(m))
            ]
        else:
            rows_all[block(0), :] = picked
    lane = lax.broadcasted_iota(jnp.int32, (tokens, LANES), 1)

    def router_probs(values):
        logits = mm(values, lanes_ref[...])
        where = lax.broadcasted_iota(jnp.int32, logits.shape, 1)
        logits = jnp.where(where < experts, logits, NEG_FILL)
        powers = jnp.exp(logits - jnp.max(logits, axis=1, keepdims=True))
        return where, powers / jnp.sum(powers, axis=1, keepdims=True)

    probs[...] = router_probs(normed)[1]
    normed_flip[...] = normed.T
    for copy in weight_copies:
        copy.wait()
    downs[2].wait()
    downs[3] = wire.send(down_parts[2], down_parts[3], ctx=c ^ 1)
    downs[1].wait()
    downs[3].wait()
    columns = [pl.ds(pl.multiple_of((c ^ j) * depth, depth), depth) for j in range(ctx_count)]

    gates = {}

    def forward(m):
        for copy, piece in zip(far[m], pieces(m)):
            copy.wait()
            half = rows_all.at[piece, own_share]
            spread[m] += [wire.send(half, half, tp=t ^ k) for k in shares]

    def experts_on(m, hook):
        here = block(m)
        where, chance = router_probs(rows_all[here, :])
        gate = jnp.sum(jnp.where(where == d, chance, 0.0), axis=1, keepdims=True)
        rows = jnp.concatenate([rows_all[here, part] for part in columns], axis=1)
        grad_rows = jnp.concatenate([scaled_all[here, part] for part in columns], axis=1)
        rows_all[here, :] = rows
        scaled_all[here, :] = (gate * grad_rows.astype(F32)).astype(BF16)
        dots = jnp.zeros((slots, LANES), F32)
        for first in range(0, ff, FF_STEP):
            part = slice(first, min(ff, first + FF_STEP))
            value = mm(rows, in_all[0, :, part])
            up = mm(rows, in_all[1, :, part])
            back = mm(grad_rows, down_all[part, :], NT)
            bent, slope = bent_parts(value)
            act = (bent * up).astype(BF16)
            act_all[here, part] = act
            dots += jnp.sum(act.astype(F32) * back, axis=1, keepdims=True)
            scaled = gate * back
            gate_all[here, part] = (scaled * up * slope).astype(BF16)
            up_all[here, part] = (scaled * bent).astype(BF16)
        if hook is not None:
            hook()
        dot_parts[m] = dots.T[:8]
        dot_returned[m] = [
            wire.send(dot_parts.at[m], dot_in.at[k - 1, m], tp=t ^ k) for k in shares
        ]
        for k in list(shares) + [0]:
            for i in range(share // depth):
                piece = ((t ^ k) * (share // depth) + i) ^ c
                part = pl.ds(pl.multiple_of(piece * depth, depth), depth)
                row = mm(gate_all[here, :], in_all[0, part, :], NT)
                row += mm(up_all[here, :], in_all[1, part, :], NT)
                row_parts[k, m, :, i * depth : (i + 1) * depth] = row.astype(BF16)
            if k:
                returned.setdefault(m, []).append(
                    [
                        wire.send(row_parts.at[k, m, here], row_in.at[k - 1, m, here], tp=t ^ k)
                        for here in pieces(0)
                    ]
                )
        gates[m] = gate

    def outputs_of(m):
        here = block(m)
        for k in range(tp_count):
            for i in range(share // depth):
                piece = ((t ^ k) * (share // depth) + i) ^ c
                part = pl.ds(pl.multiple_of(piece * depth, depth), depth)
                out_parts[k, m, :, i * depth : (i + 1) * depth] = (
                    gates[m] * mm(act_all[here, :], down_all[:, part])
                ).astype(BF16)

    homeward, dots_homeward = [], []

    def send_home(m):
        for copy in dot_returned[m]:
            copy.wait()
        dots = tree_sum([dot_parts[m]] + [dot_in[k - 1, m] for k in shares])
        if m:
            dot_home[m] = dots
            dots_homeward.append(wire.send(dot_home.at[m], dot_back.at[m], dp=d ^ m))
        else:
            dot_back[0] = dots
        for i, (here, there) in enumerate(zip(pieces(0), pieces(m))):
            total = row_parts[0, m, here].astype(F32)
            for k, copies in zip(shares, returned[m]):
                copies[i].wait()
                total = total + row_in[k - 1, m, here].astype(F32)
            if m:
                row_parts[0, m, here] = total.astype(BF16)
                homeward.append(wire.send(row_parts.at[0, m, here], row_back.at[there], dp=d ^ m))
            else:
                row_back[there, :] = total.astype(BF16)

    for i, m in enumerate(order):
        for copy in spread.get(m, []):
            copy.wait()
            copy.sent()
        hook = functools.partial(forward, order[i + 1]) if i + 1 < len(order) else None
        experts_on(m, hook)
        if i:
            send_home(order[i - 1])

    def in_grads(j):
        part = slice(j * depth, (j + 1) * depth)
        for side, right in enumerate((gate_all, up_all)):
            in_all[side, part, :] = mm(rows_all[:, part], right[...], TN).astype(BF16)

    def part_of(j):
        return slice(j * depth, (j + 1) * depth)

    for m in order:
        outputs_of(m)
    out_copies = [
        wire.send(out_parts.at[k, m], out_in.at[k - 1, m], tp=t ^ k)
        for m in order[1:-1]
        for k in shares
    ]
    for k in range(tp_count):
        keep(out_parts.at[k, :2], near_parts[k])
    downs[3].sent()
    for first in range(0, ff, BLOCK):
        part = slice(first, min(ff, first + BLOCK))
        down_all[part, :] = mm(act_all[:, part], scaled_all[...], TN).astype(BF16)
    near = [
        wire.send(down_parts[3], down_land_far, ctx=c ^ 1),
        wire.send(down_parts[1], down_core, ctx=c ^ 1),
    ]
    keep(down_parts[0], down_keep)
    send_home(order[-1])
    in_grads(3)
    near.append(wire.send(in_all.at[:, part_of(3), :], in_land_far, ctx=c ^ 1))
    near[0].wait()
    down_all[:, part_of(2)] = (
        down_all[:, part_of(2)].astype(F32) + down_land_far[...].astype(F32)
    ).astype(BF16)
    near.append(wire.send(down_parts[2], down_far, ctx=c ^ 2))
    in_grads(1)
    near.append(wire.send(in_all.at[:, part_of(1), :], in_core, ctx=c ^ 1))
    in_grads(2)
    near[2].wait()
    for side in range(2):
        in_all[side, part_of(2), :] = (
            in_all[side, part_of(2), :].astype(F32) + in_land_far[side].astype(F32)
        ).astype(BF16)
    keep(in_all.at[:, part_of(2), :], in_sum)
    in_grads(0)
    keep(in_all.at[:, part_of(0), :], in_keep)

    for copy in dots_homeward:
        copy.wait()
    prob_grad = jnp.zeros((tokens, LANES), F32)
    for m in range(dp_count):
        high = dot_back[m].astype(BF16)
        rest = dot_back[m] - high.astype(F32)
        middle_part = rest.astype(BF16)
        tiny = (rest - middle_part.astype(F32)).astype(BF16)
        total = mm(picker_ref[:, block(m)], high, NT)
        total += mm(picker_ref[:, block(m)], middle_part, NT)
        total += mm(picker_ref[:, block(m)], tiny, NT)
        prob_grad = jnp.where(lane == (d ^ m), total[:, 0:1], prob_grad)
    chance = probs[...]
    logit = chance * (prob_grad - jnp.sum(chance * prob_grad, axis=1, keepdims=True))
    more = lax.dot_general(
        logit, lanes_ref[own_share, :].astype(F32), NT, precision=lax.Precision.HIGHEST,
        preferred_element_type=F32,
    )
    for copy in homeward:
        copy.wait()
    result = mm(picker_ref[...], row_back[...])
    whole[:, own_share] = (result + more).astype(BF16)
    arrivals = [wire.send(whole.at[:, own_share], whole.at[:, own_share], tp=t ^ k) for k in shares]
    logit_high = logit.astype(BF16)
    logit_rest = logit - logit_high.astype(F32)
    logit_low = logit_rest.astype(BF16)
    logit_tiny = (logit_rest - logit_low.astype(F32)).astype(BF16)
    router_grad = mm(normed_flip[...], logit_high)
    router_grad += mm(normed_flip[...], logit_low)
    router_grad += mm(normed_flip[...], logit_tiny)
    router_grad_ref[...] = router_grad
    for copy in out_copies:
        copy.wait()
    for m in range(2, dp_count):
        parts = [out_parts[0, m]] + [out_in[k - 1, m] for k in shares]
        out_sums[m - 2][...] = tree_sum([part.astype(F32) for part in parts]).astype(BF16)
    for copy in arrivals:
        copy.wait()
    middle = middle_ref[...]
    gradient = whole[...].astype(F32)
    scale = lax.rsqrt(jnp.mean(middle * middle, axis=-1, keepdims=True) + NORM_EPS)
    weighted = gains_ref[1:2, :] * gradient
    inner = jnp.mean(middle * weighted, axis=-1, keepdims=True)
    gain_ref[...] = fold_sum(gradient * middle * scale)
    total = out_grad_ref[...].astype(F32) + (
        scale * weighted - middle * (scale * scale * scale) * inner
    )
    grad_ref[...] = total
    low_ref[...] = total.astype(BF16)
    attended_grad_ref[...] = mm(low_ref[...], out_all[:, own_lanes]).astype(BF16)
    for copy in keeps:
        copy.wait()
    for copy in near:
        copy.wait()
    wire.finish()


def expert_step(
    firsts, attended, hidden, out_grad, gains, lanes, picker_flip, picker_rows, out, grads_own,
    grads, expert, expert_land, down, experts,
):
    dp_count, ctx_count, tp_count = (lax.axis_size(a) for a in ("dp", "ctx", "tp"))
    tokens, width = attended.shape[0], firsts[0].shape[1] + attended.shape[1]
    slots = grads_own.shape[0]
    share = D // tp_count
    depth, ff = expert.shape[1], expert.shape[2]
    all_slots = dp_count * slots
    others = tp_count - 1
    copies = others * (2 + 8 * dp_count) + 5 * dp_count + 8
    vmem = pl.BlockSpec(memory_space=pltpu.VMEM)
    hbm = pl.BlockSpec(memory_space=pl.ANY)
    shape = jax.ShapeDtypeStruct
    return pl.pallas_call(
        functools.partial(expert_kernel, experts, dp_count, ctx_count, tp_count),
        in_specs=[vmem] * 3 + [hbm] * 4 + [vmem] * tp_count + [hbm] * (4 + dp_count),
        out_specs=[hbm] + [vmem] * (3 + dp_count) + [hbm] * (tp_count + 7),
        out_shape=[
            shape((tokens, D), F32),
            shape((D, LANES), F32),
            shape((tokens, D), F32),
            shape((tokens, D), BF16),
            shape((tokens, width), BF16),
            shape((8, D), F32),
        ]
        + [shape((slots, share), BF16)] * (dp_count - 2)
        + [shape((2, slots, share), BF16)] * tp_count
        + [shape((tokens, width), BF16)]
        + [shape((2, depth, ff), BF16)] * 3
        + [shape((ff, depth), BF16)] * 3,
        scratch_shapes=[
            pltpu.VMEM((tokens, tp_count * width), BF16),
            pltpu.VMEM((D, tp_count * width), BF16),
            pltpu.VMEM((2, D, ff), BF16),
            pltpu.VMEM((ff, D), BF16),
            pltpu.VMEM((all_slots, D), BF16),
            pltpu.VMEM((all_slots, D), BF16),
            pltpu.VMEM((all_slots, ff), BF16),
            pltpu.VMEM((all_slots, ff), BF16),
            pltpu.VMEM((all_slots, ff), BF16),
            pltpu.VMEM((dp_count - 1, slots, D), BF16),
            pltpu.VMEM((tp_count, dp_count, slots, share), BF16),
            pltpu.VMEM((others, dp_count, slots, share), BF16),
            pltpu.VMEM((all_slots, share), BF16),
            pltpu.VMEM((dp_count, 8, slots), F32),
            pltpu.VMEM((others, dp_count, 8, slots), F32),
            pltpu.VMEM((dp_count, 8, slots), F32),
            pltpu.VMEM((dp_count, 8, slots), F32),
            pltpu.VMEM((tokens, LANES), F32),
            pltpu.VMEM((tokens, D), BF16),
            pltpu.VMEM((D, tokens), BF16),
            pltpu.VMEM((2, depth, ff), BF16),
            pltpu.VMEM((ff, depth), BF16),
            pltpu.VMEM((tp_count, dp_count, slots, share), BF16),
            pltpu.VMEM((others, dp_count, slots, share), BF16),
            pltpu.VMEM((tokens, D), BF16),
            pltpu.VMEM((tokens, D), BF16),
            pltpu.VMEM((tokens, all_slots), BF16),
            pltpu.VMEM((all_slots, tokens), BF16),
            pltpu.VMEM((tokens, D), F32),
            pltpu.SemaphoreType.DMA((copies,)),
            pltpu.SemaphoreType.DMA((copies,)),
            pltpu.SemaphoreType.DMA((6 + ctx_count + dp_count,)),
            pltpu.SemaphoreType.DMA((5 + tp_count,)),
        ],
        compiler_params=pltpu.CompilerParams(
            vmem_limit_bytes=VMEM_CAP, collective_id=3, has_side_effects=True
        ),
        cost_estimate=cost(120),
        name="expert_step",
    )(
        attended, gains, lanes, hidden, out_grad, picker_flip, picker_rows, *firsts, out,
        grads_own, *grads, expert, expert_land, down,
    )


def final_kernel(
    experts, dp_count, ctx_count, tp_count,
    key_ref, value_ref, gains_ref, gain_two_ref, bias_ref, *refs,
):
    late, refs = refs[:10], refs[10:]
    near_outs, refs = refs[:tp_count], refs[tp_count:]
    far_outs, refs = refs[: dp_count - 2], refs[dp_count - 2 :]
    (input_grad_ref, output_ref, bias_out_ref, first_ref, second_ref, tail_ref, out_back,
     mixed, bias_send, bias_in, near_in, far_send, far_in, rows_all, token_grad, token_in,
     gain_send, gain_in, out_send) = refs[:19]
    first, value, key = (refs[19 + 5 * k : 24 + 5 * k] for k in range(3))
    targets, refs = refs[34:44], refs[44:]
    (query_grad_ref, normed_ref, low_ref, attended_ref, weight_ref, hidden_ref,
     router_grad_ref, picker_ref, middle_ref, middle_grad_ref) = targets
    near_land, (sends, receives, late_sems, near_sems) = refs[:tp_count], refs[tp_count:]
    loads = [
        pltpu.make_async_copy(source, target, late_sems.at[k])
        for k, (source, target) in enumerate(zip(late, targets))
    ]
    near_loads = [
        pltpu.make_async_copy(source, target, near_sems.at[k])
        for k, (source, target) in enumerate(zip(near_outs, near_land))
    ]
    d, c, t = lax.axis_index("dp"), lax.axis_index("ctx"), lax.axis_index("tp")
    tokens, width = query_grad_ref.shape
    dp_bits = bits_down(dp_count)[::-1]
    assert ctx_count == 4
    halves = (0, 1)
    greet(
        [{"ctx": c ^ 1}, {"ctx": c ^ 2}]
        + [{"dp": d ^ bit} for bit in dp_bits]
        + [{"tp": t ^ k} for k in range(1, tp_count)]
    )
    wire = Wire(sends, receives)

    bias_steps = [{"ctx": c ^ 1}, {"ctx": c ^ 2}] + [{"dp": d ^ bit} for bit in dp_bits]
    bias_total, bias_copies = [bias_ref[...]], []

    def bias_begin():
        level = len(bias_copies)
        bias_send[level] = bias_total[-1]
        bias_copies.append(
            wire.send(bias_send.at[level], bias_in.at[level], **bias_steps[level])
        )

    def bias_end():
        level = len(bias_copies) - 1
        bias_copies[level].wait()
        bias_total.append(bias_total[-1] + bias_in[level])

    def split(values):
        return values.astype(BF16).reshape(dp_count, ctx_count, -1, values.shape[1])

    def cross(part):
        return [
            wire.send(part[0].at[:, c ^ (2 * k + 1)], part[1].at[k], ctx=c ^ 1) for k in halves
        ]

    def add_core(part, copies):
        for k, copy in zip(halves, copies):
            copy.wait()
            own = part[0][:, pl.ds(c ^ (2 * k), 1)][:, 0]
            part[2][k] = (own.astype(F32) + part[1][k].astype(F32)).astype(BF16)

    def dp_send(part, level, sides):
        copies, bit = [], dp_bits[level]
        for m in range(bit, dp_count, 2 * bit):
            for k in sides:
                spot = part[3].at[level, k, d ^ m]
                copies.append((m ^ bit, k, wire.send(part[2].at[k, d ^ m], spot, dp=d ^ bit)))
        return copies

    def dp_add(part, level, copies):
        for m, k, copy in copies:
            copy.wait()
            own = part[2][k, pl.ds(d ^ m, 1)][0]
            other = part[3][level, k, pl.ds(d ^ m, 1)][0]
            part[2][k, pl.ds(d ^ m, 1)] = (own.astype(F32) + other.astype(F32)).astype(BF16)[None]

    def x_send(part):
        return wire.send(part[2].at[1], part[4], ctx=c ^ 2)

    def x_add(part, copy):
        copy.wait()
        part[2][0] = (part[2][0].astype(F32) + part[4][...].astype(F32)).astype(BF16)

    bias_begin()
    sources = (value_ref, key_ref)
    near = [
        [
            wire.send(ref.at[(2 * k + 1) * tokens : (2 * k + 2) * tokens], near_in.at[side, k],
                      ctx=c ^ 1)
            for k in (1, 0)
        ]
        for side, ref in enumerate(sources)
    ]
    slots, share = out_send.shape
    far_loads = [
        pltpu.make_async_copy(
            source, out_back.at[(k + 2) * slots : (k + 3) * slots], near_sems.at[tp_count + k]
        )
        for k, source in enumerate(far_outs)
    ]
    for copy in near_loads + loads + far_loads:
        copy.start()
    for copy in near_loads:
        copy.wait()
    sums = [tree_sum([land[m].astype(F32) for land in near_land]) for m in range(2)]
    out_back[:slots, :] = sums[0].astype(BF16)
    out_send[...] = sums[1].astype(BF16)
    out_home = wire.send(out_send, out_back.at[slots : 2 * slots], dp=d ^ 1)
    far_copies = []
    for side, ref in enumerate(sources):
        for k, copy in zip((1, 0), near[side]):
            copy.wait()
            rows = slice(2 * k * tokens, (2 * k + 1) * tokens)
            far_send[side, k] = (
                ref[rows, :].astype(F32) + near_in[side, k].astype(F32)
            ).astype(BF16)
            if k:
                if side == 0:
                    bias_end()
                    bias_begin()
                far_copies.append(wire.send(far_send.at[side, 1], far_in.at[side], ctx=c ^ 2))

    for copy in loads[:5]:
        copy.wait()
    first[0][:, :, :, :width] = split(mm(normed_ref[...], query_grad_ref[...]))
    first[0][:, :, :, width:] = split(mm(low_ref[...], attended_ref[...], TN))
    first_crossed = cross(first)
    token_grad[...] = mm(query_grad_ref[...], weight_ref[:, :width], NT)
    add_core(first, first_crossed)
    bias_end()
    bias_begin()
    first_moving = dp_send(first, 0, halves)
    for copy in loads[5:]:
        copy.wait()
    out_home.wait()
    for copy in far_loads:
        copy.wait()
    own_share = pl.ds(pl.multiple_of(t * share, share), share)
    mixed[:, own_share] = mm(picker_ref[...], out_back[...]).astype(BF16)
    mixed_part = mixed.at[:, own_share]
    mixed_copies = [wire.send(mixed_part, mixed_part, tp=t ^ k) for k in range(1, tp_count)]

    def land(side, columns):
        far_copies[side].wait()
        rows_all[:, columns] = (
            far_send[side, 0].astype(F32) + far_in[side].astype(F32)
        ).astype(BF16)

    key_columns, value_columns = slice(width, 2 * width), slice(2 * width, 3 * width)
    land(0, value_columns)
    value[0][...] = split(mm(normed_ref[...], rows_all[:, value_columns]))
    value_crossed = cross(value)
    token_grad[...] += mm(rows_all[:, value_columns], weight_ref[:, value_columns], NT)
    add_core(value, value_crossed)
    value_far = x_send(value)
    inputs = hidden_ref[...].astype(F32)
    scale = lax.rsqrt(jnp.mean(inputs * inputs, axis=-1, keepdims=True) + NORM_EPS)

    land(1, key_columns)
    part = token_grad[...] + mm(rows_all[:, key_columns], weight_ref[:, key_columns], NT)
    part_low = part.astype(BF16)
    gain_send[0] = fold_sum(part_low.astype(F32) * inputs * scale)
    token_in[0] = part_low
    gain_total = gain_send[0]
    gain_copies, token_copies = [], []
    tp_bits = bits_down(tp_count)[::-1]
    gain_copies.append(wire.send(gain_send.at[0], gain_in.at[0], tp=t ^ tp_bits[0]))
    token_copies.append(wire.send(token_in.at[0], token_in.at[1], tp=t ^ tp_bits[0]))
    key[0][:, :, :, :width] = split(mm(normed_ref[...], rows_all[:, key_columns]))
    for level, bit in enumerate(tp_bits):
        if level:
            gain_send[level] = gain_total
            gain_copies.append(wire.send(gain_send.at[level], gain_in.at[level], tp=t ^ bit))
        gain_copies[level].wait()
        gain_total = gain_total + gain_in[level]
    gain_one = jnp.sum(gain_total, axis=0, keepdims=True)
    gain_two = jnp.sum(gain_two_ref[...], axis=0, keepdims=True)
    row = lax.broadcasted_iota(jnp.int32, (LANES, D), 0)
    gain_rows = jnp.where(row == experts, gain_one, jnp.where(row == experts + 1, gain_two, 0.0))
    key[0][:, :, :, width:] = split(router_grad_ref[...] + gain_rows.T)
    key_crossed = cross(key)
    add_core(key, key_crossed)
    key_far = x_send(key)

    moving = {}
    first_far = None
    for level in range(len(dp_bits)):
        dp_add(first, level, first_moving)
        bias_end()
        if level + 1 < len(dp_bits):
            bias_begin()
            first_moving = dp_send(first, level + 1, halves)
        else:
            first_far = wire.send(first[2].at[1, d], first[4], ctx=c ^ 2)
        for name, weights, copy in (("value", value, value_far), ("key", key, key_far)):
            if level == 0:
                x_add(weights, copy)
            else:
                dp_add(weights, level - 1, moving[name])
            moving[name] = dp_send(weights, level, [0])
    total = part_low.astype(F32)
    for level, bit in enumerate(tp_bits):
        if level:
            token_in[2 * level] = total.astype(BF16)
            total = token_in[2 * level].astype(F32)
            token_copies.append(
                wire.send(token_in.at[2 * level], token_in.at[2 * level + 1], tp=t ^ bit)
            )
        token_copies[level].wait()
        total = total + token_in[2 * level + 1].astype(F32)
    weighted = gains_ref[0:1, :] * total
    inner = jnp.mean(inputs * weighted, axis=-1, keepdims=True)
    input_grad_ref[...] = (
        middle_grad_ref[...] + scale * weighted - inputs * (scale * scale * scale) * inner
    )
    bias_out_ref[...] = bias_total[-1]
    first_far.wait()
    first_ref[...] = first[2][0, pl.ds(d, 1)][0].astype(F32) + first[4][...].astype(F32)
    last = len(dp_bits) - 1
    dp_add(value, last, moving["value"])
    second_ref[:, width:] = value[2][0, pl.ds(d, 1)][0].astype(F32)
    dp_add(key, last, moving["key"])
    result = key[2][0, pl.ds(d, 1)][0].astype(F32)
    second_ref[:, :width] = result[:, :width]
    rest = jnp.zeros((LANES - result.shape[0], LANES), F32)
    tail_ref[...] = jnp.concatenate([result[:, width:], rest], axis=0).T
    for copy in mixed_copies:
        copy.wait()
    output_ref[...] = middle_ref[...] + mixed[...].astype(F32)
    wire.finish()


def final_step(
    query_grad, key_part, value_part, normed, weight, low, attended, router_grad, hidden,
    gains, gain_two, middle_grad, middle, picker, bias, outs, experts,
):
    tokens, width = query_grad.shape
    slots, share = outs[0].shape[1:]
    dp_count, ctx_count, tp_count = (lax.axis_size(a) for a in ("dp", "ctx", "tp"))
    rows = D // (dp_count * ctx_count)
    levels = len(bits_down(dp_count))
    tp_levels = len(bits_down(tp_count))
    copies = 7 + 2 + levels + 3 * 2 + 4 * dp_count + 3 + 2 * tp_levels + tp_count
    hbm = pl.BlockSpec(memory_space=pl.ANY)
    vmem = pl.BlockSpec(memory_space=pltpu.VMEM)
    shape = jax.ShapeDtypeStruct

    late = (
        query_grad, normed, low, attended, weight, hidden, router_grad, picker, middle,
        middle_grad,
    )

    def buffers(columns, far_shape, sides):
        return [
            pltpu.VMEM((dp_count, ctx_count, rows, columns), BF16),
            pltpu.VMEM((2, dp_count, rows, columns), BF16),
            pltpu.VMEM((2, dp_count, rows, columns), BF16),
            pltpu.VMEM((levels, sides, dp_count, rows, columns), BF16),
            pltpu.VMEM(far_shape + (columns,), BF16),
        ]

    return pl.pallas_call(
        functools.partial(final_kernel, experts, dp_count, ctx_count, tp_count),
        in_specs=[vmem] * 5 + [hbm] * (10 + len(outs)),
        out_specs=[vmem] * 6,
        out_shape=[
            shape((tokens, D), F32),
            shape((tokens, D), F32),
            shape(bias.shape, F32),
            shape((rows, 2 * width), F32),
            shape((rows, 2 * width), F32),
            shape((LANES, LANES), F32),
        ],
        scratch_shapes=[
            pltpu.VMEM((dp_count * slots, share), BF16),
            pltpu.VMEM((tokens, D), BF16),
            pltpu.VMEM((2 + levels,) + bias.shape, F32),
            pltpu.VMEM((2 + levels,) + bias.shape, F32),
            pltpu.VMEM((2, 2, tokens, width), BF16),
            pltpu.VMEM((2, 2, tokens, width), BF16),
            pltpu.VMEM((2, tokens, width), BF16),
            pltpu.VMEM((tokens, 3 * width), BF16),
            pltpu.VMEM((tokens, D), F32),
            pltpu.VMEM((2 * tp_levels, tokens, D), BF16),
            pltpu.VMEM((tp_levels, 8, D), F32),
            pltpu.VMEM((tp_levels, 8, D), F32),
            pltpu.VMEM((slots, share), BF16),
        ]
        + buffers(2 * width, (rows,), 2)
        + buffers(width, (dp_count, rows), 1)
        + buffers(width + LANES, (dp_count, rows), 1)
        + [pltpu.VMEM(array.shape, array.dtype) for array in late]
        + [pltpu.VMEM((2, slots, share), BF16)] * tp_count
        + [
            pltpu.SemaphoreType.DMA((copies,)),
            pltpu.SemaphoreType.DMA((copies,)),
            pltpu.SemaphoreType.DMA((10,)),
            pltpu.SemaphoreType.DMA((tp_count + dp_count,)),
        ],
        compiler_params=pltpu.CompilerParams(
            vmem_limit_bytes=VMEM_CAP, collective_id=2, has_side_effects=True
        ),
        cost_estimate=cost(87),
        name="final_step",
    )(key_part, value_part, gains, gain_two, bias, *late, *outs)


def adam_kernel(*refs):
    weight, first, second = refs[:3]
    parts, outs = refs[3:-4], refs[-4:]
    gradient = parts[0][...].astype(F32) + parts[1][...].astype(F32) + parts[2][...].astype(F32)
    first_new = BETA_ONE * first[...] + (1.0 - BETA_ONE) * gradient
    second_new = BETA_TWO * second[...] + (1.0 - BETA_TWO) * gradient * gradient
    outs[0][...] = gradient
    outs[1][...] = first_new
    outs[2][...] = second_new
    outs[3][...] = -MAIN_RATE * (
        first_new * (1.0 / FIX_ONE) / (jnp.sqrt(second_new * (1.0 / FIX_TWO)) + ADAM_EPS)
        + WEIGHT_DECAY * weight[...].astype(F32)
    )


def adam(weight, first, second, kept, arrived, far):
    count, rows, columns = weight.shape
    sizes = [size for size in range(16, rows + 1, 16) if rows % size == 0]
    step = max(k for k in sizes if k * columns <= 400000 and count * rows >= 2 * k)
    plain = pl.BlockSpec((1, step, columns), lambda i, j: (i, j, 0))
    shape = jax.ShapeDtypeStruct(weight.shape, F32)
    return pl.pallas_call(
        adam_kernel,
        grid=(count, rows // step),
        in_specs=[plain] * 6,
        out_specs=[plain] * 4,
        out_shape=[shape] * 4,
        compiler_params=pltpu.CompilerParams(vmem_limit_bytes=VMEM_CAP),
        cost_estimate=cost(5),
        name="adam",
    )(weight, first, second, kept, arrived, far)


def small_adam_kernel(experts, pairs, *refs):
    first_ref, second_ref, tail_ref, bias_ref = refs[:4]
    inputs, outs = refs[4:19], refs[19:]

    def step(k, gradient, part, rate):
        weight, first, second = (ref[part].astype(F32) for ref in inputs[3 * k : 3 * k + 3])
        first_new = BETA_ONE * first + (1.0 - BETA_ONE) * gradient
        second_new = BETA_TWO * second + (1.0 - BETA_TWO) * gradient * gradient
        update = -rate * (
            first_new * (1.0 / FIX_ONE) / (jnp.sqrt(second_new * (1.0 / FIX_TWO)) + ADAM_EPS)
            + WEIGHT_DECAY * weight
        )
        for out, values in zip(
            outs[4 * k : 4 * k + 4], (gradient, first_new, second_new, update)
        ):
            out[part] = values

    rows, width = inputs[3].shape
    whole = slice(None)
    step(0, first_ref[:, :width], 0, MAIN_RATE)
    step(0, second_ref[:, :width], 1, MAIN_RATE)
    step(0, second_ref[:, width:], 2, MAIN_RATE)
    step(1, first_ref[:, width:], whole, MAIN_RATE)
    step(2, tail_ref[:experts, :rows], whole, MAIN_RATE)
    step(3, tail_ref[experts : experts + 2, :rows], whole, MAIN_RATE)
    bias = jnp.concatenate([bias_ref[p, :2] for p in range(pairs)], axis=0)
    step(4, bias, whole, BIAS_RATE)


def small_adam(first_total, second_total, tail_total, bias_total, triples, experts):
    flat = [array for triple in triples for array in triple]
    vmem = pl.BlockSpec(memory_space=pltpu.VMEM)
    results = pl.pallas_call(
        functools.partial(small_adam_kernel, experts, bias_total.shape[0]),
        in_specs=[vmem] * (4 + len(flat)),
        out_specs=[vmem] * (4 * len(triples)),
        out_shape=[
            jax.ShapeDtypeStruct(triple[0].shape, F32) for triple in triples for _ in range(4)
        ],
        compiler_params=pltpu.CompilerParams(vmem_limit_bytes=VMEM_CAP),
        cost_estimate=cost(2),
        name="small_adam",
    )(first_total, second_total, tail_total, bias_total, *flat)
    return [results[4 * k : 4 * k + 4] for k in range(len(triples))]


def shards(
    hidden_in,
    out_grad,
    segments,
    routes,
    bucket_table,
    qkv_weight,
    out_weight,
    router,
    norm_gains,
    position_bias,
    expert_in,
    expert_down,
    qkv_first,
    qkv_second,
    out_first,
    out_second,
    router_first,
    router_second,
    gains_first,
    gains_second,
    bias_first,
    bias_second,
    in_first,
    in_second,
    down_first,
    down_second,
):
    tokens = hidden_in.shape[0]
    dp_count, ctx_count, tp_count = (lax.axis_size(a) for a in ("dp", "ctx", "tp"))
    dp_place, ctx_place, tp_place = (lax.axis_index(a) for a in ("dp", "ctx", "tp"))
    length = tokens * ctx_count
    heads_here = position_bias.shape[0]
    width_here = heads_here * HEAD_DIM
    pairs = heads_here // 2
    expert_count = router.shape[1]
    top_count = routes.shape[1]
    own_rows = router.shape[0]

    capacity = max(2, min(tokens, 5 * top_count * tokens // (4 * expert_count)))
    window_width = tokens + length
    table = jnp.pad(bucket_table[::-1], (0, 1), constant_values=BUCKETS)
    table = lax.dynamic_slice(table, (ctx_place * tokens,), (window_width,))
    table = jnp.broadcast_to(table[None], (8, window_width))
    qkv_view = [array.transpose(1, 0, 2) for array in (qkv_weight, qkv_first, qkv_second)]
    out_view = [array.T for array in (out_weight, out_first, out_second)]
    router_view = [array.T for array in (router, router_first, router_second)]
    (queries, key_values, normed_flip, qkv_flat, out_own, lanes, gains, info, doc_row, doc_col,
     picker_flip, picker_rows, grads_own, grads_half, early_land, expert_land) = start(
        qkv_view[0], out_view[0], router_view[0], norm_gains, hidden_in, segments, routes.T,
        out_grad, expert_in[0], capacity,
    )
    early = early_blocks(dp_count)
    arrived = [
        early_land[early.index(m)] if m in early else swap(grads_half[m - 1], "dp", m)
        for m in range(1, dp_count)
    ]
    half = pairs // 2
    attended_first, totals = attention(
        info, queries, key_values, position_bias, table, doc_row, doc_col, 0, half, ()
    )
    first_sides = gather_xor(attended_first, "tp")
    attended_second, totals = attention(
        info, queries, key_values, position_bias, table, doc_row, doc_col, half, pairs - half,
        (totals,),
    )
    results = expert_step(
        first_sides, attended_second, hidden_in, out_grad, gains, lanes, picker_flip, picker_rows,
        out_own, grads_own, arrived, expert_in[0], expert_land, expert_down[0], expert_count,
    )
    middle, router_grad, middle_grad, middle_low, attended_grad, gain_two_grad = results[:6]
    out_sums, results = results[6 : 4 + dp_count], results[4 + dp_count :]
    near_parts, results = results[:tp_count], results[tp_count:]
    attended, in_keep, in_core, in_sum, down_keep, down_core, down_far = results

    in_far = swap(in_sum, "ctx", 2)
    out_far = [swap(near_parts[k], "tp", k) for k in range(1, tp_count)]
    out_far += [swap(out_sums[m - 2], "dp", m) for m in range(2, dp_count)]
    query_grad, key_part, value_part, bias_part = attention_back(
        info, queries, key_values, attended_grad, totals, position_bias, table, doc_row, doc_col
    )
    query_grad, in_far, out_far = lax.optimization_barrier((query_grad, in_far, out_far))
    input_grad, output, bias_total, first_total, second_total, tail_total = final_step(
        query_grad, key_part, value_part, normed_flip, qkv_flat, middle_low, attended,
        router_grad, hidden_in, gains, gain_two_grad, middle_grad, middle, picker_flip, bias_part,
        [near_parts[0]] + out_far, expert_count,
    )
    qkv_all, out_new, router_new, gains_new, bias_new = small_adam(
        first_total, second_total, tail_total, bias_total,
        [
            qkv_view,
            out_view,
            router_view,
            (norm_gains, gains_first, gains_second),
            (position_bias, bias_first, bias_second),
        ],
        expert_count,
    )
    in_new = [
        values[None]
        for values in adam(
            expert_in[0], in_first[0], in_second[0], in_keep, in_core, in_far
        )
    ]
    down_new = adam(
        expert_down, down_first, down_second, down_keep[None], down_core[None], down_far[None]
    )
    return (
        output,
        input_grad,
        *[array.transpose(1, 0, 2) for array in qkv_all],
        *[array.T for array in out_new],
        *[array.T for array in router_new],
        *gains_new,
        *bias_new,
        *in_new,
        *down_new,
    )


def solution(mesh):
    token_rows = P(("dp", "ctx"), None)
    qkv = P(("dp", "ctx"), None, "tp")
    out = P("tp", ("dp", "ctx"))
    gains = P(None, ("dp", "ctx"))
    bias = P("tp", None)
    expert_in = P("dp", None, "ctx", "tp")
    expert_down = P("dp", "tp", "ctx")
    placed = (
        token_rows, token_rows, P("dp", "ctx"), token_rows, P(),
        qkv, out, token_rows, gains, bias, expert_in, expert_down,
        qkv, qkv, out, out, token_rows, token_rows, gains, gains, bias, bias,
        expert_in, expert_in, expert_down, expert_down,
    )
    return jax.shard_map(
        shards,
        mesh=mesh,
        in_specs=placed,
        out_specs=(token_rows, token_rows)
        + (qkv,) * 4
        + (out,) * 4
        + (token_rows,) * 4
        + (gains,) * 4
        + (bias,) * 4
        + (expert_in,) * 4
        + (expert_down,) * 4,
        check_vma=False,
    )
```

```python
import functools

import jax
import jax.numpy as jnp
from jax import lax
from jax.experimental import pallas as pl
from jax.experimental.pallas import tpu as pltpu
from jax.sharding import PartitionSpec as P

D = 1024
HEAD_DIM = 64
BUCKETS = 32

NORM_EPS = 1e-06
NEG_FILL = -1e30
BETA_ONE = 0.9
BETA_TWO = 0.95
FIX_ONE = 1.0 - 0.9**10
FIX_TWO = 1.0 - 0.95**10
ADAM_EPS = 1e-08
WEIGHT_DECAY = 0.1
MAIN_RATE = 0.02
BIAS_RATE = 0.2

F32 = jnp.float32
BF16 = jnp.bfloat16
LANES = 128
BLOCK = 256
FF_STEP = 256
VMEM_CAP = 60 * 1024 * 1024
GELU_K = 0.7978845608028654
GELU_C = 0.044715


def tree_sum(values):
    while len(values) > 1:
        values = [values[k] + values[k + 1] for k in range(0, len(values), 2)]
    return values[0]


def rms_scale(values):
    return lax.rsqrt(jnp.mean(values * values, axis=-1, keepdims=True) + NORM_EPS)


def norm_back(values, scale_here, gain_here, gradient):
    weighted = gain_here * gradient
    row_inner = jnp.mean(values * weighted, axis=-1, keepdims=True)
    input_part = scale_here * weighted - values * scale_here**3 * row_inner
    return (input_part, jnp.sum(gradient * values * scale_here, axis=0))


def adamw_step(weight, gradient, first_moment, second_moment, step_rate):
    first_new = BETA_ONE * first_moment + (1.0 - BETA_ONE) * gradient
    second_new = BETA_TWO * second_moment + (1.0 - BETA_TWO) * gradient * gradient
    update = -step_rate * (
        first_new / FIX_ONE / (jnp.sqrt(second_new / FIX_TWO) + ADAM_EPS) + WEIGHT_DECAY * weight
    )
    return (first_new, second_new, update)


def cost(micros):
    return pl.CostEstimate(flops=int(micros * 1.15e9), bytes_accessed=1 << 20, transcendentals=0)


def swap(values, axis, bits):
    count = lax.axis_size(axis)
    return lax.ppermute(values, axis, [(i, i ^ bits) for i in range(count)])


def gather_xor(values, axis):
    pieces = {0: values}
    bit = lax.axis_size(axis) >> 1
    while bit:
        for key in list(pieces):
            pieces[key | bit] = swap(pieces[key], axis, bit)
        bit >>= 1
    return [pieces[m] for m in range(len(pieces))]


def scatter_sum(parts, axis):
    live = dict(enumerate(parts))
    bit = 1
    while bit < lax.axis_size(axis):
        left = {}
        for key in live:
            if key & bit == 0:
                moved = swap(live[key | bit].astype(BF16), axis, bit)
                left[key] = live[key].astype(F32) + moved.astype(F32)
        live = left
        bit <<= 1
    return live[0]


def all_sum(values, axis):
    bit = 1
    while bit < lax.axis_size(axis):
        values = values + swap(values, axis, bit)
        bit <<= 1
    return values


def in_order(pieces, place, dim):
    bit = 1
    while bit < len(pieces):
        odd = (place & bit) > 0
        pieces = [jnp.where(odd, pieces[m ^ bit], pieces[m]) for m in range(len(pieces))]
        bit <<= 1
    return jnp.concatenate(pieces, axis=dim)


MESH = pl.DeviceIdType.MESH


class Wire:
    def __init__(self, sends, receives):
        self.sends, self.receives, self.count, self.copies = sends, receives, 0, []

    def send(self, source, target, **device):
        copy = pltpu.make_async_remote_copy(
            src_ref=source,
            dst_ref=target,
            send_sem=self.sends.at[self.count],
            recv_sem=self.receives.at[self.count],
            device_id=device,
            device_id_type=MESH,
        )
        copy.start()
        self.count += 1
        self.copies.append(Arrival(copy))
        return self.copies[-1]

    def finish(self):
        for copy in self.copies:
            copy.sent()


class Arrival:
    def __init__(self, copy):
        self.copy, self.waited, self.gone = copy, False, False

    def sent(self):
        if not self.gone:
            self.copy.wait_send()
        self.gone = True

    def wait(self):
        if not self.waited:
            self.copy.wait_recv()
        self.waited = True


def greet(partners):
    barrier = pltpu.get_barrier_semaphore()
    for device in partners:
        pl.semaphore_signal(barrier, inc=1, device_id=device, device_id_type=MESH)
    pl.semaphore_wait(barrier, len(partners))


def bits_down(count):
    bits, bit = [], count >> 1
    while bit:
        bits.append(bit)
        bit >>= 1
    return bits


def xor_order(count):
    order = [0]
    for bit in bits_down(count):
        order = order + [k | bit for k in order]
    return order


NT = (((1,), (1,)), ((), ()))
NN = (((1,), (0,)), ((), ()))
TN = (((0,), (0,)), ((), ()))


def mm(left, right, dims=NN):
    return lax.dot_general(left, right, dims, preferred_element_type=F32)


def fold_max(values):
    return jnp.max(values.reshape(values.shape[0] // 8, 8, values.shape[1]), axis=0)


def fold_sum(values):
    return jnp.sum(values.reshape(values.shape[0] // 8, 8, values.shape[1]), axis=0)


def skewed(row):
    width = row.shape[1]
    tall = jnp.broadcast_to(row, (LANES, width))
    return pltpu.roll(tall, width - (LANES - 1), 1, stride=1, stride_axis=0)


def unskew_sum(field):
    half = field.shape[0] // 2
    while half >= 1:
        field = pltpu.roll(field[:half], half, 1) + field[half:]
        half //= 2
    return field


def head_masks(rows):
    lane = lax.broadcasted_iota(jnp.int32, (rows, LANES), 1)
    return [(lane < HEAD_DIM).astype(BF16), (lane >= HEAD_DIM).astype(BF16)]


def score_tile(key_block, query_head, skew_ref, head, first, same):
    scores = mm(key_block, query_head, NT)
    tiles = []
    for s in range(BLOCK // LANES):
        column = pl.multiple_of(first - s * LANES, LANES)
        tiles.append(skew_ref[head, :, pl.ds(column, BLOCK)])
    return jnp.where(same, scores + jnp.concatenate(tiles, axis=0), NEG_FILL)


def bucket_lanes(table_ref):
    row = lax.broadcasted_iota(jnp.int32, (BUCKETS, table_ref.shape[1]), 0)
    return (row == table_ref[0:1, :]).astype(F32)


def spread_bias(bias_ref, table_ref, skew_ref, first=0):
    rows = bias_ref[pl.ds((pl.program_id(0) + first) * 2, 2), :]
    window = jnp.dot(
        jnp.concatenate([rows] * 4, axis=0), bucket_lanes(table_ref),
        precision=lax.Precision.HIGHEST, preferred_element_type=F32,
    )
    for h in range(2):
        skew_ref[h] = skewed(window[h : h + 1, :])


def over_blocks(info_ref, qb, query_blocks, step):
    @pl.loop(0, info_ref[query_blocks + qb, 0])
    def _(i):
        blocks = [info_ref[qb, 2 * i + k] for k in range(2)]
        step(
            [pl.ds(pl.multiple_of(kb * BLOCK, BLOCK), BLOCK) for kb in blocks],
            [info_ref[2 * query_blocks, kb] + qb * BLOCK for kb in blocks],
        )


def attention_kernel(
    first, info_ref, query_ref, key_ref, value_ref, bias_ref, table_ref, doc_row_ref,
    doc_col_ref, *refs,
):
    out_ref, total_ref, skew_ref, flip_ref, score_ref, most_ref, sum_ref, mix_ref = refs[-8:]
    tokens, length = query_ref.shape[0], key_ref.shape[0]
    key_blocks, query_blocks = length // BLOCK, tokens // BLOCK
    masks = head_masks(BLOCK)
    spread_bias(bias_ref, table_ref, skew_ref, first)

    @pl.loop(0, key_blocks)
    def _(kb):
        rows = pl.ds(pl.multiple_of(kb * BLOCK, BLOCK), BLOCK)
        flip_ref[:, rows] = value_ref[rows, :].T

    for qb in range(query_blocks):
        here = slice(qb * BLOCK, (qb + 1) * BLOCK)
        pair = query_ref[here, :] * jnp.asarray(HEAD_DIM**-0.5, BF16)
        query_heads = [pair * mask for mask in masks]
        doc_row = doc_row_ref[0:1, here]
        most_ref[...] = jnp.full_like(most_ref, NEG_FILL)
        sum_ref[...] = jnp.zeros_like(sum_ref)
        mix_ref[...] = jnp.zeros_like(mix_ref)

        def scores(spans, firsts):
            for rows, first_column in zip(spans, firsts):
                column = doc_col_ref[rows, :]
                same = jnp.concatenate([column] * (BLOCK // LANES), axis=1) == doc_row
                for h in range(2):
                    tile = score_tile(
                        key_ref[rows, :], query_heads[h], skew_ref, h, first_column, same
                    )
                    score_ref[h, rows, :] = tile
                    most_ref[h] = jnp.maximum(most_ref[h], fold_max(tile))

        over_blocks(info_ref, qb, query_blocks, scores)
        most = [jnp.max(most_ref[h], axis=0, keepdims=True) for h in range(2)]

        def mixes(spans, firsts):
            for h in range(2):
                heads = slice(h * HEAD_DIM, (h + 1) * HEAD_DIM)
                total, mix = sum_ref[h], mix_ref[h]
                for rows in spans:
                    weights = jnp.exp(score_ref[h, rows, :] - most[h])
                    total += fold_sum(weights)
                    mix += mm(flip_ref[heads, rows], weights.astype(BF16))
                sum_ref[h] = total
                mix_ref[h] = mix

        over_blocks(info_ref, qb, query_blocks, mixes)
        columns = []
        for h in range(2):
            total = jnp.sum(sum_ref[h], axis=0, keepdims=True)
            columns.append(mix_ref[h] / total)
            total_ref[0, h : h + 1, here] = most[h] + jnp.log(total)
        out_ref[here, :] = jnp.concatenate(columns, axis=0).T.astype(BF16)


def attention_back_kernel(
    info_ref, query_ref, key_ref, value_ref, grad_ref, total_ref, bias_ref, table_ref,
    doc_row_ref, doc_col_ref,
    query_grad_ref, key_grad_ref, value_grad_ref, bias_grad_ref,
    skew_ref, field_ref, flip_ref, weight_ref, change_ref, inner_ref, mix_ref, key_sum, value_sum,
):
    tokens, length = query_ref.shape[0], key_ref.shape[0]
    key_blocks, query_blocks = length // BLOCK, tokens // BLOCK
    masks = head_masks(BLOCK)
    spread_bias(bias_ref, table_ref, skew_ref)
    field_ref[...] = jnp.zeros_like(field_ref)
    key_sum[...] = jnp.zeros_like(key_sum)
    value_sum[...] = jnp.zeros_like(value_sum)

    @pl.loop(0, key_blocks)
    def _(kb):
        rows = pl.ds(pl.multiple_of(kb * BLOCK, BLOCK), BLOCK)
        flip_ref[:, rows] = key_ref[rows, :].T

    for qb in range(query_blocks):
        here = slice(qb * BLOCK, (qb + 1) * BLOCK)
        pair = query_ref[here, :] * jnp.asarray(HEAD_DIM**-0.5, BF16)
        query_heads = [pair * mask for mask in masks]
        grad_pair = grad_ref[here, :]
        grad_heads = [grad_pair * mask for mask in masks]
        doc_row = doc_row_ref[0:1, here]
        inner_ref[...] = jnp.zeros_like(inner_ref)
        mix_ref[...] = jnp.zeros_like(mix_ref)
        totals = [total_ref[0, h : h + 1, here] for h in range(2)]

        def changes(spans, firsts):
            for rows, first_column in zip(spans, firsts):
                column = doc_col_ref[rows, :]
                same = jnp.concatenate([column] * (BLOCK // LANES), axis=1) == doc_row
                for h in range(2):
                    tile = score_tile(
                        key_ref[rows, :], query_heads[h], skew_ref, h, first_column, same
                    )
                    weights = jnp.exp(tile - totals[h])
                    change = mm(value_ref[rows, :], grad_heads[h], NT)
                    weight_ref[h, rows, :] = weights
                    change_ref[h, rows, :] = change
                    inner_ref[h] += fold_sum(weights * change)

        over_blocks(info_ref, qb, query_blocks, changes)
        inner = [jnp.sum(inner_ref[h], axis=0, keepdims=True) for h in range(2)]

        def gradients(spans, firsts):
            mixes = [mix_ref[h] for h in range(2)]
            for rows, first_column in zip(spans, firsts):
                key_part = value_part = None
                for h in range(2):
                    weights = weight_ref[h, rows, :]
                    score_grad = weights * (change_ref[h, rows, :] - inner[h])
                    for s in range(BLOCK // LANES):
                        first = pl.multiple_of(first_column - s * LANES, LANES)
                        field_ref[h, :, pl.ds(first, BLOCK)] += score_grad[
                            s * LANES : (s + 1) * LANES
                        ]
                    low = score_grad.astype(BF16)
                    key_here = mm(low, query_heads[h])
                    value_here = mm(weights.astype(BF16), grad_heads[h])
                    key_part = key_here if h == 0 else key_part + key_here
                    value_part = value_here if h == 0 else value_part + value_here
                    heads = slice(h * HEAD_DIM, (h + 1) * HEAD_DIM)
                    mixes[h] += mm(flip_ref[heads, rows], low)
                key_sum[rows, :] += key_part
                value_sum[rows, :] += value_part
            for h in range(2):
                mix_ref[h] = mixes[h]

        over_blocks(info_ref, qb, query_blocks, gradients)
        both = jnp.concatenate([mix_ref[0], mix_ref[1]], axis=0) * HEAD_DIM**-0.5
        query_grad_ref[here, :] = both.T.astype(BF16)

    key_grad_ref[...] = key_sum[...].astype(BF16)
    value_grad_ref[...] = value_sum[...].astype(BF16)
    offsets = jnp.concatenate([unskew_sum(field_ref[h]) for h in range(2)] * 4, axis=0)
    bias_grad_ref[0] = lax.dot_general(
        offsets, bucket_lanes(table_ref), NT, precision=lax.Precision.HIGHEST,
        preferred_element_type=F32,
    )


def attention_specs(tokens, length, pairs, heads, width, first=0):
    smem = pl.BlockSpec(memory_space=pltpu.SMEM)
    return dict(
        info=smem,
        query=pl.BlockSpec((tokens, LANES), lambda i: (0, i + first)),
        key=pl.BlockSpec((length, LANES), lambda i: (0, i + first)),
        value=pl.BlockSpec((length, LANES), lambda i: (0, i + first + pairs)),
        bias=pl.BlockSpec((heads, BUCKETS), lambda i: (0, 0)),
        table=pl.BlockSpec((8, width), lambda i: (0, 0)),
        total=pl.BlockSpec((1, 8, tokens), lambda i: (i + first, 0, 0)),
        bias_grad=pl.BlockSpec((1, 8, BUCKETS), lambda i: (i, 0, 0)),
        doc_row=pl.BlockSpec((8, tokens), lambda i: (0, 0)),
        doc_col=pl.BlockSpec((length, LANES), lambda i: (0, 0)),
    )


def attention(info, queries, key_values, bias, table, doc_row, doc_col, first, count, held):
    tokens, length = queries.shape[0], key_values.shape[0]
    pairs, width = bias.shape[0] // 2, table.shape[1]
    specs = attention_specs(tokens, length, pairs, bias.shape[0], width, first)
    return pl.pallas_call(
        functools.partial(attention_kernel, first),
        grid=(count,),
        in_specs=[
            specs["info"], specs["query"], specs["key"], specs["value"], specs["bias"],
            specs["table"], specs["doc_row"], specs["doc_col"],
        ]
        + [pl.BlockSpec(memory_space=pl.ANY)] * len(held),
        out_specs=[pl.BlockSpec((tokens, LANES), lambda i: (0, i)), specs["total"]],
        out_shape=[
            jax.ShapeDtypeStruct((tokens, count * LANES), BF16),
            jax.ShapeDtypeStruct((pairs, 8, tokens), F32),
        ],
        scratch_shapes=[
            pltpu.VMEM((2, LANES, width), F32),
            pltpu.VMEM((LANES, length), BF16),
            pltpu.VMEM((2, length, BLOCK), F32),
            pltpu.VMEM((2, 8, BLOCK), F32),
            pltpu.VMEM((2, 8, BLOCK), F32),
            pltpu.VMEM((2, HEAD_DIM, BLOCK), F32),
        ],
        input_output_aliases={8: 1} if held else {},
        compiler_params=pltpu.CompilerParams(vmem_limit_bytes=VMEM_CAP),
        cost_estimate=cost(20 if first == 0 else 1),
        name="attention_forward",
    )(info, queries, key_values, key_values, bias, table, doc_row, doc_col, *held)


def attention_back(info, queries, key_values, grads, totals, bias, table, doc_row, doc_col):
    tokens, length = queries.shape[0], key_values.shape[0]
    pairs, width = bias.shape[0] // 2, table.shape[1]
    specs = attention_specs(tokens, length, pairs, bias.shape[0], width)
    return pl.pallas_call(
        attention_back_kernel,
        grid=(pairs,),
        in_specs=[
            specs["info"], specs["query"], specs["key"], specs["value"], specs["query"],
            specs["total"], specs["bias"], specs["table"], specs["doc_row"], specs["doc_col"],
        ],
        out_specs=[specs["query"], specs["key"], specs["key"], specs["bias_grad"]],
        out_shape=[
            jax.ShapeDtypeStruct(queries.shape, BF16),
            jax.ShapeDtypeStruct((length, queries.shape[1]), BF16),
            jax.ShapeDtypeStruct((length, queries.shape[1]), BF16),
            jax.ShapeDtypeStruct((pairs, 8, BUCKETS), F32),
        ],
        scratch_shapes=[
            pltpu.VMEM((2, LANES, width), F32),
            pltpu.VMEM((2, LANES, width), F32),
            pltpu.VMEM((LANES, length), BF16),
            pltpu.VMEM((2, length, BLOCK), F32),
            pltpu.VMEM((2, length, BLOCK), F32),
            pltpu.VMEM((2, 8, BLOCK), F32),
            pltpu.VMEM((2, HEAD_DIM, BLOCK), F32),
            pltpu.VMEM((length, LANES), F32),
            pltpu.VMEM((length, LANES), F32),
        ],
        compiler_params=pltpu.CompilerParams(vmem_limit_bytes=VMEM_CAP),
        cost_estimate=cost(40),
        name="attention_backward",
    )(info, queries, key_values, key_values, grads, totals, bias, table, doc_row, doc_col)


def start_kernel(
    experts, dp_count, ctx_count, tp_count, qkv_ref, out_flip_ref, router_ref, gain_pair_ref,
    hidden_ref, segments_ref, routes_ref, out_grad_hbm, expert_ref,
    query_ref, pair_out, normed_flip_ref, weight_out, own_ref, lanes_ref, gains_ref, info_ref,
    row_ref, column_out, picker_out, picker_rows_out, grads_own_out, grads_out, early_land,
    expert_land,
    weights, out_all, hidden, docs, docs_ref, flip, pair_ref, column_ref, picker_ref,
    picker_rows_ref, grads_own_ref, grads_ref, out_grad_ref, sends, receives, out_sem, in_sem,
):
    d, c, t = lax.axis_index("dp"), lax.axis_index("ctx"), lax.axis_index("tp")
    rows = out_flip_ref.shape[0]
    tokens, width = query_ref.shape
    early = early_blocks(dp_count)
    out_grad_load = pltpu.make_async_copy(out_grad_hbm, out_grad_ref, in_sem)
    out_grad_load.start()
    stores = []

    def store(source, target):
        copy = pltpu.make_async_copy(source, target, out_sem.at[len(stores)])
        copy.start()
        stores.append(copy)

    own_rows = pl.ds(pl.multiple_of((d * ctx_count + c) * rows, rows), rows)
    own_lanes = pl.ds(pl.multiple_of(t * width, width), width)
    for part in range(3):
        weights[own_rows, part * width : (part + 1) * width] = qkv_ref[part]
    out_all[own_rows, own_lanes] = out_flip_ref[...]
    flip[...] = jnp.zeros_like(flip)
    flip[:experts, :rows] = router_ref[...].astype(F32)
    flip[experts : experts + 2, :rows] = gain_pair_ref[...].astype(F32)
    weights[own_rows, 3 * width :] = flip[:, :LANES].T[:rows].astype(BF16)
    docs_ref[...] = jnp.broadcast_to(segments_ref[...], docs_ref.shape)
    row_ref[...] = docs_ref[...]
    greet(
        [{"ctx": c ^ m} for m in range(1, ctx_count)]
        + [{"dp": d ^ m} for m in sorted(set(bits_down(dp_count) + early))]
        + [{"tp": t ^ k} for k in range(1, tp_count)]
    )
    wire = Wire(sends, receives)
    share = grads_ref.shape[2]
    own_share = pl.ds(pl.multiple_of(t * share, share), share)

    def send_shard(m, j, part, lanes=own_lanes, **device):
        index = (d ^ m) * ctx_count + (c ^ j)
        here = pl.ds(pl.multiple_of(index * rows, rows), rows)
        shard = out_all.at[here, lanes] if part else weights.at[here]
        return wire.send(shard, shard, **device)

    docs_sent = [wire.send(docs_ref, docs.at[m], ctx=c ^ m) for m in range(1, ctx_count)]
    sides, sides_far = [0], []
    parts = (0, 1)
    arrivals = {part: [] for part in range(2)}
    hidden_sent, expert_sent = {}, {}
    for bit in bits_down(ctx_count)[:-1]:
        arrivals = {
            k: [send_shard(0, j, part, ctx=c ^ bit) for j in sides]
            for k, part in enumerate(parts)
        }
        assert bit == 2
        half = hidden_ref.at[:, own_share]
        hidden_sent[2] = wire.send(half, hidden.at[2, :, own_share], ctx=c ^ 2)
        for m in [0] + list(expert_sent):
            if m:
                expert_sent[m].wait()
            source = expert_land.at[m - 1] if m else expert_ref
            expert_sent[m | bit] = wire.send(source, expert_land.at[(m | bit) - 1], ctx=c ^ bit)
        for copy in arrivals[0]:
            copy.wait()
        sides_far = sides + [j | bit for j in sides]
        if bit != 2:
            for copy in arrivals[1]:
                copy.wait()
        sides = sides_far
    hidden_sent[1] = wire.send(hidden_ref, hidden.at[1], ctx=c ^ 1)

    order = xor_order(dp_count)
    groups = [{}, {}]
    crossed, beside = [[], []], []

    def onward(k, m):
        for copy in groups[k].get(m, []):
            copy.wait()
        for bit in bits_down(dp_count):
            if m & (2 * bit - 1) == 0:
                groups[k][m | bit] = [send_shard(m, j, parts[k], dp=d ^ bit) for j in sides]
        crossed[k] += [send_shard(m, j, parts[k], ctx=c ^ 1) for j in sides]
        if k:
            for other in range(1, tp_count):
                beside.append(
                    (m, other, [send_shard(m, j, 1, tp=t ^ other) for j in sides])
                )

    onward(0, 0)
    expert_sent[1] = wire.send(expert_ref, expert_land.at[0], ctx=c ^ 1)

    lane = lax.broadcasted_iota(jnp.int32, (tokens, LANES), 1)
    flip[:8, :] = jnp.zeros((8, tokens), F32)
    flip[: routes_ref.shape[0], :] = routes_ref[...].astype(F32)
    routes = flip[...].T
    tops = [routes[:, k : k + 1].astype(jnp.int32) for k in range(routes_ref.shape[0])]
    named = jnp.zeros((tokens, LANES), F32)
    for top in tops:
        named = jnp.where(lane == top, 1.0, named)
    row_index = lax.broadcasted_iota(jnp.int32, (tokens, tokens), 0)
    column_index = lax.broadcasted_iota(jnp.int32, (tokens, tokens), 1)
    before = jnp.where(column_index < row_index, 1.0, 0.0).astype(BF16)
    earlier = mm(before, named.astype(BF16))
    slots = grads_own_ref.shape[0]
    column = lax.broadcasted_iota(jnp.int32, picker_ref.shape, 1)
    picker = jnp.zeros(picker_ref.shape, F32)
    for top in tops:
        place = jnp.sum(jnp.where(lane == top, earlier, 0.0), axis=1, keepdims=True)
        place = place.astype(jnp.int32)
        target = jnp.where(place < slots, (top ^ d) * slots + place, -1)
        picker = jnp.where(column == target, 1.0, picker)
    picker_ref[...] = picker.astype(BF16)
    picker_rows_ref[...] = picker_ref[...].T
    hidden_sent[2].wait()
    half = hidden.at[2, :, own_share]
    spread = [wire.send(half, half, tp=t ^ k) for k in range(1, tp_count)]
    out_grad_load.wait()
    for m in range(dp_count):
        chosen = picker_rows_ref[m * slots : (m + 1) * slots, :]
        if m:
            grads_ref[m - 1] = mm(chosen, out_grad_ref[:, own_share]).astype(BF16)
        else:
            grads_own_ref[...] = mm(chosen, out_grad_ref[...]).astype(BF16)

    store(picker_ref, picker_out)
    store(picker_rows_ref, picker_rows_out)
    store(grads_own_ref, grads_own_out)
    store(grads_ref, grads_out)

    key_blocks, query_blocks = tokens // BLOCK, tokens // BLOCK
    where = lax.broadcasted_iota(jnp.int32, info_ref.shape, 1)
    which = lax.broadcasted_iota(jnp.int32, info_ref.shape, 0)
    info = jnp.zeros(info_ref.shape, jnp.int32)
    met = [[] for _ in range(query_blocks)]
    for m in range(ctx_count):
        if m:
            docs_sent[m - 1].wait()
        row = docs[m] if m else docs_ref[...]
        tall = jnp.broadcast_to(row[0:1, :].astype(F32), (LANES, tokens))
        column_ref[m * tokens : (m + 1) * tokens, :] = tall.T.astype(jnp.int32)
        for k in range(key_blocks):
            spot = m * key_blocks + k
            low = row[0:1, k * BLOCK : k * BLOCK + 1]
            high = row[0:1, (k + 1) * BLOCK - 1 : (k + 1) * BLOCK]
            for q in range(query_blocks):
                query_low = docs_ref[0:1, q * BLOCK : q * BLOCK + 1]
                query_high = docs_ref[0:1, (q + 1) * BLOCK - 1 : (q + 1) * BLOCK]
                meets = ((high >= query_low) & (low <= query_high)).astype(jnp.int32)
                met[q].append(meets)
            base = (ctx_count * tokens - LANES) - ((c ^ m) * tokens + k * BLOCK)
            info = jnp.where((where == spot) & (which == 2 * query_blocks), base, info)
    for q in range(query_blocks):
        count = sum(met[q][1:], met[q][0])
        inside, outside = jnp.zeros_like(count), count
        for spot, meets in enumerate(met[q]):
            place = jnp.where(meets > 0, inside, outside)
            info = jnp.where((where == place) & (which == q), spot, info)
            inside, outside = inside + meets, outside + (1 - meets)
        steps = lax.shift_right_logical(count + 1, 1)
        info = jnp.where(which == query_blocks + q, steps, info)
    info_ref[...] = info
    store(column_ref, column_out)

    early_copies = []
    for i, m in enumerate(order[1:]):
        onward(0, m)
        if i == 0:
            for copy in arrivals[1]:
                copy.wait()
            onward(1, 0)
    for i, m in enumerate(order[1:]):
        onward(1, m)
        if i == 0:
            early_copies = [
                wire.send(grads_ref.at[n - 1], early_land.at[k], dp=d ^ n)
                for k, n in enumerate(early)
            ]
    for copy in spread:
        copy.wait()
    hidden_sent[3] = wire.send(hidden.at[2], hidden.at[3], ctx=c ^ 1)
    for copy in crossed[0]:
        copy.wait()
    store(weights.at[:, : 3 * width], weight_out)
    small = weights[:, 3 * width : 3 * width + LANES].astype(F32)
    lane = lax.broadcasted_iota(jnp.int32, small.shape, 1)
    lanes_ref[...] = jnp.where(lane < experts, small, 0.0).astype(BF16)
    gain_one = jnp.sum(jnp.where(lane == experts, small, 0.0), axis=1, keepdims=True)
    gain_two = jnp.sum(jnp.where(lane == experts + 1, small, 0.0), axis=1, keepdims=True)
    both = jnp.where(lane == 0, gain_one, jnp.where(lane == 1, gain_two, 0.0)).T
    gains_ref[...] = both[:8]
    gain = both[0:1]
    for m in range(ctx_count):
        if m:
            hidden_sent[m].wait()
        values = (hidden[m] if m else hidden_ref[...]).astype(F32)
        scale = lax.rsqrt(jnp.mean(values * values, axis=-1, keepdims=True) + NORM_EPS)
        normed = (values * scale * gain).astype(BF16)
        pair_ref[m * tokens : (m + 1) * tokens, :] = mm(
            normed, weights[:, width : 3 * width]
        ).astype(BF16)
        here = pl.ds(m * tokens, tokens)
        store(pair_ref.at[here], pair_out.at[here])
        if m == 0:
            normed_flip_ref[...] = normed.T
            query_ref[...] = mm(normed, weights[:, :width]).astype(BF16)
            for n, other, copies in beside:
                for copy in copies:
                    copy.wait()
                lanes = pl.ds(pl.multiple_of((t ^ other) * width, width), width)
                crossed[1] += [send_shard(n, j, 1, lanes, ctx=c ^ 1) for j in sides]
    for copy in crossed[1]:
        copy.wait()
    store(out_all, own_ref)
    for k in [k for k in expert_sent if k > 1]:
        expert_sent[k].wait()
        expert_sent[k | 1] = wire.send(expert_land.at[k - 1], expert_land.at[k], ctx=c ^ 1)
    for k in range(1, ctx_count):
        expert_sent[k].wait()
    for copy in early_copies:
        copy.wait()
    for copy in stores:
        copy.wait()
    wire.finish()


def early_blocks(dp_count):
    return list(range(2, dp_count))[:1]


def start(qkv, out_flip, router, gain_pair, hidden, segments, routes, out_grad, expert, slots):
    tokens, (experts, _), width = hidden.shape[0], router.shape, qkv.shape[2]
    columns = 4 * width + LANES
    dp_count, ctx_count, tp_count = (lax.axis_size(a) for a in ("dp", "ctx", "tp"))
    copies = 5 * ctx_count + (2 + tp_count) * dp_count * ctx_count + tp_count + dp_count + 1
    vmem = pl.BlockSpec(memory_space=pltpu.VMEM)
    hbm = pl.BlockSpec(memory_space=pl.ANY)
    shape = jax.ShapeDtypeStruct
    return pl.pallas_call(
        functools.partial(start_kernel, experts, dp_count, ctx_count, tp_count),
        in_specs=[vmem] * 7 + [hbm] * 2,
        out_specs=[vmem, hbm, vmem] + [hbm] * 2 + [vmem] * 4 + [hbm] * 7,
        out_shape=[
            shape((tokens, width), BF16),
            shape((tokens * ctx_count, 2 * width), BF16),
            shape((D, tokens), BF16),
            shape((D, 3 * width), BF16),
            shape((D, tp_count * width), BF16),
            shape((D, LANES), BF16),
            shape((8, D), F32),
            shape((8, LANES), jnp.int32),
            shape((8, tokens), jnp.int32),
            shape((tokens * ctx_count, LANES), jnp.int32),
            shape((tokens, dp_count * slots), BF16),
            shape((dp_count * slots, tokens), BF16),
            shape((slots, D), BF16),
            shape((dp_count - 1, slots, D // tp_count), BF16),
            shape((len(early_blocks(dp_count)), slots, D // tp_count), BF16),
            shape((ctx_count - 1,) + expert.shape, BF16),
        ],
        scratch_shapes=[
            pltpu.VMEM((D, columns - width), BF16),
            pltpu.VMEM((D, tp_count * width), BF16),
            pltpu.VMEM((ctx_count, tokens, D), BF16),
            pltpu.VMEM((ctx_count, 8, tokens), jnp.int32),
            pltpu.VMEM((8, tokens), jnp.int32),
            pltpu.VMEM((LANES, tokens), F32),
            pltpu.VMEM((tokens * ctx_count, 2 * width), BF16),
            pltpu.VMEM((tokens * ctx_count, LANES), jnp.int32),
            pltpu.VMEM((tokens, dp_count * slots), BF16),
            pltpu.VMEM((dp_count * slots, tokens), BF16),
            pltpu.VMEM((slots, D), BF16),
            pltpu.VMEM((dp_count - 1, slots, D // tp_count), BF16),
            pltpu.VMEM((tokens, D), BF16),
            pltpu.SemaphoreType.DMA((copies,)),
            pltpu.SemaphoreType.DMA((copies,)),
            pltpu.SemaphoreType.DMA((7 + ctx_count,)),
            pltpu.SemaphoreType.DMA(()),
        ],
        compiler_params=pltpu.CompilerParams(
            vmem_limit_bytes=VMEM_CAP, collective_id=1, has_side_effects=True
        ),
        cost_estimate=cost(60),
        name="start",
    )(qkv, out_flip, router, gain_pair, hidden, segments, routes, out_grad, expert)


def bent_parts(value):
    square = value * value
    wave = jnp.tanh(GELU_K * value * (1.0 + GELU_C * square))
    half = 0.5 * (1.0 + wave)
    slope = half + 0.5 * value * (1.0 - wave * wave) * (GELU_K * (1.0 + 3.0 * GELU_C * square))
    return value * half, slope


def expert_kernel(
    experts, dp_count, ctx_count, tp_count, attended_ref, gains_ref, lanes_ref, hidden_hbm,
    out_grad_hbm, picker_hbm, picker_rows_hbm, *refs,
):
    d, c, t = lax.axis_index("dp"), lax.axis_index("ctx"), lax.axis_index("tp")
    firsts, refs = refs[:tp_count], refs[tp_count:]
    out_ref, grads_own, refs = refs[0], refs[1], refs[2:]
    grads_land, refs = refs[: dp_count - 1], refs[dp_count - 1 :]
    in_own, in_land, refs = refs[0], refs[1], refs[2:]
    ins = [in_own] + [in_land.at[j] for j in range(ctx_count - 1)]
    down_own, refs = refs[0], refs[1:]
    middle_out, router_grad_ref, grad_ref, low_ref, attended_grad_ref, gain_ref = refs[:6]
    out_sums, refs = refs[6 : 4 + dp_count], refs[4 + dp_count :]
    near_parts, refs = refs[:tp_count], refs[tp_count:]
    (attended_out, in_keep, in_core, in_sum, down_keep, down_core, down_far,
     mixed, out_all, in_all, down_all, rows_all, scaled_all, act_all, gate_all, up_all, send_rows,
     row_parts, row_in, row_back, dot_parts, dot_in, dot_home, dot_back, probs, whole,
     normed_flip, in_land_far, down_land_far, out_parts, out_in, hidden_ref, out_grad_ref,
     picker_ref, picker_rows_ref, middle_ref, sends, receives, in_sems, keep_sems) = refs
    tokens, second_width = attended_ref.shape
    first_width = firsts[0].shape[1]
    width = first_width + second_width
    share = D // tp_count
    slots = rows_all.shape[0] // dp_count
    depth, ff = in_own.shape[1], in_own.shape[2]
    shares = range(1, tp_count)
    order = [0] + list(range(2, dp_count)) + [1]

    local = []

    def load(source, target):
        copy = pltpu.make_async_copy(source, target, in_sems.at[len(local)])
        copy.start()
        local.append(copy)
        return copy

    keeps = []

    def keep(source, target):
        copy = pltpu.make_async_copy(source, target, keep_sems.at[len(keeps)])
        copy.start()
        keeps.append(copy)

    out_copies = [
        load(out_ref, out_all),
        load(hidden_hbm, hidden_ref),
        load(picker_rows_hbm, picker_rows_ref),
    ]
    weight_copies, down_parts = [], []
    for j in range(ctx_count):
        part = slice(j * depth, (j + 1) * depth)
        weight_copies.append(load(ins[j], in_all.at[:, part, :]))
        down_parts.append(down_all.at[:, part])
    weight_copies.append(load(down_own, down_parts[0]))
    weight_copies.append(load(picker_hbm, picker_ref))
    weight_copies.append(load(out_grad_hbm, out_grad_ref))
    own_share = pl.ds(pl.multiple_of(t * share, share), share)
    weight_copies.append(load(grads_own, scaled_all.at[:slots]))
    grad_copies = [
        load(grads_land[m - 1], scaled_all.at[m * slots : (m + 1) * slots, own_share])
        for m in range(1, dp_count)
    ]
    own_lanes = pl.ds(pl.multiple_of(t * width, width), width)
    second_lanes = pl.ds(pl.multiple_of(t * width + first_width, LANES), second_width)
    mixed[:, second_lanes] = attended_ref[...]
    for m in range(tp_count):
        start = pl.multiple_of((t ^ m) * width, width)
        mixed[:, pl.ds(start, first_width)] = firsts[m][...]
    keep(mixed.at[:, own_lanes], attended_out)
    greet(
        [{"tp": t ^ k} for k in shares]
        + [{"dp": d ^ m} for m in range(1, dp_count)]
        + [{"ctx": c ^ 1}, {"ctx": c ^ 2}]
    )
    wire = Wire(sends, receives)
    assert ctx_count == 4
    downs = {j: wire.send(down_own, down_parts[j], ctx=c ^ j) for j in (2, 1)}
    second_part = mixed.at[:, second_lanes]
    arrivals = [wire.send(second_part, second_part, tp=t ^ k) for k in shares]
    spread, returned, dot_returned = {}, {}, {}
    for copy in grad_copies:
        copy.wait()

    def spread_grads(m):
        half = scaled_all.at[m * slots : (m + 1) * slots, own_share]
        spread[m] = [wire.send(half, half, tp=t ^ k) for k in shares]

    for m in order[1:]:
        spread_grads(m)
    for copy in out_copies:
        copy.wait()
    for copy in arrivals:
        copy.wait()
    middle = hidden_ref[...].astype(F32) + mm(mixed[...], out_all[...], NT)
    middle_ref[...] = middle
    keep(middle_ref, middle_out)
    scale = lax.rsqrt(jnp.mean(middle * middle, axis=-1, keepdims=True) + NORM_EPS)
    normed = (middle * scale * gains_ref[1:2, :]).astype(BF16)
    far = {}
    cut = slots // 2 if slots % 32 == 0 else slots

    def block(m):
        return slice(m * slots, (m + 1) * slots)

    def pieces(m):
        return [slice(m * slots + k, m * slots + k + cut) for k in range(0, slots, cut)]

    for m in order[1:] + [0]:
        picked = mm(picker_rows_ref[block(m), :], normed).astype(BF16)
        if m:
            send_rows[m - 1] = picked
            far[m] = [
                wire.send(
                    send_rows.at[m - 1, here, own_share], rows_all.at[there, own_share], dp=d ^ m
                )
                for here, there in zip(pieces(0), pieces(m))
            ]
        else:
            rows_all[block(0), :] = picked
    lane = lax.broadcasted_iota(jnp.int32, (tokens, LANES), 1)

    def router_probs(values):
        logits = mm(values, lanes_ref[...])
        where = lax.broadcasted_iota(jnp.int32, logits.shape, 1)
        logits = jnp.where(where < experts, logits, NEG_FILL)
        powers = jnp.exp(logits - jnp.max(logits, axis=1, keepdims=True))
        return where, powers / jnp.sum(powers, axis=1, keepdims=True)

    probs[...] = router_probs(normed)[1]
    normed_flip[...] = normed.T
    for copy in weight_copies:
        copy.wait()
    downs[2].wait()
    downs[3] = wire.send(down_parts[2], down_parts[3], ctx=c ^ 1)
    downs[1].wait()
    downs[3].wait()
    columns = [pl.ds(pl.multiple_of((c ^ j) * depth, depth), depth) for j in range(ctx_count)]

    gates = {}

    def forward(m):
        for copy, piece in zip(far[m], pieces(m)):
            copy.wait()
            half = rows_all.at[piece, own_share]
            spread[m] += [wire.send(half, half, tp=t ^ k) for k in shares]

    def experts_on(m, hook):
        here = block(m)
        where, chance = router_probs(rows_all[here, :])
        gate = jnp.sum(jnp.where(where == d, chance, 0.0), axis=1, keepdims=True)
        rows = jnp.concatenate([rows_all[here, part] for part in columns], axis=1)
        grad_rows = jnp.concatenate([scaled_all[here, part] for part in columns], axis=1)
        rows_all[here, :] = rows
        scaled_all[here, :] = (gate * grad_rows.astype(F32)).astype(BF16)
        dots = jnp.zeros((slots, LANES), F32)
        for first in range(0, ff, FF_STEP):
            part = slice(first, min(ff, first + FF_STEP))
            value = mm(rows, in_all[0, :, part])
            up = mm(rows, in_all[1, :, part])
            back = mm(grad_rows, down_all[part, :], NT)
            bent, slope = bent_parts(value)
            act = (bent * up).astype(BF16)
            act_all[here, part] = act
            dots += jnp.sum(act.astype(F32) * back, axis=1, keepdims=True)
            scaled = gate * back
            gate_all[here, part] = (scaled * up * slope).astype(BF16)
            up_all[here, part] = (scaled * bent).astype(BF16)
        if hook is not None:
            hook()
        dot_parts[m] = dots.T[:8]
        dot_returned[m] = [
            wire.send(dot_parts.at[m], dot_in.at[k - 1, m], tp=t ^ k) for k in shares
        ]
        for k in list(shares) + [0]:
            for i in range(share // depth):
                piece = ((t ^ k) * (share // depth) + i) ^ c
                part = pl.ds(pl.multiple_of(piece * depth, depth), depth)
                row = mm(gate_all[here, :], in_all[0, part, :], NT)
                row += mm(up_all[here, :], in_all[1, part, :], NT)
                row_parts[k, m, :, i * depth : (i + 1) * depth] = row.astype(BF16)
            if k:
                returned.setdefault(m, []).append(
                    [
                        wire.send(row_parts.at[k, m, here], row_in.at[k - 1, m, here], tp=t ^ k)
                        for here in pieces(0)
                    ]
                )
        gates[m] = gate

    def outputs_of(m):
        here = block(m)
        for k in range(tp_count):
            for i in range(share // depth):
                piece = ((t ^ k) * (share // depth) + i) ^ c
                part = pl.ds(pl.multiple_of(piece * depth, depth), depth)
                out_parts[k, m, :, i * depth : (i + 1) * depth] = (
                    gates[m] * mm(act_all[here, :], down_all[:, part])
                ).astype(BF16)

    homeward, dots_homeward = [], []

    def send_home(m):
        for copy in dot_returned[m]:
            copy.wait()
        dots = tree_sum([dot_parts[m]] + [dot_in[k - 1, m] for k in shares])
        if m:
            dot_home[m] = dots
            dots_homeward.append(wire.send(dot_home.at[m], dot_back.at[m], dp=d ^ m))
        else:
            dot_back[0] = dots
        for i, (here, there) in enumerate(zip(pieces(0), pieces(m))):
            total = row_parts[0, m, here].astype(F32)
            for k, copies in zip(shares, returned[m]):
                copies[i].wait()
                total = total + row_in[k - 1, m, here].astype(F32)
            if m:
                row_parts[0, m, here] = total.astype(BF16)
                homeward.append(wire.send(row_parts.at[0, m, here], row_back.at[there], dp=d ^ m))
            else:
                row_back[there, :] = total.astype(BF16)

    for i, m in enumerate(order):
        for copy in spread.get(m, []):
            copy.wait()
            copy.sent()
        hook = functools.partial(forward, order[i + 1]) if i + 1 < len(order) else None
        experts_on(m, hook)
        if i:
            send_home(order[i - 1])

    def in_grads(j):
        part = slice(j * depth, (j + 1) * depth)
        for side, right in enumerate((gate_all, up_all)):
            in_all[side, part, :] = mm(rows_all[:, part], right[...], TN).astype(BF16)

    def part_of(j):
        return slice(j * depth, (j + 1) * depth)

    for m in order:
        outputs_of(m)
    out_copies = [
        wire.send(out_parts.at[k, m], out_in.at[k - 1, m], tp=t ^ k)
        for m in order[1:-1]
        for k in shares
    ]
    for k in range(tp_count):
        keep(out_parts.at[k, :2], near_parts[k])
    downs[3].sent()
    for first in range(0, ff, BLOCK):
        part = slice(first, min(ff, first + BLOCK))
        down_all[part, :] = mm(act_all[:, part], scaled_all[...], TN).astype(BF16)
    near = [
        wire.send(down_parts[3], down_land_far, ctx=c ^ 1),
        wire.send(down_parts[1], down_core, ctx=c ^ 1),
    ]
    keep(down_parts[0], down_keep)
    send_home(order[-1])
    in_grads(3)
    near.append(wire.send(in_all.at[:, part_of(3), :], in_land_far, ctx=c ^ 1))
    near[0].wait()
    down_all[:, part_of(2)] = (
        down_all[:, part_of(2)].astype(F32) + down_land_far[...].astype(F32)
    ).astype(BF16)
    near.append(wire.send(down_parts[2], down_far, ctx=c ^ 2))
    in_grads(1)
    near.append(wire.send(in_all.at[:, part_of(1), :], in_core, ctx=c ^ 1))
    in_grads(2)
    near[2].wait()
    for side in range(2):
        in_all[side, part_of(2), :] = (
            in_all[side, part_of(2), :].astype(F32) + in_land_far[side].astype(F32)
        ).astype(BF16)
    keep(in_all.at[:, part_of(2), :], in_sum)
    in_grads(0)
    keep(in_all.at[:, part_of(0), :], in_keep)

    for copy in dots_homeward:
        copy.wait()
    prob_grad = jnp.zeros((tokens, LANES), F32)
    for m in range(dp_count):
        high = dot_back[m].astype(BF16)
        rest = dot_back[m] - high.astype(F32)
        middle_part = rest.astype(BF16)
        tiny = (rest - middle_part.astype(F32)).astype(BF16)
        total = mm(picker_ref[:, block(m)], high, NT)
        total += mm(picker_ref[:, block(m)], middle_part, NT)
        total += mm(picker_ref[:, block(m)], tiny, NT)
        prob_grad = jnp.where(lane == (d ^ m), total[:, 0:1], prob_grad)
    chance = probs[...]
    logit = chance * (prob_grad - jnp.sum(chance * prob_grad, axis=1, keepdims=True))
    more = lax.dot_general(
        logit, lanes_ref[own_share, :].astype(F32), NT, precision=lax.Precision.HIGHEST,
        preferred_element_type=F32,
    )
    for copy in homeward:
        copy.wait()
    result = mm(picker_ref[...], row_back[...])
    whole[:, own_share] = (result + more).astype(BF16)
    arrivals = [wire.send(whole.at[:, own_share], whole.at[:, own_share], tp=t ^ k) for k in shares]
    logit_high = logit.astype(BF16)
    logit_rest = logit - logit_high.astype(F32)
    logit_low = logit_rest.astype(BF16)
    logit_tiny = (logit_rest - logit_low.astype(F32)).astype(BF16)
    router_grad = mm(normed_flip[...], logit_high)
    router_grad += mm(normed_flip[...], logit_low)
    router_grad += mm(normed_flip[...], logit_tiny)
    router_grad_ref[...] = router_grad
    for copy in out_copies:
        copy.wait()
    for m in range(2, dp_count):
        parts = [out_parts[0, m]] + [out_in[k - 1, m] for k in shares]
        out_sums[m - 2][...] = tree_sum([part.astype(F32) for part in parts]).astype(BF16)
    for copy in arrivals:
        copy.wait()
    middle = middle_ref[...]
    gradient = whole[...].astype(F32)
    scale = lax.rsqrt(jnp.mean(middle * middle, axis=-1, keepdims=True) + NORM_EPS)
    weighted = gains_ref[1:2, :] * gradient
    inner = jnp.mean(middle * weighted, axis=-1, keepdims=True)
    gain_ref[...] = fold_sum(gradient * middle * scale)
    total = out_grad_ref[...].astype(F32) + (
        scale * weighted - middle * (scale * scale * scale) * inner
    )
    grad_ref[...] = total
    low_ref[...] = total.astype(BF16)
    attended_grad_ref[...] = mm(low_ref[...], out_all[:, own_lanes]).astype(BF16)
    for copy in keeps:
        copy.wait()
    for copy in near:
        copy.wait()
    wire.finish()


def expert_step(
    firsts, attended, hidden, out_grad, gains, lanes, picker_flip, picker_rows, out, grads_own,
    grads, expert, expert_land, down, experts,
):
    dp_count, ctx_count, tp_count = (lax.axis_size(a) for a in ("dp", "ctx", "tp"))
    tokens, width = attended.shape[0], firsts[0].shape[1] + attended.shape[1]
    slots = grads_own.shape[0]
    share = D // tp_count
    depth, ff = expert.shape[1], expert.shape[2]
    all_slots = dp_count * slots
    others = tp_count - 1
    copies = others * (2 + 8 * dp_count) + 5 * dp_count + 8
    vmem = pl.BlockSpec(memory_space=pltpu.VMEM)
    hbm = pl.BlockSpec(memory_space=pl.ANY)
    shape = jax.ShapeDtypeStruct
    return pl.pallas_call(
        functools.partial(expert_kernel, experts, dp_count, ctx_count, tp_count),
        in_specs=[vmem] * 3 + [hbm] * 4 + [vmem] * tp_count + [hbm] * (4 + dp_count),
        out_specs=[hbm] + [vmem] * (3 + dp_count) + [hbm] * (tp_count + 7),
        out_shape=[
            shape((tokens, D), F32),
            shape((D, LANES), F32),
            shape((tokens, D), F32),
            shape((tokens, D), BF16),
            shape((tokens, width), BF16),
            shape((8, D), F32),
        ]
        + [shape((slots, share), BF16)] * (dp_count - 2)
        + [shape((2, slots, share), BF16)] * tp_count
        + [shape((tokens, width), BF16)]
        + [shape((2, depth, ff), BF16)] * 3
        + [shape((ff, depth), BF16)] * 3,
        scratch_shapes=[
            pltpu.VMEM((tokens, tp_count * width), BF16),
            pltpu.VMEM((D, tp_count * width), BF16),
            pltpu.VMEM((2, D, ff), BF16),
            pltpu.VMEM((ff, D), BF16),
            pltpu.VMEM((all_slots, D), BF16),
            pltpu.VMEM((all_slots, D), BF16),
            pltpu.VMEM((all_slots, ff), BF16),
            pltpu.VMEM((all_slots, ff), BF16),
            pltpu.VMEM((all_slots, ff), BF16),
            pltpu.VMEM((dp_count - 1, slots, D), BF16),
            pltpu.VMEM((tp_count, dp_count, slots, share), BF16),
            pltpu.VMEM((others, dp_count, slots, share), BF16),
            pltpu.VMEM((all_slots, share), BF16),
            pltpu.VMEM((dp_count, 8, slots), F32),
            pltpu.VMEM((others, dp_count, 8, slots), F32),
            pltpu.VMEM((dp_count, 8, slots), F32),
            pltpu.VMEM((dp_count, 8, slots), F32),
            pltpu.VMEM((tokens, LANES), F32),
            pltpu.VMEM((tokens, D), BF16),
            pltpu.VMEM((D, tokens), BF16),
            pltpu.VMEM((2, depth, ff), BF16),
            pltpu.VMEM((ff, depth), BF16),
            pltpu.VMEM((tp_count, dp_count, slots, share), BF16),
            pltpu.VMEM((others, dp_count, slots, share), BF16),
            pltpu.VMEM((tokens, D), BF16),
            pltpu.VMEM((tokens, D), BF16),
            pltpu.VMEM((tokens, all_slots), BF16),
            pltpu.VMEM((all_slots, tokens), BF16),
            pltpu.VMEM((tokens, D), F32),
            pltpu.SemaphoreType.DMA((copies,)),
            pltpu.SemaphoreType.DMA((copies,)),
            pltpu.SemaphoreType.DMA((6 + ctx_count + dp_count,)),
            pltpu.SemaphoreType.DMA((5 + tp_count,)),
        ],
        compiler_params=pltpu.CompilerParams(
            vmem_limit_bytes=VMEM_CAP, collective_id=3, has_side_effects=True
        ),
        cost_estimate=cost(120),
        name="expert_step",
    )(
        attended, gains, lanes, hidden, out_grad, picker_flip, picker_rows, *firsts, out,
        grads_own, *grads, expert, expert_land, down,
    )


def final_kernel(
    experts, dp_count, ctx_count, tp_count,
    key_ref, value_ref, gains_ref, gain_two_ref, bias_ref, *refs,
):
    late, refs = refs[:10], refs[10:]
    near_outs, refs = refs[:tp_count], refs[tp_count:]
    far_outs, refs = refs[: dp_count - 2], refs[dp_count - 2 :]
    (input_grad_ref, output_ref, bias_out_ref, first_ref, second_ref, tail_ref, out_back,
     mixed, bias_send, bias_in, near_in, far_send, far_in, rows_all, token_grad, token_in,
     gain_send, gain_in, out_send) = refs[:19]
    first, value, key = (refs[19 + 5 * k : 24 + 5 * k] for k in range(3))
    targets, refs = refs[34:44], refs[44:]
    (query_grad_ref, normed_ref, low_ref, attended_ref, weight_ref, hidden_ref,
     router_grad_ref, picker_ref, middle_ref, middle_grad_ref) = targets
    near_land, (sends, receives, late_sems, near_sems) = refs[:tp_count], refs[tp_count:]
    loads = [
        pltpu.make_async_copy(source, target, late_sems.at[k])
        for k, (source, target) in enumerate(zip(late, targets))
    ]
    near_loads = [
        pltpu.make_async_copy(source, target, near_sems.at[k])
        for k, (source, target) in enumerate(zip(near_outs, near_land))
    ]
    d, c, t = lax.axis_index("dp"), lax.axis_index("ctx"), lax.axis_index("tp")
    tokens, width = query_grad_ref.shape
    dp_bits = bits_down(dp_count)[::-1]
    assert ctx_count == 4
    halves = (0, 1)
    greet(
        [{"ctx": c ^ 1}, {"ctx": c ^ 2}]
        + [{"dp": d ^ bit} for bit in dp_bits]
        + [{"tp": t ^ k} for k in range(1, tp_count)]
    )
    wire = Wire(sends, receives)

    bias_steps = [{"ctx": c ^ 1}, {"ctx": c ^ 2}] + [{"dp": d ^ bit} for bit in dp_bits]
    bias_total, bias_copies = [bias_ref[...]], []

    def bias_begin():
        level = len(bias_copies)
        bias_send[level] = bias_total[-1]
        bias_copies.append(
            wire.send(bias_send.at[level], bias_in.at[level], **bias_steps[level])
        )

    def bias_end():
        level = len(bias_copies) - 1
        bias_copies[level].wait()
        bias_total.append(bias_total[-1] + bias_in[level])

    def split(values):
        return values.astype(BF16).reshape(dp_count, ctx_count, -1, values.shape[1])

    def cross(part):
        return [
            wire.send(part[0].at[:, c ^ (2 * k + 1)], part[1].at[k], ctx=c ^ 1) for k in halves
        ]

    def add_core(part, copies):
        for k, copy in zip(halves, copies):
            copy.wait()
            own = part[0][:, pl.ds(c ^ (2 * k), 1)][:, 0]
            part[2][k] = (own.astype(F32) + part[1][k].astype(F32)).astype(BF16)

    def dp_send(part, level, sides):
        copies, bit = [], dp_bits[level]
        for m in range(bit, dp_count, 2 * bit):
            for k in sides:
                spot = part[3].at[level, k, d ^ m]
                copies.append((m ^ bit, k, wire.send(part[2].at[k, d ^ m], spot, dp=d ^ bit)))
        return copies

    def dp_add(part, level, copies):
        for m, k, copy in copies:
            copy.wait()
            own = part[2][k, pl.ds(d ^ m, 1)][0]
            other = part[3][level, k, pl.ds(d ^ m, 1)][0]
            part[2][k, pl.ds(d ^ m, 1)] = (own.astype(F32) + other.astype(F32)).astype(BF16)[None]

    def x_send(part):
        return wire.send(part[2].at[1], part[4], ctx=c ^ 2)

    def x_add(part, copy):
        copy.wait()
        part[2][0] = (part[2][0].astype(F32) + part[4][...].astype(F32)).astype(BF16)

    bias_begin()
    sources = (value_ref, key_ref)
    near = [
        [
            wire.send(ref.at[(2 * k + 1) * tokens : (2 * k + 2) * tokens], near_in.at[side, k],
                      ctx=c ^ 1)
            for k in (1, 0)
        ]
        for side, ref in enumerate(sources)
    ]
    slots, share = out_send.shape
    far_loads = [
        pltpu.make_async_copy(
            source, out_back.at[(k + 2) * slots : (k + 3) * slots], near_sems.at[tp_count + k]
        )
        for k, source in enumerate(far_outs)
    ]
    for copy in near_loads + loads + far_loads:
        copy.start()
    for copy in near_loads:
        copy.wait()
    sums = [tree_sum([land[m].astype(F32) for land in near_land]) for m in range(2)]
    out_back[:slots, :] = sums[0].astype(BF16)
    out_send[...] = sums[1].astype(BF16)
    out_home = wire.send(out_send, out_back.at[slots : 2 * slots], dp=d ^ 1)
    far_copies = []
    for side, ref in enumerate(sources):
        for k, copy in zip((1, 0), near[side]):
            copy.wait()
            rows = slice(2 * k * tokens, (2 * k + 1) * tokens)
            far_send[side, k] = (
                ref[rows, :].astype(F32) + near_in[side, k].astype(F32)
            ).astype(BF16)
            if k:
                if side == 0:
                    bias_end()
                    bias_begin()
                far_copies.append(wire.send(far_send.at[side, 1], far_in.at[side], ctx=c ^ 2))

    for copy in loads[:5]:
        copy.wait()
    first[0][:, :, :, :width] = split(mm(normed_ref[...], query_grad_ref[...]))
    first[0][:, :, :, width:] = split(mm(low_ref[...], attended_ref[...], TN))
    first_crossed = cross(first)
    token_grad[...] = mm(query_grad_ref[...], weight_ref[:, :width], NT)
    add_core(first, first_crossed)
    bias_end()
    bias_begin()
    first_moving = dp_send(first, 0, halves)
    for copy in loads[5:]:
        copy.wait()
    out_home.wait()
    for copy in far_loads:
        copy.wait()
    own_share = pl.ds(pl.multiple_of(t * share, share), share)
    mixed[:, own_share] = mm(picker_ref[...], out_back[...]).astype(BF16)
    mixed_part = mixed.at[:, own_share]
    mixed_copies = [wire.send(mixed_part, mixed_part, tp=t ^ k) for k in range(1, tp_count)]

    def land(side, columns):
        far_copies[side].wait()
        rows_all[:, columns] = (
            far_send[side, 0].astype(F32) + far_in[side].astype(F32)
        ).astype(BF16)

    key_columns, value_columns = slice(width, 2 * width), slice(2 * width, 3 * width)
    land(0, value_columns)
    value[0][...] = split(mm(normed_ref[...], rows_all[:, value_columns]))
    value_crossed = cross(value)
    token_grad[...] += mm(rows_all[:, value_columns], weight_ref[:, value_columns], NT)
    add_core(value, value_crossed)
    value_far = x_send(value)
    inputs = hidden_ref[...].astype(F32)
    scale = lax.rsqrt(jnp.mean(inputs * inputs, axis=-1, keepdims=True) + NORM_EPS)

    land(1, key_columns)
    part = token_grad[...] + mm(rows_all[:, key_columns], weight_ref[:, key_columns], NT)
    part_low = part.astype(BF16)
    gain_send[0] = fold_sum(part_low.astype(F32) * inputs * scale)
    token_in[0] = part_low
    gain_total = gain_send[0]
    gain_copies, token_copies = [], []
    tp_bits = bits_down(tp_count)[::-1]
    gain_copies.append(wire.send(gain_send.at[0], gain_in.at[0], tp=t ^ tp_bits[0]))
    token_copies.append(wire.send(token_in.at[0], token_in.at[1], tp=t ^ tp_bits[0]))
    key[0][:, :, :, :width] = split(mm(normed_ref[...], rows_all[:, key_columns]))
    for level, bit in enumerate(tp_bits):
        if level:
            gain_send[level] = gain_total
            gain_copies.append(wire.send(gain_send.at[level], gain_in.at[level], tp=t ^ bit))
        gain_copies[level].wait()
        gain_total = gain_total + gain_in[level]
    gain_one = jnp.sum(gain_total, axis=0, keepdims=True)
    gain_two = jnp.sum(gain_two_ref[...], axis=0, keepdims=True)
    row = lax.broadcasted_iota(jnp.int32, (LANES, D), 0)
    gain_rows = jnp.where(row == experts, gain_one, jnp.where(row == experts + 1, gain_two, 0.0))
    key[0][:, :, :, width:] = split(router_grad_ref[...] + gain_rows.T)
    key_crossed = cross(key)
    add_core(key, key_crossed)
    key_far = x_send(key)

    moving = {}
    first_far = None
    for level in range(len(dp_bits)):
        dp_add(first, level, first_moving)
        bias_end()
        if level + 1 < len(dp_bits):
            bias_begin()
            first_moving = dp_send(first, level + 1, halves)
        else:
            first_far = wire.send(first[2].at[1, d], first[4], ctx=c ^ 2)
        for name, weights, copy in (("value", value, value_far), ("key", key, key_far)):
            if level == 0:
                x_add(weights, copy)
            else:
                dp_add(weights, level - 1, moving[name])
            moving[name] = dp_send(weights, level, [0])
    total = part_low.astype(F32)
    for level, bit in enumerate(tp_bits):
        if level:
            token_in[2 * level] = total.astype(BF16)
            total = token_in[2 * level].astype(F32)
            token_copies.append(
                wire.send(token_in.at[2 * level], token_in.at[2 * level + 1], tp=t ^ bit)
            )
        token_copies[level].wait()
        total = total + token_in[2 * level + 1].astype(F32)
    weighted = gains_ref[0:1, :] * total
    inner = jnp.mean(inputs * weighted, axis=-1, keepdims=True)
    input_grad_ref[...] = (
        middle_grad_ref[...] + scale * weighted - inputs * (scale * scale * scale) * inner
    )
    bias_out_ref[...] = bias_total[-1]
    first_far.wait()
    first_ref[...] = first[2][0, pl.ds(d, 1)][0].astype(F32) + first[4][...].astype(F32)
    last = len(dp_bits) - 1
    dp_add(value, last, moving["value"])
    second_ref[:, width:] = value[2][0, pl.ds(d, 1)][0].astype(F32)
    dp_add(key, last, moving["key"])
    result = key[2][0, pl.ds(d, 1)][0].astype(F32)
    second_ref[:, :width] = result[:, :width]
    rest = jnp.zeros((LANES - result.shape[0], LANES), F32)
    tail_ref[...] = jnp.concatenate([result[:, width:], rest], axis=0).T
    for copy in mixed_copies:
        copy.wait()
    output_ref[...] = middle_ref[...] + mixed[...].astype(F32)
    wire.finish()


def final_step(
    query_grad, key_part, value_part, normed, weight, low, attended, router_grad, hidden,
    gains, gain_two, middle_grad, middle, picker, bias, outs, experts,
):
    tokens, width = query_grad.shape
    slots, share = outs[0].shape[1:]
    dp_count, ctx_count, tp_count = (lax.axis_size(a) for a in ("dp", "ctx", "tp"))
    rows = D // (dp_count * ctx_count)
    levels = len(bits_down(dp_count))
    tp_levels = len(bits_down(tp_count))
    copies = 7 + 2 + levels + 3 * 2 + 4 * dp_count + 3 + 2 * tp_levels + tp_count
    hbm = pl.BlockSpec(memory_space=pl.ANY)
    vmem = pl.BlockSpec(memory_space=pltpu.VMEM)
    shape = jax.ShapeDtypeStruct

    late = (
        query_grad, normed, low, attended, weight, hidden, router_grad, picker, middle,
        middle_grad,
    )

    def buffers(columns, far_shape, sides):
        return [
            pltpu.VMEM((dp_count, ctx_count, rows, columns), BF16),
            pltpu.VMEM((2, dp_count, rows, columns), BF16),
            pltpu.VMEM((2, dp_count, rows, columns), BF16),
            pltpu.VMEM((levels, sides, dp_count, rows, columns), BF16),
            pltpu.VMEM(far_shape + (columns,), BF16),
        ]

    return pl.pallas_call(
        functools.partial(final_kernel, experts, dp_count, ctx_count, tp_count),
        in_specs=[vmem] * 5 + [hbm] * (10 + len(outs)),
        out_specs=[vmem] * 6,
        out_shape=[
            shape((tokens, D), F32),
            shape((tokens, D), F32),
            shape(bias.shape, F32),
            shape((rows, 2 * width), F32),
            shape((rows, 2 * width), F32),
            shape((LANES, LANES), F32),
        ],
        scratch_shapes=[
            pltpu.VMEM((dp_count * slots, share), BF16),
            pltpu.VMEM((tokens, D), BF16),
            pltpu.VMEM((2 + levels,) + bias.shape, F32),
            pltpu.VMEM((2 + levels,) + bias.shape, F32),
            pltpu.VMEM((2, 2, tokens, width), BF16),
            pltpu.VMEM((2, 2, tokens, width), BF16),
            pltpu.VMEM((2, tokens, width), BF16),
            pltpu.VMEM((tokens, 3 * width), BF16),
            pltpu.VMEM((tokens, D), F32),
            pltpu.VMEM((2 * tp_levels, tokens, D), BF16),
            pltpu.VMEM((tp_levels, 8, D), F32),
            pltpu.VMEM((tp_levels, 8, D), F32),
            pltpu.VMEM((slots, share), BF16),
        ]
        + buffers(2 * width, (rows,), 2)
        + buffers(width, (dp_count, rows), 1)
        + buffers(width + LANES, (dp_count, rows), 1)
        + [pltpu.VMEM(array.shape, array.dtype) for array in late]
        + [pltpu.VMEM((2, slots, share), BF16)] * tp_count
        + [
            pltpu.SemaphoreType.DMA((copies,)),
            pltpu.SemaphoreType.DMA((copies,)),
            pltpu.SemaphoreType.DMA((10,)),
            pltpu.SemaphoreType.DMA((tp_count + dp_count,)),
        ],
        compiler_params=pltpu.CompilerParams(
            vmem_limit_bytes=VMEM_CAP, collective_id=2, has_side_effects=True
        ),
        cost_estimate=cost(87),
        name="final_step",
    )(key_part, value_part, gains, gain_two, bias, *late, *outs)


def adam_kernel(*refs):
    weight, first, second = refs[:3]
    parts, outs = refs[3:-4], refs[-4:]
    gradient = parts[0][...].astype(F32) + parts[1][...].astype(F32) + parts[2][...].astype(F32)
    first_new = BETA_ONE * first[...] + (1.0 - BETA_ONE) * gradient
    second_new = BETA_TWO * second[...] + (1.0 - BETA_TWO) * gradient * gradient
    outs[0][...] = gradient
    outs[1][...] = first_new
    outs[2][...] = second_new
    outs[3][...] = -MAIN_RATE * (
        first_new * (1.0 / FIX_ONE) / (jnp.sqrt(second_new * (1.0 / FIX_TWO)) + ADAM_EPS)
        + WEIGHT_DECAY * weight[...].astype(F32)
    )


def adam(weight, first, second, kept, arrived, far):
    count, rows, columns = weight.shape
    sizes = [size for size in range(16, rows + 1, 16) if rows % size == 0]
    step = max(k for k in sizes if k * columns <= 400000 and count * rows >= 2 * k)
    plain = pl.BlockSpec((1, step, columns), lambda i, j: (i, j, 0))
    shape = jax.ShapeDtypeStruct(weight.shape, F32)
    return pl.pallas_call(
        adam_kernel,
        grid=(count, rows // step),
        in_specs=[plain] * 6,
        out_specs=[plain] * 4,
        out_shape=[shape] * 4,
        compiler_params=pltpu.CompilerParams(vmem_limit_bytes=VMEM_CAP),
        cost_estimate=cost(5),
        name="adam",
    )(weight, first, second, kept, arrived, far)


def small_adam_kernel(experts, pairs, *refs):
    first_ref, second_ref, tail_ref, bias_ref = refs[:4]
    inputs, outs = refs[4:19], refs[19:]

    def step(k, gradient, part, rate):
        weight, first, second = (ref[part].astype(F32) for ref in inputs[3 * k : 3 * k + 3])
        first_new = BETA_ONE * first + (1.0 - BETA_ONE) * gradient
        second_new = BETA_TWO * second + (1.0 - BETA_TWO) * gradient * gradient
        update = -rate * (
            first_new * (1.0 / FIX_ONE) / (jnp.sqrt(second_new * (1.0 / FIX_TWO)) + ADAM_EPS)
            + WEIGHT_DECAY * weight
        )
        for out, values in zip(
            outs[4 * k : 4 * k + 4], (gradient, first_new, second_new, update)
        ):
            out[part] = values

    rows, width = inputs[3].shape
    whole = slice(None)
    step(0, first_ref[:, :width], 0, MAIN_RATE)
    step(0, second_ref[:, :width], 1, MAIN_RATE)
    step(0, second_ref[:, width:], 2, MAIN_RATE)
    step(1, first_ref[:, width:], whole, MAIN_RATE)
    step(2, tail_ref[:experts, :rows], whole, MAIN_RATE)
    step(3, tail_ref[experts : experts + 2, :rows], whole, MAIN_RATE)
    bias = jnp.concatenate([bias_ref[p, :2] for p in range(pairs)], axis=0)
    step(4, bias, whole, BIAS_RATE)


def small_adam(first_total, second_total, tail_total, bias_total, triples, experts):
    flat = [array for triple in triples for array in triple]
    vmem = pl.BlockSpec(memory_space=pltpu.VMEM)
    results = pl.pallas_call(
        functools.partial(small_adam_kernel, experts, bias_total.shape[0]),
        in_specs=[vmem] * (4 + len(flat)),
        out_specs=[vmem] * (4 * len(triples)),
        out_shape=[
            jax.ShapeDtypeStruct(triple[0].shape, F32) for triple in triples for _ in range(4)
        ],
        compiler_params=pltpu.CompilerParams(vmem_limit_bytes=VMEM_CAP),
        cost_estimate=cost(2),
        name="small_adam",
    )(first_total, second_total, tail_total, bias_total, *flat)
    return [results[4 * k : 4 * k + 4] for k in range(len(triples))]


def shards(
    hidden_in,
    out_grad,
    segments,
    routes,
    bucket_table,
    qkv_weight,
    out_weight,
    router,
    norm_gains,
    position_bias,
    expert_in,
    expert_down,
    qkv_first,
    qkv_second,
    out_first,
    out_second,
    router_first,
    router_second,
    gains_first,
    gains_second,
    bias_first,
    bias_second,
    in_first,
    in_second,
    down_first,
    down_second,
):
    tokens = hidden_in.shape[0]
    dp_count, ctx_count, tp_count = (lax.axis_size(a) for a in ("dp", "ctx", "tp"))
    dp_place, ctx_place, tp_place = (lax.axis_index(a) for a in ("dp", "ctx", "tp"))
    length = tokens * ctx_count
    heads_here = position_bias.shape[0]
    width_here = heads_here * HEAD_DIM
    pairs = heads_here // 2
    expert_count = router.shape[1]
    top_count = routes.shape[1]
    own_rows = router.shape[0]

    capacity = max(2, min(tokens, 5 * top_count * tokens // (4 * expert_count)))
    window_width = tokens + length
    table = jnp.pad(bucket_table[::-1], (0, 1), constant_values=BUCKETS)
    table = lax.dynamic_slice(table, (ctx_place * tokens,), (window_width,))
    table = jnp.broadcast_to(table[None], (8, window_width))
    qkv_view = [array.transpose(1, 0, 2) for array in (qkv_weight, qkv_first, qkv_second)]
    out_view = [array.T for array in (out_weight, out_first, out_second)]
    router_view = [array.T for array in (router, router_first, router_second)]
    (queries, key_values, normed_flip, qkv_flat, out_own, lanes, gains, info, doc_row, doc_col,
     picker_flip, picker_rows, grads_own, grads_half, early_land, expert_land) = start(
        qkv_view[0], out_view[0], router_view[0], norm_gains, hidden_in, segments, routes.T,
        out_grad, expert_in[0], capacity,
    )
    early = early_blocks(dp_count)
    arrived = [
        early_land[early.index(m)] if m in early else swap(grads_half[m - 1], "dp", m)
        for m in range(1, dp_count)
    ]
    half = pairs // 2
    attended_first, totals = attention(
        info, queries, key_values, position_bias, table, doc_row, doc_col, 0, half, ()
    )
    first_sides = gather_xor(attended_first, "tp")
    attended_second, totals = attention(
        info, queries, key_values, position_bias, table, doc_row, doc_col, half, pairs - half,
        (totals,),
    )
    results = expert_step(
        first_sides, attended_second, hidden_in, out_grad, gains, lanes, picker_flip, picker_rows,
        out_own, grads_own, arrived, expert_in[0], expert_land, expert_down[0], expert_count,
    )
    middle, router_grad, middle_grad, middle_low, attended_grad, gain_two_grad = results[:6]
    out_sums, results = results[6 : 4 + dp_count], results[4 + dp_count :]
    near_parts, results = results[:tp_count], results[tp_count:]
    attended, in_keep, in_core, in_sum, down_keep, down_core, down_far = results

    in_far = swap(in_sum, "ctx", 2)
    out_far = [swap(near_parts[k], "tp", k) for k in range(1, tp_count)]
    out_far += [swap(out_sums[m - 2], "dp", m) for m in range(2, dp_count)]
    query_grad, key_part, value_part, bias_part = attention_back(
        info, queries, key_values, attended_grad, totals, position_bias, table, doc_row, doc_col
    )
    query_grad, in_far, out_far = lax.optimization_barrier((query_grad, in_far, out_far))
    input_grad, output, bias_total, first_total, second_total, tail_total = final_step(
        query_grad, key_part, value_part, normed_flip, qkv_flat, middle_low, attended,
        router_grad, hidden_in, gains, gain_two_grad, middle_grad, middle, picker_flip, bias_part,
        [near_parts[0]] + out_far, expert_count,
    )
    qkv_all, out_new, router_new, gains_new, bias_new = small_adam(
        first_total, second_total, tail_total, bias_total,
        [
            qkv_view,
            out_view,
            router_view,
            (norm_gains, gains_first, gains_second),
            (position_bias, bias_first, bias_second),
        ],
        expert_count,
    )
    in_new = [
        values[None]
        for values in adam(
            expert_in[0], in_first[0], in_second[0], in_keep, in_core, in_far
        )
    ]
    down_new = adam(
        expert_down, down_first, down_second, down_keep[None], down_core[None], down_far[None]
    )
    return (
        output,
        input_grad,
        *[array.transpose(1, 0, 2) for array in qkv_all],
        *[array.T for array in out_new],
        *[array.T for array in router_new],
        *gains_new,
        *bias_new,
        *in_new,
        *down_new,
    )


def solution(mesh):
    token_rows = P(("dp", "ctx"), None)
    qkv = P(("dp", "ctx"), None, "tp")
    out = P("tp", ("dp", "ctx"))
    gains = P(None, ("dp", "ctx"))
    bias = P("tp", None)
    expert_in = P("dp", None, "ctx", "tp")
    expert_down = P("dp", "tp", "ctx")
    placed = (
        token_rows, token_rows, P("dp", "ctx"), token_rows, P(),
        qkv, out, token_rows, gains, bias, expert_in, expert_down,
        qkv, qkv, out, out, token_rows, token_rows, gains, gains, bias, bias,
        expert_in, expert_in, expert_down, expert_down,
    )
    return jax.shard_map(
        shards,
        mesh=mesh,
        in_specs=placed,
        out_specs=(token_rows, token_rows)
        + (qkv,) * 4
        + (out,) * 4
        + (token_rows,) * 4
        + (gains,) * 4
        + (bias,) * 4
        + (expert_in,) * 4
        + (expert_down,) * 4,
        check_vma=False,
    )
```
